32 devices in a mesh: ctx: 4 (over y, x), tp: 8 (over z, core).
Axes of the slice: x: 2, y: 2, z: 4, core: 2. Of those that a mesh axis runs over, the one named last changes fastest.
Arguments:
- tokens: bfloat16 [512, 4096], P('ctx'), may hold values from -6 to 6
- new_token_states: bfloat16 [4, 4096], replicated, may hold values from -6.0625 to 6.0625
- w_query: bfloat16 [4096, 2048], P('ctx', 'tp'), may hold values from -0.12162204 to 0.12162204
- key_matrix: bfloat16 [4096, 1024], P('ctx', 'tp'), may hold values from -0.12162204 to 0.12162204
- value_matrix: bfloat16 [4096, 1024], P('ctx', 'tp'), may hold values from -0.09375 to 0.09375
- w_out: bfloat16 [2048, 4096], P('tp', 'ctx'), may hold values from -0.125 to 0.125
- lengths: int32 [4], replicated, may hold values from 1 to 256, 512 in all
- block_map: int32 [8], replicated, may hold values from 0 to 7, each once
Outputs:
- prefill_out: bfloat16 [512, 4096], P('ctx', 'tp')
- decode_out: bfloat16 [4, 4096], P(None, 'tp')
The draws below stay inside these ranges and needn't reach their ends.
Inputs may be any that keep to these rules, and one draw needn't show every extreme that they name: The lengths sum to 512, and some request has exactly 256 tokens. `block_map`: each of the 8 initial blocks is held exactly once.
All inputs are finite; a program needn't handle non-finite values.
Results may differ from the reference program's by a relative error of at most 0.015.
Values may be sent and summed in bfloat16 or wider, within the bound.
No kernel may reach another device: no remote copies, remote signals or barrier semaphores. Data moves between devices by JAX's collectives and lax.ppermute only.
A program may use at most 64 MiB of HBM per device.

```python
import math
import jax
import jax.numpy as jnp
import numpy as np
from jax import lax

MODEL_WIDTH = 4096
QUERY_HEAD_COUNT = 16
KEY_VALUE_HEADS = 8
HEAD_SIZE = 128
REQUEST_COUNT = 4
BLOCK = 64
PROMPT_TOKENS = 512
NBLOCKS = 8
LONGEST_PROMPT = 256


def draw_w_query(key, part):
    random_jitter = jax.random.truncated_normal(jax.random.fold_in(key, 101), -6.0, 6.0, (MODEL_WIDTH, QUERY_HEAD_COUNT * HEAD_SIZE), jnp.float32)
    random_jitter = random_jitter * MODEL_WIDTH ** (-0.5)
    return random_jitter.astype(jnp.bfloat16)


def draw_key_matrix(key, part):
    random_jitter = jax.random.truncated_normal(jax.random.fold_in(key, 202), -6.0, 6.0, (MODEL_WIDTH, KEY_VALUE_HEADS * HEAD_SIZE), jnp.float32)
    random_jitter = random_jitter * MODEL_WIDTH ** (-0.5)
    return random_jitter.astype(jnp.bfloat16)


def draw_new_token_states(key, part):
    values = jax.random.truncated_normal(jax.random.fold_in(key, 303), -6.0, 6.0, (REQUEST_COUNT, MODEL_WIDTH), jnp.float32)
    return values.astype(jnp.bfloat16)


def block_levels(key, dims, pieces, low, high):
    gain, own = 1.0, jax.random.fold_in(key, 6)
    for position, blocks in pieces:
        steps = jnp.exp(jax.random.uniform(jax.random.fold_in(own, position), (blocks,), jnp.float32, low / len(pieces), high / len(pieces)))
        gain = gain * jnp.repeat(steps, dims[position] // blocks).reshape([-1 if axis == position else 1 for axis in range(len(dims))])
    return gain


def length_profile(amount, total, reach, skew):
    weights = [(1 << 20) // math.isqrt(grade ** skew) + 1 for grade in range(2, amount + 1)]
    surplus, counts = total - reach - (amount - 1), [1] * (amount - 1)
    while surplus > 0:
        free = [i for i in range(amount - 1) if counts[i] < reach]
        mass, budget = sum([weights[i] for i in free]), surplus
        for i in free:
            addition = min(reach - counts[i], max(1, budget * weights[i] // mass), surplus)
            counts[i] = counts[i] + addition
            surplus = surplus - addition
    return np.array([reach] + counts)


def ragged_sizes(key, count, total, reach, lean):
    if count == 2:
        one = jax.random.randint(key, (), max(1, total - reach), min(reach, total - 1) + 1)
        return jnp.stack([one, total - one])
    sizes = jnp.asarray(length_profile(count, total, reach, lean), jnp.int32)
    pairs = (count - 1) // 2
    source_of, receiver = sizes[1:1 + 2 * pairs:2], sizes[2:2 + 2 * pairs:2]
    room = jnp.minimum(source_of - 1, reach - receiver)
    moved = jax.random.randint(jax.random.fold_in(key, 1), (pairs,), 0, 1 << 20) % (room + 1)
    sizes = sizes.at[1:1 + 2 * pairs:2].set(source_of - moved).at[2:2 + 2 * pairs:2].set(receiver + moved)
    return sizes[jax.random.permutation(jax.random.fold_in(key, 2), count)]


def normal_values(rng, dims, spread, bound, cuts=(), kind=jnp.bfloat16):
    drawn = jax.random.normal(rng, dims, jnp.float32) * spread
    if len(cuts) > 0:
        drawn = block_levels(rng, dims, cuts, -0.22, 0.18) * drawn
    return jnp.clip(drawn, min=-bound, max=bound).astype(kind)


def setup_inputs(seed: int = 0) -> dict:
    keys = jax.random.split(jax.random.key(seed), 9)
    tokens = normal_values(keys[0], (PROMPT_TOKENS, MODEL_WIDTH), 1.0, 6.0, ((0, 4),))
    new_token_states = draw_new_token_states(jax.random.fold_in(keys[8], 71), 0)
    w_query = draw_w_query(jax.random.fold_in(keys[8], 71), 0)
    key_matrix = draw_key_matrix(jax.random.fold_in(keys[8], 71), 0)
    value_matrix = normal_values(keys[4], (MODEL_WIDTH, KEY_VALUE_HEADS * HEAD_SIZE), MODEL_WIDTH ** -0.5, 0.09375, ((0, 4), (1, 8)))
    w_out = normal_values(keys[5], (QUERY_HEAD_COUNT * HEAD_SIZE, MODEL_WIDTH), (QUERY_HEAD_COUNT * HEAD_SIZE) ** -0.5, 0.125, ((0, 8), (1, 4)))
    lengths = ragged_sizes(keys[6], REQUEST_COUNT, PROMPT_TOKENS, LONGEST_PROMPT, 2).astype(jnp.int32)
    block_map = jax.random.permutation(keys[7], NBLOCKS).astype(jnp.int32)
    return dict(tokens=tokens, new_token_states=new_token_states, w_query=w_query, key_matrix=key_matrix, value_matrix=value_matrix, w_out=w_out, lengths=lengths, block_map=block_map)


def initial_positions(block_map, row_count):
    row_ids = jnp.arange(row_count, dtype=jnp.int32)
    return block_map[row_ids // BLOCK] * BLOCK + row_ids % BLOCK

def request_index(positions, lengths):
    request_ends = jnp.cumsum(lengths).astype(jnp.int32)
    return lax.optimization_barrier(jnp.sum((positions[:, None] >= request_ends[None, :]).astype(jnp.int32), axis=1))

def project_rows(inputs, weight):
    return jnp.dot(inputs, weight, preferred_element_type=jnp.float32).astype(jnp.bfloat16)

def round_weights(weights):
    rounded = weights.astype(jnp.bfloat16)
    rounded = lax.optimization_barrier(rounded)
    return rounded.astype(jnp.float32)

def reference(tokens, new_token_states, w_query, key_matrix, value_matrix, w_out, lengths, block_map):
    query_group_count = QUERY_HEAD_COUNT // KEY_VALUE_HEADS
    score_scale = 1.0 / math.sqrt(HEAD_SIZE)
    queries = project_rows(tokens, w_query).reshape(PROMPT_TOKENS, QUERY_HEAD_COUNT, HEAD_SIZE)
    projected_key_rows = project_rows(tokens, key_matrix).reshape(PROMPT_TOKENS, KEY_VALUE_HEADS, HEAD_SIZE)
    projected_value_rows = project_rows(tokens, value_matrix).reshape(PROMPT_TOKENS, KEY_VALUE_HEADS, HEAD_SIZE)
    positions = initial_positions(block_map, PROMPT_TOKENS)
    inverse = jnp.zeros((PROMPT_TOKENS,), jnp.int32).at[positions].set(jnp.arange(PROMPT_TOKENS, dtype=jnp.int32))
    query_orig = queries[inverse]
    key_baseline = projected_key_rows[inverse]
    value_baseline = projected_value_rows[inverse]
    request_orig = request_index(jnp.arange(PROMPT_TOKENS, dtype=jnp.int32), lengths)
    filled_key_cache = jnp.concatenate([jnp.zeros((LONGEST_PROMPT, KEY_VALUE_HEADS, HEAD_SIZE), jnp.bfloat16), key_baseline], axis=0)
    filled_value_cache = jnp.concatenate([jnp.zeros((LONGEST_PROMPT, KEY_VALUE_HEADS, HEAD_SIZE), jnp.bfloat16), value_baseline], axis=0)
    padded_request = jnp.concatenate([jnp.full((LONGEST_PROMPT,), -1, jnp.int32), request_orig], axis=0)
    block_rows = min(256, PROMPT_TOKENS)
    window = LONGEST_PROMPT + block_rows

    def attend_block(block_index):
        first_row = (block_index * block_rows).astype(jnp.int32)
        query_block = lax.dynamic_slice_in_dim(query_orig, first_row, block_rows, 0).astype(jnp.float32)
        key_block = lax.dynamic_slice_in_dim(filled_key_cache, first_row, window, 0).astype(jnp.float32)
        value_block = lax.dynamic_slice_in_dim(filled_value_cache, first_row, window, 0).astype(jnp.float32)
        request_query = lax.dynamic_slice_in_dim(request_orig, first_row, block_rows, 0)
        request_key = lax.dynamic_slice_in_dim(padded_request, first_row, window, 0)
        query_pos = first_row + jnp.arange(block_rows, dtype=jnp.int32)
        key_pos = first_row - LONGEST_PROMPT + jnp.arange(window, dtype=jnp.int32)
        allowed = (request_key[None, :] == request_query[:, None]) & (key_pos[None, :] <= query_pos[:, None])
        key_heads = jnp.repeat(key_block, query_group_count, axis=1)
        value_heads = jnp.repeat(value_block, query_group_count, axis=1)
        scores = jnp.einsum('qhd,khd->hqk', query_block, key_heads) * score_scale
        scores = jnp.where(allowed[None], scores, -jnp.inf)
        row_peak = lax.optimization_barrier(jnp.max(scores, axis=2, keepdims=True))
        weights = jnp.exp(scores - row_peak)
        denominator = lax.optimization_barrier(jnp.sum(weights, axis=2))
        mixed_sum = jnp.einsum('hqk,khd->qhd', round_weights(weights), value_heads)
        return (mixed_sum / denominator.T[:, :, None]).astype(jnp.bfloat16)
    attended = lax.map(attend_block, jnp.arange(PROMPT_TOKENS // block_rows, dtype=jnp.int32))
    attended = attended.reshape(PROMPT_TOKENS, QUERY_HEAD_COUNT * HEAD_SIZE)[positions]
    dec_query = project_rows(new_token_states, w_query).reshape(REQUEST_COUNT, QUERY_HEAD_COUNT, HEAD_SIZE).astype(jnp.float32)
    decode_key_rows = jnp.repeat(project_rows(new_token_states, key_matrix).reshape(REQUEST_COUNT, KEY_VALUE_HEADS, HEAD_SIZE).astype(jnp.float32), query_group_count, axis=1)
    decode_value_rows = jnp.repeat(project_rows(new_token_states, value_matrix).reshape(REQUEST_COUNT, KEY_VALUE_HEADS, HEAD_SIZE).astype(jnp.float32), query_group_count, axis=1)
    key_all = jnp.repeat(key_baseline.astype(jnp.float32), query_group_count, axis=1)
    value_all = jnp.repeat(value_baseline.astype(jnp.float32), query_group_count, axis=1)
    cache_scores = jnp.einsum('rhd,thd->rht', dec_query, key_all) * score_scale
    owned = request_orig[None, :] == jnp.arange(REQUEST_COUNT, dtype=jnp.int32)[:, None]
    cache_scores = jnp.where(owned[:, None, :], cache_scores, -jnp.inf)
    self_scores = lax.optimization_barrier(jnp.sum(dec_query * decode_key_rows, axis=2)) * score_scale
    row_peak = jnp.maximum(lax.optimization_barrier(jnp.max(cache_scores, axis=2)), self_scores)
    cache_weights = jnp.exp(cache_scores - row_peak[:, :, None])
    self_weights = jnp.exp(self_scores - row_peak)
    denominator = lax.optimization_barrier(jnp.sum(cache_weights, axis=2)) + self_weights
    mixed_sum = jnp.einsum('rht,thd->rhd', round_weights(cache_weights), value_all)
    mixed_sum = mixed_sum + round_weights(self_weights)[:, :, None] * decode_value_rows
    dec_attn = (mixed_sum / denominator[:, :, None]).astype(jnp.bfloat16).reshape(REQUEST_COUNT, QUERY_HEAD_COUNT * HEAD_SIZE)
    prefill_out = jnp.dot(attended, w_out, preferred_element_type=jnp.float32).astype(jnp.bfloat16)
    decode_out = jnp.dot(dec_attn, w_out, preferred_element_type=jnp.float32).astype(jnp.bfloat16)
    return (prefill_out, decode_out)
```

```python
import functools
import math

import jax
import jax.numpy as jnp
from jax import lax
from jax.experimental import pallas as pl
from jax.experimental.pallas import tpu as pltpu
from jax.sharding import PartitionSpec as P

HEAD_SIZE = 128
FLOOR = -1e30
LAST = 1 << 30
ROW_TILE = 8
VMEM_BYTES = 48 * 1024 * 1024


def vmem():
    return pl.BlockSpec(memory_space=pltpu.VMEM)


def smem():
    return pl.BlockSpec(memory_space=pltpu.SMEM)


def hbm():
    return pl.BlockSpec(memory_space=pl.ANY)


def params():
    return pltpu.CompilerParams(vmem_limit_bytes=VMEM_BYTES)


def slice_kernel(place, tokens, *rest):
    outs, sem = rest[:-1], rest[-1]
    rows, width = outs[0].shape
    first = pl.multiple_of(place[2] * rows, rows)
    copies = []
    for step, out in enumerate(outs, 1):
        column = pl.multiple_of((place[0] ^ step) * width, width)
        copies.append(
            pltpu.make_async_copy(
                tokens.at[pl.ds(first, rows), pl.ds(column, width)], out, sem.at[step - 1]
            )
        )
    for copy in copies:
        copy.start()
    for copy in copies:
        copy.wait()


def project_kernel(steps, place, own, *rest):
    blocks, rest = (own,) + rest[: steps - 1], rest[steps - 1 :]
    new, wq, wq2, wk, wk2, wv, wv2 = rest[:7]
    outs, inputs = rest[7 : 7 + steps], rest[7 + steps]
    rows = own.shape[0]
    count = new.shape[0]
    tail = steps * rows
    for step, block in enumerate(blocks):
        inputs[step * rows : (step + 1) * rows, :] = block[...]
    inputs[tail:, :] = jnp.zeros_like(inputs[tail:, :])
    inputs[tail : tail + count, :] = new[...]
    x = inputs[...]
    column = 0
    pad = outs[0].shape[0] - rows
    for first, second in ((wq, wq2), (wk, wk2), (wv, wv2)):
        weight = jnp.concatenate([first[...], second[...]], axis=1)
        part = jnp.dot(x, weight, preferred_element_type=jnp.float32)
        to = slice(column, column + weight.shape[1])
        for step, out in enumerate(outs):
            out[:rows, to] = part[step * rows : (step + 1) * rows].astype(out.dtype)
            out[rows:, to] = part[tail : tail + pad].astype(out.dtype)
        column += weight.shape[1]


def add_kernel(steps, *refs):
    parts, (query, keyval, new) = refs[:steps], refs[steps:]
    rows = query.shape[0]
    total = parts[0][...]
    for part in parts[1:]:
        total = total + part[...].astype(jnp.float32)
    total = total.astype(jnp.bfloat16)
    half = query.shape[1]
    query[...] = total[:rows, :half]
    keyval[...] = total[:rows, half:]
    new[...] = total[rows:]


def request_of(position, ends):
    found = jnp.zeros_like(position)
    for end in ends:
        found = found + jnp.where(position >= end, 1, 0)
    return found


def attend_kernel(steps, count, scale, place, block_map, lengths, *refs):
    queries, refs = refs[:steps], refs[steps:]
    mine, refs = refs[:steps], refs[steps:]
    theirs, refs = refs[:steps], refs[steps:]
    new, w_own, w_other = refs[:3]
    outs, (q_all, key_all, value_all, attended, result) = refs[3 : 3 + 2 * steps], refs[3 + 2 * steps :]
    rows, q_width = queries[0].shape
    kv_width = q_width // 2
    head = HEAD_SIZE
    groups = kv_width // head
    per_group = q_width // kv_width
    pad = new.shape[0]
    tail = steps * rows
    q_rows = q_all.shape[0]
    k_rows = key_all.shape[0]
    k_tail = 2 * tail
    c, z, k = place[0], place[1], place[2]

    q_all[tail:, :] = jnp.zeros_like(q_all[tail:, :])
    key_all[k_tail:, :] = jnp.zeros_like(key_all[k_tail:, :])
    value_all[k_tail:, :] = jnp.zeros_like(value_all[k_tail:, :])
    for step in range(steps):
        at = slice(step * rows, (step + 1) * rows)
        q_all[at, :] = queries[step][...]
        key_all[at, :] = mine[step][:, :kv_width]
        value_all[at, :] = mine[step][:, kv_width:]
        at = slice(tail + step * rows, tail + (step + 1) * rows)
        half = kv_width // 2
        key_all[at, :half] = theirs[step][:, half:kv_width]
        key_all[at, half:] = theirs[step][:, :half]
        value_all[at, :half] = theirs[step][:, kv_width + half :]
        value_all[at, half:] = theirs[step][:, kv_width : kv_width + half]
    q_all[tail : tail + pad, :] = new[:, :q_width]
    key_all[k_tail : k_tail + pad, :] = new[:, q_width : q_width + kv_width]
    value_all[k_tail : k_tail + pad, :] = new[:, q_width + kv_width :]

    ends, total = [], 0
    for request in range(count):
        total = total + lengths[request]
        ends.append(total)

    def labels(shape, axis, halves):
        index = lax.broadcasted_iota(jnp.int32, shape, axis)
        position = jnp.zeros(shape, jnp.int32)
        for number in range(halves * steps):
            held = 2 * (c ^ (number % steps)) + (k ^ (number // steps))
            inside = (index >= number * rows) & (index < (number + 1) * rows)
            position = jnp.where(inside, block_map[held] * rows + index - number * rows, position)
        last = halves * tail
        is_new = index >= last
        request = jnp.where(is_new, index - last, request_of(position, ends))
        return jnp.where(is_new, LAST, position), request

    q_position, q_request = labels((q_rows, 1), 0, 1)
    k_position, k_request = labels((1, k_rows), 1, 2)
    allowed = (q_request == k_request) & (k_position <= q_position)

    for group in range(groups):
        keys = key_all[:, group * head : (group + 1) * head]
        values = value_all[:, group * head : (group + 1) * head]
        for member in range(per_group):
            at = (group * per_group + member) * head
            scores = lax.dot_general(
                q_all[:, at : at + head],
                keys,
                (((1,), (1,)), ((), ())),
                preferred_element_type=jnp.float32,
            )
            scores = jnp.where(allowed, scores * scale, FLOOR)
            weights = jnp.exp(scores - jnp.max(scores, axis=1, keepdims=True))
            denom = jnp.sum(weights, axis=1, keepdims=True)
            mixed = jnp.dot(
                weights.astype(jnp.bfloat16), values, preferred_element_type=jnp.float32
            )
            attended[:, at : at + head] = (mixed / denom).astype(jnp.bfloat16)

    rows_own = w_own.shape[0]
    result[...] = (
        jnp.dot(attended[:, :rows_own], w_own[...], preferred_element_type=jnp.float32)
        + jnp.dot(attended[:, rows_own:], w_other[...], preferred_element_type=jnp.float32)
    ).astype(jnp.bfloat16)
    width = outs[0].shape[1]
    for step in range(steps):
        first = pl.multiple_of((c ^ z ^ step) * rows, rows)
        for other in range(2):
            column = pl.multiple_of((k ^ other) * width, width)
            out = outs[2 * step + other]
            out[:rows, :] = result[pl.ds(first, rows), pl.ds(column, width)]
            out[rows:, :] = result[tail : tail + pad, pl.ds(column, width)]


def finish_kernel(steps, place, *refs):
    parts, (prefill, decode) = refs[: 2 * steps], refs[2 * steps :]
    rows = prefill.shape[0] // 2
    count = decode.shape[0]

    def tree(terms):
        while len(terms) > 1:
            terms = [a + b for a, b in zip(terms[::2], terms[1::2])]
        return terms[0]

    for other in range(2):
        total = tree([parts[2 * step + other][...].astype(jnp.float32) for step in range(steps)])
        total = total.astype(jnp.bfloat16)
        prefill[pl.ds(pl.multiple_of((place[2] ^ other) * rows, rows), rows), :] = total[:rows]
        if other == 0:
            decode[...] = total[rows : rows + count]


def on_device_small(
    steps, tp, tokens, new_token_states, w_query, key_matrix, value_matrix, w_out, lengths, block_map
):
    bf16, f32 = jnp.bfloat16, jnp.float32
    rows = tokens.shape[0] // 2
    depth = w_query.shape[0]
    count = new_token_states.shape[0]
    pad = -(-count // ROW_TILE) * ROW_TILE
    q_width = 2 * w_query.shape[1]
    kv_width = 2 * key_matrix.shape[1]
    features = q_width + 2 * kv_width
    width = w_out.shape[1] // 2
    c, t = lax.axis_index("ctx"), lax.axis_index("tp")
    place = jnp.stack([c, t // 2, t % 2]).astype(jnp.int32)

    def to_core(value):
        return lax.ppermute(value, "tp", [(i, i ^ 1) for i in range(tp)])

    def to_ctx(value, step):
        return lax.ppermute(value, "ctx", [(i, i ^ step) for i in range(steps)])

    sent = pl.pallas_call(
        slice_kernel,
        out_shape=[jax.ShapeDtypeStruct((rows, depth), bf16)] * (steps - 1),
        in_specs=[smem(), hbm()],
        out_specs=[hbm()] * (steps - 1),
        scratch_shapes=[pltpu.SemaphoreType.DMA((steps - 1,))],
        name="slice_tokens",
    )(place, tokens)
    got = [to_ctx(value, step) for step, value in enumerate(sent, 1)]
    wq2, wk2, wv2, wo2 = (to_core(w) for w in (w_query, key_matrix, value_matrix, w_out))

    def whole(shape):
        return pl.BlockSpec(shape, lambda i, at: (0,) * len(shape))

    part_shape = (rows + pad, features)
    x_rows = -(-(steps * rows + pad) // 16) * 16
    weights = (w_query, wq2, key_matrix, wk2, value_matrix, wv2)
    parts = pl.pallas_call(
        functools.partial(project_kernel, steps),
        out_shape=[jax.ShapeDtypeStruct(part_shape, f32)]
        + [jax.ShapeDtypeStruct(part_shape, bf16)] * (steps - 1),
        grid_spec=pltpu.PrefetchScalarGridSpec(
            num_scalar_prefetch=1,
            grid=(1,),
            in_specs=[pl.BlockSpec((rows, depth), lambda i, at: (at[2], at[0]))]
            + [whole((rows, depth))] * (steps - 1)
            + [pl.BlockSpec((count, depth), lambda i, at: (0, at[0]))]
            + [whole(w.shape) for w in weights],
            out_specs=[whole(part_shape)] * steps,
            scratch_shapes=[pltpu.VMEM((x_rows, depth), bf16)],
        ),
        compiler_params=params(),
        name="project",
    )(place, tokens, *got, new_token_states, *weights)

    parts = [parts[0]] + [to_ctx(part, step) for step, part in enumerate(parts[1:], 1)]
    query, keyval, new = pl.pallas_call(
        functools.partial(add_kernel, steps),
        out_shape=[
            jax.ShapeDtypeStruct((rows, q_width), bf16),
            jax.ShapeDtypeStruct((rows, 2 * kv_width), bf16),
            jax.ShapeDtypeStruct((pad, features), bf16),
        ],
        in_specs=[vmem()] * steps,
        out_specs=[vmem()] * 3,
        compiler_params=params(),
        name="add_parts",
    )(*parts)

    mine = [keyval] + [to_ctx(keyval, step) for step in range(1, steps)]
    queries = [query] + [to_ctx(query, step) for step in range(1, steps)]
    theirs = [to_core(value) for value in mine]

    k_rows = -(-(2 * steps * rows + pad) // 128) * 128
    out_shape = (rows + pad, width)
    outs = pl.pallas_call(
        functools.partial(attend_kernel, steps, count, 1.0 / math.sqrt(HEAD_SIZE)),
        out_shape=[jax.ShapeDtypeStruct(out_shape, bf16)] * (2 * steps),
        in_specs=[smem()] * 3 + [vmem()] * (3 * steps + 3),
        out_specs=[vmem()] * (2 * steps),
        scratch_shapes=[
            pltpu.VMEM((x_rows, q_width), bf16),
            pltpu.VMEM((k_rows, kv_width), bf16),
            pltpu.VMEM((k_rows, kv_width), bf16),
            pltpu.VMEM((x_rows, q_width), bf16),
            pltpu.VMEM((x_rows, 2 * width), bf16),
        ],
        compiler_params=params(),
        name="attend",
    )(place, block_map, lengths, *queries, *mine, *theirs, new, w_out, wo2)

    def to_owner(value, step, other):
        pairs = []
        for source in range(steps * tp):
            at, rest = divmod(source, tp)
            z, core = divmod(rest, 2)
            pairs.append((source, (z ^ step) * tp + 2 * at + (core ^ other)))
        return lax.ppermute(value, ("ctx", "tp"), pairs)

    arrived = [to_owner(value, i // 2, i % 2) for i, value in enumerate(outs)]
    return tuple(
        pl.pallas_call(
            functools.partial(finish_kernel, steps),
            out_shape=[
                jax.ShapeDtypeStruct((2 * rows, width), bf16),
                jax.ShapeDtypeStruct((count, width), bf16),
            ],
            in_specs=[smem()] + [vmem()] * (2 * steps),
            out_specs=[vmem()] * 2,
            compiler_params=params(),
            name="finish",
        )(place, *arrived)
    )


floor_value = -1e30


def initial_positions(block_map, first_row, row_count, block_rows):
    row_ids = first_row + jnp.arange(row_count, dtype=jnp.int32)
    block_ids = row_ids // block_rows
    table_ids = jnp.arange(block_map.shape[0], dtype=jnp.int32)
    mapped = jnp.sum(
        jnp.where(block_ids[:, None] == table_ids[None, :], block_map[None, :], 0), axis=1
    )
    return mapped * block_rows + row_ids % block_rows


def request_index(positions, request_ends):
    return jnp.sum((positions[:, None] >= request_ends[None, :]).astype(jnp.int32), axis=1)


def round_weights(weights):
    rounded = weights.astype(jnp.bfloat16)
    rounded = lax.optimization_barrier(rounded)
    return rounded.astype(jnp.float32)


def softmax_parts(
    dec_heads, projected_key_rows, projected_value_rows, owned, kv_heads, head_dim, score_scale
):
    row_count = projected_key_rows.shape[0]
    scores = (
        jnp.einsum(
            "rgjd,tgd->rgjt",
            dec_heads,
            projected_key_rows.reshape(row_count, kv_heads, head_dim),
            preferred_element_type=jnp.float32,
        )
        * score_scale
    )
    scores = jnp.where(owned, scores, floor_value)
    part_peak = jnp.max(scores, axis=3)
    weights = jnp.where(owned, jnp.exp(scores - part_peak[..., None]), 0.0)
    part_total = jnp.sum(weights, axis=3)
    part_mixed = jnp.einsum(
        "rgjt,tgd->rgjd",
        weights.astype(jnp.bfloat16),
        projected_value_rows.reshape(row_count, kv_heads, head_dim),
        preferred_element_type=jnp.float32,
    )
    return (part_peak, part_total, part_mixed)


def on_device_large(
    tokens, new_token_states, w_query, key_matrix, value_matrix, w_out, lengths, block_map
):
    local_rows = tokens.shape[0]
    block_rows = local_rows // 2
    request_count = new_token_states.shape[0]
    head_dim = HEAD_SIZE
    query_width = w_query.shape[1]
    kv_width = key_matrix.shape[1]
    kv_heads = kv_width // head_dim
    query_group_count = query_width // kv_width
    score_scale = 1.0 / math.sqrt(head_dim)
    device = lax.axis_index("ctx")
    request_ends = jnp.cumsum(lengths)
    inputs = jnp.concatenate([tokens, new_token_states], axis=0)
    shard_pieces = (
        lax.all_gather(w_query, "ctx", axis=0, tiled=True),
        lax.all_gather(key_matrix, "ctx", axis=0, tiled=True),
        lax.all_gather(value_matrix, "ctx", axis=0, tiled=True),
    )
    query_all, key_all, value_all = tuple(
        (jnp.dot(inputs, weight, preferred_element_type=jnp.float32) for weight in shard_pieces)
    )
    query_all = query_all.astype(jnp.bfloat16)
    key_all = key_all.astype(jnp.bfloat16)
    value_all = value_all.astype(jnp.bfloat16)
    local_query = query_all[:local_rows]
    local_keys = key_all[:local_rows]
    local_values = value_all[:local_rows]
    dec_query = query_all[local_rows:]
    decode_key_rows = key_all[local_rows:]
    decode_value_rows = value_all[local_rows:]
    token_pos = initial_positions(block_map, device * local_rows, local_rows, block_rows)
    token_request = request_index(token_pos, request_ends)
    query_heads = local_query.reshape(local_rows, kv_heads, query_group_count, head_dim)

    def attend(running, shard_pieces, first_row):
        peak_run, total_run, mixed_run = running
        key_piece, value_piece = shard_pieces
        row_count = key_piece.shape[0]
        key_pos = initial_positions(block_map, first_row, row_count, block_rows)
        key_request = request_index(key_pos, request_ends)
        allowed = (key_request[None, :] == token_request[:, None]) & (
            key_pos[None, :] <= token_pos[:, None]
        )
        scores = (
            jnp.einsum(
                "tgjd,kgd->gjtk",
                query_heads,
                key_piece.reshape(row_count, kv_heads, head_dim),
                preferred_element_type=jnp.float32,
            )
            * score_scale
        )
        scores = jnp.where(allowed, scores, floor_value)
        peak_new = jnp.maximum(peak_run, jnp.max(scores, axis=3))
        weights = jnp.where(allowed, jnp.exp(scores - peak_new[..., None]), 0.0)
        rescale = jnp.exp(peak_run - peak_new)
        total_new = total_run * rescale + jnp.sum(weights, axis=3)
        mixed_new = mixed_run * rescale[..., None] + jnp.einsum(
            "gjtk,kgd->gjtd",
            weights.astype(jnp.bfloat16),
            value_piece.reshape(row_count, kv_heads, head_dim),
            preferred_element_type=jnp.float32,
        )
        return (peak_new, total_new, mixed_new)

    start_state = (
        jnp.full((kv_heads, query_group_count, local_rows), floor_value, jnp.float32),
        jnp.zeros((kv_heads, query_group_count, local_rows), jnp.float32),
        jnp.zeros((kv_heads, query_group_count, local_rows, head_dim), jnp.float32),
    )
    dec_heads = dec_query.reshape(request_count, kv_heads, query_group_count, head_dim)
    request_ids = jnp.arange(request_count, dtype=jnp.int32)
    cache_keys, cache_values = (
        lax.all_gather(local_keys, "ctx", axis=0, tiled=True),
        lax.all_gather(local_values, "ctx", axis=0, tiled=True),
    )
    total_rows = cache_keys.shape[0]
    shard_count = total_rows // local_rows
    limit = max(1, 1024 // local_rows)
    step_rows = local_rows * math.gcd(shard_count, 1 << limit.bit_length() - 1)

    def key_step(running, step_index):
        first_row = step_index * step_rows
        pieces = (
            lax.dynamic_slice_in_dim(cache_keys, first_row, step_rows, 0),
            lax.dynamic_slice_in_dim(cache_values, first_row, step_rows, 0),
        )
        return (attend(running, pieces, first_row), None)

    final_state, unused = lax.scan(
        key_step, start_state, jnp.arange(total_rows // step_rows, dtype=jnp.int32)
    )
    peak_run, total_run, mixed_run = final_state
    cache_pos = (
        block_map[:, None] * block_rows + jnp.arange(block_rows, dtype=jnp.int32)[None, :]
    ).reshape(total_rows)
    cache_request = request_index(cache_pos, request_ends)
    owned = (cache_request[None, :] == request_ids[:, None])[:, None, None, :]
    cache_peak, cache_total, cache_mixed = softmax_parts(
        dec_heads, cache_keys, cache_values, owned, kv_heads, head_dim, score_scale
    )
    attended = (
        (mixed_run / total_run[..., None]).transpose(2, 0, 1, 3).reshape(local_rows, query_width)
    )
    attended = attended.astype(jnp.bfloat16)
    own_keys = decode_key_rows.reshape(request_count, kv_heads, 1, head_dim).astype(jnp.float32)
    own_values = decode_value_rows.reshape(request_count, kv_heads, 1, head_dim).astype(jnp.float32)
    self_scores = jnp.sum(dec_heads.astype(jnp.float32) * own_keys, axis=3) * score_scale
    peak_all = jnp.maximum(cache_peak, self_scores)
    rescale = jnp.exp(cache_peak - peak_all)
    self_weights = jnp.exp(self_scores - peak_all)
    dec_total = cache_total * rescale + self_weights
    dec_mixed = (
        cache_mixed * rescale[..., None] + round_weights(self_weights)[..., None] * own_values
    )
    dec_attn = (
        (dec_mixed / dec_total[..., None]).reshape(request_count, query_width).astype(jnp.bfloat16)
    )
    attended_all = jnp.concatenate([attended, dec_attn], axis=0)
    head_block = lax.all_gather(w_out, "ctx", axis=1, tiled=True)
    column_block = lax.all_to_all(head_block, "tp", split_axis=1, concat_axis=0, tiled=True)
    summed_rows = jnp.dot(
        lax.all_gather(attended_all, "tp", axis=1, tiled=True),
        column_block,
        preferred_element_type=jnp.float32,
    )
    summed_rows = summed_rows.astype(jnp.bfloat16)
    return (summed_rows[:local_rows], summed_rows[local_rows:])

def solution(mesh):
    steps, tp = mesh.shape["ctx"], mesh.shape["tp"]

    def on_device(tokens, *rest):
        small = tp == 2 * steps and steps & (steps - 1) == 0 and tokens.shape[0] * steps <= 1024
        if small:
            return on_device_small(steps, tp, tokens, *rest)
        return on_device_large(tokens, *rest)

    return jax.shard_map(
        on_device,
        mesh=mesh,
        in_specs=(
            P("ctx", None),
            P(),
            P("ctx", "tp"),
            P("ctx", "tp"),
            P("ctx", "tp"),
            P("tp", "ctx"),
            P(),
            P(),
        ),
        out_specs=(P("ctx", "tp"), P(None, "tp")),
        check_vma=False,
    )
```

```python
import functools
import math

import jax
import jax.numpy as jnp
from jax import lax
from jax.experimental import pallas as pl
from jax.experimental.pallas import tpu as pltpu
from jax.sharding import PartitionSpec as P

HEAD_SIZE = 128
FLOOR = -1e30
LAST = 1 << 30
ROW_TILE = 8
VMEM_BYTES = 48 * 1024 * 1024


def vmem():
    return pl.BlockSpec(memory_space=pltpu.VMEM)


def smem():
    return pl.BlockSpec(memory_space=pltpu.SMEM)


def hbm():
    return pl.BlockSpec(memory_space=pl.ANY)


def params():
    return pltpu.CompilerParams(vmem_limit_bytes=VMEM_BYTES)


def place():
    t = lax.axis_index("tp")
    return lax.axis_index("ctx"), t // 2, t % 2


def slice_kernel(steps, tokens, new, *rest):
    outs, new_out, sem = rest[:steps], rest[steps], rest[steps + 1]
    c, _, k = place()
    rows, width = outs[0].shape
    first = pl.multiple_of(k * rows, rows)
    copies = []
    for step, out in enumerate(outs):
        column = pl.multiple_of((c ^ step) * width, width)
        copies.append(
            pltpu.make_async_copy(
                tokens.at[pl.ds(first, rows), pl.ds(column, width)], out, sem.at[step]
            )
        )
    for copy in copies:
        copy.start()
    new_out[...] = new[:, pl.ds(pl.multiple_of(c * width, width), width)]
    for copy in copies:
        copy.wait()


def pack_kernel(*refs):
    out = refs[-1]
    out[...] = jnp.concatenate([ref[...] for ref in refs[:-1]], axis=1)


def project_kernel(steps, parts_of, *refs):
    blocks, (new, own, other), refs = refs[:steps], refs[steps : steps + 3], refs[steps + 3 :]
    outs, inputs = refs[:steps], refs[steps]
    rows = blocks[0].shape[0]
    count = new.shape[0]
    tail = steps * rows
    for step, block in enumerate(blocks):
        inputs[step * rows : (step + 1) * rows, :] = block[...]
    inputs[tail:, :] = jnp.zeros_like(inputs[tail:, :])
    inputs[tail : tail + count, :] = new[...]
    x = inputs[...]
    pad = outs[0].shape[0] - rows
    column = 0
    for start, stop in parts_of:
        weight = jnp.concatenate([own[:, start:stop], other[:, start:stop]], axis=1)
        part = jnp.dot(x, weight, preferred_element_type=jnp.float32)
        to = slice(column, column + weight.shape[1])
        for step, out in enumerate(outs):
            out[:rows, to] = part[step * rows : (step + 1) * rows].astype(out.dtype)
            out[rows:, to] = part[tail : tail + pad].astype(out.dtype)
        column += weight.shape[1]


def add_kernel(steps, *refs):
    parts, (held, new) = refs[:steps], refs[steps:]
    rows = held.shape[0]
    total = parts[0][...]
    for part in parts[1:]:
        total = total + part[...].astype(jnp.float32)
    total = total.astype(jnp.bfloat16)
    held[...] = total[:rows]
    new[...] = total[rows:]


def request_of(position, ends):
    found = jnp.zeros_like(position)
    for end in ends:
        found = found + jnp.where(position >= end, 1, 0)
    return found


def attend_kernel(steps, count, scale, block_map, lengths, *refs):
    mine, refs = refs[:steps], refs[steps:]
    theirs, refs = refs[:steps], refs[steps:]
    new, w_own, w_other = refs[:3]
    outs, (q_all, key_all, value_all, attended) = refs[3 : 3 + steps], refs[3 + steps :]
    rows = mine[0].shape[0]
    q_width, kv_width = q_all.shape[1], key_all.shape[1]
    head = HEAD_SIZE
    groups = kv_width // head
    per_group = q_width // kv_width
    pad = new.shape[0]
    tail = steps * rows
    q_rows = q_all.shape[0]
    k_rows = key_all.shape[0]
    k_tail = 2 * tail
    half = kv_width // 2
    k_at, v_at = q_width, q_width + kv_width
    c, _, k = place()

    q_all[tail:, :] = jnp.zeros_like(q_all[tail:, :])
    key_all[k_tail:, :] = jnp.zeros_like(key_all[k_tail:, :])
    value_all[k_tail:, :] = jnp.zeros_like(value_all[k_tail:, :])
    for step in range(steps):
        at = slice(step * rows, (step + 1) * rows)
        q_all[at, :] = mine[step][:, :q_width]
        key_all[at, :] = mine[step][:, k_at:v_at]
        value_all[at, :] = mine[step][:, v_at:]
        at = slice(tail + step * rows, tail + (step + 1) * rows)
        key_all[at, :half] = theirs[step][:, k_at + half : v_at]
        key_all[at, half:] = theirs[step][:, k_at : k_at + half]
        value_all[at, :half] = theirs[step][:, v_at + half :]
        value_all[at, half:] = theirs[step][:, v_at : v_at + half]
    q_all[tail : tail + pad, :] = new[:, :q_width]
    key_all[k_tail : k_tail + pad, :] = new[:, k_at:v_at]
    value_all[k_tail : k_tail + pad, :] = new[:, v_at:]

    ends, total = [], 0
    for request in range(count):
        total = total + lengths[request]
        ends.append(total)

    def labels(shape, axis, halves):
        index = lax.broadcasted_iota(jnp.int32, shape, axis)
        position = jnp.zeros(shape, jnp.int32)
        for number in range(halves * steps):
            held = 2 * (c ^ (number % steps)) + (k ^ (number // steps))
            inside = (index >= number * rows) & (index < (number + 1) * rows)
            position = jnp.where(inside, block_map[held] * rows + index - number * rows, position)
        last = halves * tail
        is_new = index >= last
        request = jnp.where(is_new, index - last, request_of(position, ends))
        return jnp.where(is_new, LAST, position), request

    q_position, q_request = labels((q_rows, 1), 0, 1)
    k_position, k_request = labels((1, k_rows), 1, 2)
    allowed = (q_request == k_request) & (k_position <= q_position)

    for group in range(groups):
        keys = key_all[:, group * head : (group + 1) * head]
        values = value_all[:, group * head : (group + 1) * head]
        for member in range(per_group):
            at = (group * per_group + member) * head
            scores = lax.dot_general(
                q_all[:, at : at + head],
                keys,
                (((1,), (1,)), ((), ())),
                preferred_element_type=jnp.float32,
            )
            scores = jnp.where(allowed, scores * scale, FLOOR)
            weights = jnp.exp(scores - jnp.max(scores, axis=1, keepdims=True))
            denom = jnp.sum(weights, axis=1, keepdims=True)
            mixed = jnp.dot(
                weights.astype(jnp.bfloat16), values, preferred_element_type=jnp.float32
            )
            attended[:, at : at + head] = (mixed / denom).astype(jnp.bfloat16)

    rows_own = w_own.shape[0]
    result = (
        jnp.dot(attended[:, :rows_own], w_own[...], preferred_element_type=jnp.float32)
        + jnp.dot(attended[:, rows_own:], w_other[...], preferred_element_type=jnp.float32)
    ).astype(jnp.bfloat16)
    for step, out in enumerate(outs):
        out[:rows, :] = result[step * rows : (step + 1) * rows]
        out[rows:, :] = result[tail : tail + pad]


def relay_kernel(steps, *refs):
    blocks, outs = refs[:steps], refs[steps:]
    c, z, _ = place()
    for slot, out in enumerate(outs):
        for step, block in enumerate(blocks):

            @pl.when((c ^ z ^ slot) == step)
            def _(out=out, block=block):
                out[...] = block[...]


def sum_kernel(steps, *refs):
    parts, (keep, send) = refs[:steps], refs[steps:]
    width = keep.shape[1]
    rows = send.shape[0]
    _, _, k = place()
    for out, core in ((keep, k), (send, 1 - k)):
        column = pl.ds(pl.multiple_of(core * width, width), width)
        terms = [part[:, column].astype(jnp.float32) for part in parts]
        while len(terms) > 1:
            terms = [a + b for a, b in zip(terms[::2], terms[1::2])]
        out[...] = terms[0][: out.shape[0]].astype(out.dtype)


def finish_kernel(keep, other, prefill, decode):
    _, _, k = place()
    rows = other.shape[0]
    prefill[pl.ds(pl.multiple_of(k * rows, rows), rows), :] = keep[:rows]
    prefill[pl.ds(pl.multiple_of((1 - k) * rows, rows), rows), :] = other[...]
    decode[...] = keep[rows : rows + decode.shape[0]]


def on_device_small(
    steps, tp, tokens, new_token_states, w_query, key_matrix, value_matrix, w_out, lengths, block_map
):
    bf16, f32 = jnp.bfloat16, jnp.float32
    rows = tokens.shape[0] // 2
    depth = w_query.shape[0]
    count = new_token_states.shape[0]
    pad = -(-count // ROW_TILE) * ROW_TILE
    q_width = 2 * w_query.shape[1]
    kv_width = 2 * key_matrix.shape[1]
    features = q_width + 2 * kv_width
    out_width = w_out.shape[1]

    def to_core(value):
        return lax.ppermute(value, "tp", [(i, i ^ 1) for i in range(tp)])

    def to_ctx(value, step):
        return lax.ppermute(value, "ctx", [(i, i ^ step) for i in range(steps)])

    def to_chip(value, step):
        return lax.ppermute(value, "tp", [(i, i ^ (2 * step)) for i in range(tp)])

    def call(kernel, name, inputs, shapes, scratch=(), spaces=None):
        return pl.pallas_call(
            kernel,
            out_shape=[jax.ShapeDtypeStruct(shape, kind) for shape, kind in shapes],
            in_specs=spaces or [vmem()] * len(inputs),
            out_specs=[vmem()] * len(shapes),
            scratch_shapes=list(scratch),
            compiler_params=params(),
            name=name,
        )(*inputs)

    *sent, new_columns = call(
        functools.partial(slice_kernel, steps),
        "slice_tokens",
        (tokens, new_token_states),
        [((rows, depth), bf16)] * steps + [((count, depth), bf16)],
        [pltpu.SemaphoreType.DMA((steps,))],
        [hbm(), vmem()],
    )
    blocks = [sent[0]] + [to_ctx(value, step) for step, value in enumerate(sent[1:], 1)]
    weights = (w_query, key_matrix, value_matrix)
    (own,) = call(
        pack_kernel, "pack_weights", weights, [((depth, features // 2), bf16)]
    )
    other = to_core(own)
    w_out_late, _ = lax.optimization_barrier((w_out, blocks[1]))
    w_other = to_core(w_out_late)

    part_shape = (rows + pad, features)
    x_rows = -(-(steps * rows + pad) // 16) * 16
    edges = [0, q_width // 2, (q_width + kv_width) // 2, features // 2]
    parts = call(
        functools.partial(project_kernel, steps, list(zip(edges, edges[1:]))),
        "project",
        (*blocks, new_columns, own, other),
        [(part_shape, f32)] + [(part_shape, bf16)] * (steps - 1),
        [pltpu.VMEM((x_rows, depth), bf16)],
    )

    parts = [parts[0]] + [to_ctx(part, step) for step, part in enumerate(parts[1:], 1)]
    held, new = call(
        functools.partial(add_kernel, steps),
        "add_parts",
        parts,
        [((rows, features), bf16), ((pad, features), bf16)],
    )

    mine = [held] + [to_ctx(held, step) for step in range(1, steps)]
    theirs = [to_core(value) for value in mine]

    k_rows = -(-(2 * steps * rows + pad) // 128) * 128
    outs = call(
        functools.partial(attend_kernel, steps, count, 1.0 / math.sqrt(HEAD_SIZE)),
        "attend",
        (block_map, lengths, *mine, *theirs, new, w_out, w_other),
        [((rows + pad, out_width), bf16)] * steps,
        [
            pltpu.VMEM((x_rows, q_width), bf16),
            pltpu.VMEM((k_rows, kv_width), bf16),
            pltpu.VMEM((k_rows, kv_width), bf16),
            pltpu.VMEM((x_rows, q_width), bf16),
        ],
        [smem()] * 2 + [vmem()] * (2 * steps + 3),
    )

    arrived = [outs[0]] + [to_ctx(out, step) for step, out in enumerate(outs[1:], 1)]
    slots = call(
        functools.partial(relay_kernel, steps),
        "relay",
        arrived,
        [((rows + pad, out_width), bf16)] * steps,
    )
    slots = [slots[0]] + [to_chip(slot, step) for step, slot in enumerate(slots[1:], 1)]
    keep, send = call(
        functools.partial(sum_kernel, steps),
        "sum_heads",
        slots,
        [((rows + pad, out_width // 2), bf16), ((rows, out_width // 2), bf16)],
    )
    return tuple(
        call(
            finish_kernel,
            "finish",
            (keep, to_core(send)),
            [((2 * rows, out_width // 2), bf16), ((count, out_width // 2), bf16)],
        )
    )


floor_value = -1e30


def initial_positions(block_map, first_row, row_count, block_rows):
    row_ids = first_row + jnp.arange(row_count, dtype=jnp.int32)
    block_ids = row_ids // block_rows
    table_ids = jnp.arange(block_map.shape[0], dtype=jnp.int32)
    mapped = jnp.sum(
        jnp.where(block_ids[:, None] == table_ids[None, :], block_map[None, :], 0), axis=1
    )
    return mapped * block_rows + row_ids % block_rows


def request_index(positions, request_ends):
    return jnp.sum((positions[:, None] >= request_ends[None, :]).astype(jnp.int32), axis=1)


def round_weights(weights):
    rounded = weights.astype(jnp.bfloat16)
    rounded = lax.optimization_barrier(rounded)
    return rounded.astype(jnp.float32)


def softmax_parts(
    dec_heads, projected_key_rows, projected_value_rows, owned, kv_heads, head_dim, score_scale
):
    row_count = projected_key_rows.shape[0]
    scores = (
        jnp.einsum(
            "rgjd,tgd->rgjt",
            dec_heads,
            projected_key_rows.reshape(row_count, kv_heads, head_dim),
            preferred_element_type=jnp.float32,
        )
        * score_scale
    )
    scores = jnp.where(owned, scores, floor_value)
    part_peak = jnp.max(scores, axis=3)
    weights = jnp.where(owned, jnp.exp(scores - part_peak[..., None]), 0.0)
    part_total = jnp.sum(weights, axis=3)
    part_mixed = jnp.einsum(
        "rgjt,tgd->rgjd",
        weights.astype(jnp.bfloat16),
        projected_value_rows.reshape(row_count, kv_heads, head_dim),
        preferred_element_type=jnp.float32,
    )
    return (part_peak, part_total, part_mixed)


def on_device_large(
    tokens, new_token_states, w_query, key_matrix, value_matrix, w_out, lengths, block_map
):
    local_rows = tokens.shape[0]
    block_rows = local_rows // 2
    request_count = new_token_states.shape[0]
    head_dim = HEAD_SIZE
    query_width = w_query.shape[1]
    kv_width = key_matrix.shape[1]
    kv_heads = kv_width // head_dim
    query_group_count = query_width // kv_width
    score_scale = 1.0 / math.sqrt(head_dim)
    device = lax.axis_index("ctx")
    request_ends = jnp.cumsum(lengths)
    inputs = jnp.concatenate([tokens, new_token_states], axis=0)
    shard_pieces = (
        lax.all_gather(w_query, "ctx", axis=0, tiled=True),
        lax.all_gather(key_matrix, "ctx", axis=0, tiled=True),
        lax.all_gather(value_matrix, "ctx", axis=0, tiled=True),
    )
    query_all, key_all, value_all = tuple(
        (jnp.dot(inputs, weight, preferred_element_type=jnp.float32) for weight in shard_pieces)
    )
    query_all = query_all.astype(jnp.bfloat16)
    key_all = key_all.astype(jnp.bfloat16)
    value_all = value_all.astype(jnp.bfloat16)
    local_query = query_all[:local_rows]
    local_keys = key_all[:local_rows]
    local_values = value_all[:local_rows]
    dec_query = query_all[local_rows:]
    decode_key_rows = key_all[local_rows:]
    decode_value_rows = value_all[local_rows:]
    token_pos = initial_positions(block_map, device * local_rows, local_rows, block_rows)
    token_request = request_index(token_pos, request_ends)
    query_heads = local_query.reshape(local_rows, kv_heads, query_group_count, head_dim)

    def attend(running, shard_pieces, first_row):
        peak_run, total_run, mixed_run = running
        key_piece, value_piece = shard_pieces
        row_count = key_piece.shape[0]
        key_pos = initial_positions(block_map, first_row, row_count, block_rows)
        key_request = request_index(key_pos, request_ends)
        allowed = (key_request[None, :] == token_request[:, None]) & (
            key_pos[None, :] <= token_pos[:, None]
        )
        scores = (
            jnp.einsum(
                "tgjd,kgd->gjtk",
                query_heads,
                key_piece.reshape(row_count, kv_heads, head_dim),
                preferred_element_type=jnp.float32,
            )
            * score_scale
        )
        scores = jnp.where(allowed, scores, floor_value)
        peak_new = jnp.maximum(peak_run, jnp.max(scores, axis=3))
        weights = jnp.where(allowed, jnp.exp(scores - peak_new[..., None]), 0.0)
        rescale = jnp.exp(peak_run - peak_new)
        total_new = total_run * rescale + jnp.sum(weights, axis=3)
        mixed_new = mixed_run * rescale[..., None] + jnp.einsum(
            "gjtk,kgd->gjtd",
            weights.astype(jnp.bfloat16),
            value_piece.reshape(row_count, kv_heads, head_dim),
            preferred_element_type=jnp.float32,
        )
        return (peak_new, total_new, mixed_new)

    start_state = (
        jnp.full((kv_heads, query_group_count, local_rows), floor_value, jnp.float32),
        jnp.zeros((kv_heads, query_group_count, local_rows), jnp.float32),
        jnp.zeros((kv_heads, query_group_count, local_rows, head_dim), jnp.float32),
    )
    dec_heads = dec_query.reshape(request_count, kv_heads, query_group_count, head_dim)
    request_ids = jnp.arange(request_count, dtype=jnp.int32)
    cache_keys, cache_values = (
        lax.all_gather(local_keys, "ctx", axis=0, tiled=True),
        lax.all_gather(local_values, "ctx", axis=0, tiled=True),
    )
    total_rows = cache_keys.shape[0]
    shard_count = total_rows // local_rows
    limit = max(1, 1024 // local_rows)
    step_rows = local_rows * math.gcd(shard_count, 1 << limit.bit_length() - 1)

    def key_step(running, step_index):
        first_row = step_index * step_rows
        pieces = (
            lax.dynamic_slice_in_dim(cache_keys, first_row, step_rows, 0),
            lax.dynamic_slice_in_dim(cache_values, first_row, step_rows, 0),
        )
        return (attend(running, pieces, first_row), None)

    final_state, unused = lax.scan(
        key_step, start_state, jnp.arange(total_rows // step_rows, dtype=jnp.int32)
    )
    peak_run, total_run, mixed_run = final_state
    cache_pos = (
        block_map[:, None] * block_rows + jnp.arange(block_rows, dtype=jnp.int32)[None, :]
    ).reshape(total_rows)
    cache_request = request_index(cache_pos, request_ends)
    owned = (cache_request[None, :] == request_ids[:, None])[:, None, None, :]
    cache_peak, cache_total, cache_mixed = softmax_parts(
        dec_heads, cache_keys, cache_values, owned, kv_heads, head_dim, score_scale
    )
    attended = (
        (mixed_run / total_run[..., None]).transpose(2, 0, 1, 3).reshape(local_rows, query_width)
    )
    attended = attended.astype(jnp.bfloat16)
    own_keys = decode_key_rows.reshape(request_count, kv_heads, 1, head_dim).astype(jnp.float32)
    own_values = decode_value_rows.reshape(request_count, kv_heads, 1, head_dim).astype(jnp.float32)
    self_scores = jnp.sum(dec_heads.astype(jnp.float32) * own_keys, axis=3) * score_scale
    peak_all = jnp.maximum(cache_peak, self_scores)
    rescale = jnp.exp(cache_peak - peak_all)
    self_weights = jnp.exp(self_scores - peak_all)
    dec_total = cache_total * rescale + self_weights
    dec_mixed = (
        cache_mixed * rescale[..., None] + round_weights(self_weights)[..., None] * own_values
    )
    dec_attn = (
        (dec_mixed / dec_total[..., None]).reshape(request_count, query_width).astype(jnp.bfloat16)
    )
    attended_all = jnp.concatenate([attended, dec_attn], axis=0)
    head_block = lax.all_gather(w_out, "ctx", axis=1, tiled=True)
    column_block = lax.all_to_all(head_block, "tp", split_axis=1, concat_axis=0, tiled=True)
    summed_rows = jnp.dot(
        lax.all_gather(attended_all, "tp", axis=1, tiled=True),
        column_block,
        preferred_element_type=jnp.float32,
    )
    summed_rows = summed_rows.astype(jnp.bfloat16)
    return (summed_rows[:local_rows], summed_rows[local_rows:])

def solution(mesh):
    steps, tp = mesh.shape["ctx"], mesh.shape["tp"]

    def on_device(tokens, *rest):
        small = tp == 2 * steps and steps & (steps - 1) == 0 and tokens.shape[0] * steps <= 1024
        if small:
            return on_device_small(steps, tp, tokens, *rest)
        return on_device_large(tokens, *rest)

    return jax.shard_map(
        on_device,
        mesh=mesh,
        in_specs=(
            P("ctx", None),
            P(),
            P("ctx", "tp"),
            P("ctx", "tp"),
            P("ctx", "tp"),
            P("tp", "ctx"),
            P(),
            P(),
        ),
        out_specs=(P("ctx", "tp"), P(None, "tp")),
        check_vma=False,
    )
```

```python
import functools
import math

import jax
import jax.numpy as jnp
from jax import lax
from jax.experimental import pallas as pl
from jax.experimental.pallas import tpu as pltpu
from jax.sharding import PartitionSpec as P

HEAD_SIZE = 128
FLOOR = -1e30
LAST = 1 << 30
ROW_TILE = 8
VMEM_BYTES = 48 * 1024 * 1024
LOAD_VMEM_BYTES = 62 * 1024 * 1024


def vmem():
    return pl.BlockSpec(memory_space=pltpu.VMEM)


def smem():
    return pl.BlockSpec(memory_space=pltpu.SMEM)


def hbm():
    return pl.BlockSpec(memory_space=pltpu.HBM)


def place():
    t = lax.axis_index("tp")
    return lax.axis_index("ctx"), t // 2, t % 2


def load_kernel(steps, *refs):
    (tokens, new, *weights), refs = refs[:5], refs[5:]
    outs, (new_out, packed, sem) = refs[:steps], refs[steps:]
    c, _, k = place()
    rows, width = outs[0].shape
    first = pl.multiple_of(k * rows, rows)
    pairs = []
    for step, out in enumerate(outs):
        column = pl.multiple_of((c ^ step) * width, width)
        pairs.append((tokens.at[pl.ds(first, rows), pl.ds(column, width)], out))
    column = 0
    for weight in weights:
        pairs.append((weight, packed.at[:, pl.ds(column, weight.shape[1])]))
        column += weight.shape[1]
    copies = [pltpu.make_async_copy(*pair, sem.at[i]) for i, pair in enumerate(pairs)]
    for copy in copies:
        copy.start()
    new_out[...] = new[:, pl.ds(pl.multiple_of(c * width, width), width)]
    for copy in copies:
        copy.wait()


def project(x, own, other, parts_of):
    results = []
    for start, stop in parts_of:
        weight = jnp.concatenate([own[:, start:stop], other[:, start:stop]], axis=1)
        results.append(jnp.dot(x, weight, preferred_element_type=jnp.float32))
    return jnp.concatenate(results, axis=1)


def project_own_kernel(parts_of, block, new, own, other, out, new_out, inputs):
    rows, count = block.shape[0], new.shape[0]
    inputs[:rows, :] = block[...]
    inputs[rows:, :] = jnp.zeros_like(inputs[rows:, :])
    inputs[rows : rows + count, :] = new[...]
    part = project(inputs[...], own, other, parts_of)
    out[...] = part[: out.shape[0]]
    new_out[...] = part[rows : out.shape[0]].astype(new_out.dtype)


def project_kernel(number, parts_of, *refs):
    blocks, (new, own, other), refs = refs[:number], refs[number : number + 3], refs[number + 3 :]
    outs = refs[:number]
    rows = blocks[0].shape[0]
    x = jnp.concatenate([block[...] for block in blocks], axis=0)
    part = project(x, own, other, parts_of)
    for step, out in enumerate(outs):
        out[:rows, :] = part[step * rows : (step + 1) * rows].astype(out.dtype)
        out[rows:, :] = new[...]


def add_kernel(first, second, out):
    out[...] = first[...] + second[...].astype(jnp.float32)


def add_last_kernel(*refs):
    parts, (held, new) = refs[:-2], refs[-2:]
    rows = held.shape[0]
    total = parts[0][...]
    for part in parts[1:]:
        total = total + part[...].astype(jnp.float32)
    total = total.astype(jnp.bfloat16)
    held[...] = total[:rows]
    new[...] = total[rows:]


def request_of(position, ends):
    found = jnp.zeros_like(position)
    for end in ends:
        found = found + jnp.where(position >= end, 1, 0)
    return found


def attend_kernel(steps, step, count, scale, block_map, lengths, *refs):
    mine, refs = refs[:steps], refs[steps:]
    theirs, refs = refs[:steps], refs[steps:]
    new, w_own, w_other = refs[:3]
    if step is not None:
        new_out, refs = refs[3], refs[1:]
    out, q_all, key_all, value_all, attended = refs[3:]
    rows = mine[0].shape[0]
    q_width, kv_width = q_all.shape[1], key_all.shape[1]
    head = HEAD_SIZE
    groups = kv_width // head
    per_group = q_width // kv_width
    pad = new.shape[0]
    tail = steps * rows
    q_rows = q_all.shape[0]
    k_rows = key_all.shape[0]
    k_tail = 2 * tail
    half = kv_width // 2
    k_at, v_at = q_width, q_width + kv_width
    c, _, k = place()

    key_all[k_tail:, :] = jnp.zeros_like(key_all[k_tail:, :])
    value_all[k_tail:, :] = jnp.zeros_like(value_all[k_tail:, :])
    for number in range(steps):
        at = slice(number * rows, (number + 1) * rows)
        key_all[at, :] = mine[number][:, k_at:v_at]
        value_all[at, :] = mine[number][:, v_at:]
        at = slice(tail + number * rows, tail + (number + 1) * rows)
        key_all[at, :half] = theirs[number][:, k_at + half : v_at]
        key_all[at, half:] = theirs[number][:, k_at : k_at + half]
        value_all[at, :half] = theirs[number][:, v_at + half :]
        value_all[at, half:] = theirs[number][:, v_at : v_at + half]
    key_all[k_tail : k_tail + pad, :] = new[:, k_at:v_at]
    value_all[k_tail : k_tail + pad, :] = new[:, v_at:]
    if step is None:
        q_all[...] = jnp.zeros_like(q_all)
        q_all[:pad, :] = new[:, :q_width]
    else:
        q_all[...] = mine[step][:, :q_width]

    ends, total = [], 0
    for request in range(count):
        total = total + lengths[request]
        ends.append(total)

    def labels(shape, axis, held, last):
        index = lax.broadcasted_iota(jnp.int32, shape, axis)
        position = jnp.zeros(shape, jnp.int32)
        for number, block in enumerate(held):
            inside = (index >= number * rows) & (index < (number + 1) * rows)
            position = jnp.where(inside, block_map[block] * rows + index - number * rows, position)
        is_new = index >= last
        request = jnp.where(is_new, index - last, request_of(position, ends))
        return jnp.where(is_new, LAST, position), request

    if step is None:
        q_position, q_request = labels((q_rows, 1), 0, [], 0)
    else:
        q_position, q_request = labels((q_rows, 1), 0, [2 * (c ^ step) + k], rows)
    held = [2 * (c ^ number) + (k ^ other) for other in range(2) for number in range(steps)]
    k_position, k_request = labels((1, k_rows), 1, held, k_tail)
    allowed = (q_request == k_request) & (k_position <= q_position)
    allowed = jnp.concatenate([allowed] * per_group, axis=0)

    for group in range(groups):
        keys = key_all[:, group * head : (group + 1) * head]
        values = value_all[:, group * head : (group + 1) * head]
        places = [(group * per_group + member) * head for member in range(per_group)]
        query = jnp.concatenate([q_all[:, at : at + head] for at in places], axis=0)
        scores = lax.dot_general(
            query, keys, (((1,), (1,)), ((), ())), preferred_element_type=jnp.float32
        )
        scores = jnp.where(allowed, scores * scale, FLOOR)
        weights = jnp.exp(scores - jnp.max(scores, axis=1, keepdims=True))
        denom = jnp.sum(weights, axis=1, keepdims=True)
        mixed = jnp.dot(weights.astype(jnp.bfloat16), values, preferred_element_type=jnp.float32)
        mixed = (mixed / denom).astype(jnp.bfloat16)
        for member, at in enumerate(places):
            attended[:, at : at + head] = mixed[member * q_rows : (member + 1) * q_rows]

    rows_own = w_own.shape[0]
    result = (
        jnp.dot(attended[:, :rows_own], w_own[...], preferred_element_type=jnp.float32)
        + jnp.dot(attended[:, rows_own:], w_other[...], preferred_element_type=jnp.float32)
    ).astype(jnp.bfloat16)
    if step is None:
        out[...] = result[:pad]
    else:
        out[:rows, :] = result
        out[rows:, :] = new_out[...]


def relay_kernel(steps, *refs):
    blocks, outs = refs[:steps], refs[steps:]
    c, z, _ = place()
    for slot, out in enumerate(outs):
        for step, block in enumerate(blocks):

            @pl.when((c ^ z ^ slot) == step)
            def _(out=out, block=block):
                out[...] = block[...]


def sum_kernel(steps, *refs):
    parts, (keep, send) = refs[:steps], refs[steps:]
    width = keep.shape[1]
    rows = send.shape[0]
    _, _, k = place()
    for out, core in ((keep, k), (send, 1 - k)):
        column = pl.ds(pl.multiple_of(core * width, width), width)
        terms = [part[:, column].astype(jnp.float32) for part in parts]
        while len(terms) > 1:
            terms = [a + b for a, b in zip(terms[::2], terms[1::2])]
        out[...] = terms[0][: out.shape[0]].astype(out.dtype)


def finish_kernel(keep, other, prefill, decode):
    _, _, k = place()
    rows = other.shape[0]
    prefill[pl.ds(pl.multiple_of(k * rows, rows), rows), :] = keep[:rows]
    prefill[pl.ds(pl.multiple_of((1 - k) * rows, rows), rows), :] = other[...]
    decode[...] = keep[rows : rows + decode.shape[0]]


def on_device_small(
    steps, tp, tokens, new_token_states, w_query, key_matrix, value_matrix, w_out, lengths, block_map
):
    bf16, f32 = jnp.bfloat16, jnp.float32
    rows = tokens.shape[0] // 2
    depth = w_query.shape[0]
    count = new_token_states.shape[0]
    pad = -(-count // ROW_TILE) * ROW_TILE
    q_width = 2 * w_query.shape[1]
    kv_width = 2 * key_matrix.shape[1]
    features = q_width + 2 * kv_width
    out_width = w_out.shape[1]

    def to_core(value):
        return lax.ppermute(value, "tp", [(i, i ^ 1) for i in range(tp)])

    def to_ctx(value, step):
        return lax.ppermute(value, "ctx", [(i, i ^ step) for i in range(steps)])

    def to_chip(value, step):
        return lax.ppermute(value, "tp", [(i, i ^ (2 * step)) for i in range(tp)])

    def call(kernel, name, inputs, shapes, scratch=(), spaces=None, limit=VMEM_BYTES, flops=0):
        moved = sum(2 * math.prod(shape) for shape, _ in shapes) + sum(2 * x.size for x in inputs)
        return pl.pallas_call(
            kernel,
            out_shape=[jax.ShapeDtypeStruct(shape, kind) for shape, kind in shapes],
            in_specs=spaces or [vmem()] * len(inputs),
            out_specs=[vmem()] * len(shapes),
            scratch_shapes=list(scratch),
            compiler_params=pltpu.CompilerParams(vmem_limit_bytes=limit),
            cost_estimate=pl.CostEstimate(flops=flops, bytes_accessed=moved, transcendentals=0),
            name=name,
        )(*inputs)

    weights = (w_query, key_matrix, value_matrix)
    *sent, new_columns, own = call(
        functools.partial(load_kernel, steps),
        "load",
        (tokens, new_token_states, *weights),
        [((rows, depth), bf16)] * steps + [((count, depth), bf16), ((depth, features // 2), bf16)],
        [pltpu.SemaphoreType.DMA((steps + len(weights),))],
        [hbm(), vmem()] + [hbm()] * len(weights),
        LOAD_VMEM_BYTES,
    )
    blocks = [sent[0]] + [to_ctx(value, step) for step, value in enumerate(sent[1:], 1)]
    other = to_core(own)
    w_out_late, _ = lax.optimization_barrier((w_out, blocks[1]))
    w_other = to_core(w_out_late)

    part_shape = (rows + pad, features)
    x_rows = -(-(rows + pad) // 16) * 16
    edges = [0, q_width // 2, (q_width + kv_width) // 2, features // 2]
    edges = list(zip(edges, edges[1:]))
    flops = 2 * rows * depth * features
    own_part, new_part = call(
        functools.partial(project_own_kernel, edges),
        "project_own",
        (blocks[0], new_columns, own, other),
        [(part_shape, f32), ((pad, features), bf16)],
        [pltpu.VMEM((x_rows, depth), bf16)],
        flops=flops,
    )
    parts = [own_part]
    for group in (blocks[1:2], blocks[2:]):
        parts += call(
            functools.partial(project_kernel, len(group), edges),
            "project",
            (*group, new_part, own, other),
            [(part_shape, bf16)] * len(group),
            flops=flops * len(group),
        )

    parts = [parts[0]] + [to_ctx(part, step) for step, part in enumerate(parts[1:], 1)]
    (total,) = call(add_kernel, "add_first", parts[:2], [(part_shape, f32)])
    held, new = call(
        add_last_kernel,
        "add_parts",
        (total, *parts[2:]),
        [((rows, features), bf16), ((pad, features), bf16)],
    )

    mine = [held] + [to_ctx(held, step) for step in range(1, steps)]
    theirs = [to_core(value) for value in mine]

    k_rows = -(-(2 * steps * rows + pad) // 128) * 128
    def attend(step, *extra):
        q_rows = 2 * ROW_TILE if step is None else rows
        (out,) = call(
            functools.partial(attend_kernel, steps, step, count, 1.0 / math.sqrt(HEAD_SIZE)),
            "attend",
            (block_map, lengths, *mine, *theirs, new, w_out, w_other, *extra),
            [((pad if step is None else rows + pad, out_width), bf16)],
            [
                pltpu.VMEM((q_rows, q_width), bf16),
                pltpu.VMEM((k_rows, kv_width), bf16),
                pltpu.VMEM((k_rows, kv_width), bf16),
                pltpu.VMEM((q_rows, q_width), bf16),
            ],
            [smem()] * 2 + [vmem()] * (2 * steps + 3 + len(extra)),
            flops=2 * q_rows * q_width * (2 * k_rows + out_width),
        )
        return out

    new_out = attend(None)
    outs = [attend(step, new_out) for step in range(steps)]

    arrived = [outs[0]] + [to_ctx(out, step) for step, out in enumerate(outs[1:], 1)]
    slots = call(
        functools.partial(relay_kernel, steps),
        "relay",
        arrived,
        [((rows + pad, out_width), bf16)] * steps,
    )
    slots = [slots[0]] + [to_chip(slot, step) for step, slot in enumerate(slots[1:], 1)]
    keep, send = call(
        functools.partial(sum_kernel, steps),
        "sum_heads",
        slots,
        [((rows + pad, out_width // 2), bf16), ((rows, out_width // 2), bf16)],
    )
    return tuple(
        call(
            finish_kernel,
            "finish",
            (keep, to_core(send)),
            [((2 * rows, out_width // 2), bf16), ((count, out_width // 2), bf16)],
        )
    )


floor_value = -1e30


def initial_positions(block_map, first_row, row_count, block_rows):
    row_ids = first_row + jnp.arange(row_count, dtype=jnp.int32)
    block_ids = row_ids // block_rows
    table_ids = jnp.arange(block_map.shape[0], dtype=jnp.int32)
    mapped = jnp.sum(
        jnp.where(block_ids[:, None] == table_ids[None, :], block_map[None, :], 0), axis=1
    )
    return mapped * block_rows + row_ids % block_rows


def request_index(positions, request_ends):
    return jnp.sum((positions[:, None] >= request_ends[None, :]).astype(jnp.int32), axis=1)


def round_weights(weights):
    rounded = weights.astype(jnp.bfloat16)
    rounded = lax.optimization_barrier(rounded)
    return rounded.astype(jnp.float32)


def softmax_parts(
    dec_heads, projected_key_rows, projected_value_rows, owned, kv_heads, head_dim, score_scale
):
    row_count = projected_key_rows.shape[0]
    scores = (
        jnp.einsum(
            "rgjd,tgd->rgjt",
            dec_heads,
            projected_key_rows.reshape(row_count, kv_heads, head_dim),
            preferred_element_type=jnp.float32,
        )
        * score_scale
    )
    scores = jnp.where(owned, scores, floor_value)
    part_peak = jnp.max(scores, axis=3)
    weights = jnp.where(owned, jnp.exp(scores - part_peak[..., None]), 0.0)
    part_total = jnp.sum(weights, axis=3)
    part_mixed = jnp.einsum(
        "rgjt,tgd->rgjd",
        weights.astype(jnp.bfloat16),
        projected_value_rows.reshape(row_count, kv_heads, head_dim),
        preferred_element_type=jnp.float32,
    )
    return (part_peak, part_total, part_mixed)


def on_device_large(
    tokens, new_token_states, w_query, key_matrix, value_matrix, w_out, lengths, block_map
):
    local_rows = tokens.shape[0]
    block_rows = local_rows // 2
    request_count = new_token_states.shape[0]
    head_dim = HEAD_SIZE
    query_width = w_query.shape[1]
    kv_width = key_matrix.shape[1]
    kv_heads = kv_width // head_dim
    query_group_count = query_width // kv_width
    score_scale = 1.0 / math.sqrt(head_dim)
    device = lax.axis_index("ctx")
    request_ends = jnp.cumsum(lengths)
    inputs = jnp.concatenate([tokens, new_token_states], axis=0)
    shard_pieces = (
        lax.all_gather(w_query, "ctx", axis=0, tiled=True),
        lax.all_gather(key_matrix, "ctx", axis=0, tiled=True),
        lax.all_gather(value_matrix, "ctx", axis=0, tiled=True),
    )
    query_all, key_all, value_all = tuple(
        (jnp.dot(inputs, weight, preferred_element_type=jnp.float32) for weight in shard_pieces)
    )
    query_all = query_all.astype(jnp.bfloat16)
    key_all = key_all.astype(jnp.bfloat16)
    value_all = value_all.astype(jnp.bfloat16)
    local_query = query_all[:local_rows]
    local_keys = key_all[:local_rows]
    local_values = value_all[:local_rows]
    dec_query = query_all[local_rows:]
    decode_key_rows = key_all[local_rows:]
    decode_value_rows = value_all[local_rows:]
    token_pos = initial_positions(block_map, device * local_rows, local_rows, block_rows)
    token_request = request_index(token_pos, request_ends)
    query_heads = local_query.reshape(local_rows, kv_heads, query_group_count, head_dim)

    def attend(running, shard_pieces, first_row):
        peak_run, total_run, mixed_run = running
        key_piece, value_piece = shard_pieces
        row_count = key_piece.shape[0]
        key_pos = initial_positions(block_map, first_row, row_count, block_rows)
        key_request = request_index(key_pos, request_ends)
        allowed = (key_request[None, :] == token_request[:, None]) & (
            key_pos[None, :] <= token_pos[:, None]
        )
        scores = (
            jnp.einsum(
                "tgjd,kgd->gjtk",
                query_heads,
                key_piece.reshape(row_count, kv_heads, head_dim),
                preferred_element_type=jnp.float32,
            )
            * score_scale
        )
        scores = jnp.where(allowed, scores, floor_value)
        peak_new = jnp.maximum(peak_run, jnp.max(scores, axis=3))
        weights = jnp.where(allowed, jnp.exp(scores - peak_new[..., None]), 0.0)
        rescale = jnp.exp(peak_run - peak_new)
        total_new = total_run * rescale + jnp.sum(weights, axis=3)
        mixed_new = mixed_run * rescale[..., None] + jnp.einsum(
            "gjtk,kgd->gjtd",
            weights.astype(jnp.bfloat16),
            value_piece.reshape(row_count, kv_heads, head_dim),
            preferred_element_type=jnp.float32,
        )
        return (peak_new, total_new, mixed_new)

    start_state = (
        jnp.full((kv_heads, query_group_count, local_rows), floor_value, jnp.float32),
        jnp.zeros((kv_heads, query_group_count, local_rows), jnp.float32),
        jnp.zeros((kv_heads, query_group_count, local_rows, head_dim), jnp.float32),
    )
    dec_heads = dec_query.reshape(request_count, kv_heads, query_group_count, head_dim)
    request_ids = jnp.arange(request_count, dtype=jnp.int32)
    cache_keys, cache_values = (
        lax.all_gather(local_keys, "ctx", axis=0, tiled=True),
        lax.all_gather(local_values, "ctx", axis=0, tiled=True),
    )
    total_rows = cache_keys.shape[0]
    shard_count = total_rows // local_rows
    limit = max(1, 1024 // local_rows)
    step_rows = local_rows * math.gcd(shard_count, 1 << limit.bit_length() - 1)

    def key_step(running, step_index):
        first_row = step_index * step_rows
        pieces = (
            lax.dynamic_slice_in_dim(cache_keys, first_row, step_rows, 0),
            lax.dynamic_slice_in_dim(cache_values, first_row, step_rows, 0),
        )
        return (attend(running, pieces, first_row), None)

    final_state, unused = lax.scan(
        key_step, start_state, jnp.arange(total_rows // step_rows, dtype=jnp.int32)
    )
    peak_run, total_run, mixed_run = final_state
    cache_pos = (
        block_map[:, None] * block_rows + jnp.arange(block_rows, dtype=jnp.int32)[None, :]
    ).reshape(total_rows)
    cache_request = request_index(cache_pos, request_ends)
    owned = (cache_request[None, :] == request_ids[:, None])[:, None, None, :]
    cache_peak, cache_total, cache_mixed = softmax_parts(
        dec_heads, cache_keys, cache_values, owned, kv_heads, head_dim, score_scale
    )
    attended = (
        (mixed_run / total_run[..., None]).transpose(2, 0, 1, 3).reshape(local_rows, query_width)
    )
    attended = attended.astype(jnp.bfloat16)
    own_keys = decode_key_rows.reshape(request_count, kv_heads, 1, head_dim).astype(jnp.float32)
    own_values = decode_value_rows.reshape(request_count, kv_heads, 1, head_dim).astype(jnp.float32)
    self_scores = jnp.sum(dec_heads.astype(jnp.float32) * own_keys, axis=3) * score_scale
    peak_all = jnp.maximum(cache_peak, self_scores)
    rescale = jnp.exp(cache_peak - peak_all)
    self_weights = jnp.exp(self_scores - peak_all)
    dec_total = cache_total * rescale + self_weights
    dec_mixed = (
        cache_mixed * rescale[..., None] + round_weights(self_weights)[..., None] * own_values
    )
    dec_attn = (
        (dec_mixed / dec_total[..., None]).reshape(request_count, query_width).astype(jnp.bfloat16)
    )
    attended_all = jnp.concatenate([attended, dec_attn], axis=0)
    head_block = lax.all_gather(w_out, "ctx", axis=1, tiled=True)
    column_block = lax.all_to_all(head_block, "tp", split_axis=1, concat_axis=0, tiled=True)
    summed_rows = jnp.dot(
        lax.all_gather(attended_all, "tp", axis=1, tiled=True),
        column_block,
        preferred_element_type=jnp.float32,
    )
    summed_rows = summed_rows.astype(jnp.bfloat16)
    return (summed_rows[:local_rows], summed_rows[local_rows:])

def solution(mesh):
    steps, tp = mesh.shape["ctx"], mesh.shape["tp"]

    def on_device(tokens, *rest):
        small = tp == 2 * steps and steps & (steps - 1) == 0 and tokens.shape[0] * steps <= 1024
        if small:
            return on_device_small(steps, tp, tokens, *rest)
        return on_device_large(tokens, *rest)

    return jax.shard_map(
        on_device,
        mesh=mesh,
        in_specs=(
            P("ctx", None),
            P(),
            P("ctx", "tp"),
            P("ctx", "tp"),
            P("ctx", "tp"),
            P("tp", "ctx"),
            P(),
            P(),
        ),
        out_specs=(P("ctx", "tp"), P(None, "tp")),
        check_vma=False,
    )
```

```python
import functools
import math

import jax
import jax.numpy as jnp
from jax import lax
from jax.experimental import pallas as pl
from jax.experimental.pallas import tpu as pltpu
from jax.sharding import PartitionSpec as P

HEAD_SIZE = 128
FLOOR = -1e30
LAST = 1 << 30
ROW_TILE = 8
VMEM_BYTES = 48 * 1024 * 1024


def vmem():
    return pl.BlockSpec(memory_space=pltpu.VMEM)


def smem():
    return pl.BlockSpec(memory_space=pltpu.SMEM)


def way(steps):
    return [0] + list(range(steps - 1, 0, -1))


def place():
    t = lax.axis_index("tp")
    return lax.axis_index("ctx"), t // 2, t % 2


def pack_kernel(*refs):
    out = refs[-1]
    out[...] = jnp.concatenate([ref[...] for ref in refs[:-1]], axis=1)


def project_kernel(steps, parts_of, *refs):
    blocks, (new, own, other), refs = refs[:steps], refs[steps : steps + 3], refs[steps + 3 :]
    outs, inputs = refs[:steps], refs[steps]
    rows = blocks[0].shape[0]
    count = new.shape[0]
    tail = steps * rows
    for step, block in enumerate(blocks):
        inputs[step * rows : (step + 1) * rows, :] = block[...]
    inputs[tail:, :] = jnp.zeros_like(inputs[tail:, :])
    inputs[tail : tail + count, :] = new[...]
    x = inputs[...]
    pad = outs[0].shape[0] - rows
    column = 0
    for start, stop in parts_of:
        weight = jnp.concatenate([own[:, start:stop], other[:, start:stop]], axis=1)
        part = jnp.dot(x, weight, preferred_element_type=jnp.float32)
        to = slice(column, column + weight.shape[1])
        for step, out in enumerate(outs):
            out[:rows, to] = part[step * rows : (step + 1) * rows].astype(out.dtype)
            out[rows:, to] = part[tail : tail + pad].astype(out.dtype)
        column += weight.shape[1]


def add_kernel(steps, *refs):
    parts, (held, new) = refs[:steps], refs[steps:]
    rows = held.shape[0]
    total = parts[0][...]
    for part in parts[1:]:
        total = total + part[...].astype(jnp.float32)
    total = total.astype(jnp.bfloat16)
    held[...] = total[:rows]
    new[...] = total[rows:]


def request_of(position, ends):
    found = jnp.zeros_like(position)
    for end in ends:
        found = found + jnp.where(position >= end, 1, 0)
    return found


def attend_kernel(steps, count, scale, block_map, lengths, *refs):
    mine, refs = refs[:steps], refs[steps:]
    theirs, refs = refs[:steps], refs[steps:]
    new, w_own, w_other = refs[:3]
    outs, (q_all, key_all, value_all, attended) = refs[3 : 3 + steps], refs[3 + steps :]
    rows = mine[0].shape[0]
    q_width, kv_width = q_all.shape[1], key_all.shape[1]
    head = HEAD_SIZE
    groups = kv_width // head
    per_group = q_width // kv_width
    pad = new.shape[0]
    tail = steps * rows
    q_rows = q_all.shape[0]
    k_rows = key_all.shape[0]
    k_tail = 2 * tail
    half = kv_width // 2
    k_at, v_at = q_width, q_width + kv_width
    c, _, k = place()

    q_all[tail:, :] = jnp.zeros_like(q_all[tail:, :])
    key_all[k_tail:, :] = jnp.zeros_like(key_all[k_tail:, :])
    value_all[k_tail:, :] = jnp.zeros_like(value_all[k_tail:, :])
    for step in range(steps):
        at = slice(step * rows, (step + 1) * rows)
        q_all[at, :] = mine[step][:, :q_width]
        key_all[at, :] = mine[step][:, k_at:v_at]
        value_all[at, :] = mine[step][:, v_at:]
        at = slice(tail + step * rows, tail + (step + 1) * rows)
        key_all[at, :half] = theirs[step][:, k_at + half : v_at]
        key_all[at, half:] = theirs[step][:, k_at : k_at + half]
        value_all[at, :half] = theirs[step][:, v_at + half :]
        value_all[at, half:] = theirs[step][:, v_at : v_at + half]
    q_all[tail : tail + pad, :] = new[:, :q_width]
    key_all[k_tail : k_tail + pad, :] = new[:, k_at:v_at]
    value_all[k_tail : k_tail + pad, :] = new[:, v_at:]

    ends, total = [], 0
    for request in range(count):
        total = total + lengths[request]
        ends.append(total)

    def labels(shape, axis, halves):
        index = lax.broadcasted_iota(jnp.int32, shape, axis)
        position = jnp.zeros(shape, jnp.int32)
        for number in range(halves * steps):
            held = 2 * (c ^ way(steps)[number % steps]) + (k ^ (number // steps))
            inside = (index >= number * rows) & (index < (number + 1) * rows)
            position = jnp.where(inside, block_map[held] * rows + index - number * rows, position)
        last = halves * tail
        is_new = index >= last
        request = jnp.where(is_new, index - last, request_of(position, ends))
        return jnp.where(is_new, LAST, position), request

    q_position, q_request = labels((q_rows, 1), 0, 1)
    k_position, k_request = labels((1, k_rows), 1, 2)
    allowed = (q_request == k_request) & (k_position <= q_position)

    for group in range(groups):
        keys = key_all[:, group * head : (group + 1) * head]
        values = value_all[:, group * head : (group + 1) * head]
        for member in range(per_group):
            at = (group * per_group + member) * head
            scores = lax.dot_general(
                q_all[:, at : at + head],
                keys,
                (((1,), (1,)), ((), ())),
                preferred_element_type=jnp.float32,
            )
            scores = jnp.where(allowed, scores * scale, FLOOR)
            weights = jnp.exp(scores - jnp.max(scores, axis=1, keepdims=True))
            denom = jnp.sum(weights, axis=1, keepdims=True)
            mixed = jnp.dot(
                weights.astype(jnp.bfloat16), values, preferred_element_type=jnp.float32
            )
            attended[:, at : at + head] = (mixed / denom).astype(jnp.bfloat16)

    rows_own = w_own.shape[0]
    result = (
        jnp.dot(attended[:, :rows_own], w_own[...], preferred_element_type=jnp.float32)
        + jnp.dot(attended[:, rows_own:], w_other[...], preferred_element_type=jnp.float32)
    ).astype(jnp.bfloat16)
    for step, out in enumerate(outs):
        out[:rows, :] = result[step * rows : (step + 1) * rows]
        out[rows:, :] = result[tail : tail + pad]


def relay_kernel(steps, *refs):
    blocks, outs = refs[:steps], refs[steps:]
    c, z, _ = place()
    for slot, out in zip(way(steps), outs):
        for step, block in zip(way(steps), blocks):

            @pl.when((c ^ z ^ slot) == step)
            def _(out=out, block=block):
                out[...] = block[...]


def sum_kernel(steps, *refs):
    parts, (keep, send) = refs[:steps], refs[steps:]
    width = keep.shape[1]
    rows = send.shape[0]
    _, _, k = place()
    for out, core in ((keep, k), (send, 1 - k)):
        column = pl.ds(pl.multiple_of(core * width, width), width)
        terms = [part[:, column].astype(jnp.float32) for part in parts]
        terms = [terms[way(steps).index(m)] for m in range(steps)]
        while len(terms) > 1:
            terms = [a + b for a, b in zip(terms[::2], terms[1::2])]
        out[...] = terms[0][: out.shape[0]].astype(out.dtype)


def finish_kernel(keep, other, prefill, decode):
    _, _, k = place()
    rows = other.shape[0]
    prefill[pl.ds(pl.multiple_of(k * rows, rows), rows), :] = keep[:rows]
    prefill[pl.ds(pl.multiple_of((1 - k) * rows, rows), rows), :] = other[...]
    decode[...] = keep[rows : rows + decode.shape[0]]


def on_device_small(
    steps, tp, tokens, new_token_states, w_query, key_matrix, value_matrix, w_out, lengths, block_map
):
    bf16, f32 = jnp.bfloat16, jnp.float32
    rows = tokens.shape[0] // 2
    depth = w_query.shape[0]
    count = new_token_states.shape[0]
    pad = -(-count // ROW_TILE) * ROW_TILE
    q_width = 2 * w_query.shape[1]
    kv_width = 2 * key_matrix.shape[1]
    features = q_width + 2 * kv_width
    out_width = w_out.shape[1]

    def to_core(value):
        return lax.ppermute(value, "tp", [(i, i ^ 1) for i in range(tp)])

    def to_ctx(value, step):
        return lax.ppermute(value, "ctx", [(i, i ^ step) for i in range(steps)])

    def to_chip(value, step):
        return lax.ppermute(value, "tp", [(i, i ^ (2 * step)) for i in range(tp)])

    def all_to_ctx(values):
        values = list(values)
        return values[:1] + [to_ctx(value, m) for value, m in zip(values[1:], way(steps)[1:])]

    def all_to_chip(values):
        values = list(values)
        return values[:1] + [to_chip(value, m) for value, m in zip(values[1:], way(steps)[1:])]

    def call(kernel, name, inputs, shapes, scratch=(), spaces=None):
        return pl.pallas_call(
            kernel,
            out_shape=[jax.ShapeDtypeStruct(shape, kind) for shape, kind in shapes],
            in_specs=spaces or [vmem()] * len(inputs),
            out_specs=[vmem()] * len(shapes),
            scratch_shapes=list(scratch),
            compiler_params=pltpu.CompilerParams(vmem_limit_bytes=VMEM_BYTES),
            name=name,
        )(*inputs)

    c, _, k = place()
    sent = [
        lax.dynamic_slice(tokens, (k * rows, (c ^ m) * depth), (rows, depth)) for m in way(steps)
    ]
    new_columns = lax.dynamic_slice_in_dim(new_token_states, c * depth, depth, 1)
    blocks = all_to_ctx(sent)
    *weights, _ = lax.optimization_barrier((w_query, key_matrix, value_matrix, sent[1]))
    (own,) = call(pack_kernel, "pack_weights", weights, [((depth, features // 2), bf16)])
    other = to_core(own)

    part_shape = (rows + pad, features)
    x_rows = -(-(steps * rows + pad) // 16) * 16
    edges = [0, q_width // 2, (q_width + kv_width) // 2, features // 2]
    parts = call(
        functools.partial(project_kernel, steps, list(zip(edges, edges[1:]))),
        "project",
        (*blocks, new_columns, own, other),
        [(part_shape, f32)] + [(part_shape, bf16)] * (steps - 1),
        [pltpu.VMEM((x_rows, depth), bf16)],
    )

    w_out_late, _ = lax.optimization_barrier((w_out, parts[0]))
    parts = all_to_ctx(parts)
    w_other = to_core(w_out_late)
    held, new = call(
        functools.partial(add_kernel, steps),
        "add_parts",
        parts,
        [((rows, features), bf16), ((pad, features), bf16)],
    )

    mine = all_to_ctx([held] * steps)
    theirs = [to_core(value) for value in mine]

    k_rows = -(-(2 * steps * rows + pad) // 128) * 128
    outs = call(
        functools.partial(attend_kernel, steps, count, 1.0 / math.sqrt(HEAD_SIZE)),
        "attend",
        (block_map, lengths, *mine, *theirs, new, w_out, w_other),
        [((rows + pad, out_width), bf16)] * steps,
        [
            pltpu.VMEM((x_rows, q_width), bf16),
            pltpu.VMEM((k_rows, kv_width), bf16),
            pltpu.VMEM((k_rows, kv_width), bf16),
            pltpu.VMEM((x_rows, q_width), bf16),
        ],
        [smem()] * 2 + [vmem()] * (2 * steps + 3),
    )

    arrived = all_to_ctx(outs)
    slots = call(
        functools.partial(relay_kernel, steps),
        "relay",
        arrived,
        [((rows + pad, out_width), bf16)] * steps,
    )
    slots = all_to_chip(slots)
    keep, send = call(
        functools.partial(sum_kernel, steps),
        "sum_heads",
        slots,
        [((rows + pad, out_width // 2), bf16), ((rows, out_width // 2), bf16)],
    )
    return tuple(
        call(
            finish_kernel,
            "finish",
            (keep, to_core(send)),
            [((2 * rows, out_width // 2), bf16), ((count, out_width // 2), bf16)],
        )
    )


floor_value = -1e30


def initial_positions(block_map, first_row, row_count, block_rows):
    row_ids = first_row + jnp.arange(row_count, dtype=jnp.int32)
    block_ids = row_ids // block_rows
    table_ids = jnp.arange(block_map.shape[0], dtype=jnp.int32)
    mapped = jnp.sum(
        jnp.where(block_ids[:, None] == table_ids[None, :], block_map[None, :], 0), axis=1
    )
    return mapped * block_rows + row_ids % block_rows


def request_index(positions, request_ends):
    return jnp.sum((positions[:, None] >= request_ends[None, :]).astype(jnp.int32), axis=1)


def round_weights(weights):
    rounded = weights.astype(jnp.bfloat16)
    rounded = lax.optimization_barrier(rounded)
    return rounded.astype(jnp.float32)


def softmax_parts(
    dec_heads, projected_key_rows, projected_value_rows, owned, kv_heads, head_dim, score_scale
):
    row_count = projected_key_rows.shape[0]
    scores = (
        jnp.einsum(
            "rgjd,tgd->rgjt",
            dec_heads,
            projected_key_rows.reshape(row_count, kv_heads, head_dim),
            preferred_element_type=jnp.float32,
        )
        * score_scale
    )
    scores = jnp.where(owned, scores, floor_value)
    part_peak = jnp.max(scores, axis=3)
    weights = jnp.where(owned, jnp.exp(scores - part_peak[..., None]), 0.0)
    part_total = jnp.sum(weights, axis=3)
    part_mixed = jnp.einsum(
        "rgjt,tgd->rgjd",
        weights.astype(jnp.bfloat16),
        projected_value_rows.reshape(row_count, kv_heads, head_dim),
        preferred_element_type=jnp.float32,
    )
    return (part_peak, part_total, part_mixed)


def on_device_large(
    tokens, new_token_states, w_query, key_matrix, value_matrix, w_out, lengths, block_map
):
    local_rows = tokens.shape[0]
    block_rows = local_rows // 2
    request_count = new_token_states.shape[0]
    head_dim = HEAD_SIZE
    query_width = w_query.shape[1]
    kv_width = key_matrix.shape[1]
    kv_heads = kv_width // head_dim
    query_group_count = query_width // kv_width
    score_scale = 1.0 / math.sqrt(head_dim)
    device = lax.axis_index("ctx")
    request_ends = jnp.cumsum(lengths)
    inputs = jnp.concatenate([tokens, new_token_states], axis=0)
    shard_pieces = (
        lax.all_gather(w_query, "ctx", axis=0, tiled=True),
        lax.all_gather(key_matrix, "ctx", axis=0, tiled=True),
        lax.all_gather(value_matrix, "ctx", axis=0, tiled=True),
    )
    query_all, key_all, value_all = tuple(
        (jnp.dot(inputs, weight, preferred_element_type=jnp.float32) for weight in shard_pieces)
    )
    query_all = query_all.astype(jnp.bfloat16)
    key_all = key_all.astype(jnp.bfloat16)
    value_all = value_all.astype(jnp.bfloat16)
    local_query = query_all[:local_rows]
    local_keys = key_all[:local_rows]
    local_values = value_all[:local_rows]
    dec_query = query_all[local_rows:]
    decode_key_rows = key_all[local_rows:]
    decode_value_rows = value_all[local_rows:]
    token_pos = initial_positions(block_map, device * local_rows, local_rows, block_rows)
    token_request = request_index(token_pos, request_ends)
    query_heads = local_query.reshape(local_rows, kv_heads, query_group_count, head_dim)

    def attend(running, shard_pieces, first_row):
        peak_run, total_run, mixed_run = running
        key_piece, value_piece = shard_pieces
        row_count = key_piece.shape[0]
        key_pos = initial_positions(block_map, first_row, row_count, block_rows)
        key_request = request_index(key_pos, request_ends)
        allowed = (key_request[None, :] == token_request[:, None]) & (
            key_pos[None, :] <= token_pos[:, None]
        )
        scores = (
            jnp.einsum(
                "tgjd,kgd->gjtk",
                query_heads,
                key_piece.reshape(row_count, kv_heads, head_dim),
                preferred_element_type=jnp.float32,
            )
            * score_scale
        )
        scores = jnp.where(allowed, scores, floor_value)
        peak_new = jnp.maximum(peak_run, jnp.max(scores, axis=3))
        weights = jnp.where(allowed, jnp.exp(scores - peak_new[..., None]), 0.0)
        rescale = jnp.exp(peak_run - peak_new)
        total_new = total_run * rescale + jnp.sum(weights, axis=3)
        mixed_new = mixed_run * rescale[..., None] + jnp.einsum(
            "gjtk,kgd->gjtd",
            weights.astype(jnp.bfloat16),
            value_piece.reshape(row_count, kv_heads, head_dim),
            preferred_element_type=jnp.float32,
        )
        return (peak_new, total_new, mixed_new)

    start_state = (
        jnp.full((kv_heads, query_group_count, local_rows), floor_value, jnp.float32),
        jnp.zeros((kv_heads, query_group_count, local_rows), jnp.float32),
        jnp.zeros((kv_heads, query_group_count, local_rows, head_dim), jnp.float32),
    )
    dec_heads = dec_query.reshape(request_count, kv_heads, query_group_count, head_dim)
    request_ids = jnp.arange(request_count, dtype=jnp.int32)
    cache_keys, cache_values = (
        lax.all_gather(local_keys, "ctx", axis=0, tiled=True),
        lax.all_gather(local_values, "ctx", axis=0, tiled=True),
    )
    total_rows = cache_keys.shape[0]
    shard_count = total_rows // local_rows
    limit = max(1, 1024 // local_rows)
    step_rows = local_rows * math.gcd(shard_count, 1 << limit.bit_length() - 1)

    def key_step(running, step_index):
        first_row = step_index * step_rows
        pieces = (
            lax.dynamic_slice_in_dim(cache_keys, first_row, step_rows, 0),
            lax.dynamic_slice_in_dim(cache_values, first_row, step_rows, 0),
        )
        return (attend(running, pieces, first_row), None)

    final_state, unused = lax.scan(
        key_step, start_state, jnp.arange(total_rows // step_rows, dtype=jnp.int32)
    )
    peak_run, total_run, mixed_run = final_state
    cache_pos = (
        block_map[:, None] * block_rows + jnp.arange(block_rows, dtype=jnp.int32)[None, :]
    ).reshape(total_rows)
    cache_request = request_index(cache_pos, request_ends)
    owned = (cache_request[None, :] == request_ids[:, None])[:, None, None, :]
    cache_peak, cache_total, cache_mixed = softmax_parts(
        dec_heads, cache_keys, cache_values, owned, kv_heads, head_dim, score_scale
    )
    attended = (
        (mixed_run / total_run[..., None]).transpose(2, 0, 1, 3).reshape(local_rows, query_width)
    )
    attended = attended.astype(jnp.bfloat16)
    own_keys = decode_key_rows.reshape(request_count, kv_heads, 1, head_dim).astype(jnp.float32)
    own_values = decode_value_rows.reshape(request_count, kv_heads, 1, head_dim).astype(jnp.float32)
    self_scores = jnp.sum(dec_heads.astype(jnp.float32) * own_keys, axis=3) * score_scale
    peak_all = jnp.maximum(cache_peak, self_scores)
    rescale = jnp.exp(cache_peak - peak_all)
    self_weights = jnp.exp(self_scores - peak_all)
    dec_total = cache_total * rescale + self_weights
    dec_mixed = (
        cache_mixed * rescale[..., None] + round_weights(self_weights)[..., None] * own_values
    )
    dec_attn = (
        (dec_mixed / dec_total[..., None]).reshape(request_count, query_width).astype(jnp.bfloat16)
    )
    attended_all = jnp.concatenate([attended, dec_attn], axis=0)
    head_block = lax.all_gather(w_out, "ctx", axis=1, tiled=True)
    column_block = lax.all_to_all(head_block, "tp", split_axis=1, concat_axis=0, tiled=True)
    summed_rows = jnp.dot(
        lax.all_gather(attended_all, "tp", axis=1, tiled=True),
        column_block,
        preferred_element_type=jnp.float32,
    )
    summed_rows = summed_rows.astype(jnp.bfloat16)
    return (summed_rows[:local_rows], summed_rows[local_rows:])

def solution(mesh):
    steps, tp = mesh.shape["ctx"], mesh.shape["tp"]

    def on_device(tokens, *rest):
        small = tp == 2 * steps and steps & (steps - 1) == 0 and tokens.shape[0] * steps <= 1024
        if small:
            return on_device_small(steps, tp, tokens, *rest)
        return on_device_large(tokens, *rest)

    return jax.shard_map(
        on_device,
        mesh=mesh,
        in_specs=(
            P("ctx", None),
            P(),
            P("ctx", "tp"),
            P("ctx", "tp"),
            P("ctx", "tp"),
            P("tp", "ctx"),
            P(),
            P(),
        ),
        out_specs=(P("ctx", "tp"), P(None, "tp")),
        check_vma=False,
    )
```

```python
import functools
import math

import jax
import jax.numpy as jnp
from jax import lax
from jax.experimental import pallas as pl
from jax.experimental.pallas import tpu as pltpu
from jax.sharding import PartitionSpec as P

HEAD_SIZE = 128
FLOOR = -1e30
LAST = 1 << 30
ROW_TILE = 8
VMEM_BYTES = 48 * 1024 * 1024


def vmem():
    return pl.BlockSpec(memory_space=pltpu.VMEM)


def smem():
    return pl.BlockSpec(memory_space=pltpu.SMEM)


def partners(core):
    return [0, 2 - core, 1 + core, 3]


def place():
    t = lax.axis_index("tp")
    return lax.axis_index("ctx"), t // 2, t % 2


def pack_kernel(*refs):
    out = refs[-1]
    out[...] = jnp.concatenate([ref[...] for ref in refs[:-1]], axis=1)


def project_kernel(parts_of, *refs):
    blocks, (new, own, other), refs = refs[:4], refs[4:7], refs[7:]
    (held, new_held), outs, inputs = refs[:2], refs[2:5], refs[5]
    rows = held.shape[0]
    count = new.shape[0]
    pad = new_held.shape[0]
    tail = len(blocks) * rows
    for step, block in enumerate(blocks):
        inputs[step * rows : (step + 1) * rows, :] = block[...]
    inputs[tail:, :] = jnp.zeros_like(inputs[tail:, :])
    inputs[tail : tail + count, :] = new[...]
    x = inputs[...]
    column = 0
    for start, stop in parts_of:
        weight = jnp.concatenate([own[:, start:stop], other[:, start:stop]], axis=1)
        part = jnp.dot(x, weight, preferred_element_type=jnp.float32)
        to = slice(column, column + weight.shape[1])
        held[:, to] = part[:rows]
        news = part[tail : tail + pad].astype(new_held.dtype)
        new_held[:, to] = news
        for step, out in enumerate(outs, 1):
            out[:rows, to] = part[step * rows : (step + 1) * rows].astype(out.dtype)
            out[rows:, to] = news
        column += weight.shape[1]


def add_kernel(own, new_own, first, second, both, held, keyval, new):
    rows = held.shape[0]

    def total(own, at):
        parts = [own[...].astype(jnp.float32)]
        parts += [ref[at, :].astype(jnp.float32) for ref in (first, second, both)]
        return ((parts[0] + parts[1]) + (parts[2] + parts[3])).astype(held.dtype)

    sums = total(own, slice(0, rows))
    held[...] = sums
    keyval[...] = sums[:, held.shape[1] - keyval.shape[1] :]
    new[...] = total(new_own, slice(rows, None))


def request_of(position, ends):
    found = jnp.zeros_like(position)
    for end in ends:
        found = found + jnp.where(position >= end, 1, 0)
    return found


def attend_kernel(count, scale, block_map, lengths, *refs):
    mine, theirs, refs = refs[:4], refs[4:8], refs[8:]
    new, columns, refs = refs[0], (refs[1:3], refs[3:5]), refs[5:]
    keep, send, q_all, key_all, value_all, attended = refs
    steps = len(mine)
    rows, features = mine[0].shape
    q_width, kv_width = q_all.shape[1], key_all.shape[1]
    head = HEAD_SIZE
    groups = kv_width // head
    per_group = q_width // kv_width
    pad = new.shape[0]
    tail = 2 * rows
    q_rows = q_all.shape[0]
    k_rows = key_all.shape[0]
    k_tail = 2 * steps * rows
    half = kv_width // 2
    c, _, k = place()

    key_all[k_tail:, :] = jnp.zeros_like(key_all[k_tail:, :])
    value_all[k_tail:, :] = jnp.zeros_like(value_all[k_tail:, :])
    for number in range(steps):
        at = slice(number * rows, (number + 1) * rows)
        v_at = mine[number].shape[1] - kv_width
        key_all[at, :] = mine[number][:, v_at - kv_width : v_at]
        value_all[at, :] = mine[number][:, v_at:]
        at = slice((steps + number) * rows, (steps + number + 1) * rows)
        v_at = theirs[number].shape[1] - kv_width
        k_at = v_at - kv_width
        key_all[at, :half] = theirs[number][:, k_at + half : v_at]
        key_all[at, half:] = theirs[number][:, k_at : k_at + half]
        value_all[at, :half] = theirs[number][:, v_at + half :]
        value_all[at, half:] = theirs[number][:, v_at : v_at + half]
    key_all[k_tail : k_tail + pad, :] = new[:, q_width : q_width + kv_width]
    value_all[k_tail : k_tail + pad, :] = new[:, q_width + kv_width :]
    q_all[tail:, :] = jnp.zeros_like(q_all[tail:, :])
    for number in range(2):
        q_all[number * rows : (number + 1) * rows, :] = mine[number][:, :q_width]
    q_all[tail : tail + pad, :] = new[:, :q_width]

    ends, total = [], 0
    for request in range(count):
        total = total + lengths[request]
        ends.append(total)

    def labels(shape, axis, held):
        index = lax.broadcasted_iota(jnp.int32, shape, axis)
        position = jnp.zeros(shape, jnp.int32)
        for number, block in enumerate(held):
            inside = (index >= number * rows) & (index < (number + 1) * rows)
            position = jnp.where(inside, block_map[block] * rows + index - number * rows, position)
        last = len(held) * rows
        is_new = index >= last
        request = jnp.where(is_new, index - last, request_of(position, ends))
        return jnp.where(is_new, LAST, position), request

    held = [2 * (c ^ mask) + core for core in (k, 1 - k) for mask in partners(core)]
    q_position, q_request = labels((q_rows, 1), 0, held[:2])
    k_position, k_request = labels((1, k_rows), 1, held)
    allowed = (q_request == k_request) & (k_position <= q_position)

    for group in range(groups):
        keys = key_all[:, group * head : (group + 1) * head]
        values = value_all[:, group * head : (group + 1) * head]
        for member in range(per_group):
            at = (group * per_group + member) * head
            scores = lax.dot_general(
                q_all[:, at : at + head],
                keys,
                (((1,), (1,)), ((), ())),
                preferred_element_type=jnp.float32,
            )
            scores = jnp.where(allowed, scores * scale, FLOOR)
            weights = jnp.exp(scores - jnp.max(scores, axis=1, keepdims=True))
            denom = jnp.sum(weights, axis=1, keepdims=True)
            mixed = jnp.dot(
                weights.astype(jnp.bfloat16), values, preferred_element_type=jnp.float32
            )
            attended[:, at : at + head] = (mixed / denom).astype(jnp.bfloat16)

    for number, (w_own, w_other) in enumerate(columns):
        rows_own = w_own.shape[0]
        result = (
            jnp.dot(attended[:, :rows_own], w_own[...], preferred_element_type=jnp.float32)
            + jnp.dot(attended[:, rows_own:], w_other[...], preferred_element_type=jnp.float32)
        ).astype(jnp.bfloat16)
        for out, block in ((keep, 0), (send, 1)):
            at = number * (rows + pad)
            out[at : at + rows, :] = result[block * rows : (block + 1) * rows]
            out[at + rows : at + rows + pad, :] = result[tail : tail + pad]


def relay_kernel(keep, got, *outs):
    c, z, k = place()
    rows = outs[0].shape[0]
    blocks = [(ref, number) for ref in (keep, got) for number in range(2)]
    masks = [partners(k)[i] for i in (0, 2, 1, 3)]
    for slot, out in enumerate(outs):
        for mask, (ref, number) in zip(masks, blocks):

            @pl.when((c ^ z ^ slot) == mask)
            def _(out=out, ref=ref, number=number):
                out[...] = ref[number * rows : (number + 1) * rows, :]


def sum_kernel(*refs):
    parts, (keep, send) = refs[:-2], refs[-2:]
    width = keep.shape[1]
    rows = send.shape[0]
    _, _, k = place()
    for out, core in ((keep, k), (send, 1 - k)):
        column = pl.ds(pl.multiple_of(core * width, width), width)
        terms = [part[:, column].astype(jnp.float32) for part in parts]
        while len(terms) > 1:
            terms = [a + b for a, b in zip(terms[::2], terms[1::2])]
        out[...] = terms[0][: out.shape[0]].astype(out.dtype)


def finish_kernel(keep, other, prefill, decode):
    _, _, k = place()
    rows = other.shape[0]
    prefill[pl.ds(pl.multiple_of(k * rows, rows), rows), :] = keep[:rows]
    prefill[pl.ds(pl.multiple_of((1 - k) * rows, rows), rows), :] = other[...]
    decode[...] = keep[rows : rows + decode.shape[0]]


def on_device_small(
    steps, tp, tokens, new_token_states, w_query, key_matrix, value_matrix, w_out, lengths, block_map
):
    bf16, f32 = jnp.bfloat16, jnp.float32
    rows = tokens.shape[0] // 2
    depth = w_query.shape[0]
    count = new_token_states.shape[0]
    pad = -(-count // ROW_TILE) * ROW_TILE
    q_width = 2 * w_query.shape[1]
    kv_width = 2 * key_matrix.shape[1]
    features = q_width + 2 * kv_width
    out_width = w_out.shape[1]
    devices = [divmod(source, tp) for source in range(steps * tp)]

    def to_core(value):
        return lax.ppermute(value, "tp", [(i, i ^ 1) for i in range(tp)])

    def to_chip(value, step):
        return lax.ppermute(value, "tp", [(i, i ^ (2 * step)) for i in range(tp)])

    def to_partner(value, number, swap=0):
        pairs = [
            (c * tp + t, (c ^ partners((t ^ swap) % 2)[number]) * tp + (t ^ swap))
            for c, t in devices
        ]
        return lax.ppermute(value, ("ctx", "tp"), pairs)

    def to_partners(values):
        return [to_partner(value, number) for number, value in enumerate(values, 1)]

    def call(kernel, name, inputs, shapes, scratch=(), spaces=None):
        return pl.pallas_call(
            kernel,
            out_shape=[jax.ShapeDtypeStruct(shape, kind) for shape, kind in shapes],
            in_specs=spaces or [vmem()] * len(inputs),
            out_specs=[vmem()] * len(shapes),
            scratch_shapes=list(scratch),
            compiler_params=pltpu.CompilerParams(vmem_limit_bytes=VMEM_BYTES),
            name=name,
        )(*inputs)

    c, _, k = place()
    sent = [
        lax.dynamic_slice(tokens, (k * rows, (c ^ mask) * depth), (rows, depth))
        for mask in partners(k)
    ]
    new_columns = lax.dynamic_slice_in_dim(new_token_states, c * depth, depth, 1)
    blocks = [sent[0]] + to_partners(sent[1:])
    *weights, _ = lax.optimization_barrier((w_query, key_matrix, value_matrix, sent[1]))
    (own,) = call(pack_kernel, "pack_weights", weights, [((depth, features // 2), bf16)])
    other = to_core(own)

    part_shape = (rows + pad, features)
    x_rows = -(-(steps * rows + pad) // 16) * 16
    edges = [0, q_width // 2, (q_width + kv_width) // 2, features // 2]
    own_part, new_part, *parts = call(
        functools.partial(project_kernel, list(zip(edges, edges[1:]))),
        "project",
        (*blocks, new_columns, own, other),
        [((rows, features), f32), ((pad, features), bf16)] + [(part_shape, bf16)] * (steps - 1),
        [pltpu.VMEM((x_rows, depth), bf16)],
    )

    w_second = to_partner(w_out, 2)
    w_out_later, _ = lax.optimization_barrier((w_out, new_part))
    w_second_other = to_partner(w_out_later, 2, 1)

    held, keyval, new = call(
        add_kernel,
        "add_parts",
        (own_part, new_part, *to_partners(parts)),
        [((rows, features), bf16), ((rows, 2 * kv_width), bf16), ((pad, features), bf16)],
    )
    w_out_last, _, w_second = lax.optimization_barrier((w_out, new, w_second))
    w_other = to_core(w_out_last)

    mine = [held] + to_partners([held, keyval, keyval])
    theirs = [to_core(value) for value in [keyval] + mine[1:]]

    q_rows = -(-(2 * rows + pad) // 16) * 16
    k_rows = -(-(2 * steps * rows + pad) // 128) * 128
    block = (rows + pad, out_width)
    keep, send = call(
        functools.partial(attend_kernel, count, 1.0 / math.sqrt(HEAD_SIZE)),
        "attend",
        (block_map, lengths, *mine, *theirs, new, w_out, w_other, w_second, w_second_other),
        [((2 * block[0], out_width), bf16)] * 2,
        [
            pltpu.VMEM((q_rows, q_width), bf16),
            pltpu.VMEM((k_rows, kv_width), bf16),
            pltpu.VMEM((k_rows, kv_width), bf16),
            pltpu.VMEM((q_rows, q_width), bf16),
        ],
        [smem()] * 2 + [vmem()] * (2 * steps + 5),
    )

    got = to_partner(send, 1)
    slots = call(relay_kernel, "relay", (keep, got), [(block, bf16)] * steps)
    slots = [slots[0]] + [to_chip(slot, step) for step, slot in enumerate(slots[1:], 1)]
    keep, send = call(
        sum_kernel,
        "sum_heads",
        slots,
        [((rows + pad, out_width // 2), bf16), ((rows, out_width // 2), bf16)],
    )
    return tuple(
        call(
            finish_kernel,
            "finish",
            (keep, to_core(send)),
            [((2 * rows, out_width // 2), bf16), ((count, out_width // 2), bf16)],
        )
    )


floor_value = -1e30


def initial_positions(block_map, first_row, row_count, block_rows):
    row_ids = first_row + jnp.arange(row_count, dtype=jnp.int32)
    block_ids = row_ids // block_rows
    table_ids = jnp.arange(block_map.shape[0], dtype=jnp.int32)
    mapped = jnp.sum(
        jnp.where(block_ids[:, None] == table_ids[None, :], block_map[None, :], 0), axis=1
    )
    return mapped * block_rows + row_ids % block_rows


def request_index(positions, request_ends):
    return jnp.sum((positions[:, None] >= request_ends[None, :]).astype(jnp.int32), axis=1)


def round_weights(weights):
    rounded = weights.astype(jnp.bfloat16)
    rounded = lax.optimization_barrier(rounded)
    return rounded.astype(jnp.float32)


def softmax_parts(
    dec_heads, projected_key_rows, projected_value_rows, owned, kv_heads, head_dim, score_scale
):
    row_count = projected_key_rows.shape[0]
    scores = (
        jnp.einsum(
            "rgjd,tgd->rgjt",
            dec_heads,
            projected_key_rows.reshape(row_count, kv_heads, head_dim),
            preferred_element_type=jnp.float32,
        )
        * score_scale
    )
    scores = jnp.where(owned, scores, floor_value)
    part_peak = jnp.max(scores, axis=3)
    weights = jnp.where(owned, jnp.exp(scores - part_peak[..., None]), 0.0)
    part_total = jnp.sum(weights, axis=3)
    part_mixed = jnp.einsum(
        "rgjt,tgd->rgjd",
        weights.astype(jnp.bfloat16),
        projected_value_rows.reshape(row_count, kv_heads, head_dim),
        preferred_element_type=jnp.float32,
    )
    return (part_peak, part_total, part_mixed)


def on_device_large(
    tokens, new_token_states, w_query, key_matrix, value_matrix, w_out, lengths, block_map
):
    local_rows = tokens.shape[0]
    block_rows = local_rows // 2
    request_count = new_token_states.shape[0]
    head_dim = HEAD_SIZE
    query_width = w_query.shape[1]
    kv_width = key_matrix.shape[1]
    kv_heads = kv_width // head_dim
    query_group_count = query_width // kv_width
    score_scale = 1.0 / math.sqrt(head_dim)
    device = lax.axis_index("ctx")
    request_ends = jnp.cumsum(lengths)
    inputs = jnp.concatenate([tokens, new_token_states], axis=0)
    shard_pieces = (
        lax.all_gather(w_query, "ctx", axis=0, tiled=True),
        lax.all_gather(key_matrix, "ctx", axis=0, tiled=True),
        lax.all_gather(value_matrix, "ctx", axis=0, tiled=True),
    )
    query_all, key_all, value_all = tuple(
        (jnp.dot(inputs, weight, preferred_element_type=jnp.float32) for weight in shard_pieces)
    )
    query_all = query_all.astype(jnp.bfloat16)
    key_all = key_all.astype(jnp.bfloat16)
    value_all = value_all.astype(jnp.bfloat16)
    local_query = query_all[:local_rows]
    local_keys = key_all[:local_rows]
    local_values = value_all[:local_rows]
    dec_query = query_all[local_rows:]
    decode_key_rows = key_all[local_rows:]
    decode_value_rows = value_all[local_rows:]
    token_pos = initial_positions(block_map, device * local_rows, local_rows, block_rows)
    token_request = request_index(token_pos, request_ends)
    query_heads = local_query.reshape(local_rows, kv_heads, query_group_count, head_dim)

    def attend(running, shard_pieces, first_row):
        peak_run, total_run, mixed_run = running
        key_piece, value_piece = shard_pieces
        row_count = key_piece.shape[0]
        key_pos = initial_positions(block_map, first_row, row_count, block_rows)
        key_request = request_index(key_pos, request_ends)
        allowed = (key_request[None, :] == token_request[:, None]) & (
            key_pos[None, :] <= token_pos[:, None]
        )
        scores = (
            jnp.einsum(
                "tgjd,kgd->gjtk",
                query_heads,
                key_piece.reshape(row_count, kv_heads, head_dim),
                preferred_element_type=jnp.float32,
            )
            * score_scale
        )
        scores = jnp.where(allowed, scores, floor_value)
        peak_new = jnp.maximum(peak_run, jnp.max(scores, axis=3))
        weights = jnp.where(allowed, jnp.exp(scores - peak_new[..., None]), 0.0)
        rescale = jnp.exp(peak_run - peak_new)
        total_new = total_run * rescale + jnp.sum(weights, axis=3)
        mixed_new = mixed_run * rescale[..., None] + jnp.einsum(
            "gjtk,kgd->gjtd",
            weights.astype(jnp.bfloat16),
            value_piece.reshape(row_count, kv_heads, head_dim),
            preferred_element_type=jnp.float32,
        )
        return (peak_new, total_new, mixed_new)

    start_state = (
        jnp.full((kv_heads, query_group_count, local_rows), floor_value, jnp.float32),
        jnp.zeros((kv_heads, query_group_count, local_rows), jnp.float32),
        jnp.zeros((kv_heads, query_group_count, local_rows, head_dim), jnp.float32),
    )
    dec_heads = dec_query.reshape(request_count, kv_heads, query_group_count, head_dim)
    request_ids = jnp.arange(request_count, dtype=jnp.int32)
    cache_keys, cache_values = (
        lax.all_gather(local_keys, "ctx", axis=0, tiled=True),
        lax.all_gather(local_values, "ctx", axis=0, tiled=True),
    )
    total_rows = cache_keys.shape[0]
    shard_count = total_rows // local_rows
    limit = max(1, 1024 // local_rows)
    step_rows = local_rows * math.gcd(shard_count, 1 << limit.bit_length() - 1)

    def key_step(running, step_index):
        first_row = step_index * step_rows
        pieces = (
            lax.dynamic_slice_in_dim(cache_keys, first_row, step_rows, 0),
            lax.dynamic_slice_in_dim(cache_values, first_row, step_rows, 0),
        )
        return (attend(running, pieces, first_row), None)

    final_state, unused = lax.scan(
        key_step, start_state, jnp.arange(total_rows // step_rows, dtype=jnp.int32)
    )
    peak_run, total_run, mixed_run = final_state
    cache_pos = (
        block_map[:, None] * block_rows + jnp.arange(block_rows, dtype=jnp.int32)[None, :]
    ).reshape(total_rows)
    cache_request = request_index(cache_pos, request_ends)
    owned = (cache_request[None, :] == request_ids[:, None])[:, None, None, :]
    cache_peak, cache_total, cache_mixed = softmax_parts(
        dec_heads, cache_keys, cache_values, owned, kv_heads, head_dim, score_scale
    )
    attended = (
        (mixed_run / total_run[..., None]).transpose(2, 0, 1, 3).reshape(local_rows, query_width)
    )
    attended = attended.astype(jnp.bfloat16)
    own_keys = decode_key_rows.reshape(request_count, kv_heads, 1, head_dim).astype(jnp.float32)
    own_values = decode_value_rows.reshape(request_count, kv_heads, 1, head_dim).astype(jnp.float32)
    self_scores = jnp.sum(dec_heads.astype(jnp.float32) * own_keys, axis=3) * score_scale
    peak_all = jnp.maximum(cache_peak, self_scores)
    rescale = jnp.exp(cache_peak - peak_all)
    self_weights = jnp.exp(self_scores - peak_all)
    dec_total = cache_total * rescale + self_weights
    dec_mixed = (
        cache_mixed * rescale[..., None] + round_weights(self_weights)[..., None] * own_values
    )
    dec_attn = (
        (dec_mixed / dec_total[..., None]).reshape(request_count, query_width).astype(jnp.bfloat16)
    )
    attended_all = jnp.concatenate([attended, dec_attn], axis=0)
    head_block = lax.all_gather(w_out, "ctx", axis=1, tiled=True)
    column_block = lax.all_to_all(head_block, "tp", split_axis=1, concat_axis=0, tiled=True)
    summed_rows = jnp.dot(
        lax.all_gather(attended_all, "tp", axis=1, tiled=True),
        column_block,
        preferred_element_type=jnp.float32,
    )
    summed_rows = summed_rows.astype(jnp.bfloat16)
    return (summed_rows[:local_rows], summed_rows[local_rows:])

def solution(mesh):
    steps, tp = mesh.shape["ctx"], mesh.shape["tp"]

    def on_device(tokens, *rest):
        small = steps == 4 and tp == 8 and tokens.shape[0] * steps <= 1024
        if small:
            return on_device_small(steps, tp, tokens, *rest)
        return on_device_large(tokens, *rest)

    return jax.shard_map(
        on_device,
        mesh=mesh,
        in_specs=(
            P("ctx", None),
            P(),
            P("ctx", "tp"),
            P("ctx", "tp"),
            P("ctx", "tp"),
            P("tp", "ctx"),
            P(),
            P(),
        ),
        out_specs=(P("ctx", "tp"), P(None, "tp")),
        check_vma=False,
    )
```

```python
import functools
import math

import jax
import jax.numpy as jnp
from jax import lax
from jax.experimental import pallas as pl
from jax.experimental.pallas import tpu as pltpu
from jax.sharding import PartitionSpec as P

HEAD_SIZE = 128
FLOOR = -1e30
LAST = 1 << 30
ROW_TILE = 8
VMEM_BYTES = 48 * 1024 * 1024


def vmem():
    return pl.BlockSpec(memory_space=pltpu.VMEM)


def smem():
    return pl.BlockSpec(memory_space=pltpu.SMEM)


def partners(core):
    return [0, 2 - core, 1 + core, 3]


def turned(values):
    return [values[0], *values[:0:-1]]


def place():
    t = lax.axis_index("tp")
    return lax.axis_index("ctx"), t // 2, t % 2


def pack_kernel(*refs):
    out = refs[-1]
    out[...] = jnp.concatenate([ref[...] for ref in refs[:-1]], axis=1)


def project_kernel(parts_of, *refs):
    blocks, (new, own, other), refs = turned(refs[:4]), refs[4:7], refs[7:]
    (held, new_held), outs, inputs = refs[:2], refs[2:5], refs[5]
    rows = held.shape[0]
    count = new.shape[0]
    pad = new_held.shape[0]
    tail = len(blocks) * rows
    for step, block in enumerate(blocks):
        inputs[step * rows : (step + 1) * rows, :] = block[...]
    inputs[tail:, :] = jnp.zeros_like(inputs[tail:, :])
    inputs[tail : tail + count, :] = new[...]
    x = inputs[...]
    column = 0
    for start, stop in parts_of:
        weight = jnp.concatenate([own[:, start:stop], other[:, start:stop]], axis=1)
        part = jnp.dot(x, weight, preferred_element_type=jnp.float32)
        to = slice(column, column + weight.shape[1])
        held[:, to] = part[:rows]
        news = part[tail : tail + pad].astype(new_held.dtype)
        new_held[:, to] = news
        for step, out in enumerate(outs, 1):
            out[:rows, to] = part[step * rows : (step + 1) * rows].astype(out.dtype)
            out[rows:, to] = news
        column += weight.shape[1]


def add_kernel(own, new_own, first, second, both, held, new):
    rows = held.shape[0]

    def total(own, at):
        parts = [own[...].astype(jnp.float32)]
        parts += [ref[at, :].astype(jnp.float32) for ref in (first, second, both)]
        return ((parts[0] + parts[1]) + (parts[2] + parts[3])).astype(held.dtype)

    held[...] = total(own, slice(0, rows))
    new[...] = total(new_own, slice(rows, None))


def request_of(position, ends):
    found = jnp.zeros_like(position)
    for end in ends:
        found = found + jnp.where(position >= end, 1, 0)
    return found


def attend_kernel(count, scale, block_map, lengths, *refs):
    mine, theirs, refs = turned(refs[:4]), turned(refs[4:8]), refs[8:]
    (new, w_own, w_other), outs, refs = refs[:3], (refs[3:7], refs[7:11]), refs[11:]
    q_all, key_all, value_all, attended, result = refs
    steps = len(mine)
    rows, features = mine[0].shape
    q_width, kv_width = q_all.shape[1], key_all.shape[1]
    head = HEAD_SIZE
    groups = kv_width // head
    per_group = q_width // kv_width
    pad = new.shape[0]
    tail = steps * rows
    q_rows = q_all.shape[0]
    k_rows = key_all.shape[0]
    k_tail = 2 * steps * rows
    half = kv_width // 2
    c, _, k = place()

    key_all[k_tail:, :] = jnp.zeros_like(key_all[k_tail:, :])
    value_all[k_tail:, :] = jnp.zeros_like(value_all[k_tail:, :])
    for number in range(steps):
        at = slice(number * rows, (number + 1) * rows)
        v_at = mine[number].shape[1] - kv_width
        key_all[at, :] = mine[number][:, v_at - kv_width : v_at]
        value_all[at, :] = mine[number][:, v_at:]
        at = slice((steps + number) * rows, (steps + number + 1) * rows)
        v_at = theirs[number].shape[1] - kv_width
        k_at = v_at - kv_width
        key_all[at, :half] = theirs[number][:, k_at + half : v_at]
        key_all[at, half:] = theirs[number][:, k_at : k_at + half]
        value_all[at, :half] = theirs[number][:, v_at + half :]
        value_all[at, half:] = theirs[number][:, v_at : v_at + half]
    key_all[k_tail : k_tail + pad, :] = new[:, q_width : q_width + kv_width]
    value_all[k_tail : k_tail + pad, :] = new[:, q_width + kv_width :]
    q_all[tail:, :] = jnp.zeros_like(q_all[tail:, :])
    for number in range(steps):
        q_all[number * rows : (number + 1) * rows, :] = mine[number][:, :q_width]
    q_all[tail : tail + pad, :] = new[:, :q_width]

    ends, total = [], 0
    for request in range(count):
        total = total + lengths[request]
        ends.append(total)

    def labels(shape, axis, held):
        index = lax.broadcasted_iota(jnp.int32, shape, axis)
        position = jnp.zeros(shape, jnp.int32)
        for number, block in enumerate(held):
            inside = (index >= number * rows) & (index < (number + 1) * rows)
            position = jnp.where(inside, block_map[block] * rows + index - number * rows, position)
        last = len(held) * rows
        is_new = index >= last
        request = jnp.where(is_new, index - last, request_of(position, ends))
        return jnp.where(is_new, LAST, position), request

    held = [2 * (c ^ mask) + core for core in (k, 1 - k) for mask in partners(core)]
    q_position, q_request = labels((q_rows, 1), 0, held[:steps])
    k_position, k_request = labels((1, k_rows), 1, held)
    allowed = (q_request == k_request) & (k_position <= q_position)

    for group in range(groups):
        keys = key_all[:, group * head : (group + 1) * head]
        values = value_all[:, group * head : (group + 1) * head]
        for member in range(per_group):
            at = (group * per_group + member) * head
            scores = lax.dot_general(
                q_all[:, at : at + head],
                keys,
                (((1,), (1,)), ((), ())),
                preferred_element_type=jnp.float32,
            )
            scores = jnp.where(allowed, scores * scale, FLOOR)
            weights = jnp.exp(scores - jnp.max(scores, axis=1, keepdims=True))
            denom = jnp.sum(weights, axis=1, keepdims=True)
            mixed = jnp.dot(
                weights.astype(jnp.bfloat16), values, preferred_element_type=jnp.float32
            )
            attended[:, at : at + head] = (mixed / denom).astype(jnp.bfloat16)

    rows_own = w_own.shape[0]
    result[...] = (
        jnp.dot(attended[:, :rows_own], w_own[...], preferred_element_type=jnp.float32)
        + jnp.dot(attended[:, rows_own:], w_other[...], preferred_element_type=jnp.float32)
    ).astype(jnp.bfloat16)
    for core, half_outs in zip((1 - k, k), outs):
        width = half_outs[0].shape[1]
        column = pl.ds(pl.multiple_of(core * width, width), width)
        for number, out in enumerate(half_outs):
            out[:rows, :] = result[number * rows : (number + 1) * rows, column]
            out[rows:, :] = result[tail : tail + pad, column]


def relay_kernel(*refs):
    blocks, outs = refs[:4], refs[4:]
    c, z, k = place()
    for slot, out in enumerate(outs):
        for mask, block in zip(partners(k), blocks):

            @pl.when((c ^ z ^ slot) == mask)
            def _(out=out, block=block):
                out[...] = block[...]


def sum_heads(parts):
    terms = [part[...].astype(jnp.float32) for part in parts]
    return ((terms[0] + terms[1]) + (terms[2] + terms[3])).astype(jnp.bfloat16)


def sum_kernel(*refs):
    send = refs[-1]
    send[...] = sum_heads(refs[:-1])[: send.shape[0]]


def finish_kernel(*refs):
    parts, (other, prefill, decode) = refs[:4], refs[4:]
    _, _, k = place()
    rows = other.shape[0]
    total = sum_heads(parts)
    prefill[pl.ds(pl.multiple_of(k * rows, rows), rows), :] = total[:rows]
    prefill[pl.ds(pl.multiple_of((1 - k) * rows, rows), rows), :] = other[...]
    decode[...] = total[rows : rows + decode.shape[0]]


def on_device_small(
    steps, tp, tokens, new_token_states, w_query, key_matrix, value_matrix, w_out, lengths, block_map
):
    bf16, f32 = jnp.bfloat16, jnp.float32
    rows = tokens.shape[0] // 2
    depth = w_query.shape[0]
    count = new_token_states.shape[0]
    pad = -(-count // ROW_TILE) * ROW_TILE
    q_width = 2 * w_query.shape[1]
    kv_width = 2 * key_matrix.shape[1]
    features = q_width + 2 * kv_width
    out_width = w_out.shape[1]
    devices = [divmod(source, tp) for source in range(steps * tp)]

    def to_core(value):
        return lax.ppermute(value, "tp", [(i, i ^ 1) for i in range(tp)])

    def to_chip(value, step):
        return lax.ppermute(value, "tp", [(i, i ^ (2 * step)) for i in range(tp)])

    def to_partner(value, number):
        pairs = [(c * tp + t, (c ^ partners(t % 2)[number]) * tp + t) for c, t in devices]
        return lax.ppermute(value, ("ctx", "tp"), pairs)

    def to_partners(values):
        return [to_partner(value, number) for number, value in enumerate(values, 1)]

    def call(kernel, name, inputs, shapes, scratch=(), spaces=None):
        return pl.pallas_call(
            kernel,
            out_shape=[jax.ShapeDtypeStruct(shape, kind) for shape, kind in shapes],
            in_specs=spaces or [vmem()] * len(inputs),
            out_specs=[vmem()] * len(shapes),
            scratch_shapes=list(scratch),
            compiler_params=pltpu.CompilerParams(vmem_limit_bytes=VMEM_BYTES),
            name=name,
        )(*inputs)

    c, _, k = place()
    sent = [
        lax.dynamic_slice(tokens, (k * rows, (c ^ mask) * depth), (rows, depth))
        for mask in partners(k)
    ]
    new_columns = lax.dynamic_slice_in_dim(new_token_states, c * depth, depth, 1)
    blocks = [sent[0]] + to_partners(sent[1:])
    *weights, _ = lax.optimization_barrier((w_query, key_matrix, value_matrix, sent[1]))
    (own,) = call(pack_kernel, "pack_weights", weights, [((depth, features // 2), bf16)])
    other = to_core(own)

    part_shape = (rows + pad, features)
    x_rows = -(-(steps * rows + pad) // 16) * 16
    edges = [0, q_width // 2, (q_width + kv_width) // 2, features // 2]
    own_part, new_part, *parts = call(
        functools.partial(project_kernel, list(zip(edges, edges[1:]))),
        "project",
        (*turned(blocks), new_columns, own, other),
        [((rows, features), f32), ((pad, features), bf16)] + [(part_shape, bf16)] * (steps - 1),
        [pltpu.VMEM((x_rows, depth), bf16)],
    )

    w_out_later, _ = lax.optimization_barrier((w_out, new_part))
    w_other = to_core(w_out_later)

    held, new = call(
        add_kernel,
        "add_parts",
        (own_part, new_part, *to_partners(parts)),
        [((rows, features), bf16), ((pad, features), bf16)],
    )
    mine = [held] + to_partners([held] * (steps - 1))
    theirs = [to_core(value) for value in mine]

    k_rows = -(-(2 * steps * rows + pad) // 128) * 128
    block = (rows + pad, out_width // 2)
    outs = call(
        functools.partial(attend_kernel, count, 1.0 / math.sqrt(HEAD_SIZE)),
        "attend",
        (block_map, lengths, *turned(mine), *turned(theirs), new, w_out, w_other),
        [(block, bf16)] * (2 * steps),
        [
            pltpu.VMEM((x_rows, q_width), bf16),
            pltpu.VMEM((k_rows, kv_width), bf16),
            pltpu.VMEM((k_rows, kv_width), bf16),
            pltpu.VMEM((x_rows, q_width), bf16),
            pltpu.VMEM((x_rows, out_width), bf16),
        ],
        [smem()] * 2 + [vmem()] * (2 * steps + 3),
    )

    halves = []
    for half in (outs[:steps], outs[steps:]):
        got = [half[0]] + to_partners(half[1:])
        slots = call(relay_kernel, "relay", got, [(block, bf16)] * steps)
        halves.append(
            [slots[0]] + [to_chip(slot, step) for step, slot in enumerate(slots[1:], 1)]
        )
    shape = (rows, out_width // 2)
    (send,) = call(sum_kernel, "sum_heads", halves[0], [(shape, bf16)])
    return tuple(
        call(
            finish_kernel,
            "finish",
            (*halves[1], to_core(send)),
            [((2 * rows, out_width // 2), bf16), ((count, out_width // 2), bf16)],
        )
    )


floor_value = -1e30


def initial_positions(block_map, first_row, row_count, block_rows):
    row_ids = first_row + jnp.arange(row_count, dtype=jnp.int32)
    block_ids = row_ids // block_rows
    table_ids = jnp.arange(block_map.shape[0], dtype=jnp.int32)
    mapped = jnp.sum(
        jnp.where(block_ids[:, None] == table_ids[None, :], block_map[None, :], 0), axis=1
    )
    return mapped * block_rows + row_ids % block_rows


def request_index(positions, request_ends):
    return jnp.sum((positions[:, None] >= request_ends[None, :]).astype(jnp.int32), axis=1)


def round_weights(weights):
    rounded = weights.astype(jnp.bfloat16)
    rounded = lax.optimization_barrier(rounded)
    return rounded.astype(jnp.float32)


def softmax_parts(
    dec_heads, projected_key_rows, projected_value_rows, owned, kv_heads, head_dim, score_scale
):
    row_count = projected_key_rows.shape[0]
    scores = (
        jnp.einsum(
            "rgjd,tgd->rgjt",
            dec_heads,
            projected_key_rows.reshape(row_count, kv_heads, head_dim),
            preferred_element_type=jnp.float32,
        )
        * score_scale
    )
    scores = jnp.where(owned, scores, floor_value)
    part_peak = jnp.max(scores, axis=3)
    weights = jnp.where(owned, jnp.exp(scores - part_peak[..., None]), 0.0)
    part_total = jnp.sum(weights, axis=3)
    part_mixed = jnp.einsum(
        "rgjt,tgd->rgjd",
        weights.astype(jnp.bfloat16),
        projected_value_rows.reshape(row_count, kv_heads, head_dim),
        preferred_element_type=jnp.float32,
    )
    return (part_peak, part_total, part_mixed)


def on_device_large(
    tokens, new_token_states, w_query, key_matrix, value_matrix, w_out, lengths, block_map
):
    local_rows = tokens.shape[0]
    block_rows = local_rows // 2
    request_count = new_token_states.shape[0]
    head_dim = HEAD_SIZE
    query_width = w_query.shape[1]
    kv_width = key_matrix.shape[1]
    kv_heads = kv_width // head_dim
    query_group_count = query_width // kv_width
    score_scale = 1.0 / math.sqrt(head_dim)
    device = lax.axis_index("ctx")
    request_ends = jnp.cumsum(lengths)
    inputs = jnp.concatenate([tokens, new_token_states], axis=0)
    shard_pieces = (
        lax.all_gather(w_query, "ctx", axis=0, tiled=True),
        lax.all_gather(key_matrix, "ctx", axis=0, tiled=True),
        lax.all_gather(value_matrix, "ctx", axis=0, tiled=True),
    )
    query_all, key_all, value_all = tuple(
        (jnp.dot(inputs, weight, preferred_element_type=jnp.float32) for weight in shard_pieces)
    )
    query_all = query_all.astype(jnp.bfloat16)
    key_all = key_all.astype(jnp.bfloat16)
    value_all = value_all.astype(jnp.bfloat16)
    local_query = query_all[:local_rows]
    local_keys = key_all[:local_rows]
    local_values = value_all[:local_rows]
    dec_query = query_all[local_rows:]
    decode_key_rows = key_all[local_rows:]
    decode_value_rows = value_all[local_rows:]
    token_pos = initial_positions(block_map, device * local_rows, local_rows, block_rows)
    token_request = request_index(token_pos, request_ends)
    query_heads = local_query.reshape(local_rows, kv_heads, query_group_count, head_dim)

    def attend(running, shard_pieces, first_row):
        peak_run, total_run, mixed_run = running
        key_piece, value_piece = shard_pieces
        row_count = key_piece.shape[0]
        key_pos = initial_positions(block_map, first_row, row_count, block_rows)
        key_request = request_index(key_pos, request_ends)
        allowed = (key_request[None, :] == token_request[:, None]) & (
            key_pos[None, :] <= token_pos[:, None]
        )
        scores = (
            jnp.einsum(
                "tgjd,kgd->gjtk",
                query_heads,
                key_piece.reshape(row_count, kv_heads, head_dim),
                preferred_element_type=jnp.float32,
            )
            * score_scale
        )
        scores = jnp.where(allowed, scores, floor_value)
        peak_new = jnp.maximum(peak_run, jnp.max(scores, axis=3))
        weights = jnp.where(allowed, jnp.exp(scores - peak_new[..., None]), 0.0)
        rescale = jnp.exp(peak_run - peak_new)
        total_new = total_run * rescale + jnp.sum(weights, axis=3)
        mixed_new = mixed_run * rescale[..., None] + jnp.einsum(
            "gjtk,kgd->gjtd",
            weights.astype(jnp.bfloat16),
            value_piece.reshape(row_count, kv_heads, head_dim),
            preferred_element_type=jnp.float32,
        )
        return (peak_new, total_new, mixed_new)

    start_state = (
        jnp.full((kv_heads, query_group_count, local_rows), floor_value, jnp.float32),
        jnp.zeros((kv_heads, query_group_count, local_rows), jnp.float32),
        jnp.zeros((kv_heads, query_group_count, local_rows, head_dim), jnp.float32),
    )
    dec_heads = dec_query.reshape(request_count, kv_heads, query_group_count, head_dim)
    request_ids = jnp.arange(request_count, dtype=jnp.int32)
    cache_keys, cache_values = (
        lax.all_gather(local_keys, "ctx", axis=0, tiled=True),
        lax.all_gather(local_values, "ctx", axis=0, tiled=True),
    )
    total_rows = cache_keys.shape[0]
    shard_count = total_rows // local_rows
    limit = max(1, 1024 // local_rows)
    step_rows = local_rows * math.gcd(shard_count, 1 << limit.bit_length() - 1)

    def key_step(running, step_index):
        first_row = step_index * step_rows
        pieces = (
            lax.dynamic_slice_in_dim(cache_keys, first_row, step_rows, 0),
            lax.dynamic_slice_in_dim(cache_values, first_row, step_rows, 0),
        )
        return (attend(running, pieces, first_row), None)

    final_state, unused = lax.scan(
        key_step, start_state, jnp.arange(total_rows // step_rows, dtype=jnp.int32)
    )
    peak_run, total_run, mixed_run = final_state
    cache_pos = (
        block_map[:, None] * block_rows + jnp.arange(block_rows, dtype=jnp.int32)[None, :]
    ).reshape(total_rows)
    cache_request = request_index(cache_pos, request_ends)
    owned = (cache_request[None, :] == request_ids[:, None])[:, None, None, :]
    cache_peak, cache_total, cache_mixed = softmax_parts(
        dec_heads, cache_keys, cache_values, owned, kv_heads, head_dim, score_scale
    )
    attended = (
        (mixed_run / total_run[..., None]).transpose(2, 0, 1, 3).reshape(local_rows, query_width)
    )
    attended = attended.astype(jnp.bfloat16)
    own_keys = decode_key_rows.reshape(request_count, kv_heads, 1, head_dim).astype(jnp.float32)
    own_values = decode_value_rows.reshape(request_count, kv_heads, 1, head_dim).astype(jnp.float32)
    self_scores = jnp.sum(dec_heads.astype(jnp.float32) * own_keys, axis=3) * score_scale
    peak_all = jnp.maximum(cache_peak, self_scores)
    rescale = jnp.exp(cache_peak - peak_all)
    self_weights = jnp.exp(self_scores - peak_all)
    dec_total = cache_total * rescale + self_weights
    dec_mixed = (
        cache_mixed * rescale[..., None] + round_weights(self_weights)[..., None] * own_values
    )
    dec_attn = (
        (dec_mixed / dec_total[..., None]).reshape(request_count, query_width).astype(jnp.bfloat16)
    )
    attended_all = jnp.concatenate([attended, dec_attn], axis=0)
    head_block = lax.all_gather(w_out, "ctx", axis=1, tiled=True)
    column_block = lax.all_to_all(head_block, "tp", split_axis=1, concat_axis=0, tiled=True)
    summed_rows = jnp.dot(
        lax.all_gather(attended_all, "tp", axis=1, tiled=True),
        column_block,
        preferred_element_type=jnp.float32,
    )
    summed_rows = summed_rows.astype(jnp.bfloat16)
    return (summed_rows[:local_rows], summed_rows[local_rows:])

def solution(mesh):
    steps, tp = mesh.shape["ctx"], mesh.shape["tp"]

    def on_device(tokens, *rest):
        small = steps == 4 and tp == 8 and tokens.shape[0] * steps <= 1024
        if small:
            return on_device_small(steps, tp, tokens, *rest)
        return on_device_large(tokens, *rest)

    return jax.shard_map(
        on_device,
        mesh=mesh,
        in_specs=(
            P("ctx", None),
            P(),
            P("ctx", "tp"),
            P("ctx", "tp"),
            P("ctx", "tp"),
            P("tp", "ctx"),
            P(),
            P(),
        ),
        out_specs=(P("ctx", "tp"), P(None, "tp")),
        check_vma=False,
    )
```

```python
import functools
import math

import jax
import jax.numpy as jnp
from jax import lax
from jax.experimental import pallas as pl
from jax.experimental.pallas import tpu as pltpu
from jax.sharding import PartitionSpec as P

HEAD_SIZE = 128
FLOOR = -1e30
LAST = 1 << 30
ROW_TILE = 8
VMEM_BYTES = 48 * 1024 * 1024


def vmem():
    return pl.BlockSpec(memory_space=pltpu.VMEM)


def smem():
    return pl.BlockSpec(memory_space=pltpu.SMEM)


def partners(core):
    return [0, 2 - core, 1 + core, 3]


def turned(values):
    return [values[0], *values[:0:-1]]


def place():
    t = lax.axis_index("tp")
    return lax.axis_index("ctx"), t // 2, t % 2


def pack_kernel(*refs):
    out = refs[-1]
    out[...] = jnp.concatenate([ref[...] for ref in refs[:-1]], axis=1)


def project_kernel(parts_of, *refs):
    blocks, (new, own, other), refs = turned(refs[:4]), refs[4:7], refs[7:]
    held, held_second, new_held, send, inputs = refs
    rows = held.shape[0]
    count = new.shape[0]
    pad = new_held.shape[0]
    tail = len(blocks) * rows
    for step, block in enumerate(blocks):
        inputs[step * rows : (step + 1) * rows, :] = block[...]
    inputs[tail:, :] = jnp.zeros_like(inputs[tail:, :])
    inputs[tail : tail + count, :] = new[...]
    x = inputs[...]
    column = 0
    for start, stop in parts_of:
        weight = jnp.concatenate([own[:, start:stop], other[:, start:stop]], axis=1)
        part = jnp.dot(x, weight, preferred_element_type=jnp.float32)
        to = slice(column, column + weight.shape[1])
        own_rows, first, second, both = (part[i * rows : (i + 1) * rows] for i in range(4))
        held[:, to] = own_rows
        held_second[:, to] = second
        news = part[tail : tail + pad].astype(new_held.dtype)
        new_held[:, to] = news
        send[:rows, to] = first.astype(send.dtype)
        send[rows : 2 * rows, to] = both.astype(send.dtype)
        send[2 * rows :, to] = news
        column += weight.shape[1]


def add_pair_kernel(held, held_second, new_held, got, out, new_out, send):
    rows = held.shape[0]
    out[...] = held[...] + got[:rows].astype(jnp.float32)
    second = held_second[...] + got[rows : 2 * rows].astype(jnp.float32)
    send[:rows, :] = second.astype(send.dtype)
    news = new_held[...].astype(jnp.float32) + got[2 * rows :].astype(jnp.float32)
    new_out[...] = news.astype(new_out.dtype)
    send[rows:, :] = news.astype(send.dtype)


def add_last_kernel(part, new_part, got, held, new):
    rows = held.shape[0]
    held[...] = (part[...] + got[:rows].astype(jnp.float32)).astype(held.dtype)
    news = new_part[...].astype(jnp.float32) + got[rows:].astype(jnp.float32)
    new[...] = news.astype(new.dtype)


def request_of(position, ends):
    found = jnp.zeros_like(position)
    for end in ends:
        found = found + jnp.where(position >= end, 1, 0)
    return found


def attend_kernel(count, scale, block_map, lengths, *refs):
    mine, theirs, refs = turned(refs[:4]), turned(refs[4:8]), refs[8:]
    (new, w_own, w_other), outs, refs = refs[:3], (refs[3:7], refs[7:11]), refs[11:]
    q_all, key_all, value_all, attended, result = refs
    steps = len(mine)
    rows, features = mine[0].shape
    q_width, kv_width = q_all.shape[1], key_all.shape[1]
    head = HEAD_SIZE
    groups = kv_width // head
    per_group = q_width // kv_width
    pad = new.shape[0]
    tail = steps * rows
    q_rows = q_all.shape[0]
    k_rows = key_all.shape[0]
    k_tail = 2 * steps * rows
    half = kv_width // 2
    c, _, k = place()

    key_all[k_tail:, :] = jnp.zeros_like(key_all[k_tail:, :])
    value_all[k_tail:, :] = jnp.zeros_like(value_all[k_tail:, :])
    for number in range(steps):
        at = slice(number * rows, (number + 1) * rows)
        v_at = mine[number].shape[1] - kv_width
        key_all[at, :] = mine[number][:, v_at - kv_width : v_at]
        value_all[at, :] = mine[number][:, v_at:]
        at = slice((steps + number) * rows, (steps + number + 1) * rows)
        v_at = theirs[number].shape[1] - kv_width
        k_at = v_at - kv_width
        key_all[at, :half] = theirs[number][:, k_at + half : v_at]
        key_all[at, half:] = theirs[number][:, k_at : k_at + half]
        value_all[at, :half] = theirs[number][:, v_at + half :]
        value_all[at, half:] = theirs[number][:, v_at : v_at + half]
    key_all[k_tail : k_tail + pad, :] = new[:, q_width : q_width + kv_width]
    value_all[k_tail : k_tail + pad, :] = new[:, q_width + kv_width :]
    q_all[tail:, :] = jnp.zeros_like(q_all[tail:, :])
    for number in range(steps):
        q_all[number * rows : (number + 1) * rows, :] = mine[number][:, :q_width]
    q_all[tail : tail + pad, :] = new[:, :q_width]

    ends, total = [], 0
    for request in range(count):
        total = total + lengths[request]
        ends.append(total)

    def labels(shape, axis, held):
        index = lax.broadcasted_iota(jnp.int32, shape, axis)
        position = jnp.zeros(shape, jnp.int32)
        for number, block in enumerate(held):
            inside = (index >= number * rows) & (index < (number + 1) * rows)
            position = jnp.where(inside, block_map[block] * rows + index - number * rows, position)
        last = len(held) * rows
        is_new = index >= last
        request = jnp.where(is_new, index - last, request_of(position, ends))
        return jnp.where(is_new, LAST, position), request

    held = [2 * (c ^ mask) + core for core in (k, 1 - k) for mask in partners(core)]
    q_position, q_request = labels((q_rows, 1), 0, held[:steps])
    k_position, k_request = labels((1, k_rows), 1, held)
    allowed = (q_request == k_request) & (k_position <= q_position)

    for group in range(groups):
        keys = key_all[:, group * head : (group + 1) * head]
        values = value_all[:, group * head : (group + 1) * head]
        for member in range(per_group):
            at = (group * per_group + member) * head
            scores = lax.dot_general(
                q_all[:, at : at + head],
                keys,
                (((1,), (1,)), ((), ())),
                preferred_element_type=jnp.float32,
            )
            scores = jnp.where(allowed, scores * scale, FLOOR)
            weights = jnp.exp(scores - jnp.max(scores, axis=1, keepdims=True))
            denom = jnp.sum(weights, axis=1, keepdims=True)
            mixed = jnp.dot(
                weights.astype(jnp.bfloat16), values, preferred_element_type=jnp.float32
            )
            attended[:, at : at + head] = (mixed / denom).astype(jnp.bfloat16)

    rows_own = w_own.shape[0]
    result[...] = (
        jnp.dot(attended[:, :rows_own], w_own[...], preferred_element_type=jnp.float32)
        + jnp.dot(attended[:, rows_own:], w_other[...], preferred_element_type=jnp.float32)
    ).astype(jnp.bfloat16)
    for core, half_outs in zip((1 - k, k), outs):
        width = half_outs[0].shape[1]
        column = pl.ds(pl.multiple_of(core * width, width), width)
        for number, out in enumerate(half_outs):
            out[:rows, :] = result[number * rows : (number + 1) * rows, column]
            out[rows:, :] = result[tail : tail + pad, column]


def relay_kernel(*refs):
    blocks, (held, held_second, send) = refs[:4], refs[4:]
    c, z, k = place()
    rows = held.shape[0]
    slots = (held, send.at[:rows], held_second, send.at[rows:])
    for slot, out in enumerate(slots):
        for mask, block in zip(partners(k), blocks):

            @pl.when((c ^ z ^ slot) == mask)
            def _(out=out, block=block):
                out[...] = block[...]


def add_heads_kernel(held, held_second, got, out, send):
    rows = held.shape[0]
    out[...] = held[...].astype(jnp.float32) + got[:rows].astype(jnp.float32)
    second = held_second[...].astype(jnp.float32) + got[rows:].astype(jnp.float32)
    send[...] = second.astype(send.dtype)


def sum_kernel(held, got, send):
    send[...] = (held[...] + got[...].astype(jnp.float32))[: send.shape[0]].astype(send.dtype)


def finish_kernel(held, got, other, prefill, decode):
    _, _, k = place()
    rows = other.shape[0]
    total = (held[...] + got[...].astype(jnp.float32)).astype(prefill.dtype)
    prefill[pl.ds(pl.multiple_of(k * rows, rows), rows), :] = total[:rows]
    prefill[pl.ds(pl.multiple_of((1 - k) * rows, rows), rows), :] = other[...]
    decode[...] = total[rows : rows + decode.shape[0]]


def on_device_small(
    steps, tp, tokens, new_token_states, w_query, key_matrix, value_matrix, w_out, lengths, block_map
):
    bf16, f32 = jnp.bfloat16, jnp.float32
    rows = tokens.shape[0] // 2
    depth = w_query.shape[0]
    count = new_token_states.shape[0]
    pad = -(-count // ROW_TILE) * ROW_TILE
    q_width = 2 * w_query.shape[1]
    kv_width = 2 * key_matrix.shape[1]
    features = q_width + 2 * kv_width
    out_width = w_out.shape[1]
    devices = [divmod(source, tp) for source in range(steps * tp)]

    def to_core(value):
        return lax.ppermute(value, "tp", [(i, i ^ 1) for i in range(tp)])

    def to_chip(value, step):
        return lax.ppermute(value, "tp", [(i, i ^ (2 * step)) for i in range(tp)])

    def to_partner(value, number):
        pairs = [(c * tp + t, (c ^ partners(t % 2)[number]) * tp + t) for c, t in devices]
        return lax.ppermute(value, ("ctx", "tp"), pairs)

    def to_partners(values):
        return [to_partner(value, number) for number, value in enumerate(values, 1)]

    def call(kernel, name, inputs, shapes, scratch=(), spaces=None):
        return pl.pallas_call(
            kernel,
            out_shape=[jax.ShapeDtypeStruct(shape, kind) for shape, kind in shapes],
            in_specs=spaces or [vmem()] * len(inputs),
            out_specs=[vmem()] * len(shapes),
            scratch_shapes=list(scratch),
            compiler_params=pltpu.CompilerParams(vmem_limit_bytes=VMEM_BYTES),
            name=name,
        )(*inputs)

    c, _, k = place()
    sent = [
        lax.dynamic_slice(tokens, (k * rows, (c ^ mask) * depth), (rows, depth))
        for mask in partners(k)
    ]
    new_columns = lax.dynamic_slice_in_dim(new_token_states, c * depth, depth, 1)
    blocks = [sent[0]] + to_partners(sent[1:])
    *weights, _ = lax.optimization_barrier((w_query, key_matrix, value_matrix, sent[1]))
    (own,) = call(pack_kernel, "pack_weights", weights, [((depth, features // 2), bf16)])
    other = to_core(own)

    x_rows = -(-(steps * rows + pad) // 16) * 16
    edges = [0, q_width // 2, (q_width + kv_width) // 2, features // 2]
    own_part, second_part, new_part, send = call(
        functools.partial(project_kernel, list(zip(edges, edges[1:]))),
        "project",
        (*turned(blocks), new_columns, own, other),
        [((rows, features), f32)] * 2
        + [((pad, features), bf16), ((2 * rows + pad, features), bf16)],
        [pltpu.VMEM((x_rows, depth), bf16)],
    )
    w_out_later, _ = lax.optimization_barrier((w_out, new_part))
    w_other = to_core(w_out_later)

    own_part, new_part, send = call(
        add_pair_kernel,
        "add_pair",
        (own_part, second_part, new_part, to_partner(send, 1)),
        [((rows, features), f32), ((pad, features), bf16), ((rows + pad, features), bf16)],
    )
    held, new = call(
        add_last_kernel,
        "add_last",
        (own_part, new_part, to_partner(send, 2)),
        [((rows, features), bf16), ((pad, features), bf16)],
    )

    first = to_partner(held, 1)
    mine = [held, first, to_partner(held, 2), to_partner(first, 2)]
    theirs = [to_core(value) for value in mine]

    k_rows = -(-(2 * steps * rows + pad) // 128) * 128
    block = (rows + pad, out_width // 2)
    outs = call(
        functools.partial(attend_kernel, count, 1.0 / math.sqrt(HEAD_SIZE)),
        "attend",
        (block_map, lengths, *turned(mine), *turned(theirs), new, w_out, w_other),
        [(block, bf16)] * (2 * steps),
        [
            pltpu.VMEM((x_rows, q_width), bf16),
            pltpu.VMEM((k_rows, kv_width), bf16),
            pltpu.VMEM((k_rows, kv_width), bf16),
            pltpu.VMEM((x_rows, q_width), bf16),
            pltpu.VMEM((x_rows, out_width), bf16),
        ],
        [smem()] * 2 + [vmem()] * (2 * steps + 3),
    )

    halves = []
    for half in (outs[:steps], outs[steps:]):
        held, second, send = call(
            relay_kernel,
            "relay",
            [half[0]] + to_partners(half[1:]),
            [(block, bf16)] * 2 + [((2 * block[0], block[1]), bf16)],
        )
        held, send = call(
            add_heads_kernel,
            "add_heads",
            (held, second, to_chip(send, 1)),
            [(block, f32), (block, bf16)],
        )
        halves.append((held, to_chip(send, 2)))
    (send,) = call(sum_kernel, "sum_heads", halves[0], [((rows, block[1]), bf16)])
    return tuple(
        call(
            finish_kernel,
            "finish",
            (*halves[1], to_core(send)),
            [((2 * rows, block[1]), bf16), ((count, block[1]), bf16)],
        )
    )


floor_value = -1e30


def initial_positions(block_map, first_row, row_count, block_rows):
    row_ids = first_row + jnp.arange(row_count, dtype=jnp.int32)
    block_ids = row_ids // block_rows
    table_ids = jnp.arange(block_map.shape[0], dtype=jnp.int32)
    mapped = jnp.sum(
        jnp.where(block_ids[:, None] == table_ids[None, :], block_map[None, :], 0), axis=1
    )
    return mapped * block_rows + row_ids % block_rows


def request_index(positions, request_ends):
    return jnp.sum((positions[:, None] >= request_ends[None, :]).astype(jnp.int32), axis=1)


def round_weights(weights):
    rounded = weights.astype(jnp.bfloat16)
    rounded = lax.optimization_barrier(rounded)
    return rounded.astype(jnp.float32)


def softmax_parts(
    dec_heads, projected_key_rows, projected_value_rows, owned, kv_heads, head_dim, score_scale
):
    row_count = projected_key_rows.shape[0]
    scores = (
        jnp.einsum(
            "rgjd,tgd->rgjt",
            dec_heads,
            projected_key_rows.reshape(row_count, kv_heads, head_dim),
            preferred_element_type=jnp.float32,
        )
        * score_scale
    )
    scores = jnp.where(owned, scores, floor_value)
    part_peak = jnp.max(scores, axis=3)
    weights = jnp.where(owned, jnp.exp(scores - part_peak[..., None]), 0.0)
    part_total = jnp.sum(weights, axis=3)
    part_mixed = jnp.einsum(
        "rgjt,tgd->rgjd",
        weights.astype(jnp.bfloat16),
        projected_value_rows.reshape(row_count, kv_heads, head_dim),
        preferred_element_type=jnp.float32,
    )
    return (part_peak, part_total, part_mixed)


def on_device_large(
    tokens, new_token_states, w_query, key_matrix, value_matrix, w_out, lengths, block_map
):
    local_rows = tokens.shape[0]
    block_rows = local_rows // 2
    request_count = new_token_states.shape[0]
    head_dim = HEAD_SIZE
    query_width = w_query.shape[1]
    kv_width = key_matrix.shape[1]
    kv_heads = kv_width // head_dim
    query_group_count = query_width // kv_width
    score_scale = 1.0 / math.sqrt(head_dim)
    device = lax.axis_index("ctx")
    request_ends = jnp.cumsum(lengths)
    inputs = jnp.concatenate([tokens, new_token_states], axis=0)
    shard_pieces = (
        lax.all_gather(w_query, "ctx", axis=0, tiled=True),
        lax.all_gather(key_matrix, "ctx", axis=0, tiled=True),
        lax.all_gather(value_matrix, "ctx", axis=0, tiled=True),
    )
    query_all, key_all, value_all = tuple(
        (jnp.dot(inputs, weight, preferred_element_type=jnp.float32) for weight in shard_pieces)
    )
    query_all = query_all.astype(jnp.bfloat16)
    key_all = key_all.astype(jnp.bfloat16)
    value_all = value_all.astype(jnp.bfloat16)
    local_query = query_all[:local_rows]
    local_keys = key_all[:local_rows]
    local_values = value_all[:local_rows]
    dec_query = query_all[local_rows:]
    decode_key_rows = key_all[local_rows:]
    decode_value_rows = value_all[local_rows:]
    token_pos = initial_positions(block_map, device * local_rows, local_rows, block_rows)
    token_request = request_index(token_pos, request_ends)
    query_heads = local_query.reshape(local_rows, kv_heads, query_group_count, head_dim)

    def attend(running, shard_pieces, first_row):
        peak_run, total_run, mixed_run = running
        key_piece, value_piece = shard_pieces
        row_count = key_piece.shape[0]
        key_pos = initial_positions(block_map, first_row, row_count, block_rows)
        key_request = request_index(key_pos, request_ends)
        allowed = (key_request[None, :] == token_request[:, None]) & (
            key_pos[None, :] <= token_pos[:, None]
        )
        scores = (
            jnp.einsum(
                "tgjd,kgd->gjtk",
                query_heads,
                key_piece.reshape(row_count, kv_heads, head_dim),
                preferred_element_type=jnp.float32,
            )
            * score_scale
        )
        scores = jnp.where(allowed, scores, floor_value)
        peak_new = jnp.maximum(peak_run, jnp.max(scores, axis=3))
        weights = jnp.where(allowed, jnp.exp(scores - peak_new[..., None]), 0.0)
        rescale = jnp.exp(peak_run - peak_new)
        total_new = total_run * rescale + jnp.sum(weights, axis=3)
        mixed_new = mixed_run * rescale[..., None] + jnp.einsum(
            "gjtk,kgd->gjtd",
            weights.astype(jnp.bfloat16),
            value_piece.reshape(row_count, kv_heads, head_dim),
            preferred_element_type=jnp.float32,
        )
        return (peak_new, total_new, mixed_new)

    start_state = (
        jnp.full((kv_heads, query_group_count, local_rows), floor_value, jnp.float32),
        jnp.zeros((kv_heads, query_group_count, local_rows), jnp.float32),
        jnp.zeros((kv_heads, query_group_count, local_rows, head_dim), jnp.float32),
    )
    dec_heads = dec_query.reshape(request_count, kv_heads, query_group_count, head_dim)
    request_ids = jnp.arange(request_count, dtype=jnp.int32)
    cache_keys, cache_values = (
        lax.all_gather(local_keys, "ctx", axis=0, tiled=True),
        lax.all_gather(local_values, "ctx", axis=0, tiled=True),
    )
    total_rows = cache_keys.shape[0]
    shard_count = total_rows // local_rows
    limit = max(1, 1024 // local_rows)
    step_rows = local_rows * math.gcd(shard_count, 1 << limit.bit_length() - 1)

    def key_step(running, step_index):
        first_row = step_index * step_rows
        pieces = (
            lax.dynamic_slice_in_dim(cache_keys, first_row, step_rows, 0),
            lax.dynamic_slice_in_dim(cache_values, first_row, step_rows, 0),
        )
        return (attend(running, pieces, first_row), None)

    final_state, unused = lax.scan(
        key_step, start_state, jnp.arange(total_rows // step_rows, dtype=jnp.int32)
    )
    peak_run, total_run, mixed_run = final_state
    cache_pos = (
        block_map[:, None] * block_rows + jnp.arange(block_rows, dtype=jnp.int32)[None, :]
    ).reshape(total_rows)
    cache_request = request_index(cache_pos, request_ends)
    owned = (cache_request[None, :] == request_ids[:, None])[:, None, None, :]
    cache_peak, cache_total, cache_mixed = softmax_parts(
        dec_heads, cache_keys, cache_values, owned, kv_heads, head_dim, score_scale
    )
    attended = (
        (mixed_run / total_run[..., None]).transpose(2, 0, 1, 3).reshape(local_rows, query_width)
    )
    attended = attended.astype(jnp.bfloat16)
    own_keys = decode_key_rows.reshape(request_count, kv_heads, 1, head_dim).astype(jnp.float32)
    own_values = decode_value_rows.reshape(request_count, kv_heads, 1, head_dim).astype(jnp.float32)
    self_scores = jnp.sum(dec_heads.astype(jnp.float32) * own_keys, axis=3) * score_scale
    peak_all = jnp.maximum(cache_peak, self_scores)
    rescale = jnp.exp(cache_peak - peak_all)
    self_weights = jnp.exp(self_scores - peak_all)
    dec_total = cache_total * rescale + self_weights
    dec_mixed = (
        cache_mixed * rescale[..., None] + round_weights(self_weights)[..., None] * own_values
    )
    dec_attn = (
        (dec_mixed / dec_total[..., None]).reshape(request_count, query_width).astype(jnp.bfloat16)
    )
    attended_all = jnp.concatenate([attended, dec_attn], axis=0)
    head_block = lax.all_gather(w_out, "ctx", axis=1, tiled=True)
    column_block = lax.all_to_all(head_block, "tp", split_axis=1, concat_axis=0, tiled=True)
    summed_rows = jnp.dot(
        lax.all_gather(attended_all, "tp", axis=1, tiled=True),
        column_block,
        preferred_element_type=jnp.float32,
    )
    summed_rows = summed_rows.astype(jnp.bfloat16)
    return (summed_rows[:local_rows], summed_rows[local_rows:])

def solution(mesh):
    steps, tp = mesh.shape["ctx"], mesh.shape["tp"]

    def on_device(tokens, *rest):
        small = steps == 4 and tp == 8 and tokens.shape[0] * steps <= 1024
        if small:
            return on_device_small(steps, tp, tokens, *rest)
        return on_device_large(tokens, *rest)

    return jax.shard_map(
        on_device,
        mesh=mesh,
        in_specs=(
            P("ctx", None),
            P(),
            P("ctx", "tp"),
            P("ctx", "tp"),
            P("ctx", "tp"),
            P("tp", "ctx"),
            P(),
            P(),
        ),
        out_specs=(P("ctx", "tp"), P(None, "tp")),
        check_vma=False,
    )
```

```python
import functools
import math

import jax
import jax.numpy as jnp
from jax import lax
from jax.experimental import pallas as pl
from jax.experimental.pallas import tpu as pltpu
from jax.sharding import PartitionSpec as P

HEAD_SIZE = 128
FLOOR = -1e30
LAST = 1 << 30
ROW_TILE = 8
VMEM_BYTES = 48 * 1024 * 1024


def vmem():
    return pl.BlockSpec(memory_space=pltpu.VMEM)


def smem():
    return pl.BlockSpec(memory_space=pltpu.SMEM)


def place():
    t = lax.axis_index("tp")
    return lax.axis_index("ctx"), t // 2, t % 2


def pack_kernel(*refs):
    out = refs[-1]
    out[...] = jnp.concatenate([ref[...] for ref in refs[:-1]], axis=1)


def project_kernel(parts_of, *refs):
    blocks, (new, own, other), refs = refs[:4], refs[4:7], refs[7:]
    (held, new_held), outs, inputs = refs[:2], refs[2:5], refs[5]
    rows = held.shape[0]
    count = new.shape[0]
    pad = new_held.shape[0]
    tail = len(blocks) * rows
    for step, block in enumerate(blocks):
        inputs[step * rows : (step + 1) * rows, :] = block[...]
    inputs[tail:, :] = jnp.zeros_like(inputs[tail:, :])
    inputs[tail : tail + count, :] = new[...]
    x = inputs[...]
    column = 0
    for start, stop in parts_of:
        weight = jnp.concatenate([own[:, start:stop], other[:, start:stop]], axis=1)
        part = jnp.dot(x, weight, preferred_element_type=jnp.float32)
        to = slice(column, column + weight.shape[1])
        held[:, to] = part[:rows]
        news = part[tail : tail + pad].astype(new_held.dtype)
        new_held[:, to] = news
        for step, out in enumerate(outs, 1):
            out[:rows, to] = part[step * rows : (step + 1) * rows].astype(out.dtype)
            out[rows:, to] = news
        column += weight.shape[1]


def add_kernel(own, new_own, first, second, both, held, new):
    rows = held.shape[0]

    def total(own, at):
        parts = [own[...].astype(jnp.float32)]
        parts += [ref[at, :].astype(jnp.float32) for ref in (first, second, both)]
        return ((parts[0] + parts[1]) + (parts[2] + parts[3])).astype(held.dtype)

    held[...] = total(own, slice(0, rows))
    new[...] = total(new_own, slice(rows, None))


def request_of(position, ends):
    found = jnp.zeros_like(position)
    for end in ends:
        found = found + jnp.where(position >= end, 1, 0)
    return found


def attend_kernel(sent, count, scale, block_map, lengths, *refs):
    mine, theirs, refs = refs[:4], refs[4:8], refs[8:]
    new, attended, q_all, key_all, value_all = refs
    steps = len(mine)
    rows, features = mine[0].shape
    part = rows // 2
    q_width, kv_width = q_all.shape[1], key_all.shape[1]
    head = HEAD_SIZE
    groups = kv_width // head
    per_group = q_width // kv_width
    pad = new.shape[0]
    tail = steps * part
    q_rows = q_all.shape[0]
    k_rows = key_all.shape[0]
    k_tail = 2 * steps * rows
    half = kv_width // 2
    c, z, k = place()
    first = part * (1 - z % 2 if sent else z % 2)

    key_all[k_tail:, :] = jnp.zeros_like(key_all[k_tail:, :])
    value_all[k_tail:, :] = jnp.zeros_like(value_all[k_tail:, :])
    for number in range(steps):
        at = slice(number * rows, (number + 1) * rows)
        v_at = mine[number].shape[1] - kv_width
        key_all[at, :] = mine[number][:, v_at - kv_width : v_at]
        value_all[at, :] = mine[number][:, v_at:]
        at = slice((steps + number) * rows, (steps + number + 1) * rows)
        v_at = theirs[number].shape[1] - kv_width
        k_at = v_at - kv_width
        key_all[at, :half] = theirs[number][:, k_at + half : v_at]
        key_all[at, half:] = theirs[number][:, k_at : k_at + half]
        value_all[at, :half] = theirs[number][:, v_at + half :]
        value_all[at, half:] = theirs[number][:, v_at : v_at + half]
    key_all[k_tail : k_tail + pad, :] = new[:, q_width : q_width + kv_width]
    value_all[k_tail : k_tail + pad, :] = new[:, q_width + kv_width :]
    for number in range(steps):
        at = pl.ds(pl.multiple_of(first, part), part)
        q_all[number * part : (number + 1) * part, :] = mine[number][at, :q_width]
    if sent:
        q_all[tail:, :] = jnp.zeros_like(q_all[tail:, :])
        q_all[tail : tail + pad, :] = new[:, :q_width]

    ends, total = [], 0
    for request in range(count):
        total = total + lengths[request]
        ends.append(total)

    def labels(shape, axis, held, taken, first):
        index = lax.broadcasted_iota(jnp.int32, shape, axis)
        position = jnp.zeros(shape, jnp.int32)
        for number, block in enumerate(held):
            start = number * taken
            inside = (index >= start) & (index < start + taken)
            position = jnp.where(inside, block_map[block] * rows + first + index - start, position)
        last = len(held) * taken
        is_new = index >= last
        request = jnp.where(is_new, index - last, request_of(position, ends))
        return jnp.where(is_new, LAST, position), request

    held = [2 * (c ^ mask) + core for core in (k, 1 - k) for mask in range(steps)]
    q_position, q_request = labels((q_rows, 1), 0, held[:steps], part, first)
    k_position, k_request = labels((1, k_rows), 1, held, rows, 0)
    allowed = (q_request == k_request) & (k_position <= q_position)

    for group in range(groups):
        keys = key_all[:, group * head : (group + 1) * head]
        values = value_all[:, group * head : (group + 1) * head]
        for member in range(per_group):
            at = (group * per_group + member) * head
            scores = lax.dot_general(
                q_all[:, at : at + head],
                keys,
                (((1,), (1,)), ((), ())),
                preferred_element_type=jnp.float32,
            )
            scores = jnp.where(allowed, scores * scale, FLOOR)
            weights = jnp.exp(scores - jnp.max(scores, axis=1, keepdims=True))
            denom = jnp.sum(weights, axis=1, keepdims=True)
            mixed = jnp.dot(
                weights.astype(jnp.bfloat16), values, preferred_element_type=jnp.float32
            )
            attended[:, at : at + head] = (mixed / denom).astype(jnp.bfloat16)


def output_kernel(own, sent, got, *refs):
    weights, outs = refs[:4], refs[4:]
    part = own.shape[0] // len(outs)
    tail = own.shape[0]
    pad = outs[0].shape[0] - part
    at, total = 0, None
    for mine, theirs in zip(weights[:2], weights[2:]):
        to = slice(at, at + mine.shape[0])
        at += mine.shape[0]
        x = jnp.concatenate([own[:, to], sent[tail:, to]], axis=0)
        term = jnp.dot(x, mine[...], preferred_element_type=jnp.float32)
        term += jnp.dot(got[:, to], theirs[...], preferred_element_type=jnp.float32)
        total = term if total is None else total + term
    total = total.astype(outs[0].dtype)
    for number, out in enumerate(outs):
        out[:part, :] = total[number * part : (number + 1) * part]
        out[part:, :] = total[tail : tail + pad]


def relay_kernel(*refs):
    blocks, outs = refs[:4], refs[4:]
    c, z, _ = place()
    for slot, out in enumerate(outs):
        for mask, block in enumerate(blocks):

            @pl.when((c ^ z ^ slot) == mask)
            def _(out=out, block=block):
                out[...] = block[: out.shape[0], :]


def sum_kernel(*refs):
    parts, (keep, news, send) = refs[:4], refs[4:]
    width = keep.shape[1]
    part = keep.shape[0] // 2
    count = news.shape[0]
    _, z, k = place()
    for out, core in ((keep, k), (send, 1 - k)):
        column = pl.ds(pl.multiple_of(core * width, width), width)
        for odd in range(2):
            total = sum(parts[i][:, column].astype(jnp.float32) for i in (odd, odd + 2))
            total = total.astype(out.dtype)
            first = part * (z % 2 if odd == 0 else 1 - z % 2)
            out[pl.ds(pl.multiple_of(first, part), part), :] = total[:part]
            if odd == 0 and out is keep:
                news[...] = total[part : part + count]


def finish_kernel(keep, news, other, prefill, decode):
    _, _, k = place()
    rows = other.shape[0]
    prefill[pl.ds(pl.multiple_of(k * rows, rows), rows), :] = keep[...]
    prefill[pl.ds(pl.multiple_of((1 - k) * rows, rows), rows), :] = other[...]
    decode[...] = news[...]


def on_device_small(
    steps, tp, tokens, new_token_states, w_query, key_matrix, value_matrix, w_out, lengths, block_map
):
    bf16, f32 = jnp.bfloat16, jnp.float32
    rows = tokens.shape[0] // 2
    depth = w_query.shape[0]
    count = new_token_states.shape[0]
    pad = -(-count // ROW_TILE) * ROW_TILE
    q_width = 2 * w_query.shape[1]
    kv_width = 2 * key_matrix.shape[1]
    features = q_width + 2 * kv_width
    out_width = w_out.shape[1]

    def to_core(value):
        return lax.ppermute(value, "tp", [(i, i ^ 1) for i in range(tp)])

    def to_chip(value, step):
        return lax.ppermute(value, "tp", [(i, i ^ (2 * step)) for i in range(tp)])

    def to_partners(values):
        return [
            lax.ppermute(value, "ctx", [(i, i ^ mask) for i in range(steps)])
            for mask, value in enumerate(values, 1)
        ]

    def call(kernel, name, inputs, shapes, scratch=(), spaces=None):
        return pl.pallas_call(
            kernel,
            out_shape=[jax.ShapeDtypeStruct(shape, kind) for shape, kind in shapes],
            in_specs=spaces or [vmem()] * len(inputs),
            out_specs=[vmem()] * len(shapes),
            scratch_shapes=list(scratch),
            compiler_params=pltpu.CompilerParams(vmem_limit_bytes=VMEM_BYTES),
            name=name,
        )(*inputs)

    c, _, k = place()
    sent = [
        lax.dynamic_slice(tokens, (k * rows, (c ^ mask) * depth), (rows, depth))
        for mask in range(steps)
    ]
    new_columns = lax.dynamic_slice_in_dim(new_token_states, c * depth, depth, 1)
    blocks = [sent[0]] + to_partners(sent[1:])
    *weights, _ = lax.optimization_barrier((w_query, key_matrix, value_matrix, sent[1]))
    (own,) = call(pack_kernel, "pack_weights", weights, [((depth, features // 2), bf16)])
    other = to_core(own)

    part_shape = (rows + pad, features)
    x_rows = -(-(steps * rows + pad) // 16) * 16
    edges = [0, q_width // 2, (q_width + kv_width) // 2, features // 2]
    own_part, new_part, *parts = call(
        functools.partial(project_kernel, list(zip(edges, edges[1:]))),
        "project",
        (*blocks, new_columns, own, other),
        [((rows, features), f32), ((pad, features), bf16)] + [(part_shape, bf16)] * (steps - 1),
        [pltpu.VMEM((x_rows, depth), bf16)],
    )


    w_next = to_chip(w_out, 1)
    w_out_later, _ = lax.optimization_barrier((w_out, new_part))
    w_other = to_core(w_out_later)
    new_part, w_other = lax.optimization_barrier((new_part, w_other))
    w_out_last, w_next, _ = lax.optimization_barrier((w_out, w_next, own_part))
    w_next_other = lax.ppermute(w_out_last, "tp", [(i, i ^ 3) for i in range(tp)])

    held, new = call(
        add_kernel,
        "add_parts",
        (own_part, new_part, *to_partners(parts)),
        [((rows, features), bf16), ((pad, features), bf16)],
    )
    mine = [held] + to_partners([held] * (steps - 1))
    theirs = [to_core(value) for value in mine]

    part = rows // 2
    k_rows = -(-(2 * steps * rows + pad) // 128) * 128

    def attend(sent):
        q_rows = steps * part + (-(-pad // 16) * 16 if sent else 0)
        (attended,) = call(
            functools.partial(attend_kernel, sent, count, 1.0 / math.sqrt(HEAD_SIZE)),
            "attend_sent" if sent else "attend_kept",
            (block_map, lengths, *mine, *theirs, new),
            [((q_rows, q_width), bf16)],
            [
                pltpu.VMEM((q_rows, q_width), bf16),
                pltpu.VMEM((k_rows, kv_width), bf16),
                pltpu.VMEM((k_rows, kv_width), bf16),
            ],
            [smem()] * 2 + [vmem()] * (2 * steps + 1),
        )
        return attended

    sent = attend(True)
    got = to_chip(sent, 1)
    kept = attend(False)

    block = (part + pad, out_width)
    outs = call(
        output_kernel,
        "project_out",
        (kept, sent, got, w_out, w_other, w_next, w_next_other),
        [(block, bf16)] * steps,
    )

    slots = call(
        relay_kernel,
        "relay",
        [outs[0]] + to_partners(outs[1:]),
        [(block if i % 2 == 0 else (part, out_width), bf16) for i in range(steps)],
    )
    slots = [slots[0]] + [to_chip(slot, step) for step, slot in enumerate(slots[1:], 1)]
    width = out_width // 2
    keep, news, send = call(
        sum_kernel,
        "sum_heads",
        slots,
        [((rows, width), bf16), ((count, width), bf16), ((rows, width), bf16)],
    )
    return tuple(
        call(
            finish_kernel,
            "finish",
            (keep, news, to_core(send)),
            [((2 * rows, width), bf16), ((count, width), bf16)],
        )
    )


floor_value = -1e30


def initial_positions(block_map, first_row, row_count, block_rows):
    row_ids = first_row + jnp.arange(row_count, dtype=jnp.int32)
    block_ids = row_ids // block_rows
    table_ids = jnp.arange(block_map.shape[0], dtype=jnp.int32)
    mapped = jnp.sum(
        jnp.where(block_ids[:, None] == table_ids[None, :], block_map[None, :], 0), axis=1
    )
    return mapped * block_rows + row_ids % block_rows


def request_index(positions, request_ends):
    return jnp.sum((positions[:, None] >= request_ends[None, :]).astype(jnp.int32), axis=1)


def round_weights(weights):
    rounded = weights.astype(jnp.bfloat16)
    rounded = lax.optimization_barrier(rounded)
    return rounded.astype(jnp.float32)


def softmax_parts(
    dec_heads, projected_key_rows, projected_value_rows, owned, kv_heads, head_dim, score_scale
):
    row_count = projected_key_rows.shape[0]
    scores = (
        jnp.einsum(
            "rgjd,tgd->rgjt",
            dec_heads,
            projected_key_rows.reshape(row_count, kv_heads, head_dim),
            preferred_element_type=jnp.float32,
        )
        * score_scale
    )
    scores = jnp.where(owned, scores, floor_value)
    part_peak = jnp.max(scores, axis=3)
    weights = jnp.where(owned, jnp.exp(scores - part_peak[..., None]), 0.0)
    part_total = jnp.sum(weights, axis=3)
    part_mixed = jnp.einsum(
        "rgjt,tgd->rgjd",
        weights.astype(jnp.bfloat16),
        projected_value_rows.reshape(row_count, kv_heads, head_dim),
        preferred_element_type=jnp.float32,
    )
    return (part_peak, part_total, part_mixed)


def on_device_large(
    tokens, new_token_states, w_query, key_matrix, value_matrix, w_out, lengths, block_map
):
    local_rows = tokens.shape[0]
    block_rows = local_rows // 2
    request_count = new_token_states.shape[0]
    head_dim = HEAD_SIZE
    query_width = w_query.shape[1]
    kv_width = key_matrix.shape[1]
    kv_heads = kv_width // head_dim
    query_group_count = query_width // kv_width
    score_scale = 1.0 / math.sqrt(head_dim)
    device = lax.axis_index("ctx")
    request_ends = jnp.cumsum(lengths)
    inputs = jnp.concatenate([tokens, new_token_states], axis=0)
    shard_pieces = (
        lax.all_gather(w_query, "ctx", axis=0, tiled=True),
        lax.all_gather(key_matrix, "ctx", axis=0, tiled=True),
        lax.all_gather(value_matrix, "ctx", axis=0, tiled=True),
    )
    query_all, key_all, value_all = tuple(
        (jnp.dot(inputs, weight, preferred_element_type=jnp.float32) for weight in shard_pieces)
    )
    query_all = query_all.astype(jnp.bfloat16)
    key_all = key_all.astype(jnp.bfloat16)
    value_all = value_all.astype(jnp.bfloat16)
    local_query = query_all[:local_rows]
    local_keys = key_all[:local_rows]
    local_values = value_all[:local_rows]
    dec_query = query_all[local_rows:]
    decode_key_rows = key_all[local_rows:]
    decode_value_rows = value_all[local_rows:]
    token_pos = initial_positions(block_map, device * local_rows, local_rows, block_rows)
    token_request = request_index(token_pos, request_ends)
    query_heads = local_query.reshape(local_rows, kv_heads, query_group_count, head_dim)

    def attend(running, shard_pieces, first_row):
        peak_run, total_run, mixed_run = running
        key_piece, value_piece = shard_pieces
        row_count = key_piece.shape[0]
        key_pos = initial_positions(block_map, first_row, row_count, block_rows)
        key_request = request_index(key_pos, request_ends)
        allowed = (key_request[None, :] == token_request[:, None]) & (
            key_pos[None, :] <= token_pos[:, None]
        )
        scores = (
            jnp.einsum(
                "tgjd,kgd->gjtk",
                query_heads,
                key_piece.reshape(row_count, kv_heads, head_dim),
                preferred_element_type=jnp.float32,
            )
            * score_scale
        )
        scores = jnp.where(allowed, scores, floor_value)
        peak_new = jnp.maximum(peak_run, jnp.max(scores, axis=3))
        weights = jnp.where(allowed, jnp.exp(scores - peak_new[..., None]), 0.0)
        rescale = jnp.exp(peak_run - peak_new)
        total_new = total_run * rescale + jnp.sum(weights, axis=3)
        mixed_new = mixed_run * rescale[..., None] + jnp.einsum(
            "gjtk,kgd->gjtd",
            weights.astype(jnp.bfloat16),
            value_piece.reshape(row_count, kv_heads, head_dim),
            preferred_element_type=jnp.float32,
        )
        return (peak_new, total_new, mixed_new)

    start_state = (
        jnp.full((kv_heads, query_group_count, local_rows), floor_value, jnp.float32),
        jnp.zeros((kv_heads, query_group_count, local_rows), jnp.float32),
        jnp.zeros((kv_heads, query_group_count, local_rows, head_dim), jnp.float32),
    )
    dec_heads = dec_query.reshape(request_count, kv_heads, query_group_count, head_dim)
    request_ids = jnp.arange(request_count, dtype=jnp.int32)
    cache_keys, cache_values = (
        lax.all_gather(local_keys, "ctx", axis=0, tiled=True),
        lax.all_gather(local_values, "ctx", axis=0, tiled=True),
    )
    total_rows = cache_keys.shape[0]
    shard_count = total_rows // local_rows
    limit = max(1, 1024 // local_rows)
    step_rows = local_rows * math.gcd(shard_count, 1 << limit.bit_length() - 1)

    def key_step(running, step_index):
        first_row = step_index * step_rows
        pieces = (
            lax.dynamic_slice_in_dim(cache_keys, first_row, step_rows, 0),
            lax.dynamic_slice_in_dim(cache_values, first_row, step_rows, 0),
        )
        return (attend(running, pieces, first_row), None)

    final_state, unused = lax.scan(
        key_step, start_state, jnp.arange(total_rows // step_rows, dtype=jnp.int32)
    )
    peak_run, total_run, mixed_run = final_state
    cache_pos = (
        block_map[:, None] * block_rows + jnp.arange(block_rows, dtype=jnp.int32)[None, :]
    ).reshape(total_rows)
    cache_request = request_index(cache_pos, request_ends)
    owned = (cache_request[None, :] == request_ids[:, None])[:, None, None, :]
    cache_peak, cache_total, cache_mixed = softmax_parts(
        dec_heads, cache_keys, cache_values, owned, kv_heads, head_dim, score_scale
    )
    attended = (
        (mixed_run / total_run[..., None]).transpose(2, 0, 1, 3).reshape(local_rows, query_width)
    )
    attended = attended.astype(jnp.bfloat16)
    own_keys = decode_key_rows.reshape(request_count, kv_heads, 1, head_dim).astype(jnp.float32)
    own_values = decode_value_rows.reshape(request_count, kv_heads, 1, head_dim).astype(jnp.float32)
    self_scores = jnp.sum(dec_heads.astype(jnp.float32) * own_keys, axis=3) * score_scale
    peak_all = jnp.maximum(cache_peak, self_scores)
    rescale = jnp.exp(cache_peak - peak_all)
    self_weights = jnp.exp(self_scores - peak_all)
    dec_total = cache_total * rescale + self_weights
    dec_mixed = (
        cache_mixed * rescale[..., None] + round_weights(self_weights)[..., None] * own_values
    )
    dec_attn = (
        (dec_mixed / dec_total[..., None]).reshape(request_count, query_width).astype(jnp.bfloat16)
    )
    attended_all = jnp.concatenate([attended, dec_attn], axis=0)
    head_block = lax.all_gather(w_out, "ctx", axis=1, tiled=True)
    column_block = lax.all_to_all(head_block, "tp", split_axis=1, concat_axis=0, tiled=True)
    summed_rows = jnp.dot(
        lax.all_gather(attended_all, "tp", axis=1, tiled=True),
        column_block,
        preferred_element_type=jnp.float32,
    )
    summed_rows = summed_rows.astype(jnp.bfloat16)
    return (summed_rows[:local_rows], summed_rows[local_rows:])

def solution(mesh):
    steps, tp = mesh.shape["ctx"], mesh.shape["tp"]

    def on_device(tokens, *rest):
        small = steps == 4 and tp == 8 and tokens.shape[0] * steps <= 1024
        if small:
            return on_device_small(steps, tp, tokens, *rest)
        return on_device_large(tokens, *rest)

    return jax.shard_map(
        on_device,
        mesh=mesh,
        in_specs=(
            P("ctx", None),
            P(),
            P("ctx", "tp"),
            P("ctx", "tp"),
            P("ctx", "tp"),
            P("tp", "ctx"),
            P(),
            P(),
        ),
        out_specs=(P("ctx", "tp"), P(None, "tp")),
        check_vma=False,
    )
```

```python
import functools
import math

import jax
import jax.numpy as jnp
from jax import lax
from jax.experimental import pallas as pl
from jax.experimental.pallas import tpu as pltpu
from jax.sharding import PartitionSpec as P

HEAD_SIZE = 128
FLOOR = -1e30
LAST = 1 << 30
ROW_TILE = 8
VMEM_BYTES = 48 * 1024 * 1024


def vmem():
    return pl.BlockSpec(memory_space=pltpu.VMEM)


def smem():
    return pl.BlockSpec(memory_space=pltpu.SMEM)


def turned(values):
    return [values[0], *values[:0:-1]]


def place():
    t = lax.axis_index("tp")
    return lax.axis_index("ctx"), t // 2, t % 2


def pack_kernel(*refs):
    out = refs[-1]
    out[...] = jnp.concatenate([ref[...] for ref in refs[:-1]], axis=1)


def project_kernel(parts_of, *refs):
    blocks, (new, own, other), refs = turned(refs[:4]), refs[4:7], refs[7:]
    outs, (inputs, result) = refs[:4], refs[4:]
    rows = blocks[0].shape[0]
    count = new.shape[0]
    tail = len(blocks) * rows
    c, _, k = place()
    for mask, block in enumerate(blocks):
        inputs[pl.ds(pl.multiple_of((c ^ mask) * rows, rows), rows), :] = block[...]
    inputs[tail:, :] = jnp.zeros_like(inputs[tail:, :])
    inputs[tail : tail + count, :] = new[...]
    x = inputs[...]
    starts = []
    for start, stop in parts_of:
        weight = jnp.concatenate([own[:, start:stop], other[:, start:stop]], axis=1)
        starts.append(2 * start)
        result[:, 2 * start : 2 * stop] = jnp.dot(x, weight, preferred_element_type=jnp.float32)
    head = HEAD_SIZE
    for mask, out in enumerate(outs):
        query, keyval = head_places(c ^ mask, k)
        for number, (start, at) in enumerate(zip(starts, (query, keyval, keyval))):
            column = pl.ds(pl.multiple_of(start + at * head, head), head)
            values = result[: out.shape[0], column]
            out[:, number * head : (number + 1) * head] = values.astype(out.dtype)


def head_places(number, core):
    keyval = (number // 2) ^ core
    return 2 * keyval + number % 2, keyval


def add_kernel(own, first, second, both, query, keyval):
    head = query.shape[1]
    total = own[...]
    for part in (first, second, both):
        total = total + part[...].astype(jnp.float32)
    total = total.astype(query.dtype)
    query[...] = total[:, :head]
    keyval[...] = total[:, head:]


def request_of(position, ends):
    found = jnp.zeros_like(position)
    for end in ends:
        found = found + jnp.where(position >= end, 1, 0)
    return found


def attend_kernel(steps, count, scale, block_map, lengths, query, mine, theirs, *refs):
    attended, key_all, value_all = refs
    q_rows, head = query.shape
    pad = -(-count // ROW_TILE) * ROW_TILE
    tail = q_rows - pad
    rows = tail // steps
    k_rows = key_all.shape[0]
    _, _, k = place()
    for ref, at in ((key_all, 0), (value_all, head)):
        ref[:tail, :] = mine[:tail, at : at + head]
        ref[tail : 2 * tail, :] = theirs[:tail, at : at + head]
        ref[2 * tail :, :] = jnp.zeros_like(ref[2 * tail :, :])
        ref[2 * tail : 2 * tail + pad, :] = mine[tail:, at : at + head]

    ends, total = [], 0
    for request in range(count):
        total = total + lengths[request]
        ends.append(total)

    def labels(shape, axis, held):
        index = lax.broadcasted_iota(jnp.int32, shape, axis)
        position = jnp.zeros(shape, jnp.int32)
        for number, block in enumerate(held):
            inside = (index >= number * rows) & (index < (number + 1) * rows)
            position = jnp.where(inside, block_map[block] * rows + index - number * rows, position)
        last = len(held) * rows
        is_new = index >= last
        request = jnp.where(is_new, index - last, request_of(position, ends))
        return jnp.where(is_new, LAST, position), request

    held = [2 * number + core for core in (k, 1 - k) for number in range(steps)]
    q_position, q_request = labels((q_rows, 1), 0, held[:steps])
    k_position, k_request = labels((1, k_rows), 1, held)
    allowed = (q_request == k_request) & (k_position <= q_position)
    scores = lax.dot_general(
        query[...],
        key_all[...],
        (((1,), (1,)), ((), ())),
        preferred_element_type=jnp.float32,
    )
    scores = jnp.where(allowed, scores * scale, FLOOR)
    weights = jnp.exp(scores - jnp.max(scores, axis=1, keepdims=True))
    denom = jnp.sum(weights, axis=1, keepdims=True)
    mixed = jnp.dot(
        weights.astype(jnp.bfloat16), value_all[...], preferred_element_type=jnp.float32
    )
    attended[...] = (mixed / denom).astype(jnp.bfloat16)


def output_kernel(rows, *refs):
    heads, (w_own, w_other), refs = turned(refs[:4]), refs[4:6], refs[6:]
    outs, (attended, result) = refs[:4], refs[4:]
    c, _, k = place()
    head = heads[0].shape[1]
    for mask, ref in enumerate(heads):
        at, _ = head_places(c ^ mask, k)
        attended[:, pl.ds(pl.multiple_of(at * head, head), head)] = ref[...]
    rows_own = w_own.shape[0]
    total = jnp.dot(attended[:, :rows_own], w_own[...], preferred_element_type=jnp.float32)
    total += jnp.dot(attended[:, rows_own:], w_other[...], preferred_element_type=jnp.float32)
    result[...] = total.astype(result.dtype)
    tail = 4 * rows
    for mask, out in enumerate(outs):
        out[:rows, :] = result[pl.ds(pl.multiple_of((c ^ mask) * rows, rows), rows), :]
        out[rows:, :] = result[tail:, :]


def relay_kernel(*refs):
    blocks, outs = refs[:4], refs[4:]
    c, z, _ = place()
    for slot, out in enumerate(outs):
        for mask, block in enumerate(blocks):

            @pl.when((c ^ z ^ slot) == mask)
            def _(out=out, block=block):
                out[...] = block[: out.shape[0], :]


def sum_kernel(*refs):
    parts, (keep, send) = refs[:4], refs[4:]
    width = keep.shape[1]
    _, _, k = place()
    for out, core in ((keep, k), (send, 1 - k)):
        column = pl.ds(pl.multiple_of(core * width, width), width)
        terms = [part[:, column].astype(jnp.float32) for part in parts]
        total = (terms[0] + terms[1]) + (terms[2] + terms[3])
        out[...] = total[: out.shape[0]].astype(out.dtype)


def finish_kernel(keep, other, prefill, decode):
    _, _, k = place()
    rows = other.shape[0]
    prefill[pl.ds(pl.multiple_of(k * rows, rows), rows), :] = keep[:rows]
    prefill[pl.ds(pl.multiple_of((1 - k) * rows, rows), rows), :] = other[...]
    decode[...] = keep[rows : rows + decode.shape[0]]


def on_device_small(
    steps, tp, tokens, new_token_states, w_query, key_matrix, value_matrix, w_out, lengths, block_map
):
    bf16, f32 = jnp.bfloat16, jnp.float32
    rows = tokens.shape[0] // 2
    depth = w_query.shape[0]
    count = new_token_states.shape[0]
    pad = -(-count // ROW_TILE) * ROW_TILE
    q_width = 2 * w_query.shape[1]
    kv_width = 2 * key_matrix.shape[1]
    features = q_width + 2 * kv_width
    out_width = w_out.shape[1]

    def to_core(value):
        return lax.ppermute(value, "tp", [(i, i ^ 1) for i in range(tp)])

    def to_chip(value, step):
        return lax.ppermute(value, "tp", [(i, i ^ (2 * step)) for i in range(tp)])

    def to_partners(values):
        return [
            lax.ppermute(value, "ctx", [(i, i ^ mask) for i in range(steps)])
            for mask, value in enumerate(values, 1)
        ]

    def call(kernel, name, inputs, shapes, scratch=(), spaces=None):
        return pl.pallas_call(
            kernel,
            out_shape=[jax.ShapeDtypeStruct(shape, kind) for shape, kind in shapes],
            in_specs=spaces or [vmem()] * len(inputs),
            out_specs=[vmem()] * len(shapes),
            scratch_shapes=list(scratch),
            compiler_params=pltpu.CompilerParams(vmem_limit_bytes=VMEM_BYTES),
            name=name,
        )(*inputs)

    c, _, k = place()
    sent = [
        lax.dynamic_slice(tokens, (k * rows, (c ^ mask) * depth), (rows, depth))
        for mask in range(steps)
    ]
    new_columns = lax.dynamic_slice_in_dim(new_token_states, c * depth, depth, 1)
    blocks = [sent[0]] + to_partners(sent[1:])
    *weights, _ = lax.optimization_barrier((w_query, key_matrix, value_matrix, sent[1]))
    (own,) = call(pack_kernel, "pack_weights", weights, [((depth, features // 2), bf16)])
    other = to_core(own)

    all_rows = steps * rows + pad
    x_rows = -(-all_rows // 16) * 16
    part = (all_rows, 3 * HEAD_SIZE)
    edges = [0, q_width // 2, (q_width + kv_width) // 2, features // 2]
    parts = call(
        functools.partial(project_kernel, list(zip(edges, edges[1:]))),
        "project",
        (*turned(blocks), new_columns, own, other),
        [(part, f32)] + [(part, bf16)] * (steps - 1),
        [pltpu.VMEM((x_rows, depth), bf16), pltpu.VMEM((x_rows, features), f32)],
    )
    w_out_later, _ = lax.optimization_barrier((w_out, parts[0]))
    w_other = to_core(w_out_later)

    query, keyval = call(
        add_kernel,
        "add_parts",
        (parts[0], *to_partners(parts[1:])),
        [((all_rows, HEAD_SIZE), bf16), ((all_rows, 2 * HEAD_SIZE), bf16)],
    )
    k_rows = -(-(2 * steps * rows + pad) // 128) * 128
    (attended,) = call(
        functools.partial(attend_kernel, steps, count, 1.0 / math.sqrt(HEAD_SIZE)),
        "attend",
        (block_map, lengths, query, keyval, to_core(keyval)),
        [((all_rows, HEAD_SIZE), bf16)],
        [pltpu.VMEM((k_rows, HEAD_SIZE), bf16)] * 2,
        [smem()] * 2 + [vmem()] * 3,
    )

    block = (rows + pad, out_width)
    outs = call(
        functools.partial(output_kernel, rows),
        "project_out",
        (*turned([attended, *to_partners([attended] * (steps - 1))]), w_out, w_other),
        [(block, bf16)] * steps,
        [pltpu.VMEM((all_rows, q_width), bf16), pltpu.VMEM((all_rows, out_width), bf16)],
    )

    slots = call(
        relay_kernel,
        "relay",
        [outs[0]] + to_partners(outs[1:]),
        [(block, bf16)] * steps,
    )
    slots = [slots[0]] + [to_chip(slot, step) for step, slot in enumerate(slots[1:], 1)]
    width = out_width // 2
    keep, send = call(
        sum_kernel, "sum_heads", slots, [((rows + pad, width), bf16), ((rows, width), bf16)]
    )
    return tuple(
        call(
            finish_kernel,
            "finish",
            (keep, to_core(send)),
            [((2 * rows, width), bf16), ((count, width), bf16)],
        )
    )


floor_value = -1e30


def initial_positions(block_map, first_row, row_count, block_rows):
    row_ids = first_row + jnp.arange(row_count, dtype=jnp.int32)
    block_ids = row_ids // block_rows
    table_ids = jnp.arange(block_map.shape[0], dtype=jnp.int32)
    mapped = jnp.sum(
        jnp.where(block_ids[:, None] == table_ids[None, :], block_map[None, :], 0), axis=1
    )
    return mapped * block_rows + row_ids % block_rows


def request_index(positions, request_ends):
    return jnp.sum((positions[:, None] >= request_ends[None, :]).astype(jnp.int32), axis=1)


def round_weights(weights):
    rounded = weights.astype(jnp.bfloat16)
    rounded = lax.optimization_barrier(rounded)
    return rounded.astype(jnp.float32)


def softmax_parts(
    dec_heads, projected_key_rows, projected_value_rows, owned, kv_heads, head_dim, score_scale
):
    row_count = projected_key_rows.shape[0]
    scores = (
        jnp.einsum(
            "rgjd,tgd->rgjt",
            dec_heads,
            projected_key_rows.reshape(row_count, kv_heads, head_dim),
            preferred_element_type=jnp.float32,
        )
        * score_scale
    )
    scores = jnp.where(owned, scores, floor_value)
    part_peak = jnp.max(scores, axis=3)
    weights = jnp.where(owned, jnp.exp(scores - part_peak[..., None]), 0.0)
    part_total = jnp.sum(weights, axis=3)
    part_mixed = jnp.einsum(
        "rgjt,tgd->rgjd",
        weights.astype(jnp.bfloat16),
        projected_value_rows.reshape(row_count, kv_heads, head_dim),
        preferred_element_type=jnp.float32,
    )
    return (part_peak, part_total, part_mixed)


def on_device_large(
    tokens, new_token_states, w_query, key_matrix, value_matrix, w_out, lengths, block_map
):
    local_rows = tokens.shape[0]
    block_rows = local_rows // 2
    request_count = new_token_states.shape[0]
    head_dim = HEAD_SIZE
    query_width = w_query.shape[1]
    kv_width = key_matrix.shape[1]
    kv_heads = kv_width // head_dim
    query_group_count = query_width // kv_width
    score_scale = 1.0 / math.sqrt(head_dim)
    device = lax.axis_index("ctx")
    request_ends = jnp.cumsum(lengths)
    inputs = jnp.concatenate([tokens, new_token_states], axis=0)
    shard_pieces = (
        lax.all_gather(w_query, "ctx", axis=0, tiled=True),
        lax.all_gather(key_matrix, "ctx", axis=0, tiled=True),
        lax.all_gather(value_matrix, "ctx", axis=0, tiled=True),
    )
    query_all, key_all, value_all = tuple(
        (jnp.dot(inputs, weight, preferred_element_type=jnp.float32) for weight in shard_pieces)
    )
    query_all = query_all.astype(jnp.bfloat16)
    key_all = key_all.astype(jnp.bfloat16)
    value_all = value_all.astype(jnp.bfloat16)
    local_query = query_all[:local_rows]
    local_keys = key_all[:local_rows]
    local_values = value_all[:local_rows]
    dec_query = query_all[local_rows:]
    decode_key_rows = key_all[local_rows:]
    decode_value_rows = value_all[local_rows:]
    token_pos = initial_positions(block_map, device * local_rows, local_rows, block_rows)
    token_request = request_index(token_pos, request_ends)
    query_heads = local_query.reshape(local_rows, kv_heads, query_group_count, head_dim)

    def attend(running, shard_pieces, first_row):
        peak_run, total_run, mixed_run = running
        key_piece, value_piece = shard_pieces
        row_count = key_piece.shape[0]
        key_pos = initial_positions(block_map, first_row, row_count, block_rows)
        key_request = request_index(key_pos, request_ends)
        allowed = (key_request[None, :] == token_request[:, None]) & (
            key_pos[None, :] <= token_pos[:, None]
        )
        scores = (
            jnp.einsum(
                "tgjd,kgd->gjtk",
                query_heads,
                key_piece.reshape(row_count, kv_heads, head_dim),
                preferred_element_type=jnp.float32,
            )
            * score_scale
        )
        scores = jnp.where(allowed, scores, floor_value)
        peak_new = jnp.maximum(peak_run, jnp.max(scores, axis=3))
        weights = jnp.where(allowed, jnp.exp(scores - peak_new[..., None]), 0.0)
        rescale = jnp.exp(peak_run - peak_new)
        total_new = total_run * rescale + jnp.sum(weights, axis=3)
        mixed_new = mixed_run * rescale[..., None] + jnp.einsum(
            "gjtk,kgd->gjtd",
            weights.astype(jnp.bfloat16),
            value_piece.reshape(row_count, kv_heads, head_dim),
            preferred_element_type=jnp.float32,
        )
        return (peak_new, total_new, mixed_new)

    start_state = (
        jnp.full((kv_heads, query_group_count, local_rows), floor_value, jnp.float32),
        jnp.zeros((kv_heads, query_group_count, local_rows), jnp.float32),
        jnp.zeros((kv_heads, query_group_count, local_rows, head_dim), jnp.float32),
    )
    dec_heads = dec_query.reshape(request_count, kv_heads, query_group_count, head_dim)
    request_ids = jnp.arange(request_count, dtype=jnp.int32)
    cache_keys, cache_values = (
        lax.all_gather(local_keys, "ctx", axis=0, tiled=True),
        lax.all_gather(local_values, "ctx", axis=0, tiled=True),
    )
    total_rows = cache_keys.shape[0]
    shard_count = total_rows // local_rows
    limit = max(1, 1024 // local_rows)
    step_rows = local_rows * math.gcd(shard_count, 1 << limit.bit_length() - 1)

    def key_step(running, step_index):
        first_row = step_index * step_rows
        pieces = (
            lax.dynamic_slice_in_dim(cache_keys, first_row, step_rows, 0),
            lax.dynamic_slice_in_dim(cache_values, first_row, step_rows, 0),
        )
        return (attend(running, pieces, first_row), None)

    final_state, unused = lax.scan(
        key_step, start_state, jnp.arange(total_rows // step_rows, dtype=jnp.int32)
    )
    peak_run, total_run, mixed_run = final_state
    cache_pos = (
        block_map[:, None] * block_rows + jnp.arange(block_rows, dtype=jnp.int32)[None, :]
    ).reshape(total_rows)
    cache_request = request_index(cache_pos, request_ends)
    owned = (cache_request[None, :] == request_ids[:, None])[:, None, None, :]
    cache_peak, cache_total, cache_mixed = softmax_parts(
        dec_heads, cache_keys, cache_values, owned, kv_heads, head_dim, score_scale
    )
    attended = (
        (mixed_run / total_run[..., None]).transpose(2, 0, 1, 3).reshape(local_rows, query_width)
    )
    attended = attended.astype(jnp.bfloat16)
    own_keys = decode_key_rows.reshape(request_count, kv_heads, 1, head_dim).astype(jnp.float32)
    own_values = decode_value_rows.reshape(request_count, kv_heads, 1, head_dim).astype(jnp.float32)
    self_scores = jnp.sum(dec_heads.astype(jnp.float32) * own_keys, axis=3) * score_scale
    peak_all = jnp.maximum(cache_peak, self_scores)
    rescale = jnp.exp(cache_peak - peak_all)
    self_weights = jnp.exp(self_scores - peak_all)
    dec_total = cache_total * rescale + self_weights
    dec_mixed = (
        cache_mixed * rescale[..., None] + round_weights(self_weights)[..., None] * own_values
    )
    dec_attn = (
        (dec_mixed / dec_total[..., None]).reshape(request_count, query_width).astype(jnp.bfloat16)
    )
    attended_all = jnp.concatenate([attended, dec_attn], axis=0)
    head_block = lax.all_gather(w_out, "ctx", axis=1, tiled=True)
    column_block = lax.all_to_all(head_block, "tp", split_axis=1, concat_axis=0, tiled=True)
    summed_rows = jnp.dot(
        lax.all_gather(attended_all, "tp", axis=1, tiled=True),
        column_block,
        preferred_element_type=jnp.float32,
    )
    summed_rows = summed_rows.astype(jnp.bfloat16)
    return (summed_rows[:local_rows], summed_rows[local_rows:])

def solution(mesh):
    steps, tp = mesh.shape["ctx"], mesh.shape["tp"]

    def on_device(tokens, *rest):
        chip_heads = 2 * rest[1].shape[1] // HEAD_SIZE
        small = steps == 4 and tp == 8 and chip_heads == 4 and tokens.shape[0] * steps <= 1024
        if small:
            return on_device_small(steps, tp, tokens, *rest)
        return on_device_large(tokens, *rest)

    return jax.shard_map(
        on_device,
        mesh=mesh,
        in_specs=(
            P("ctx", None),
            P(),
            P("ctx", "tp"),
            P("ctx", "tp"),
            P("ctx", "tp"),
            P("tp", "ctx"),
            P(),
            P(),
        ),
        out_specs=(P("ctx", "tp"), P(None, "tp")),
        check_vma=False,
    )
```

```python
import functools
import math

import jax
import jax.numpy as jnp
from jax import lax
from jax.experimental import pallas as pl
from jax.experimental.pallas import tpu as pltpu
from jax.sharding import PartitionSpec as P

HEAD_SIZE = 128
FLOOR = -1e30
LAST = 1 << 30
ROW_TILE = 8
VMEM_BYTES = 48 * 1024 * 1024


def vmem():
    return pl.BlockSpec(memory_space=pltpu.VMEM)


def smem():
    return pl.BlockSpec(memory_space=pltpu.SMEM)


def place():
    t = lax.axis_index("tp")
    return lax.axis_index("ctx"), t // 2, t % 2


def project_kernel(rows, own, *refs):
    (mine, theirs), refs = ([refs[2], *refs[:2]], [refs[5], *refs[3:5]]), refs[6:]
    (new, *weights), refs = refs[:4], refs[4:]
    held, new_held, *outs, inputs = refs
    count = new.shape[0]
    pad = new_held.shape[0]
    tail = 4 * rows
    _, _, k = place()
    inputs[:rows, :] = own[...]
    for number, pair in enumerate(zip(mine, theirs), 1):
        for core, block in zip((k, 1 - k), pair):
            first = number * rows + core * block.shape[0]
            inputs[pl.ds(pl.multiple_of(first, block.shape[0]), block.shape[0]), :] = block[...]
    inputs[tail:, :] = jnp.zeros_like(inputs[tail:, :])
    inputs[tail : tail + count, :] = new[...]
    x = inputs[...]
    column = 0
    for weight in (weights[0][...], jnp.concatenate([weights[1][...], weights[2][...]], axis=1)):
        part = jnp.dot(x, weight, preferred_element_type=jnp.float32)
        to = slice(column, column + weight.shape[1])
        held[:, to] = part[:rows]
        news = part[tail : tail + pad].astype(new_held.dtype)
        new_held[:, to] = news
        for step, out in enumerate(outs, 1):
            out[:rows, to] = part[step * rows : (step + 1) * rows].astype(out.dtype)
            out[rows:, to] = news
        column += weight.shape[1]


def add_kernel(own, new_own, first, second, both, held, new):
    rows = held.shape[0]

    def total(own, at):
        parts = [own[...].astype(jnp.float32)]
        parts += [ref[at, :].astype(jnp.float32) for ref in (first, second, both)]
        return ((parts[0] + parts[1]) + (parts[2] + parts[3])).astype(held.dtype)

    held[...] = total(own, slice(0, rows))
    new[...] = total(new_own, slice(rows, None))


def request_of(position, ends):
    found = jnp.zeros_like(position)
    for end in ends:
        found = found + jnp.where(position >= end, 1, 0)
    return found


def attend_kernel(block_rows, count, scale, block_map, lengths, *refs):
    blocks, new, attended = (refs[0], *refs[3:0:-1]), refs[4], refs[5]
    rows, features = blocks[0].shape
    head = HEAD_SIZE
    q_width = features - 2 * head
    pad = new.shape[0]
    tail = len(blocks) * rows
    c, _, _ = place()

    def column(number):
        at = slice(number * head, (number + 1) * head)
        news = jnp.concatenate([new[:, at], jnp.zeros((head - pad, head), new.dtype)], axis=0)
        return jnp.concatenate([block[:, at] for block in blocks], axis=0), news

    keys, new_keys = column(q_width // head)
    values, new_values = column(q_width // head + 1)

    ends, total = [], 0
    for request in range(count):
        total = total + lengths[request]
        ends.append(total)

    def labels(shape, axis):
        index = lax.broadcasted_iota(jnp.int32, shape, axis)
        position = jnp.zeros(shape, jnp.int32)
        per_device = rows // block_rows
        for number in range(len(blocks) * per_device):
            held = per_device * (c ^ (number // per_device)) + number % per_device
            start = number * block_rows
            inside = (index >= start) & (index < start + block_rows)
            position = jnp.where(inside, block_map[held] * block_rows + index - start, position)
        return position, request_of(position, ends)

    q_position, q_request = labels((tail, 1), 0)
    k_position, k_request = labels((1, tail), 1)
    allowed = (q_request == k_request) & (k_position <= q_position)
    new_rows = 2 * ROW_TILE
    new_request = lax.broadcasted_iota(jnp.int32, (new_rows, 1), 0)
    new_allowed = new_request == k_request
    own_allowed = new_request == lax.broadcasted_iota(jnp.int32, (1, head), 1)

    def scores_of(query, keys, allowed):
        scores = lax.dot_general(
            query, keys, (((1,), (1,)), ((), ())), preferred_element_type=jnp.float32
        )
        return jnp.where(allowed, scores * scale, FLOOR)

    def mix(weights, values):
        return jnp.dot(weights.astype(jnp.bfloat16), values, preferred_element_type=jnp.float32)

    for number in range(q_width // head):
        at = slice(number * head, (number + 1) * head)
        query, new_query = column(number)
        scores = scores_of(query, keys, allowed)
        weights = jnp.exp(scores - jnp.max(scores, axis=1, keepdims=True))
        denom = jnp.sum(weights, axis=1, keepdims=True)
        attended[:tail, at] = (mix(weights, values) / denom).astype(jnp.bfloat16)
        new_query = new_query[:new_rows]
        scores = scores_of(new_query, keys, new_allowed)
        own_scores = scores_of(new_query, new_keys, own_allowed)
        peak = jnp.maximum(
            jnp.max(scores, axis=1, keepdims=True), jnp.max(own_scores, axis=1, keepdims=True)
        )
        weights, own_weights = jnp.exp(scores - peak), jnp.exp(own_scores - peak)
        denom = jnp.sum(weights, axis=1, keepdims=True)
        denom += jnp.sum(own_weights, axis=1, keepdims=True)
        mixed = (mix(weights, values) + mix(own_weights, new_values)) / denom
        attended[tail:, at] = mixed[:pad].astype(jnp.bfloat16)


def output_kernel(rows, mine, theirs, w_own, w_other, *outs):
    _, _, k = place()
    width = w_other.shape[1]
    w_mine = w_own[:, pl.ds(pl.multiple_of(k * width, width), width)]
    total = jnp.dot(mine[...], w_mine, preferred_element_type=jnp.float32)
    total += jnp.dot(theirs[...], w_other[...], preferred_element_type=jnp.float32)
    total = total.astype(outs[0].dtype)
    for number, out in enumerate(outs):
        out[:rows, :] = total[number * rows : (number + 1) * rows]
        out[rows:, :] = total[len(outs) * rows :]


def relay_kernel(*refs):
    blocks, outs = refs[:4], refs[4:]
    c, z, _ = place()
    for slot, out in enumerate(outs):
        for mask, block in enumerate(blocks):

            @pl.when((c ^ z ^ slot) == mask)
            def _(out=out, block=block):
                out[...] = block[: out.shape[0], :]


def finish_kernel(*refs):
    parts, (prefill, decode) = refs[:4], refs[4:]
    terms = [part[...].astype(jnp.float32) for part in parts]
    total = ((terms[0] + terms[1]) + (terms[2] + terms[3])).astype(prefill.dtype)
    rows = prefill.shape[0]
    prefill[...] = total[:rows]
    decode[...] = total[rows : rows + decode.shape[0]]


def on_device_small(
    steps, tp, tokens, new_token_states, w_query, key_matrix, value_matrix, w_out, lengths, block_map
):
    bf16, f32 = jnp.bfloat16, jnp.float32
    rows = tokens.shape[0]
    half = rows // 2
    depth = w_query.shape[0]
    count = new_token_states.shape[0]
    pad = -(-count // ROW_TILE) * ROW_TILE
    q_width = w_query.shape[1]
    features = q_width + 2 * key_matrix.shape[1]
    width = w_out.shape[1] // 2
    all_rows = steps * rows + pad

    def to_core(value):
        return lax.ppermute(value, "tp", [(i, i ^ 1) for i in range(tp)])

    def to_chip(value, step):
        return lax.ppermute(value, "tp", [(i, i ^ (2 * step)) for i in range(tp)])

    def to_partners(values):
        return [
            lax.ppermute(value, "ctx", [(i, i ^ mask) for i in range(steps)])
            for mask, value in enumerate(values, 1)
        ]

    def call(kernel, name, inputs, shapes, scratch=(), spaces=None):
        return pl.pallas_call(
            kernel,
            out_shape=[jax.ShapeDtypeStruct(shape, kind) for shape, kind in shapes],
            in_specs=spaces or [vmem()] * len(inputs),
            out_specs=[vmem()] * len(shapes),
            scratch_shapes=list(scratch),
            compiler_params=pltpu.CompilerParams(vmem_limit_bytes=VMEM_BYTES),
            name=name,
        )(*inputs)

    c, _, k = place()
    sent = [
        lax.dynamic_slice(tokens, (k * half, (c ^ mask) * depth), (half, depth))
        for mask in range(1, steps)
    ]
    own = lax.dynamic_slice_in_dim(tokens, c * depth, depth, 1)
    new_columns = lax.dynamic_slice_in_dim(new_token_states, c * depth, depth, 1)
    mine = to_partners(sent)
    theirs = [to_core(value) for value in mine]

    part = (rows + pad, features)
    own_part, new_part, *parts = call(
        functools.partial(project_kernel, rows),
        "project",
        (own, *mine[1:], mine[0], *theirs[1:], theirs[0], new_columns, w_query, key_matrix, value_matrix),
        [((rows, features), f32), ((pad, features), bf16)] + [(part, bf16)] * (steps - 1),
        [pltpu.VMEM((-(-all_rows // 16) * 16, depth), bf16)],
    )

    w_sent = lax.dynamic_slice_in_dim(w_out, (1 - k) * width, width, 1)
    w_sent, _ = lax.optimization_barrier((w_sent, new_part))
    w_other = to_core(w_sent)
    new_part, w_other = lax.optimization_barrier((new_part, w_other))

    held, new = call(
        add_kernel,
        "add_parts",
        (own_part, new_part, *to_partners(parts)),
        [((rows, features), bf16), ((pad, features), bf16)],
    )

    (attended,) = call(
        functools.partial(
            attend_kernel, steps * rows // block_map.shape[0], count, 1.0 / math.sqrt(HEAD_SIZE)
        ),
        "attend",
        (block_map, lengths, held, *to_partners([held] * (steps - 1))[::-1], new),
        [((all_rows, q_width), bf16)],
        spaces=[smem()] * 2 + [vmem()] * (steps + 1),
    )

    block = (rows + pad, width)
    outs = call(
        functools.partial(output_kernel, rows),
        "project_out",
        (attended, to_core(attended), w_out, w_other),
        [(block, bf16)] * steps,
    )

    slots = call(
        relay_kernel, "relay", [outs[0]] + to_partners(outs[1:]), [(block, bf16)] * steps
    )
    slots = [slots[0]] + [to_chip(slot, step) for step, slot in enumerate(slots[1:], 1)]
    return tuple(
        call(finish_kernel, "finish", slots, [((rows, width), bf16), ((count, width), bf16)])
    )


floor_value = -1e30


def initial_positions(block_map, first_row, row_count, block_rows):
    row_ids = first_row + jnp.arange(row_count, dtype=jnp.int32)
    block_ids = row_ids // block_rows
    table_ids = jnp.arange(block_map.shape[0], dtype=jnp.int32)
    mapped = jnp.sum(
        jnp.where(block_ids[:, None] == table_ids[None, :], block_map[None, :], 0), axis=1
    )
    return mapped * block_rows + row_ids % block_rows


def request_index(positions, request_ends):
    return jnp.sum((positions[:, None] >= request_ends[None, :]).astype(jnp.int32), axis=1)


def round_weights(weights):
    rounded = weights.astype(jnp.bfloat16)
    rounded = lax.optimization_barrier(rounded)
    return rounded.astype(jnp.float32)


def softmax_parts(
    dec_heads, projected_key_rows, projected_value_rows, owned, kv_heads, head_dim, score_scale
):
    row_count = projected_key_rows.shape[0]
    scores = (
        jnp.einsum(
            "rgjd,tgd->rgjt",
            dec_heads,
            projected_key_rows.reshape(row_count, kv_heads, head_dim),
            preferred_element_type=jnp.float32,
        )
        * score_scale
    )
    scores = jnp.where(owned, scores, floor_value)
    part_peak = jnp.max(scores, axis=3)
    weights = jnp.where(owned, jnp.exp(scores - part_peak[..., None]), 0.0)
    part_total = jnp.sum(weights, axis=3)
    part_mixed = jnp.einsum(
        "rgjt,tgd->rgjd",
        weights.astype(jnp.bfloat16),
        projected_value_rows.reshape(row_count, kv_heads, head_dim),
        preferred_element_type=jnp.float32,
    )
    return (part_peak, part_total, part_mixed)


def on_device_large(
    tokens, new_token_states, w_query, key_matrix, value_matrix, w_out, lengths, block_map
):
    local_rows = tokens.shape[0]
    block_rows = local_rows // 2
    request_count = new_token_states.shape[0]
    head_dim = HEAD_SIZE
    query_width = w_query.shape[1]
    kv_width = key_matrix.shape[1]
    kv_heads = kv_width // head_dim
    query_group_count = query_width // kv_width
    score_scale = 1.0 / math.sqrt(head_dim)
    device = lax.axis_index("ctx")
    request_ends = jnp.cumsum(lengths)
    inputs = jnp.concatenate([tokens, new_token_states], axis=0)
    shard_pieces = (
        lax.all_gather(w_query, "ctx", axis=0, tiled=True),
        lax.all_gather(key_matrix, "ctx", axis=0, tiled=True),
        lax.all_gather(value_matrix, "ctx", axis=0, tiled=True),
    )
    query_all, key_all, value_all = tuple(
        (jnp.dot(inputs, weight, preferred_element_type=jnp.float32) for weight in shard_pieces)
    )
    query_all = query_all.astype(jnp.bfloat16)
    key_all = key_all.astype(jnp.bfloat16)
    value_all = value_all.astype(jnp.bfloat16)
    local_query = query_all[:local_rows]
    local_keys = key_all[:local_rows]
    local_values = value_all[:local_rows]
    dec_query = query_all[local_rows:]
    decode_key_rows = key_all[local_rows:]
    decode_value_rows = value_all[local_rows:]
    token_pos = initial_positions(block_map, device * local_rows, local_rows, block_rows)
    token_request = request_index(token_pos, request_ends)
    query_heads = local_query.reshape(local_rows, kv_heads, query_group_count, head_dim)

    def attend(running, shard_pieces, first_row):
        peak_run, total_run, mixed_run = running
        key_piece, value_piece = shard_pieces
        row_count = key_piece.shape[0]
        key_pos = initial_positions(block_map, first_row, row_count, block_rows)
        key_request = request_index(key_pos, request_ends)
        allowed = (key_request[None, :] == token_request[:, None]) & (
            key_pos[None, :] <= token_pos[:, None]
        )
        scores = (
            jnp.einsum(
                "tgjd,kgd->gjtk",
                query_heads,
                key_piece.reshape(row_count, kv_heads, head_dim),
                preferred_element_type=jnp.float32,
            )
            * score_scale
        )
        scores = jnp.where(allowed, scores, floor_value)
        peak_new = jnp.maximum(peak_run, jnp.max(scores, axis=3))
        weights = jnp.where(allowed, jnp.exp(scores - peak_new[..., None]), 0.0)
        rescale = jnp.exp(peak_run - peak_new)
        total_new = total_run * rescale + jnp.sum(weights, axis=3)
        mixed_new = mixed_run * rescale[..., None] + jnp.einsum(
            "gjtk,kgd->gjtd",
            weights.astype(jnp.bfloat16),
            value_piece.reshape(row_count, kv_heads, head_dim),
            preferred_element_type=jnp.float32,
        )
        return (peak_new, total_new, mixed_new)

    start_state = (
        jnp.full((kv_heads, query_group_count, local_rows), floor_value, jnp.float32),
        jnp.zeros((kv_heads, query_group_count, local_rows), jnp.float32),
        jnp.zeros((kv_heads, query_group_count, local_rows, head_dim), jnp.float32),
    )
    dec_heads = dec_query.reshape(request_count, kv_heads, query_group_count, head_dim)
    request_ids = jnp.arange(request_count, dtype=jnp.int32)
    cache_keys, cache_values = (
        lax.all_gather(local_keys, "ctx", axis=0, tiled=True),
        lax.all_gather(local_values, "ctx", axis=0, tiled=True),
    )
    total_rows = cache_keys.shape[0]
    shard_count = total_rows // local_rows
    limit = max(1, 1024 // local_rows)
    step_rows = local_rows * math.gcd(shard_count, 1 << limit.bit_length() - 1)

    def key_step(running, step_index):
        first_row = step_index * step_rows
        pieces = (
            lax.dynamic_slice_in_dim(cache_keys, first_row, step_rows, 0),
            lax.dynamic_slice_in_dim(cache_values, first_row, step_rows, 0),
        )
        return (attend(running, pieces, first_row), None)

    final_state, unused = lax.scan(
        key_step, start_state, jnp.arange(total_rows // step_rows, dtype=jnp.int32)
    )
    peak_run, total_run, mixed_run = final_state
    cache_pos = (
        block_map[:, None] * block_rows + jnp.arange(block_rows, dtype=jnp.int32)[None, :]
    ).reshape(total_rows)
    cache_request = request_index(cache_pos, request_ends)
    owned = (cache_request[None, :] == request_ids[:, None])[:, None, None, :]
    cache_peak, cache_total, cache_mixed = softmax_parts(
        dec_heads, cache_keys, cache_values, owned, kv_heads, head_dim, score_scale
    )
    attended = (
        (mixed_run / total_run[..., None]).transpose(2, 0, 1, 3).reshape(local_rows, query_width)
    )
    attended = attended.astype(jnp.bfloat16)
    own_keys = decode_key_rows.reshape(request_count, kv_heads, 1, head_dim).astype(jnp.float32)
    own_values = decode_value_rows.reshape(request_count, kv_heads, 1, head_dim).astype(jnp.float32)
    self_scores = jnp.sum(dec_heads.astype(jnp.float32) * own_keys, axis=3) * score_scale
    peak_all = jnp.maximum(cache_peak, self_scores)
    rescale = jnp.exp(cache_peak - peak_all)
    self_weights = jnp.exp(self_scores - peak_all)
    dec_total = cache_total * rescale + self_weights
    dec_mixed = (
        cache_mixed * rescale[..., None] + round_weights(self_weights)[..., None] * own_values
    )
    dec_attn = (
        (dec_mixed / dec_total[..., None]).reshape(request_count, query_width).astype(jnp.bfloat16)
    )
    attended_all = jnp.concatenate([attended, dec_attn], axis=0)
    head_block = lax.all_gather(w_out, "ctx", axis=1, tiled=True)
    column_block = lax.all_to_all(head_block, "tp", split_axis=1, concat_axis=0, tiled=True)
    summed_rows = jnp.dot(
        lax.all_gather(attended_all, "tp", axis=1, tiled=True),
        column_block,
        preferred_element_type=jnp.float32,
    )
    summed_rows = summed_rows.astype(jnp.bfloat16)
    return (summed_rows[:local_rows], summed_rows[local_rows:])

def solution(mesh):
    steps, tp = mesh.shape["ctx"], mesh.shape["tp"]

    def on_device(tokens, *rest):
        one_head = rest[2].shape[1] == HEAD_SIZE
        small = steps == 4 and tp == 8 and one_head and tokens.shape[0] * steps <= 1024
        if small:
            return on_device_small(steps, tp, tokens, *rest)
        return on_device_large(tokens, *rest)

    return jax.shard_map(
        on_device,
        mesh=mesh,
        in_specs=(
            P("ctx", None),
            P(),
            P("ctx", "tp"),
            P("ctx", "tp"),
            P("ctx", "tp"),
            P("tp", "ctx"),
            P(),
            P(),
        ),
        out_specs=(P("ctx", "tp"), P(None, "tp")),
        check_vma=False,
    )
```

```python
import functools
import math

import jax
import jax.numpy as jnp
from jax import lax
from jax.experimental import pallas as pl
from jax.experimental.pallas import tpu as pltpu
from jax.sharding import PartitionSpec as P

HEAD_SIZE = 128
FLOOR = -1e30
LAST = 1 << 30
ROW_TILE = 8
VMEM_BYTES = 48 * 1024 * 1024


def vmem():
    return pl.BlockSpec(memory_space=pltpu.VMEM)


def smem():
    return pl.BlockSpec(memory_space=pltpu.SMEM)


def place():
    t = lax.axis_index("tp")
    return lax.axis_index("ctx"), t // 2, t % 2


def project_kernel(rows, own, *refs):
    (mine, theirs), refs = (refs[:3], refs[3:6]), refs[6:]
    (new, *weights), refs = refs[:4], refs[4:]
    held, new_held, *outs, inputs = refs
    count = new.shape[0]
    pad = new_held.shape[0]
    tail = 4 * rows
    _, _, k = place()
    inputs[:rows, :] = own[...]
    for number, pair in enumerate(zip(mine, theirs), 1):
        for core, block in zip((k, 1 - k), pair):
            first = number * rows + core * block.shape[0]
            inputs[pl.ds(pl.multiple_of(first, block.shape[0]), block.shape[0]), :] = block[...]
    inputs[tail:, :] = jnp.zeros_like(inputs[tail:, :])
    inputs[tail : tail + count, :] = new[...]
    x = inputs[...]
    column = 0
    for weight in (weights[0][...], jnp.concatenate([weights[1][...], weights[2][...]], axis=1)):
        part = jnp.dot(x, weight, preferred_element_type=jnp.float32)
        to = slice(column, column + weight.shape[1])
        held[:, to] = part[:rows]
        news = part[tail : tail + pad].astype(new_held.dtype)
        new_held[:, to] = news
        for step, out in enumerate(outs, 1):
            out[:rows, to] = part[step * rows : (step + 1) * rows].astype(out.dtype)
            out[rows:, to] = news
        column += weight.shape[1]


def add_kernel(own, new_own, first, second, both, held, new):
    rows = held.shape[0]

    def total(own, at):
        parts = [own[...].astype(jnp.float32)]
        parts += [ref[at, :].astype(jnp.float32) for ref in (first, second, both)]
        return ((parts[0] + parts[1]) + (parts[2] + parts[3])).astype(held.dtype)

    held[...] = total(own, slice(0, rows))
    new[...] = total(new_own, slice(rows, None))


def request_of(position, ends):
    found = jnp.zeros_like(position)
    for end in ends:
        found = found + jnp.where(position >= end, 1, 0)
    return found


def attend_kernel(block_rows, count, scale, block_map, lengths, *refs):
    blocks, new, attended = (refs[0], refs[2], refs[3], refs[1]), refs[4], refs[5]
    rows, features = blocks[0].shape
    head = HEAD_SIZE
    q_width = features - 2 * head
    pad = new.shape[0]
    tail = len(blocks) * rows
    c, _, _ = place()

    def column(number):
        at = slice(number * head, (number + 1) * head)
        news = jnp.concatenate([new[:, at], jnp.zeros((head - pad, head), new.dtype)], axis=0)
        return jnp.concatenate([block[:, at] for block in blocks], axis=0), news

    keys, new_keys = column(q_width // head)
    values, new_values = column(q_width // head + 1)

    ends, total = [], 0
    for request in range(count):
        total = total + lengths[request]
        ends.append(total)

    def labels(shape, axis):
        index = lax.broadcasted_iota(jnp.int32, shape, axis)
        position = jnp.zeros(shape, jnp.int32)
        per_device = rows // block_rows
        for number in range(len(blocks) * per_device):
            held = per_device * (c ^ (number // per_device)) + number % per_device
            start = number * block_rows
            inside = (index >= start) & (index < start + block_rows)
            position = jnp.where(inside, block_map[held] * block_rows + index - start, position)
        return position, request_of(position, ends)

    q_position, q_request = labels((tail, 1), 0)
    k_position, k_request = labels((1, tail), 1)
    allowed = (q_request == k_request) & (k_position <= q_position)
    new_rows = 2 * ROW_TILE
    new_request = lax.broadcasted_iota(jnp.int32, (new_rows, 1), 0)
    new_allowed = new_request == k_request
    own_allowed = new_request == lax.broadcasted_iota(jnp.int32, (1, head), 1)

    def scores_of(query, keys, allowed):
        scores = lax.dot_general(
            query, keys, (((1,), (1,)), ((), ())), preferred_element_type=jnp.float32
        )
        return jnp.where(allowed, scores * scale, FLOOR)

    def mix(weights, values):
        return jnp.dot(weights.astype(jnp.bfloat16), values, preferred_element_type=jnp.float32)

    for number in range(q_width // head):
        at = slice(number * head, (number + 1) * head)
        query, new_query = column(number)
        scores = scores_of(query, keys, allowed)
        weights = jnp.exp(scores - jnp.max(scores, axis=1, keepdims=True))
        denom = jnp.sum(weights, axis=1, keepdims=True)
        attended[:tail, at] = (mix(weights, values) / denom).astype(jnp.bfloat16)
        new_query = new_query[:new_rows]
        scores = scores_of(new_query, keys, new_allowed)
        own_scores = scores_of(new_query, new_keys, own_allowed)
        peak = jnp.maximum(
            jnp.max(scores, axis=1, keepdims=True), jnp.max(own_scores, axis=1, keepdims=True)
        )
        weights, own_weights = jnp.exp(scores - peak), jnp.exp(own_scores - peak)
        denom = jnp.sum(weights, axis=1, keepdims=True)
        denom += jnp.sum(own_weights, axis=1, keepdims=True)
        mixed = (mix(weights, values) + mix(own_weights, new_values)) / denom
        attended[tail:, at] = mixed[:pad].astype(jnp.bfloat16)


def output_kernel(rows, mine, theirs, w_own, w_other, *outs):
    _, _, k = place()
    width = w_other.shape[1]
    w_mine = w_own[:, pl.ds(pl.multiple_of(k * width, width), width)]
    total = jnp.dot(mine[...], w_mine, preferred_element_type=jnp.float32)
    total += jnp.dot(theirs[...], w_other[...], preferred_element_type=jnp.float32)
    total = total.astype(outs[0].dtype)
    for number, out in enumerate(outs):
        out[:rows, :] = total[number * rows : (number + 1) * rows]
        out[rows:, :] = total[len(outs) * rows :]


def relay_kernel(*refs):
    blocks, outs = refs[:4], refs[4:]
    c, z, _ = place()
    for slot, out in enumerate(outs):
        for mask, block in enumerate(blocks):

            @pl.when((c ^ z ^ slot) == mask)
            def _(out=out, block=block):
                out[...] = block[: out.shape[0], :]


def finish_kernel(*refs):
    parts, (prefill, decode) = refs[:4], refs[4:]
    terms = [part[...].astype(jnp.float32) for part in parts]
    total = ((terms[0] + terms[1]) + (terms[2] + terms[3])).astype(prefill.dtype)
    rows = prefill.shape[0]
    prefill[...] = total[:rows]
    decode[...] = total[rows : rows + decode.shape[0]]


def on_device_small(
    steps, tp, tokens, new_token_states, w_query, key_matrix, value_matrix, w_out, lengths, block_map
):
    bf16, f32 = jnp.bfloat16, jnp.float32
    rows = tokens.shape[0]
    half = rows // 2
    depth = w_query.shape[0]
    count = new_token_states.shape[0]
    pad = -(-count // ROW_TILE) * ROW_TILE
    q_width = w_query.shape[1]
    features = q_width + 2 * key_matrix.shape[1]
    width = w_out.shape[1] // 2
    all_rows = steps * rows + pad

    def to_core(value):
        return lax.ppermute(value, "tp", [(i, i ^ 1) for i in range(tp)])

    def to_chip(value, step):
        return lax.ppermute(value, "tp", [(i, i ^ (2 * step)) for i in range(tp)])

    def to_partners(values):
        return [
            lax.ppermute(value, "ctx", [(i, i ^ mask) for i in range(steps)])
            for mask, value in enumerate(values, 1)
        ]

    def call(kernel, name, inputs, shapes, scratch=(), spaces=None):
        return pl.pallas_call(
            kernel,
            out_shape=[jax.ShapeDtypeStruct(shape, kind) for shape, kind in shapes],
            in_specs=spaces or [vmem()] * len(inputs),
            out_specs=[vmem()] * len(shapes),
            scratch_shapes=list(scratch),
            compiler_params=pltpu.CompilerParams(vmem_limit_bytes=VMEM_BYTES),
            name=name,
        )(*inputs)

    c, _, k = place()
    sent = [
        lax.dynamic_slice(tokens, (k * half, (c ^ mask) * depth), (half, depth))
        for mask in range(1, steps)
    ]
    own = lax.dynamic_slice_in_dim(tokens, c * depth, depth, 1)
    new_columns = lax.dynamic_slice_in_dim(new_token_states, c * depth, depth, 1)
    mine = to_partners(sent)
    theirs = [to_core(value) for value in mine]

    part = (rows + pad, features)
    own_part, new_part, *parts = call(
        functools.partial(project_kernel, rows),
        "project",
        (own, *mine, *theirs, new_columns, w_query, key_matrix, value_matrix),
        [((rows, features), f32), ((pad, features), bf16)] + [(part, bf16)] * (steps - 1),
        [pltpu.VMEM((-(-all_rows // 16) * 16, depth), bf16)],
    )

    held, new = call(
        add_kernel,
        "add_parts",
        (own_part, new_part, *to_partners(parts)),
        [((rows, features), bf16), ((pad, features), bf16)],
    )

    first, second, both = to_partners([held] * (steps - 1))
    (attended,) = call(
        functools.partial(
            attend_kernel, steps * rows // block_map.shape[0], count, 1.0 / math.sqrt(HEAD_SIZE)
        ),
        "attend",
        (block_map, lengths, held, both, first, second, new),
        [((all_rows, q_width), bf16)],
        spaces=[smem()] * 2 + [vmem()] * (steps + 1),
    )

    w_sent = lax.dynamic_slice_in_dim(w_out, (1 - k) * width, width, 1)
    w_sent, _ = lax.optimization_barrier((w_sent, held))
    w_other = to_core(w_sent)

    block = (rows + pad, width)
    outs = call(
        functools.partial(output_kernel, rows),
        "project_out",
        (attended, to_core(attended), w_out, w_other),
        [(block, bf16)] * steps,
    )

    slots = call(
        relay_kernel, "relay", [outs[0]] + to_partners(outs[1:]), [(block, bf16)] * steps
    )
    slots = [slots[0]] + [to_chip(slot, step) for step, slot in enumerate(slots[1:], 1)]
    return tuple(
        call(finish_kernel, "finish", slots, [((rows, width), bf16), ((count, width), bf16)])
    )


floor_value = -1e30


def initial_positions(block_map, first_row, row_count, block_rows):
    row_ids = first_row + jnp.arange(row_count, dtype=jnp.int32)
    block_ids = row_ids // block_rows
    table_ids = jnp.arange(block_map.shape[0], dtype=jnp.int32)
    mapped = jnp.sum(
        jnp.where(block_ids[:, None] == table_ids[None, :], block_map[None, :], 0), axis=1
    )
    return mapped * block_rows + row_ids % block_rows


def request_index(positions, request_ends):
    return jnp.sum((positions[:, None] >= request_ends[None, :]).astype(jnp.int32), axis=1)


def round_weights(weights):
    rounded = weights.astype(jnp.bfloat16)
    rounded = lax.optimization_barrier(rounded)
    return rounded.astype(jnp.float32)


def softmax_parts(
    dec_heads, projected_key_rows, projected_value_rows, owned, kv_heads, head_dim, score_scale
):
    row_count = projected_key_rows.shape[0]
    scores = (
        jnp.einsum(
            "rgjd,tgd->rgjt",
            dec_heads,
            projected_key_rows.reshape(row_count, kv_heads, head_dim),
            preferred_element_type=jnp.float32,
        )
        * score_scale
    )
    scores = jnp.where(owned, scores, floor_value)
    part_peak = jnp.max(scores, axis=3)
    weights = jnp.where(owned, jnp.exp(scores - part_peak[..., None]), 0.0)
    part_total = jnp.sum(weights, axis=3)
    part_mixed = jnp.einsum(
        "rgjt,tgd->rgjd",
        weights.astype(jnp.bfloat16),
        projected_value_rows.reshape(row_count, kv_heads, head_dim),
        preferred_element_type=jnp.float32,
    )
    return (part_peak, part_total, part_mixed)


def on_device_large(
    tokens, new_token_states, w_query, key_matrix, value_matrix, w_out, lengths, block_map
):
    local_rows = tokens.shape[0]
    block_rows = local_rows // 2
    request_count = new_token_states.shape[0]
    head_dim = HEAD_SIZE
    query_width = w_query.shape[1]
    kv_width = key_matrix.shape[1]
    kv_heads = kv_width // head_dim
    query_group_count = query_width // kv_width
    score_scale = 1.0 / math.sqrt(head_dim)
    device = lax.axis_index("ctx")
    request_ends = jnp.cumsum(lengths)
    inputs = jnp.concatenate([tokens, new_token_states], axis=0)
    shard_pieces = (
        lax.all_gather(w_query, "ctx", axis=0, tiled=True),
        lax.all_gather(key_matrix, "ctx", axis=0, tiled=True),
        lax.all_gather(value_matrix, "ctx", axis=0, tiled=True),
    )
    query_all, key_all, value_all = tuple(
        (jnp.dot(inputs, weight, preferred_element_type=jnp.float32) for weight in shard_pieces)
    )
    query_all = query_all.astype(jnp.bfloat16)
    key_all = key_all.astype(jnp.bfloat16)
    value_all = value_all.astype(jnp.bfloat16)
    local_query = query_all[:local_rows]
    local_keys = key_all[:local_rows]
    local_values = value_all[:local_rows]
    dec_query = query_all[local_rows:]
    decode_key_rows = key_all[local_rows:]
    decode_value_rows = value_all[local_rows:]
    token_pos = initial_positions(block_map, device * local_rows, local_rows, block_rows)
    token_request = request_index(token_pos, request_ends)
    query_heads = local_query.reshape(local_rows, kv_heads, query_group_count, head_dim)

    def attend(running, shard_pieces, first_row):
        peak_run, total_run, mixed_run = running
        key_piece, value_piece = shard_pieces
        row_count = key_piece.shape[0]
        key_pos = initial_positions(block_map, first_row, row_count, block_rows)
        key_request = request_index(key_pos, request_ends)
        allowed = (key_request[None, :] == token_request[:, None]) & (
            key_pos[None, :] <= token_pos[:, None]
        )
        scores = (
            jnp.einsum(
                "tgjd,kgd->gjtk",
                query_heads,
                key_piece.reshape(row_count, kv_heads, head_dim),
                preferred_element_type=jnp.float32,
            )
            * score_scale
        )
        scores = jnp.where(allowed, scores, floor_value)
        peak_new = jnp.maximum(peak_run, jnp.max(scores, axis=3))
        weights = jnp.where(allowed, jnp.exp(scores - peak_new[..., None]), 0.0)
        rescale = jnp.exp(peak_run - peak_new)
        total_new = total_run * rescale + jnp.sum(weights, axis=3)
        mixed_new = mixed_run * rescale[..., None] + jnp.einsum(
            "gjtk,kgd->gjtd",
            weights.astype(jnp.bfloat16),
            value_piece.reshape(row_count, kv_heads, head_dim),
            preferred_element_type=jnp.float32,
        )
        return (peak_new, total_new, mixed_new)

    start_state = (
        jnp.full((kv_heads, query_group_count, local_rows), floor_value, jnp.float32),
        jnp.zeros((kv_heads, query_group_count, local_rows), jnp.float32),
        jnp.zeros((kv_heads, query_group_count, local_rows, head_dim), jnp.float32),
    )
    dec_heads = dec_query.reshape(request_count, kv_heads, query_group_count, head_dim)
    request_ids = jnp.arange(request_count, dtype=jnp.int32)
    cache_keys, cache_values = (
        lax.all_gather(local_keys, "ctx", axis=0, tiled=True),
        lax.all_gather(local_values, "ctx", axis=0, tiled=True),
    )
    total_rows = cache_keys.shape[0]
    shard_count = total_rows // local_rows
    limit = max(1, 1024 // local_rows)
    step_rows = local_rows * math.gcd(shard_count, 1 << limit.bit_length() - 1)

    def key_step(running, step_index):
        first_row = step_index * step_rows
        pieces = (
            lax.dynamic_slice_in_dim(cache_keys, first_row, step_rows, 0),
            lax.dynamic_slice_in_dim(cache_values, first_row, step_rows, 0),
        )
        return (attend(running, pieces, first_row), None)

    final_state, unused = lax.scan(
        key_step, start_state, jnp.arange(total_rows // step_rows, dtype=jnp.int32)
    )
    peak_run, total_run, mixed_run = final_state
    cache_pos = (
        block_map[:, None] * block_rows + jnp.arange(block_rows, dtype=jnp.int32)[None, :]
    ).reshape(total_rows)
    cache_request = request_index(cache_pos, request_ends)
    owned = (cache_request[None, :] == request_ids[:, None])[:, None, None, :]
    cache_peak, cache_total, cache_mixed = softmax_parts(
        dec_heads, cache_keys, cache_values, owned, kv_heads, head_dim, score_scale
    )
    attended = (
        (mixed_run / total_run[..., None]).transpose(2, 0, 1, 3).reshape(local_rows, query_width)
    )
    attended = attended.astype(jnp.bfloat16)
    own_keys = decode_key_rows.reshape(request_count, kv_heads, 1, head_dim).astype(jnp.float32)
    own_values = decode_value_rows.reshape(request_count, kv_heads, 1, head_dim).astype(jnp.float32)
    self_scores = jnp.sum(dec_heads.astype(jnp.float32) * own_keys, axis=3) * score_scale
    peak_all = jnp.maximum(cache_peak, self_scores)
    rescale = jnp.exp(cache_peak - peak_all)
    self_weights = jnp.exp(self_scores - peak_all)
    dec_total = cache_total * rescale + self_weights
    dec_mixed = (
        cache_mixed * rescale[..., None] + round_weights(self_weights)[..., None] * own_values
    )
    dec_attn = (
        (dec_mixed / dec_total[..., None]).reshape(request_count, query_width).astype(jnp.bfloat16)
    )
    attended_all = jnp.concatenate([attended, dec_attn], axis=0)
    head_block = lax.all_gather(w_out, "ctx", axis=1, tiled=True)
    column_block = lax.all_to_all(head_block, "tp", split_axis=1, concat_axis=0, tiled=True)
    summed_rows = jnp.dot(
        lax.all_gather(attended_all, "tp", axis=1, tiled=True),
        column_block,
        preferred_element_type=jnp.float32,
    )
    summed_rows = summed_rows.astype(jnp.bfloat16)
    return (summed_rows[:local_rows], summed_rows[local_rows:])

def solution(mesh):
    steps, tp = mesh.shape["ctx"], mesh.shape["tp"]

    def on_device(tokens, *rest):
        one_head = rest[2].shape[1] == HEAD_SIZE
        small = steps == 4 and tp == 8 and one_head and tokens.shape[0] * steps <= 1024
        if small:
            return on_device_small(steps, tp, tokens, *rest)
        return on_device_large(tokens, *rest)

    return jax.shard_map(
        on_device,
        mesh=mesh,
        in_specs=(
            P("ctx", None),
            P(),
            P("ctx", "tp"),
            P("ctx", "tp"),
            P("ctx", "tp"),
            P("tp", "ctx"),
            P(),
            P(),
        ),
        out_specs=(P("ctx", "tp"), P(None, "tp")),
        check_vma=False,
    )
```

```python
import functools
import math

import jax
import jax.numpy as jnp
from jax import lax
from jax.experimental import pallas as pl
from jax.experimental.pallas import tpu as pltpu
from jax.sharding import PartitionSpec as P

HEAD_SIZE = 128
FLOOR = -1e30
LAST = 1 << 30
ROW_TILE = 8
VMEM_BYTES = 48 * 1024 * 1024


def vmem():
    return pl.BlockSpec(memory_space=pltpu.VMEM)


def smem():
    return pl.BlockSpec(memory_space=pltpu.SMEM)


def place():
    t = lax.axis_index("tp")
    return lax.axis_index("ctx"), t // 2, t % 2


def project_kernel(rows, own, *refs):
    (mine, theirs), refs = ((refs[2], *refs[:2]), (refs[5], *refs[3:5])), refs[6:]
    (new, *weights), refs = refs[:4], refs[4:]
    held, new_held, *outs, inputs = refs
    count = new.shape[0]
    pad = new_held.shape[0]
    tail = 4 * rows
    _, _, k = place()
    inputs[:rows, :] = own[...]
    for number, pair in enumerate(zip(mine, theirs), 1):
        for core, block in zip((k, 1 - k), pair):
            first = number * rows + core * block.shape[0]
            inputs[pl.ds(pl.multiple_of(first, block.shape[0]), block.shape[0]), :] = block[...]
    inputs[tail:, :] = jnp.zeros_like(inputs[tail:, :])
    inputs[tail : tail + count, :] = new[...]
    x = inputs[...]
    column = 0
    for weight in (weights[0][...], jnp.concatenate([weights[1][...], weights[2][...]], axis=1)):
        part = jnp.dot(x, weight, preferred_element_type=jnp.float32)
        to = slice(column, column + weight.shape[1])
        held[:, to] = part[:rows]
        news = part[tail : tail + pad].astype(new_held.dtype)
        new_held[:, to] = news
        for step, out in enumerate(outs, 1):
            out[:rows, to] = part[step * rows : (step + 1) * rows].astype(out.dtype)
            out[rows:, to] = news
        column += weight.shape[1]


def add_kernel(own, new_own, first, second, both, held, new):
    rows = held.shape[0]

    def total(own, at):
        parts = [own[...].astype(jnp.float32)]
        parts += [ref[at, :].astype(jnp.float32) for ref in (first, second, both)]
        return ((parts[0] + parts[1]) + (parts[2] + parts[3])).astype(held.dtype)

    held[...] = total(own, slice(0, rows))
    new[...] = total(new_own, slice(rows, None))


def request_of(position, ends):
    found = jnp.zeros_like(position)
    for end in ends:
        found = found + jnp.where(position >= end, 1, 0)
    return found


def attend_kernel(sent, block_rows, count, scale, block_map, lengths, *refs):
    blocks, new, refs = (refs[0], *refs[3:0:-1]), refs[4], refs[5:]
    attended = refs[-1]
    rows, features = blocks[0].shape
    head = HEAD_SIZE
    q_width = features - 2 * head
    pad = new.shape[0]
    per_device = rows // block_rows
    tail = len(blocks) * block_rows
    c, z, _ = place()
    half = 1 - z % 2 if sent else z % 2

    def whole(number):
        at = slice(number * head, (number + 1) * head)
        return jnp.concatenate([block[:, at] for block in blocks], axis=0)

    def with_zeros(number):
        at = slice(number * head, (number + 1) * head)
        return jnp.concatenate([new[:, at], jnp.zeros((head - pad, head), new.dtype)], axis=0)

    def queries(number):
        at = slice(number * head, (number + 1) * head)
        taken = pl.ds(pl.multiple_of(half * block_rows, block_rows), block_rows)
        return jnp.concatenate([block[taken, at] for block in blocks], axis=0)

    key_at, value_at = q_width // head, q_width // head + 1
    keys, values = whole(key_at), whole(value_at)

    ends, total = [], 0
    for request in range(count):
        total = total + lengths[request]
        ends.append(total)

    def labels(shape, axis, held):
        index = lax.broadcasted_iota(jnp.int32, shape, axis)
        position = jnp.zeros(shape, jnp.int32)
        for number, block in enumerate(held):
            start = number * block_rows
            inside = (index >= start) & (index < start + block_rows)
            position = jnp.where(inside, block_map[block] * block_rows + index - start, position)
        return position, request_of(position, ends)

    devices = [per_device * (c ^ mask) for mask in range(len(blocks))]
    q_position, q_request = labels((tail, 1), 0, [first + half for first in devices])
    held = [first + number for first in devices for number in range(per_device)]
    k_position, k_request = labels((1, len(blocks) * rows), 1, held)
    allowed = (q_request == k_request) & (k_position <= q_position)

    def scores_of(query, keys, allowed):
        scores = lax.dot_general(
            query, keys, (((1,), (1,)), ((), ())), preferred_element_type=jnp.float32
        )
        return jnp.where(allowed, scores * scale, FLOOR)

    def mix(weights, values):
        return jnp.dot(weights.astype(jnp.bfloat16), values, preferred_element_type=jnp.float32)

    for number in range(q_width // head):
        at = slice(number * head, (number + 1) * head)
        scores = scores_of(queries(number), keys, allowed)
        weights = jnp.exp(scores - jnp.max(scores, axis=1, keepdims=True))
        denom = jnp.sum(weights, axis=1, keepdims=True)
        attended[:tail, at] = (mix(weights, values) / denom).astype(jnp.bfloat16)
    if not sent:
        attended[tail:, :] = refs[0][tail:, :]
        return

    new_rows = 2 * ROW_TILE
    new_request = lax.broadcasted_iota(jnp.int32, (new_rows, 1), 0)
    new_allowed = new_request == k_request
    own_allowed = new_request == lax.broadcasted_iota(jnp.int32, (1, head), 1)
    new_keys, new_values = with_zeros(key_at), with_zeros(value_at)
    for number in range(q_width // head):
        at = slice(number * head, (number + 1) * head)
        query = with_zeros(number)[:new_rows]
        scores = scores_of(query, keys, new_allowed)
        own_scores = scores_of(query, new_keys, own_allowed)
        peak = jnp.maximum(
            jnp.max(scores, axis=1, keepdims=True), jnp.max(own_scores, axis=1, keepdims=True)
        )
        weights, own_weights = jnp.exp(scores - peak), jnp.exp(own_scores - peak)
        denom = jnp.sum(weights, axis=1, keepdims=True)
        denom += jnp.sum(own_weights, axis=1, keepdims=True)
        mixed = (mix(weights, values) + mix(own_weights, new_values)) / denom
        attended[tail:, at] = mixed[:pad].astype(jnp.bfloat16)


def output_kernel(rows, *refs):
    heads, (w_own, *weights), outs = refs[:4], refs[4:8], refs[8:]
    _, _, k = place()
    width = outs[0].shape[1]
    w_mine = w_own[:, pl.ds(pl.multiple_of(k * width, width), width)]
    total = jnp.dot(heads[0][...], w_mine, preferred_element_type=jnp.float32)
    for ref, weight in zip(heads[1:], weights):
        total += jnp.dot(ref[...], weight[...], preferred_element_type=jnp.float32)
    total = total.astype(outs[0].dtype)
    for number, out in enumerate(outs):
        out[:rows, :] = total[number * rows : (number + 1) * rows]
        out[rows:, :] = total[len(outs) * rows :]


def relay_kernel(*refs):
    blocks, outs = refs[:4], refs[4:]
    c, z, _ = place()
    for slot, out in enumerate(outs):
        for mask, block in enumerate(blocks):

            @pl.when((c ^ z ^ slot) == mask)
            def _(out=out, block=block):
                out[...] = block[: out.shape[0], :]


def finish_kernel(*refs):
    parts, (prefill, decode) = refs[:4], refs[4:]
    _, z, _ = place()
    rows = prefill.shape[0] // 2
    for odd in range(2):
        total = parts[odd][...].astype(jnp.float32) + parts[odd + 2][...].astype(jnp.float32)
        total = total.astype(prefill.dtype)
        half = z % 2 if odd == 0 else 1 - z % 2
        prefill[pl.ds(pl.multiple_of(half * rows, rows), rows), :] = total[:rows]
        if odd == 0:
            decode[...] = total[rows : rows + decode.shape[0]]


def on_device_small(
    steps, tp, tokens, new_token_states, w_query, key_matrix, value_matrix, w_out, lengths, block_map
):
    bf16, f32 = jnp.bfloat16, jnp.float32
    rows = tokens.shape[0]
    half = rows // 2
    depth = w_query.shape[0]
    count = new_token_states.shape[0]
    pad = -(-count // ROW_TILE) * ROW_TILE
    q_width = w_query.shape[1]
    features = q_width + 2 * key_matrix.shape[1]
    width = w_out.shape[1] // 2
    all_rows = steps * rows + pad

    def to_core(value):
        return lax.ppermute(value, "tp", [(i, i ^ 1) for i in range(tp)])

    def to_chip(value, step):
        return lax.ppermute(value, "tp", [(i, i ^ (2 * step)) for i in range(tp)])

    def to_partners(values):
        return [
            lax.ppermute(value, "ctx", [(i, i ^ mask) for i in range(steps)])
            for mask, value in enumerate(values, 1)
        ]

    def call(kernel, name, inputs, shapes, scratch=(), spaces=None):
        return pl.pallas_call(
            kernel,
            out_shape=[jax.ShapeDtypeStruct(shape, kind) for shape, kind in shapes],
            in_specs=spaces or [vmem()] * len(inputs),
            out_specs=[vmem()] * len(shapes),
            scratch_shapes=list(scratch),
            compiler_params=pltpu.CompilerParams(vmem_limit_bytes=VMEM_BYTES),
            name=name,
        )(*inputs)

    c, _, k = place()
    sent = [
        lax.dynamic_slice(tokens, (k * half, (c ^ mask) * depth), (half, depth))
        for mask in range(1, steps)
    ]
    own = lax.dynamic_slice_in_dim(tokens, c * depth, depth, 1)
    new_columns = lax.dynamic_slice_in_dim(new_token_states, c * depth, depth, 1)
    mine = to_partners(sent)
    theirs = [to_core(value) for value in mine]

    w_mine = lax.dynamic_slice_in_dim(w_out, k * width, width, 1)
    w_theirs = lax.dynamic_slice_in_dim(w_out, (1 - k) * width, width, 1)
    w_next = to_chip(w_mine, 1)
    new_columns, w_next = lax.optimization_barrier((new_columns, w_next))

    part = (rows + pad, features)
    own_part, new_part, *parts = call(
        functools.partial(project_kernel, rows),
        "project",
        (own, *mine[1:], mine[0], *theirs[1:], theirs[0], new_columns, w_query, key_matrix, value_matrix),
        [((rows, features), f32), ((pad, features), bf16)] + [(part, bf16)] * (steps - 1),
        [pltpu.VMEM((-(-all_rows // 16) * 16, depth), bf16)],
    )

    w_later, _ = lax.optimization_barrier((w_theirs, new_part))
    w_next_other = lax.ppermute(w_later, "tp", [(i, i ^ 3) for i in range(tp)])

    held, new = call(
        add_kernel,
        "add_parts",
        (own_part, new_part, *to_partners(parts)),
        [((rows, features), bf16), ((pad, features), bf16)],
    )

    first, second, both = to_partners([held] * (steps - 1))
    new, w_next_other = lax.optimization_barrier((new, w_next_other))
    block_rows = steps * rows // block_map.shape[0]

    def attend(sent, *extra):
        (attended,) = call(
            functools.partial(
                attend_kernel, sent, block_rows, count, 1.0 / math.sqrt(HEAD_SIZE)
            ),
            "attend_sent" if sent else "attend_kept",
            (block_map, lengths, held, both, second, first, new, *extra),
            [((steps * block_rows + pad, q_width), bf16)],
            spaces=[smem()] * 2 + [vmem()] * (steps + 1 + len(extra)),
        )
        return attended

    sent = attend(True)
    got = to_chip(sent, 1)
    kept = attend(False, sent)
    w_last, _ = lax.optimization_barrier((w_theirs, held))
    w_other = to_core(w_last)

    block = (block_rows + pad, width)
    outs = call(
        functools.partial(output_kernel, block_rows),
        "project_out",
        (kept, to_core(kept), got, to_core(got), w_out, w_other, w_next, w_next_other),
        [(block, bf16)] * steps,
    )

    slots = call(
        relay_kernel,
        "relay",
        [outs[0]] + to_partners(outs[1:]),
        [(block if i % 2 == 0 else (block_rows, width), bf16) for i in range(steps)],
    )
    slots = [slots[0]] + [to_chip(slot, step) for step, slot in enumerate(slots[1:], 1)]
    return tuple(
        call(finish_kernel, "finish", slots, [((rows, width), bf16), ((count, width), bf16)])
    )


floor_value = -1e30


def initial_positions(block_map, first_row, row_count, block_rows):
    row_ids = first_row + jnp.arange(row_count, dtype=jnp.int32)
    block_ids = row_ids // block_rows
    table_ids = jnp.arange(block_map.shape[0], dtype=jnp.int32)
    mapped = jnp.sum(
        jnp.where(block_ids[:, None] == table_ids[None, :], block_map[None, :], 0), axis=1
    )
    return mapped * block_rows + row_ids % block_rows


def request_index(positions, request_ends):
    return jnp.sum((positions[:, None] >= request_ends[None, :]).astype(jnp.int32), axis=1)


def round_weights(weights):
    rounded = weights.astype(jnp.bfloat16)
    rounded = lax.optimization_barrier(rounded)
    return rounded.astype(jnp.float32)


def softmax_parts(
    dec_heads, projected_key_rows, projected_value_rows, owned, kv_heads, head_dim, score_scale
):
    row_count = projected_key_rows.shape[0]
    scores = (
        jnp.einsum(
            "rgjd,tgd->rgjt",
            dec_heads,
            projected_key_rows.reshape(row_count, kv_heads, head_dim),
            preferred_element_type=jnp.float32,
        )
        * score_scale
    )
    scores = jnp.where(owned, scores, floor_value)
    part_peak = jnp.max(scores, axis=3)
    weights = jnp.where(owned, jnp.exp(scores - part_peak[..., None]), 0.0)
    part_total = jnp.sum(weights, axis=3)
    part_mixed = jnp.einsum(
        "rgjt,tgd->rgjd",
        weights.astype(jnp.bfloat16),
        projected_value_rows.reshape(row_count, kv_heads, head_dim),
        preferred_element_type=jnp.float32,
    )
    return (part_peak, part_total, part_mixed)


def on_device_large(
    tokens, new_token_states, w_query, key_matrix, value_matrix, w_out, lengths, block_map
):
    local_rows = tokens.shape[0]
    block_rows = local_rows // 2
    request_count = new_token_states.shape[0]
    head_dim = HEAD_SIZE
    query_width = w_query.shape[1]
    kv_width = key_matrix.shape[1]
    kv_heads = kv_width // head_dim
    query_group_count = query_width // kv_width
    score_scale = 1.0 / math.sqrt(head_dim)
    device = lax.axis_index("ctx")
    request_ends = jnp.cumsum(lengths)
    inputs = jnp.concatenate([tokens, new_token_states], axis=0)
    shard_pieces = (
        lax.all_gather(w_query, "ctx", axis=0, tiled=True),
        lax.all_gather(key_matrix, "ctx", axis=0, tiled=True),
        lax.all_gather(value_matrix, "ctx", axis=0, tiled=True),
    )
    query_all, key_all, value_all = tuple(
        (jnp.dot(inputs, weight, preferred_element_type=jnp.float32) for weight in shard_pieces)
    )
    query_all = query_all.astype(jnp.bfloat16)
    key_all = key_all.astype(jnp.bfloat16)
    value_all = value_all.astype(jnp.bfloat16)
    local_query = query_all[:local_rows]
    local_keys = key_all[:local_rows]
    local_values = value_all[:local_rows]
    dec_query = query_all[local_rows:]
    decode_key_rows = key_all[local_rows:]
    decode_value_rows = value_all[local_rows:]
    token_pos = initial_positions(block_map, device * local_rows, local_rows, block_rows)
    token_request = request_index(token_pos, request_ends)
    query_heads = local_query.reshape(local_rows, kv_heads, query_group_count, head_dim)

    def attend(running, shard_pieces, first_row):
        peak_run, total_run, mixed_run = running
        key_piece, value_piece = shard_pieces
        row_count = key_piece.shape[0]
        key_pos = initial_positions(block_map, first_row, row_count, block_rows)
        key_request = request_index(key_pos, request_ends)
        allowed = (key_request[None, :] == token_request[:, None]) & (
            key_pos[None, :] <= token_pos[:, None]
        )
        scores = (
            jnp.einsum(
                "tgjd,kgd->gjtk",
                query_heads,
                key_piece.reshape(row_count, kv_heads, head_dim),
                preferred_element_type=jnp.float32,
            )
            * score_scale
        )
        scores = jnp.where(allowed, scores, floor_value)
        peak_new = jnp.maximum(peak_run, jnp.max(scores, axis=3))
        weights = jnp.where(allowed, jnp.exp(scores - peak_new[..., None]), 0.0)
        rescale = jnp.exp(peak_run - peak_new)
        total_new = total_run * rescale + jnp.sum(weights, axis=3)
        mixed_new = mixed_run * rescale[..., None] + jnp.einsum(
            "gjtk,kgd->gjtd",
            weights.astype(jnp.bfloat16),
            value_piece.reshape(row_count, kv_heads, head_dim),
            preferred_element_type=jnp.float32,
        )
        return (peak_new, total_new, mixed_new)

    start_state = (
        jnp.full((kv_heads, query_group_count, local_rows), floor_value, jnp.float32),
        jnp.zeros((kv_heads, query_group_count, local_rows), jnp.float32),
        jnp.zeros((kv_heads, query_group_count, local_rows, head_dim), jnp.float32),
    )
    dec_heads = dec_query.reshape(request_count, kv_heads, query_group_count, head_dim)
    request_ids = jnp.arange(request_count, dtype=jnp.int32)
    cache_keys, cache_values = (
        lax.all_gather(local_keys, "ctx", axis=0, tiled=True),
        lax.all_gather(local_values, "ctx", axis=0, tiled=True),
    )
    total_rows = cache_keys.shape[0]
    shard_count = total_rows // local_rows
    limit = max(1, 1024 // local_rows)
    step_rows = local_rows * math.gcd(shard_count, 1 << limit.bit_length() - 1)

    def key_step(running, step_index):
        first_row = step_index * step_rows
        pieces = (
            lax.dynamic_slice_in_dim(cache_keys, first_row, step_rows, 0),
            lax.dynamic_slice_in_dim(cache_values, first_row, step_rows, 0),
        )
        return (attend(running, pieces, first_row), None)

    final_state, unused = lax.scan(
        key_step, start_state, jnp.arange(total_rows // step_rows, dtype=jnp.int32)
    )
    peak_run, total_run, mixed_run = final_state
    cache_pos = (
        block_map[:, None] * block_rows + jnp.arange(block_rows, dtype=jnp.int32)[None, :]
    ).reshape(total_rows)
    cache_request = request_index(cache_pos, request_ends)
    owned = (cache_request[None, :] == request_ids[:, None])[:, None, None, :]
    cache_peak, cache_total, cache_mixed = softmax_parts(
        dec_heads, cache_keys, cache_values, owned, kv_heads, head_dim, score_scale
    )
    attended = (
        (mixed_run / total_run[..., None]).transpose(2, 0, 1, 3).reshape(local_rows, query_width)
    )
    attended = attended.astype(jnp.bfloat16)
    own_keys = decode_key_rows.reshape(request_count, kv_heads, 1, head_dim).astype(jnp.float32)
    own_values = decode_value_rows.reshape(request_count, kv_heads, 1, head_dim).astype(jnp.float32)
    self_scores = jnp.sum(dec_heads.astype(jnp.float32) * own_keys, axis=3) * score_scale
    peak_all = jnp.maximum(cache_peak, self_scores)
    rescale = jnp.exp(cache_peak - peak_all)
    self_weights = jnp.exp(self_scores - peak_all)
    dec_total = cache_total * rescale + self_weights
    dec_mixed = (
        cache_mixed * rescale[..., None] + round_weights(self_weights)[..., None] * own_values
    )
    dec_attn = (
        (dec_mixed / dec_total[..., None]).reshape(request_count, query_width).astype(jnp.bfloat16)
    )
    attended_all = jnp.concatenate([attended, dec_attn], axis=0)
    head_block = lax.all_gather(w_out, "ctx", axis=1, tiled=True)
    column_block = lax.all_to_all(head_block, "tp", split_axis=1, concat_axis=0, tiled=True)
    summed_rows = jnp.dot(
        lax.all_gather(attended_all, "tp", axis=1, tiled=True),
        column_block,
        preferred_element_type=jnp.float32,
    )
    summed_rows = summed_rows.astype(jnp.bfloat16)
    return (summed_rows[:local_rows], summed_rows[local_rows:])

def solution(mesh):
    steps, tp = mesh.shape["ctx"], mesh.shape["tp"]

    def on_device(tokens, *rest):
        one_head = rest[2].shape[1] == HEAD_SIZE
        two_blocks = rest[-1].shape[0] == 2 * steps
        few = tokens.shape[0] * steps <= 1024
        small = steps == 4 and tp == 8 and one_head and two_blocks and few
        if small:
            return on_device_small(steps, tp, tokens, *rest)
        return on_device_large(tokens, *rest)

    return jax.shard_map(
        on_device,
        mesh=mesh,
        in_specs=(
            P("ctx", None),
            P(),
            P("ctx", "tp"),
            P("ctx", "tp"),
            P("ctx", "tp"),
            P("tp", "ctx"),
            P(),
            P(),
        ),
        out_specs=(P("ctx", "tp"), P(None, "tp")),
        check_vma=False,
    )
```

```python
import functools
import math

import jax
import jax.numpy as jnp
from jax import lax
from jax.experimental import pallas as pl
from jax.experimental.pallas import tpu as pltpu
from jax.sharding import PartitionSpec as P

HEAD_SIZE = 128
FLOOR = -1e30
LAST = 1 << 30
ROW_TILE = 8
VMEM_BYTES = 48 * 1024 * 1024
TOKENS, SUMS, KEYS, OUTPUTS, HEADS = (1, 2, 0), (0, 1, 2), (2, 1, 0), (0, 1, 2), (2, 1, 0)


def vmem():
    return pl.BlockSpec(memory_space=pltpu.VMEM)


def smem():
    return pl.BlockSpec(memory_space=pltpu.SMEM)


def in_order(order, values):
    return [values[i] for i in order]


def put_back(order, values):
    return [values[order.index(i)] for i in range(len(order))]


def place():
    t = lax.axis_index("tp")
    return lax.axis_index("ctx"), t // 2, t % 2


def project_kernel(rows, own, *refs):
    mine, theirs, refs = put_back(TOKENS, refs[:3]), put_back(TOKENS, refs[3:6]), refs[6:]
    (new, *weights), refs = refs[:4], refs[4:]
    held, new_held, *outs, inputs = refs
    count = new.shape[0]
    pad = new_held.shape[0]
    tail = 4 * rows
    _, _, k = place()
    inputs[:rows, :] = own[...]
    for number, pair in enumerate(zip(mine, theirs), 1):
        for core, block in zip((k, 1 - k), pair):
            first = number * rows + core * block.shape[0]
            inputs[pl.ds(pl.multiple_of(first, block.shape[0]), block.shape[0]), :] = block[...]
    inputs[tail:, :] = jnp.zeros_like(inputs[tail:, :])
    inputs[tail : tail + count, :] = new[...]
    x = inputs[...]
    column = 0
    for weight in (weights[0][...], jnp.concatenate([weights[1][...], weights[2][...]], axis=1)):
        part = jnp.dot(x, weight, preferred_element_type=jnp.float32)
        to = slice(column, column + weight.shape[1])
        held[:, to] = part[:rows]
        news = part[tail : tail + pad].astype(new_held.dtype)
        new_held[:, to] = news
        for step, out in enumerate(outs, 1):
            out[:rows, to] = part[step * rows : (step + 1) * rows].astype(out.dtype)
            out[rows:, to] = news
        column += weight.shape[1]


def add_kernel(own, new_own, *refs):
    (first, second, both), (held, new) = put_back(SUMS, refs[:3]), refs[3:]
    rows = held.shape[0]

    def total(own, at):
        parts = [own[...].astype(jnp.float32)]
        parts += [ref[at, :].astype(jnp.float32) for ref in (first, second, both)]
        return ((parts[0] + parts[1]) + (parts[2] + parts[3])).astype(held.dtype)

    held[...] = total(own, slice(0, rows))
    new[...] = total(new_own, slice(rows, None))


def request_of(position, ends):
    found = jnp.zeros_like(position)
    for end in ends:
        found = found + jnp.where(position >= end, 1, 0)
    return found


def mask_kernel(block_rows, block_map, lengths, rows_mask, new_mask):
    ends, total = [], 0
    for request in range(lengths.shape[0]):
        total = total + lengths[request]
        ends.append(total)
    c, _, _ = place()
    count = block_map.shape[0]
    per_device = 2
    devices = [per_device * (c ^ mask) for mask in range(count // per_device)]

    def labels(shape, axis, held):
        index = lax.broadcasted_iota(jnp.int32, shape, axis)
        position = jnp.zeros(shape, jnp.int32)
        for number, block in enumerate(held):
            start = number * block_rows
            inside = (index >= start) & (index < start + block_rows)
            position = jnp.where(inside, block_map[block] * block_rows + index - start, position)
        return position, request_of(position, ends)

    keys = new_mask.shape[1]
    halves = [first + number for number in range(per_device) for first in devices]
    q_position, q_request = labels((keys, 1), 0, halves)
    held = [first + number for first in devices for number in range(per_device)]
    k_position, k_request = labels((1, keys), 1, held)
    allowed = (q_request == k_request) & (k_position <= q_position)
    rows_mask[...] = jnp.where(allowed, 0.0, FLOOR)
    request = lax.broadcasted_iota(jnp.int32, (new_mask.shape[0], 1), 0)
    new_mask[...] = jnp.where(request == k_request, 0.0, FLOOR)


def attend_kernel(sent, block_rows, scale, *refs):
    blocks, (new, rows_mask, new_mask), refs = [refs[0], *put_back(KEYS, refs[1:4])], refs[4:7], refs[7:]
    attended = refs[-1]
    features = blocks[0].shape[1]
    head = HEAD_SIZE
    q_width = features - 2 * head
    pad = new.shape[0]
    tail = len(blocks) * block_rows
    _, z, _ = place()
    half = 1 - z % 2 if sent else z % 2
    mask = rows_mask[pl.ds(pl.multiple_of(half * tail, tail), tail), :]
    if sent:
        new_rows = new_mask.shape[0]
        mask = jnp.concatenate([mask, new_mask[...]], axis=0)
        zeros = jnp.zeros((new_rows - pad, features), new.dtype)
        news = jnp.concatenate([new[...], zeros], axis=0)

    def columns(number):
        return slice(number * head, (number + 1) * head)

    def whole(number):
        return jnp.concatenate([block[:, columns(number)] for block in blocks], axis=0)

    def queries(number):
        taken = pl.ds(pl.multiple_of(half * block_rows, block_rows), block_rows)
        parts = [block[taken, columns(number)] for block in blocks]
        return jnp.concatenate(parts + ([news[:, columns(number)]] if sent else []), axis=0)

    key_at, value_at = q_width // head, q_width // head + 1
    keys, values = whole(key_at), whole(value_at)
    for number in range(q_width // head):
        at = columns(number)
        scores = lax.dot_general(
            queries(number), keys, (((1,), (1,)), ((), ())), preferred_element_type=jnp.float32
        )
        scores = scores * scale + mask
        peak = jnp.max(scores, axis=1, keepdims=True)
        if sent:
            own = news[:, at].astype(jnp.float32) * news[:, columns(key_at)].astype(jnp.float32)
            own = jnp.sum(own, axis=1, keepdims=True) * scale
            new_peak = jnp.maximum(peak[tail:], own)
            peak = jnp.concatenate([peak[:tail], new_peak], axis=0)
        weights = jnp.exp(scores - peak)
        denom = jnp.sum(weights, axis=1, keepdims=True)
        mixed = jnp.dot(weights.astype(jnp.bfloat16), values, preferred_element_type=jnp.float32)
        attended[:tail, at] = (mixed[:tail] / denom[:tail]).astype(jnp.bfloat16)
        if sent:
            weight = jnp.exp(own - new_peak)
            rounded = weight.astype(jnp.bfloat16).astype(jnp.float32)
            new_mixed = mixed[tail:] + rounded * news[:, columns(value_at)].astype(jnp.float32)
            new_mixed = new_mixed / (denom[tail:] + weight)
            attended[tail:, at] = new_mixed[:pad].astype(jnp.bfloat16)
    if not sent:
        attended[tail:, :] = refs[0][tail:, :]


def output_kernel(rows, *refs):
    heads, (w_own, *weights), outs = refs[:4], refs[4:8], refs[8:]
    _, _, k = place()
    width = outs[0].shape[1]
    w_mine = w_own[:, pl.ds(pl.multiple_of(k * width, width), width)]
    total = jnp.dot(heads[0][...], w_mine, preferred_element_type=jnp.float32)
    for ref, weight in zip(heads[1:], weights):
        total += jnp.dot(ref[...], weight[...], preferred_element_type=jnp.float32)
    total = total.astype(outs[0].dtype)
    for number, out in enumerate(outs):
        out[:rows, :] = total[number * rows : (number + 1) * rows]
        out[rows:, :] = total[len(outs) * rows :]


def relay_kernel(*refs):
    blocks, outs = [refs[0], *put_back(OUTPUTS, refs[1:4])], refs[4:]
    c, z, _ = place()
    for slot, out in enumerate(outs):
        for mask, block in enumerate(blocks):

            @pl.when((c ^ z ^ slot) == mask)
            def _(out=out, block=block):
                out[...] = block[: out.shape[0], :]


def finish_kernel(*refs):
    parts, (prefill, decode) = [refs[0], *put_back(HEADS, refs[1:4])], refs[4:]
    _, z, _ = place()
    rows = prefill.shape[0] // 2
    for odd in range(2):
        total = parts[odd][...].astype(jnp.float32) + parts[odd + 2][...].astype(jnp.float32)
        total = total.astype(prefill.dtype)
        half = z % 2 if odd == 0 else 1 - z % 2
        prefill[pl.ds(pl.multiple_of(half * rows, rows), rows), :] = total[:rows]
        if odd == 0:
            decode[...] = total[rows : rows + decode.shape[0]]


def on_device_small(
    steps, tp, tokens, new_token_states, w_query, key_matrix, value_matrix, w_out, lengths, block_map
):
    bf16, f32 = jnp.bfloat16, jnp.float32
    rows = tokens.shape[0]
    half = rows // 2
    depth = w_query.shape[0]
    count = new_token_states.shape[0]
    pad = -(-count // ROW_TILE) * ROW_TILE
    q_width = w_query.shape[1]
    features = q_width + 2 * key_matrix.shape[1]
    width = w_out.shape[1] // 2
    all_rows = steps * rows + pad

    def to_core(value):
        return lax.ppermute(value, "tp", [(i, i ^ 1) for i in range(tp)])

    def to_chip(value, step):
        return lax.ppermute(value, "tp", [(i, i ^ (2 * step)) for i in range(tp)])

    def to_partners(values):
        return [
            lax.ppermute(value, "ctx", [(i, i ^ mask) for i in range(steps)])
            for mask, value in enumerate(values, 1)
        ]

    def call(kernel, name, inputs, shapes, scratch=(), spaces=None):
        return pl.pallas_call(
            kernel,
            out_shape=[jax.ShapeDtypeStruct(shape, kind) for shape, kind in shapes],
            in_specs=spaces or [vmem()] * len(inputs),
            out_specs=[vmem()] * len(shapes),
            scratch_shapes=list(scratch),
            compiler_params=pltpu.CompilerParams(vmem_limit_bytes=VMEM_BYTES),
            name=name,
        )(*inputs)

    c, _, k = place()
    sent = [
        lax.dynamic_slice(tokens, (k * half, (c ^ mask) * depth), (half, depth))
        for mask in range(1, steps)
    ]
    own = lax.dynamic_slice_in_dim(tokens, c * depth, depth, 1)
    new_columns = lax.dynamic_slice_in_dim(new_token_states, c * depth, depth, 1)
    mine = to_partners(sent)
    theirs = [to_core(value) for value in mine]

    w_mine = lax.dynamic_slice_in_dim(w_out, k * width, width, 1)
    w_theirs = lax.dynamic_slice_in_dim(w_out, (1 - k) * width, width, 1)
    w_next = to_chip(w_mine, 1)
    new_columns, w_next = lax.optimization_barrier((new_columns, w_next))

    part = (rows + pad, features)
    own_part, new_part, *parts = call(
        functools.partial(project_kernel, rows),
        "project",
        (
            own,
            *in_order(TOKENS, mine),
            *in_order(TOKENS, theirs),
            new_columns,
            w_query,
            key_matrix,
            value_matrix,
        ),
        [((rows, features), f32), ((pad, features), bf16)] + [(part, bf16)] * (steps - 1),
        [pltpu.VMEM((-(-all_rows // 16) * 16, depth), bf16)],
    )

    w_later, _ = lax.optimization_barrier((w_theirs, new_part))
    w_next_other = lax.ppermute(w_later, "tp", [(i, i ^ 3) for i in range(tp)])

    held, new = call(
        add_kernel,
        "add_parts",
        (own_part, new_part, *in_order(SUMS, to_partners(parts))),
        [((rows, features), bf16), ((pad, features), bf16)],
    )

    gathered = [held, *in_order(KEYS, to_partners([held] * (steps - 1)))]
    new, w_next_other = lax.optimization_barrier((new, w_next_other))
    block_rows = steps * rows // block_map.shape[0]

    keys = steps * rows
    masks = call(
        functools.partial(mask_kernel, block_rows),
        "mask",
        (block_map, lengths),
        [((keys, keys), f32), ((2 * ROW_TILE, keys), f32)],
        spaces=[smem()] * 2,
    )

    def attend(sent, *extra):
        (attended,) = call(
            functools.partial(attend_kernel, sent, block_rows, 1.0 / math.sqrt(HEAD_SIZE)),
            "attend_sent" if sent else "attend_kept",
            (*gathered, new, *masks, *extra),
            [((keys // 2 + pad, q_width), bf16)],
        )
        return attended

    sent = attend(True)
    got = to_chip(sent, 1)
    kept = attend(False, sent)
    w_last, _ = lax.optimization_barrier((w_theirs, held))
    w_other = to_core(w_last)

    block = (block_rows + pad, width)
    outs = call(
        functools.partial(output_kernel, block_rows),
        "project_out",
        (kept, to_core(kept), got, to_core(got), w_out, w_other, w_next, w_next_other),
        [(block, bf16)] * steps,
    )

    slots = call(
        relay_kernel,
        "relay",
        [outs[0], *in_order(OUTPUTS, to_partners(outs[1:]))],
        [(block, bf16)] * steps,
    )
    arrived = [to_chip(slot, step) for step, slot in enumerate(slots[1:], 1)]
    slots = [slots[0], *in_order(HEADS, arrived)]
    return tuple(
        call(finish_kernel, "finish", slots, [((rows, width), bf16), ((count, width), bf16)])
    )


floor_value = -1e30


def initial_positions(block_map, first_row, row_count, block_rows):
    row_ids = first_row + jnp.arange(row_count, dtype=jnp.int32)
    block_ids = row_ids // block_rows
    table_ids = jnp.arange(block_map.shape[0], dtype=jnp.int32)
    mapped = jnp.sum(
        jnp.where(block_ids[:, None] == table_ids[None, :], block_map[None, :], 0), axis=1
    )
    return mapped * block_rows + row_ids % block_rows


def request_index(positions, request_ends):
    return jnp.sum((positions[:, None] >= request_ends[None, :]).astype(jnp.int32), axis=1)


def round_weights(weights):
    rounded = weights.astype(jnp.bfloat16)
    rounded = lax.optimization_barrier(rounded)
    return rounded.astype(jnp.float32)


def softmax_parts(
    dec_heads, projected_key_rows, projected_value_rows, owned, kv_heads, head_dim, score_scale
):
    row_count = projected_key_rows.shape[0]
    scores = (
        jnp.einsum(
            "rgjd,tgd->rgjt",
            dec_heads,
            projected_key_rows.reshape(row_count, kv_heads, head_dim),
            preferred_element_type=jnp.float32,
        )
        * score_scale
    )
    scores = jnp.where(owned, scores, floor_value)
    part_peak = jnp.max(scores, axis=3)
    weights = jnp.where(owned, jnp.exp(scores - part_peak[..., None]), 0.0)
    part_total = jnp.sum(weights, axis=3)
    part_mixed = jnp.einsum(
        "rgjt,tgd->rgjd",
        weights.astype(jnp.bfloat16),
        projected_value_rows.reshape(row_count, kv_heads, head_dim),
        preferred_element_type=jnp.float32,
    )
    return (part_peak, part_total, part_mixed)


def on_device_large(
    tokens, new_token_states, w_query, key_matrix, value_matrix, w_out, lengths, block_map
):
    local_rows = tokens.shape[0]
    block_rows = local_rows // 2
    request_count = new_token_states.shape[0]
    head_dim = HEAD_SIZE
    query_width = w_query.shape[1]
    kv_width = key_matrix.shape[1]
    kv_heads = kv_width // head_dim
    query_group_count = query_width // kv_width
    score_scale = 1.0 / math.sqrt(head_dim)
    device = lax.axis_index("ctx")
    request_ends = jnp.cumsum(lengths)
    inputs = jnp.concatenate([tokens, new_token_states], axis=0)
    shard_pieces = (
        lax.all_gather(w_query, "ctx", axis=0, tiled=True),
        lax.all_gather(key_matrix, "ctx", axis=0, tiled=True),
        lax.all_gather(value_matrix, "ctx", axis=0, tiled=True),
    )
    query_all, key_all, value_all = tuple(
        (jnp.dot(inputs, weight, preferred_element_type=jnp.float32) for weight in shard_pieces)
    )
    query_all = query_all.astype(jnp.bfloat16)
    key_all = key_all.astype(jnp.bfloat16)
    value_all = value_all.astype(jnp.bfloat16)
    local_query = query_all[:local_rows]
    local_keys = key_all[:local_rows]
    local_values = value_all[:local_rows]
    dec_query = query_all[local_rows:]
    decode_key_rows = key_all[local_rows:]
    decode_value_rows = value_all[local_rows:]
    token_pos = initial_positions(block_map, device * local_rows, local_rows, block_rows)
    token_request = request_index(token_pos, request_ends)
    query_heads = local_query.reshape(local_rows, kv_heads, query_group_count, head_dim)

    def attend(running, shard_pieces, first_row):
        peak_run, total_run, mixed_run = running
        key_piece, value_piece = shard_pieces
        row_count = key_piece.shape[0]
        key_pos = initial_positions(block_map, first_row, row_count, block_rows)
        key_request = request_index(key_pos, request_ends)
        allowed = (key_request[None, :] == token_request[:, None]) & (
            key_pos[None, :] <= token_pos[:, None]
        )
        scores = (
            jnp.einsum(
                "tgjd,kgd->gjtk",
                query_heads,
                key_piece.reshape(row_count, kv_heads, head_dim),
                preferred_element_type=jnp.float32,
            )
            * score_scale
        )
        scores = jnp.where(allowed, scores, floor_value)
        peak_new = jnp.maximum(peak_run, jnp.max(scores, axis=3))
        weights = jnp.where(allowed, jnp.exp(scores - peak_new[..., None]), 0.0)
        rescale = jnp.exp(peak_run - peak_new)
        total_new = total_run * rescale + jnp.sum(weights, axis=3)
        mixed_new = mixed_run * rescale[..., None] + jnp.einsum(
            "gjtk,kgd->gjtd",
            weights.astype(jnp.bfloat16),
            value_piece.reshape(row_count, kv_heads, head_dim),
            preferred_element_type=jnp.float32,
        )
        return (peak_new, total_new, mixed_new)

    start_state = (
        jnp.full((kv_heads, query_group_count, local_rows), floor_value, jnp.float32),
        jnp.zeros((kv_heads, query_group_count, local_rows), jnp.float32),
        jnp.zeros((kv_heads, query_group_count, local_rows, head_dim), jnp.float32),
    )
    dec_heads = dec_query.reshape(request_count, kv_heads, query_group_count, head_dim)
    request_ids = jnp.arange(request_count, dtype=jnp.int32)
    cache_keys, cache_values = (
        lax.all_gather(local_keys, "ctx", axis=0, tiled=True),
        lax.all_gather(local_values, "ctx", axis=0, tiled=True),
    )
    total_rows = cache_keys.shape[0]
    shard_count = total_rows // local_rows
    limit = max(1, 1024 // local_rows)
    step_rows = local_rows * math.gcd(shard_count, 1 << limit.bit_length() - 1)

    def key_step(running, step_index):
        first_row = step_index * step_rows
        pieces = (
            lax.dynamic_slice_in_dim(cache_keys, first_row, step_rows, 0),
            lax.dynamic_slice_in_dim(cache_values, first_row, step_rows, 0),
        )
        return (attend(running, pieces, first_row), None)

    final_state, unused = lax.scan(
        key_step, start_state, jnp.arange(total_rows // step_rows, dtype=jnp.int32)
    )
    peak_run, total_run, mixed_run = final_state
    cache_pos = (
        block_map[:, None] * block_rows + jnp.arange(block_rows, dtype=jnp.int32)[None, :]
    ).reshape(total_rows)
    cache_request = request_index(cache_pos, request_ends)
    owned = (cache_request[None, :] == request_ids[:, None])[:, None, None, :]
    cache_peak, cache_total, cache_mixed = softmax_parts(
        dec_heads, cache_keys, cache_values, owned, kv_heads, head_dim, score_scale
    )
    attended = (
        (mixed_run / total_run[..., None]).transpose(2, 0, 1, 3).reshape(local_rows, query_width)
    )
    attended = attended.astype(jnp.bfloat16)
    own_keys = decode_key_rows.reshape(request_count, kv_heads, 1, head_dim).astype(jnp.float32)
    own_values = decode_value_rows.reshape(request_count, kv_heads, 1, head_dim).astype(jnp.float32)
    self_scores = jnp.sum(dec_heads.astype(jnp.float32) * own_keys, axis=3) * score_scale
    peak_all = jnp.maximum(cache_peak, self_scores)
    rescale = jnp.exp(cache_peak - peak_all)
    self_weights = jnp.exp(self_scores - peak_all)
    dec_total = cache_total * rescale + self_weights
    dec_mixed = (
        cache_mixed * rescale[..., None] + round_weights(self_weights)[..., None] * own_values
    )
    dec_attn = (
        (dec_mixed / dec_total[..., None]).reshape(request_count, query_width).astype(jnp.bfloat16)
    )
    attended_all = jnp.concatenate([attended, dec_attn], axis=0)
    head_block = lax.all_gather(w_out, "ctx", axis=1, tiled=True)
    column_block = lax.all_to_all(head_block, "tp", split_axis=1, concat_axis=0, tiled=True)
    summed_rows = jnp.dot(
        lax.all_gather(attended_all, "tp", axis=1, tiled=True),
        column_block,
        preferred_element_type=jnp.float32,
    )
    summed_rows = summed_rows.astype(jnp.bfloat16)
    return (summed_rows[:local_rows], summed_rows[local_rows:])

def solution(mesh):
    steps, tp = mesh.shape["ctx"], mesh.shape["tp"]

    def on_device(tokens, *rest):
        one_head = rest[2].shape[1] == HEAD_SIZE
        two_blocks = rest[-1].shape[0] == 2 * steps
        few = tokens.shape[0] * steps <= 1024
        small = steps == 4 and tp == 8 and one_head and two_blocks and few
        if small:
            return on_device_small(steps, tp, tokens, *rest)
        return on_device_large(tokens, *rest)

    return jax.shard_map(
        on_device,
        mesh=mesh,
        in_specs=(
            P("ctx", None),
            P(),
            P("ctx", "tp"),
            P("ctx", "tp"),
            P("ctx", "tp"),
            P("tp", "ctx"),
            P(),
            P(),
        ),
        out_specs=(P("ctx", "tp"), P(None, "tp")),
        check_vma=False,
    )
```

```python
import functools
import math

import jax
import jax.numpy as jnp
from jax import lax
from jax.experimental import pallas as pl
from jax.experimental.pallas import tpu as pltpu
from jax.sharding import PartitionSpec as P

HEAD_SIZE = 128
FLOOR = -1e30
LAST = 1 << 30
ROW_TILE = 8
VMEM_BYTES = 48 * 1024 * 1024
KEYS, OUTPUTS, HEADS = (2, 1, 0), (0, 1, 2), (2, 1, 0)


def vmem():
    return pl.BlockSpec(memory_space=pltpu.VMEM)


def smem():
    return pl.BlockSpec(memory_space=pltpu.SMEM)


def in_order(order, values):
    return [values[i] for i in order]


def put_back(order, values):
    return [values[order.index(i)] for i in range(len(order))]


def place():
    t = lax.axis_index("tp")
    return lax.axis_index("ctx"), t // 2, t % 2


def fill_rows(inputs, number, mine, theirs):
    _, _, k = place()
    rows = mine.shape[0]
    for core, block in ((k, mine), (1 - k, theirs)):
        first = 2 * rows * number + core * rows
        inputs[pl.ds(pl.multiple_of(first, rows), rows), :] = block[...]


def fill_new(inputs, new):
    count = new.shape[0]
    tail = inputs.shape[0] - 2 * ROW_TILE
    inputs[tail:, :] = jnp.zeros_like(inputs[tail:, :])
    inputs[tail : tail + count, :] = new[...]


def project_both_kernel(mine, theirs, new, wq, wk, wv, out, inputs):
    fill_rows(inputs, 0, mine, theirs)
    fill_new(inputs, new)
    x = inputs[...]
    column = 0
    for weight in (wq[...], jnp.concatenate([wk[...], wv[...]], axis=1)):
        part = jnp.dot(x, weight, preferred_element_type=jnp.float32)
        out[:, column : column + weight.shape[1]] = part[: out.shape[0]].astype(out.dtype)
        column += weight.shape[1]


def project_kernel(own, mine1, mine2, theirs1, theirs2, new, wq, wk, wv, *refs):
    held, first, second, inputs = refs
    rows = own.shape[0]
    tail = 3 * rows
    pad = held.shape[0] - rows
    inputs[:rows, :] = own[...]
    fill_rows(inputs, 1, mine1, theirs1)
    fill_rows(inputs, 2, mine2, theirs2)
    fill_new(inputs, new)
    x = inputs[...]
    column = 0
    for weight in (wq[...], jnp.concatenate([wk[...], wv[...]], axis=1)):
        part = jnp.dot(x, weight, preferred_element_type=jnp.float32)
        to = slice(column, column + weight.shape[1])
        for step, out in enumerate((held, first, second)):
            out[:rows, to] = part[step * rows : (step + 1) * rows].astype(out.dtype)
            out[rows:, to] = part[tail : tail + pad].astype(out.dtype)
        column += weight.shape[1]


def add_kernel(held, part, out):
    out[...] = held[...] + part[...].astype(jnp.float32)


def add_last_kernel(total, first, second, held, new):
    rows = held.shape[0]
    added = first[...].astype(jnp.float32) + second[...].astype(jnp.float32)
    added = (total[...] + added).astype(held.dtype)
    held[...] = added[:rows]
    new[...] = added[rows:]


def request_of(position, ends):
    found = jnp.zeros_like(position)
    for end in ends:
        found = found + jnp.where(position >= end, 1, 0)
    return found


def mask_kernel(block_rows, block_map, lengths, rows_mask, new_mask):
    ends, total = [], 0
    for request in range(lengths.shape[0]):
        total = total + lengths[request]
        ends.append(total)
    c, _, _ = place()
    count = block_map.shape[0]
    per_device = 2
    devices = [per_device * (c ^ mask) for mask in range(count // per_device)]

    def labels(shape, axis, held):
        index = lax.broadcasted_iota(jnp.int32, shape, axis)
        position = jnp.zeros(shape, jnp.int32)
        for number, block in enumerate(held):
            start = number * block_rows
            inside = (index >= start) & (index < start + block_rows)
            position = jnp.where(inside, block_map[block] * block_rows + index - start, position)
        return position, request_of(position, ends)

    keys = new_mask.shape[1]
    halves = [first + number for number in range(per_device) for first in devices]
    q_position, q_request = labels((keys, 1), 0, halves)
    held = [first + number for first in devices for number in range(per_device)]
    k_position, k_request = labels((1, keys), 1, held)
    allowed = (q_request == k_request) & (k_position <= q_position)
    rows_mask[...] = jnp.where(allowed, 0.0, FLOOR)
    request = lax.broadcasted_iota(jnp.int32, (new_mask.shape[0], 1), 0)
    new_mask[...] = jnp.where(request == k_request, 0.0, FLOOR)


def attend_kernel(sent, block_rows, scale, *refs):
    blocks, (new, rows_mask, new_mask), refs = [refs[0], *put_back(KEYS, refs[1:4])], refs[4:7], refs[7:]
    attended = refs[-1]
    features = blocks[0].shape[1]
    head = HEAD_SIZE
    q_width = features - 2 * head
    pad = new.shape[0]
    tail = len(blocks) * block_rows
    _, z, _ = place()
    half = 1 - z % 2 if sent else z % 2
    mask = rows_mask[pl.ds(pl.multiple_of(half * tail, tail), tail), :]
    if sent:
        new_rows = new_mask.shape[0]
        mask = jnp.concatenate([mask, new_mask[...]], axis=0)
        zeros = jnp.zeros((new_rows - pad, features), new.dtype)
        news = jnp.concatenate([new[...], zeros], axis=0)

    def columns(number):
        return slice(number * head, (number + 1) * head)

    def whole(number):
        return jnp.concatenate([block[:, columns(number)] for block in blocks], axis=0)

    def queries(number):
        taken = pl.ds(pl.multiple_of(half * block_rows, block_rows), block_rows)
        parts = [block[taken, columns(number)] for block in blocks]
        return jnp.concatenate(parts + ([news[:, columns(number)]] if sent else []), axis=0)

    key_at, value_at = q_width // head, q_width // head + 1
    keys, values = whole(key_at), whole(value_at)
    for number in range(q_width // head):
        at = columns(number)
        scores = lax.dot_general(
            queries(number), keys, (((1,), (1,)), ((), ())), preferred_element_type=jnp.float32
        )
        scores = scores * scale + mask
        peak = jnp.max(scores, axis=1, keepdims=True)
        if sent:
            own = news[:, at].astype(jnp.float32) * news[:, columns(key_at)].astype(jnp.float32)
            own = jnp.sum(own, axis=1, keepdims=True) * scale
            new_peak = jnp.maximum(peak[tail:], own)
            peak = jnp.concatenate([peak[:tail], new_peak], axis=0)
        weights = jnp.exp(scores - peak)
        denom = jnp.sum(weights, axis=1, keepdims=True)
        mixed = jnp.dot(weights.astype(jnp.bfloat16), values, preferred_element_type=jnp.float32)
        attended[:tail, at] = (mixed[:tail] / denom[:tail]).astype(jnp.bfloat16)
        if sent:
            weight = jnp.exp(own - new_peak)
            rounded = weight.astype(jnp.bfloat16).astype(jnp.float32)
            new_mixed = mixed[tail:] + rounded * news[:, columns(value_at)].astype(jnp.float32)
            new_mixed = new_mixed / (denom[tail:] + weight)
            attended[tail:, at] = new_mixed[:pad].astype(jnp.bfloat16)
    if not sent:
        attended[tail:, :] = refs[0][tail:, :]


def output_kernel(rows, *refs):
    heads, (w_own, *weights), outs = refs[:4], refs[4:8], refs[8:]
    _, _, k = place()
    width = outs[0].shape[1]
    w_mine = w_own[:, pl.ds(pl.multiple_of(k * width, width), width)]
    total = jnp.dot(heads[0][...], w_mine, preferred_element_type=jnp.float32)
    for ref, weight in zip(heads[1:], weights):
        total += jnp.dot(ref[...], weight[...], preferred_element_type=jnp.float32)
    total = total.astype(outs[0].dtype)
    for number, out in enumerate(outs):
        out[:rows, :] = total[number * rows : (number + 1) * rows]
        out[rows:, :] = total[len(outs) * rows :]


def relay_kernel(*refs):
    blocks, outs = [refs[0], *put_back(OUTPUTS, refs[1:4])], refs[4:]
    c, z, _ = place()
    for slot, out in enumerate(outs):
        for mask, block in enumerate(blocks):

            @pl.when((c ^ z ^ slot) == mask)
            def _(out=out, block=block):
                out[...] = block[: out.shape[0], :]


def finish_kernel(*refs):
    parts, (prefill, decode) = [refs[0], *put_back(HEADS, refs[1:4])], refs[4:]
    _, z, _ = place()
    rows = prefill.shape[0] // 2
    for odd in range(2):
        total = parts[odd][...].astype(jnp.float32) + parts[odd + 2][...].astype(jnp.float32)
        total = total.astype(prefill.dtype)
        half = z % 2 if odd == 0 else 1 - z % 2
        prefill[pl.ds(pl.multiple_of(half * rows, rows), rows), :] = total[:rows]
        if odd == 0:
            decode[...] = total[rows : rows + decode.shape[0]]


def on_device_small(
    steps, tp, tokens, new_token_states, w_query, key_matrix, value_matrix, w_out, lengths, block_map
):
    bf16, f32 = jnp.bfloat16, jnp.float32
    rows = tokens.shape[0]
    half = rows // 2
    depth = w_query.shape[0]
    count = new_token_states.shape[0]
    pad = -(-count // ROW_TILE) * ROW_TILE
    q_width = w_query.shape[1]
    features = q_width + 2 * key_matrix.shape[1]
    width = w_out.shape[1] // 2
    all_rows = steps * rows + pad

    def to_core(value):
        return lax.ppermute(value, "tp", [(i, i ^ 1) for i in range(tp)])

    def to_chip(value, step):
        return lax.ppermute(value, "tp", [(i, i ^ (2 * step)) for i in range(tp)])

    def to_partners(values):
        return [
            lax.ppermute(value, "ctx", [(i, i ^ mask) for i in range(steps)])
            for mask, value in enumerate(values, 1)
        ]

    def call(kernel, name, inputs, shapes, scratch=(), spaces=None):
        return pl.pallas_call(
            kernel,
            out_shape=[jax.ShapeDtypeStruct(shape, kind) for shape, kind in shapes],
            in_specs=spaces or [vmem()] * len(inputs),
            out_specs=[vmem()] * len(shapes),
            scratch_shapes=list(scratch),
            compiler_params=pltpu.CompilerParams(vmem_limit_bytes=VMEM_BYTES),
            name=name,
        )(*inputs)

    c, _, k = place()
    sent = [
        lax.dynamic_slice(tokens, (k * half, (c ^ mask) * depth), (half, depth))
        for mask in range(1, steps)
    ]
    own = lax.dynamic_slice_in_dim(tokens, c * depth, depth, 1)
    new_columns = lax.dynamic_slice_in_dim(new_token_states, c * depth, depth, 1)
    mine = to_partners(sent)
    theirs = [to_core(value) for value in mine]

    w_mine = lax.dynamic_slice_in_dim(w_out, k * width, width, 1)
    w_theirs = lax.dynamic_slice_in_dim(w_out, (1 - k) * width, width, 1)
    w_next = to_chip(w_mine, 1)

    part = (rows + pad, features)
    weights = (w_query, key_matrix, value_matrix)
    (both,) = call(
        project_both_kernel,
        "project_both",
        (mine[2], theirs[2], new_columns, *weights),
        [(part, bf16)],
        [pltpu.VMEM((rows + 2 * ROW_TILE, depth), bf16)],
    )
    new_columns, w_next = lax.optimization_barrier((new_columns, w_next))
    own_part, first, second = call(
        project_kernel,
        "project",
        (own, *mine[:2], *theirs[:2], new_columns, *weights),
        [(part, f32)] + [(part, bf16)] * 2,
        [pltpu.VMEM((3 * rows + 2 * ROW_TILE, depth), bf16)],
    )

    w_later, _ = lax.optimization_barrier((w_theirs, both))
    w_next_other = lax.ppermute(w_later, "tp", [(i, i ^ 3) for i in range(tp)])

    first, second, both = to_partners([first, second, both])
    (total,) = call(add_kernel, "add_both", (own_part, both), [(part, f32)])
    held, new = call(
        add_last_kernel,
        "add_last",
        (total, first, second),
        [((rows, features), bf16), ((pad, features), bf16)],
    )

    gathered = [held, *in_order(KEYS, to_partners([held] * (steps - 1)))]
    new, w_next_other = lax.optimization_barrier((new, w_next_other))
    block_rows = steps * rows // block_map.shape[0]

    keys = steps * rows
    masks = call(
        functools.partial(mask_kernel, block_rows),
        "mask",
        (block_map, lengths),
        [((keys, keys), f32), ((2 * ROW_TILE, keys), f32)],
        spaces=[smem()] * 2,
    )

    def attend(sent, *extra):
        (attended,) = call(
            functools.partial(attend_kernel, sent, block_rows, 1.0 / math.sqrt(HEAD_SIZE)),
            "attend_sent" if sent else "attend_kept",
            (*gathered, new, *masks, *extra),
            [((keys // 2 + pad, q_width), bf16)],
        )
        return attended

    sent = attend(True)
    got = to_chip(sent, 1)
    kept = attend(False, sent)
    w_last, _ = lax.optimization_barrier((w_theirs, held))
    w_other = to_core(w_last)

    block = (block_rows + pad, width)
    outs = call(
        functools.partial(output_kernel, block_rows),
        "project_out",
        (kept, to_core(kept), got, to_core(got), w_out, w_other, w_next, w_next_other),
        [(block, bf16)] * steps,
    )

    slots = call(
        relay_kernel,
        "relay",
        [outs[0], *in_order(OUTPUTS, to_partners(outs[1:]))],
        [(block if i % 2 == 0 else (block_rows, width), bf16) for i in range(steps)],
    )
    arrived = [to_chip(slot, step) for step, slot in enumerate(slots[1:], 1)]
    slots = [slots[0], *in_order(HEADS, arrived)]
    return tuple(
        call(finish_kernel, "finish", slots, [((rows, width), bf16), ((count, width), bf16)])
    )


floor_value = -1e30


def initial_positions(block_map, first_row, row_count, block_rows):
    row_ids = first_row + jnp.arange(row_count, dtype=jnp.int32)
    block_ids = row_ids // block_rows
    table_ids = jnp.arange(block_map.shape[0], dtype=jnp.int32)
    mapped = jnp.sum(
        jnp.where(block_ids[:, None] == table_ids[None, :], block_map[None, :], 0), axis=1
    )
    return mapped * block_rows + row_ids % block_rows


def request_index(positions, request_ends):
    return jnp.sum((positions[:, None] >= request_ends[None, :]).astype(jnp.int32), axis=1)


def round_weights(weights):
    rounded = weights.astype(jnp.bfloat16)
    rounded = lax.optimization_barrier(rounded)
    return rounded.astype(jnp.float32)


def softmax_parts(
    dec_heads, projected_key_rows, projected_value_rows, owned, kv_heads, head_dim, score_scale
):
    row_count = projected_key_rows.shape[0]
    scores = (
        jnp.einsum(
            "rgjd,tgd->rgjt",
            dec_heads,
            projected_key_rows.reshape(row_count, kv_heads, head_dim),
            preferred_element_type=jnp.float32,
        )
        * score_scale
    )
    scores = jnp.where(owned, scores, floor_value)
    part_peak = jnp.max(scores, axis=3)
    weights = jnp.where(owned, jnp.exp(scores - part_peak[..., None]), 0.0)
    part_total = jnp.sum(weights, axis=3)
    part_mixed = jnp.einsum(
        "rgjt,tgd->rgjd",
        weights.astype(jnp.bfloat16),
        projected_value_rows.reshape(row_count, kv_heads, head_dim),
        preferred_element_type=jnp.float32,
    )
    return (part_peak, part_total, part_mixed)


def on_device_large(
    tokens, new_token_states, w_query, key_matrix, value_matrix, w_out, lengths, block_map
):
    local_rows = tokens.shape[0]
    block_rows = local_rows // 2
    request_count = new_token_states.shape[0]
    head_dim = HEAD_SIZE
    query_width = w_query.shape[1]
    kv_width = key_matrix.shape[1]
    kv_heads = kv_width // head_dim
    query_group_count = query_width // kv_width
    score_scale = 1.0 / math.sqrt(head_dim)
    device = lax.axis_index("ctx")
    request_ends = jnp.cumsum(lengths)
    inputs = jnp.concatenate([tokens, new_token_states], axis=0)
    shard_pieces = (
        lax.all_gather(w_query, "ctx", axis=0, tiled=True),
        lax.all_gather(key_matrix, "ctx", axis=0, tiled=True),
        lax.all_gather(value_matrix, "ctx", axis=0, tiled=True),
    )
    query_all, key_all, value_all = tuple(
        (jnp.dot(inputs, weight, preferred_element_type=jnp.float32) for weight in shard_pieces)
    )
    query_all = query_all.astype(jnp.bfloat16)
    key_all = key_all.astype(jnp.bfloat16)
    value_all = value_all.astype(jnp.bfloat16)
    local_query = query_all[:local_rows]
    local_keys = key_all[:local_rows]
    local_values = value_all[:local_rows]
    dec_query = query_all[local_rows:]
    decode_key_rows = key_all[local_rows:]
    decode_value_rows = value_all[local_rows:]
    token_pos = initial_positions(block_map, device * local_rows, local_rows, block_rows)
    token_request = request_index(token_pos, request_ends)
    query_heads = local_query.reshape(local_rows, kv_heads, query_group_count, head_dim)

    def attend(running, shard_pieces, first_row):
        peak_run, total_run, mixed_run = running
        key_piece, value_piece = shard_pieces
        row_count = key_piece.shape[0]
        key_pos = initial_positions(block_map, first_row, row_count, block_rows)
        key_request = request_index(key_pos, request_ends)
        allowed = (key_request[None, :] == token_request[:, None]) & (
            key_pos[None, :] <= token_pos[:, None]
        )
        scores = (
            jnp.einsum(
                "tgjd,kgd->gjtk",
                query_heads,
                key_piece.reshape(row_count, kv_heads, head_dim),
                preferred_element_type=jnp.float32,
            )
            * score_scale
        )
        scores = jnp.where(allowed, scores, floor_value)
        peak_new = jnp.maximum(peak_run, jnp.max(scores, axis=3))
        weights = jnp.where(allowed, jnp.exp(scores - peak_new[..., None]), 0.0)
        rescale = jnp.exp(peak_run - peak_new)
        total_new = total_run * rescale + jnp.sum(weights, axis=3)
        mixed_new = mixed_run * rescale[..., None] + jnp.einsum(
            "gjtk,kgd->gjtd",
            weights.astype(jnp.bfloat16),
            value_piece.reshape(row_count, kv_heads, head_dim),
            preferred_element_type=jnp.float32,
        )
        return (peak_new, total_new, mixed_new)

    start_state = (
        jnp.full((kv_heads, query_group_count, local_rows), floor_value, jnp.float32),
        jnp.zeros((kv_heads, query_group_count, local_rows), jnp.float32),
        jnp.zeros((kv_heads, query_group_count, local_rows, head_dim), jnp.float32),
    )
    dec_heads = dec_query.reshape(request_count, kv_heads, query_group_count, head_dim)
    request_ids = jnp.arange(request_count, dtype=jnp.int32)
    cache_keys, cache_values = (
        lax.all_gather(local_keys, "ctx", axis=0, tiled=True),
        lax.all_gather(local_values, "ctx", axis=0, tiled=True),
    )
    total_rows = cache_keys.shape[0]
    shard_count = total_rows // local_rows
    limit = max(1, 1024 // local_rows)
    step_rows = local_rows * math.gcd(shard_count, 1 << limit.bit_length() - 1)

    def key_step(running, step_index):
        first_row = step_index * step_rows
        pieces = (
            lax.dynamic_slice_in_dim(cache_keys, first_row, step_rows, 0),
            lax.dynamic_slice_in_dim(cache_values, first_row, step_rows, 0),
        )
        return (attend(running, pieces, first_row), None)

    final_state, unused = lax.scan(
        key_step, start_state, jnp.arange(total_rows // step_rows, dtype=jnp.int32)
    )
    peak_run, total_run, mixed_run = final_state
    cache_pos = (
        block_map[:, None] * block_rows + jnp.arange(block_rows, dtype=jnp.int32)[None, :]
    ).reshape(total_rows)
    cache_request = request_index(cache_pos, request_ends)
    owned = (cache_request[None, :] == request_ids[:, None])[:, None, None, :]
    cache_peak, cache_total, cache_mixed = softmax_parts(
        dec_heads, cache_keys, cache_values, owned, kv_heads, head_dim, score_scale
    )
    attended = (
        (mixed_run / total_run[..., None]).transpose(2, 0, 1, 3).reshape(local_rows, query_width)
    )
    attended = attended.astype(jnp.bfloat16)
    own_keys = decode_key_rows.reshape(request_count, kv_heads, 1, head_dim).astype(jnp.float32)
    own_values = decode_value_rows.reshape(request_count, kv_heads, 1, head_dim).astype(jnp.float32)
    self_scores = jnp.sum(dec_heads.astype(jnp.float32) * own_keys, axis=3) * score_scale
    peak_all = jnp.maximum(cache_peak, self_scores)
    rescale = jnp.exp(cache_peak - peak_all)
    self_weights = jnp.exp(self_scores - peak_all)
    dec_total = cache_total * rescale + self_weights
    dec_mixed = (
        cache_mixed * rescale[..., None] + round_weights(self_weights)[..., None] * own_values
    )
    dec_attn = (
        (dec_mixed / dec_total[..., None]).reshape(request_count, query_width).astype(jnp.bfloat16)
    )
    attended_all = jnp.concatenate([attended, dec_attn], axis=0)
    head_block = lax.all_gather(w_out, "ctx", axis=1, tiled=True)
    column_block = lax.all_to_all(head_block, "tp", split_axis=1, concat_axis=0, tiled=True)
    summed_rows = jnp.dot(
        lax.all_gather(attended_all, "tp", axis=1, tiled=True),
        column_block,
        preferred_element_type=jnp.float32,
    )
    summed_rows = summed_rows.astype(jnp.bfloat16)
    return (summed_rows[:local_rows], summed_rows[local_rows:])

def solution(mesh):
    steps, tp = mesh.shape["ctx"], mesh.shape["tp"]

    def on_device(tokens, *rest):
        one_head = rest[2].shape[1] == HEAD_SIZE
        two_blocks = rest[-1].shape[0] == 2 * steps
        few = tokens.shape[0] * steps <= 1024
        small = steps == 4 and tp == 8 and one_head and two_blocks and few
        if small:
            return on_device_small(steps, tp, tokens, *rest)
        return on_device_large(tokens, *rest)

    return jax.shard_map(
        on_device,
        mesh=mesh,
        in_specs=(
            P("ctx", None),
            P(),
            P("ctx", "tp"),
            P("ctx", "tp"),
            P("ctx", "tp"),
            P("tp", "ctx"),
            P(),
            P(),
        ),
        out_specs=(P("ctx", "tp"), P(None, "tp")),
        check_vma=False,
    )
```

```python
import functools
import math

import jax
import jax.numpy as jnp
from jax import lax
from jax.experimental import pallas as pl
from jax.experimental.pallas import tpu as pltpu
from jax.sharding import PartitionSpec as P

HEAD_SIZE = 128
FLOOR = -1e30
LAST = 1 << 30
ROW_TILE = 8
VMEM_BYTES = 48 * 1024 * 1024
KEYS, OUTPUTS, HEADS = (2, 1, 0), (2, 1, 0), (2, 1, 0)


def vmem():
    return pl.BlockSpec(memory_space=pltpu.VMEM)


def smem():
    return pl.BlockSpec(memory_space=pltpu.SMEM)


def in_order(order, values):
    return [values[i] for i in order]


def put_back(order, values):
    return [values[order.index(i)] for i in range(len(order))]


def place():
    t = lax.axis_index("tp")
    return lax.axis_index("ctx"), t // 2, t % 2


def fill_rows(inputs, number, mine, theirs):
    _, _, k = place()
    rows = mine.shape[0]
    for core, block in ((k, mine), (1 - k, theirs)):
        first = 2 * rows * number + core * rows
        inputs[pl.ds(pl.multiple_of(first, rows), rows), :] = block[...]


def fill_new(inputs, new):
    count = new.shape[0]
    tail = inputs.shape[0] - 2 * ROW_TILE
    inputs[tail:, :] = jnp.zeros_like(inputs[tail:, :])
    inputs[tail : tail + count, :] = new[...]


def project_both_kernel(mine, theirs, new, wq, wk, wv, out, inputs):
    fill_rows(inputs, 0, mine, theirs)
    fill_new(inputs, new)
    x = inputs[...]
    column = 0
    for weight in (wq[...], jnp.concatenate([wk[...], wv[...]], axis=1)):
        part = jnp.dot(x, weight, preferred_element_type=jnp.float32)
        out[:, column : column + weight.shape[1]] = part[: out.shape[0]].astype(out.dtype)
        column += weight.shape[1]


def project_kernel(own, mine1, mine2, theirs1, theirs2, new, wq, wk, wv, *refs):
    held, first, second, inputs = refs
    rows = own.shape[0]
    tail = 3 * rows
    pad = held.shape[0] - rows
    inputs[:rows, :] = own[...]
    fill_rows(inputs, 1, mine1, theirs1)
    fill_rows(inputs, 2, mine2, theirs2)
    fill_new(inputs, new)
    x = inputs[...]
    column = 0
    for weight in (wq[...], jnp.concatenate([wk[...], wv[...]], axis=1)):
        part = jnp.dot(x, weight, preferred_element_type=jnp.float32)
        to = slice(column, column + weight.shape[1])
        for step, out in enumerate((held, first, second)):
            out[:rows, to] = part[step * rows : (step + 1) * rows].astype(out.dtype)
            out[rows:, to] = part[tail : tail + pad].astype(out.dtype)
        column += weight.shape[1]


def add_kernel(held, part, out):
    out[...] = held[...] + part[...].astype(jnp.float32)


def add_last_kernel(total, first, second, held, new):
    rows = held.shape[0]
    added = first[...].astype(jnp.float32) + second[...].astype(jnp.float32)
    added = (total[...] + added).astype(held.dtype)
    held[...] = added[:rows]
    new[...] = added[rows:]


def request_of(position, ends):
    found = jnp.zeros_like(position)
    for end in ends:
        found = found + jnp.where(position >= end, 1, 0)
    return found


def mask_kernel(block_rows, block_map, lengths, rows_mask, new_mask):
    ends, total = [], 0
    for request in range(lengths.shape[0]):
        total = total + lengths[request]
        ends.append(total)
    c, _, _ = place()
    count = block_map.shape[0]
    per_device = 2
    devices = [per_device * (c ^ mask) for mask in range(count // per_device)]

    def labels(shape, axis, held):
        index = lax.broadcasted_iota(jnp.int32, shape, axis)
        position = jnp.zeros(shape, jnp.int32)
        for number, block in enumerate(held):
            start = number * block_rows
            inside = (index >= start) & (index < start + block_rows)
            position = jnp.where(inside, block_map[block] * block_rows + index - start, position)
        return position, request_of(position, ends)

    keys = new_mask.shape[1]
    halves = [first + number for number in range(per_device) for first in devices]
    q_position, q_request = labels((keys, 1), 0, halves)
    held = [first + number for first in devices for number in range(per_device)]
    k_position, k_request = labels((1, keys), 1, held)
    allowed = (q_request == k_request) & (k_position <= q_position)
    rows_mask[...] = jnp.where(allowed, 0.0, FLOOR)
    request = lax.broadcasted_iota(jnp.int32, (new_mask.shape[0], 1), 0)
    new_mask[...] = jnp.where(request == k_request, 0.0, FLOOR)


def attend_kernel(sent, block_rows, scale, *refs):
    blocks, (new, rows_mask, new_mask), refs = [refs[0], *put_back(KEYS, refs[1:4])], refs[4:7], refs[7:]
    attended = refs[-1]
    features = blocks[0].shape[1]
    head = HEAD_SIZE
    q_width = features - 2 * head
    pad = new.shape[0]
    tail = len(blocks) * block_rows
    _, z, _ = place()
    half = 1 - z % 2 if sent else z % 2
    mask = rows_mask[pl.ds(pl.multiple_of(half * tail, tail), tail), :]
    if sent:
        new_rows = new_mask.shape[0]
        mask = jnp.concatenate([mask, new_mask[...]], axis=0)
        zeros = jnp.zeros((new_rows - pad, features), new.dtype)
        news = jnp.concatenate([new[...], zeros], axis=0)

    def columns(number):
        return slice(number * head, (number + 1) * head)

    def whole(number):
        return jnp.concatenate([block[:, columns(number)] for block in blocks], axis=0)

    def queries(number):
        taken = pl.ds(pl.multiple_of(half * block_rows, block_rows), block_rows)
        parts = [block[taken, columns(number)] for block in blocks]
        return jnp.concatenate(parts + ([news[:, columns(number)]] if sent else []), axis=0)

    key_at, value_at = q_width // head, q_width // head + 1
    keys, values = whole(key_at), whole(value_at)
    for number in range(q_width // head):
        at = columns(number)
        scores = lax.dot_general(
            queries(number), keys, (((1,), (1,)), ((), ())), preferred_element_type=jnp.float32
        )
        scores = scores * scale + mask
        peak = jnp.max(scores, axis=1, keepdims=True)
        if sent:
            own = news[:, at].astype(jnp.float32) * news[:, columns(key_at)].astype(jnp.float32)
            own = jnp.sum(own, axis=1, keepdims=True) * scale
            new_peak = jnp.maximum(peak[tail:], own)
            peak = jnp.concatenate([peak[:tail], new_peak], axis=0)
        weights = jnp.exp(scores - peak)
        denom = jnp.sum(weights, axis=1, keepdims=True)
        mixed = jnp.dot(weights.astype(jnp.bfloat16), values, preferred_element_type=jnp.float32)
        attended[:tail, at] = (mixed[:tail] / denom[:tail]).astype(jnp.bfloat16)
        if sent:
            weight = jnp.exp(own - new_peak)
            rounded = weight.astype(jnp.bfloat16).astype(jnp.float32)
            new_mixed = mixed[tail:] + rounded * news[:, columns(value_at)].astype(jnp.float32)
            new_mixed = new_mixed / (denom[tail:] + weight)
            attended[tail:, at] = new_mixed[:pad].astype(jnp.bfloat16)
    if not sent:
        attended[tail:, :] = refs[0][tail:, :]


def output_kernel(*refs):
    heads, (w_own, *weights), total = refs[:3], refs[3:6], refs[6]
    _, _, k = place()
    width = total.shape[1]
    w_mine = w_own[:, pl.ds(pl.multiple_of(k * width, width), width)]
    added = jnp.dot(heads[0][...], w_mine, preferred_element_type=jnp.float32)
    for ref, weight in zip(heads[1:], weights):
        added += jnp.dot(ref[...], weight[...], preferred_element_type=jnp.float32)
    total[...] = added


def output_last_kernel(rows, total, heads, weight, *outs):
    added = total[...] + jnp.dot(heads[...], weight[...], preferred_element_type=jnp.float32)
    added = added.astype(outs[0].dtype)
    for number, out in enumerate(outs):
        out[:rows, :] = added[number * rows : (number + 1) * rows]
        out[rows:, :] = added[len(outs) * rows :]


def relay_kernel(*refs):
    blocks, outs = [refs[0], *put_back(OUTPUTS, refs[1:4])], refs[4:]
    c, z, _ = place()
    for slot, out in enumerate(outs):
        for mask, block in enumerate(blocks):

            @pl.when((c ^ z ^ slot) == mask)
            def _(out=out, block=block):
                out[...] = block[: out.shape[0], :]


def finish_kernel(*refs):
    parts, (prefill, decode) = [refs[0], *put_back(HEADS, refs[1:4])], refs[4:]
    _, z, _ = place()
    rows = prefill.shape[0] // 2
    for odd in range(2):
        total = parts[odd][...].astype(jnp.float32) + parts[odd + 2][...].astype(jnp.float32)
        total = total.astype(prefill.dtype)
        half = z % 2 if odd == 0 else 1 - z % 2
        prefill[pl.ds(pl.multiple_of(half * rows, rows), rows), :] = total[:rows]
        if odd == 0:
            decode[...] = total[rows : rows + decode.shape[0]]


def on_device_small(
    steps, tp, tokens, new_token_states, w_query, key_matrix, value_matrix, w_out, lengths, block_map
):
    bf16, f32 = jnp.bfloat16, jnp.float32
    rows = tokens.shape[0]
    half = rows // 2
    depth = w_query.shape[0]
    count = new_token_states.shape[0]
    pad = -(-count // ROW_TILE) * ROW_TILE
    q_width = w_query.shape[1]
    features = q_width + 2 * key_matrix.shape[1]
    width = w_out.shape[1] // 2
    all_rows = steps * rows + pad

    def to_core(value):
        return lax.ppermute(value, "tp", [(i, i ^ 1) for i in range(tp)])

    def to_chip(value, step):
        return lax.ppermute(value, "tp", [(i, i ^ (2 * step)) for i in range(tp)])

    def to_partners(values):
        return [
            lax.ppermute(value, "ctx", [(i, i ^ mask) for i in range(steps)])
            for mask, value in enumerate(values, 1)
        ]

    def call(kernel, name, inputs, shapes, scratch=(), spaces=None):
        return pl.pallas_call(
            kernel,
            out_shape=[jax.ShapeDtypeStruct(shape, kind) for shape, kind in shapes],
            in_specs=spaces or [vmem()] * len(inputs),
            out_specs=[vmem()] * len(shapes),
            scratch_shapes=list(scratch),
            compiler_params=pltpu.CompilerParams(vmem_limit_bytes=VMEM_BYTES),
            name=name,
        )(*inputs)

    c, _, k = place()
    sent = [
        lax.dynamic_slice(tokens, (k * half, (c ^ mask) * depth), (half, depth))
        for mask in range(1, steps)
    ]
    own = lax.dynamic_slice_in_dim(tokens, c * depth, depth, 1)
    new_columns = lax.dynamic_slice_in_dim(new_token_states, c * depth, depth, 1)
    mine = to_partners(sent)
    mine[2], own = lax.optimization_barrier((mine[2], own))
    theirs = [to_core(value) for value in mine]

    w_mine = lax.dynamic_slice_in_dim(w_out, k * width, width, 1)
    w_theirs = lax.dynamic_slice_in_dim(w_out, (1 - k) * width, width, 1)
    w_next = to_chip(w_mine, 1)

    part = (rows + pad, features)
    weights = (w_query, key_matrix, value_matrix)
    (both,) = call(
        project_both_kernel,
        "project_both",
        (mine[2], theirs[2], new_columns, *weights),
        [(part, bf16)],
        [pltpu.VMEM((rows + 2 * ROW_TILE, depth), bf16)],
    )
    new_columns, w_next = lax.optimization_barrier((new_columns, w_next))
    own_part, first, second = call(
        project_kernel,
        "project",
        (own, *mine[:2], *theirs[:2], new_columns, *weights),
        [(part, f32)] + [(part, bf16)] * 2,
        [pltpu.VMEM((3 * rows + 2 * ROW_TILE, depth), bf16)],
    )

    w_later, _ = lax.optimization_barrier((w_theirs, both))
    w_next_other = lax.ppermute(w_later, "tp", [(i, i ^ 3) for i in range(tp)])

    first, second, both = to_partners([first, second, both])
    (total,) = call(add_kernel, "add_both", (own_part, both), [(part, f32)])
    held, new = call(
        add_last_kernel,
        "add_last",
        (total, first, second),
        [((rows, features), bf16), ((pad, features), bf16)],
    )

    gathered = [held, *in_order(KEYS, to_partners([held] * (steps - 1)))]
    new, w_next_other = lax.optimization_barrier((new, w_next_other))
    block_rows = steps * rows // block_map.shape[0]

    keys = steps * rows
    masks = call(
        functools.partial(mask_kernel, block_rows),
        "mask",
        (block_map, lengths),
        [((keys, keys), f32), ((2 * ROW_TILE, keys), f32)],
        spaces=[smem()] * 2,
    )

    def attend(sent, *extra):
        (attended,) = call(
            functools.partial(attend_kernel, sent, block_rows, 1.0 / math.sqrt(HEAD_SIZE)),
            "attend_sent" if sent else "attend_kept",
            (*gathered, new, *masks, *extra),
            [((keys // 2 + pad, q_width), bf16)],
        )
        return attended

    sent = attend(True)
    got = to_chip(sent, 1)
    kept = attend(False, sent)
    w_last, _ = lax.optimization_barrier((w_theirs, held))
    w_other = to_core(w_last)

    block = (block_rows + pad, width)
    (total,) = call(
        output_kernel,
        "project_out",
        (kept, to_core(kept), got, w_out, w_other, w_next),
        [((kept.shape[0], width), f32)],
    )
    outs = call(
        functools.partial(output_last_kernel, block_rows),
        "project_last",
        (total, to_core(got), w_next_other),
        [(block, bf16)] * steps,
    )

    slots = call(
        relay_kernel,
        "relay",
        [outs[0], *in_order(OUTPUTS, to_partners(outs[1:]))],
        [(block if i % 2 == 0 else (block_rows, width), bf16) for i in range(steps)],
    )
    arrived = [to_chip(slot, step) for step, slot in enumerate(slots[1:], 1)]
    slots = [slots[0], *in_order(HEADS, arrived)]
    return tuple(
        call(finish_kernel, "finish", slots, [((rows, width), bf16), ((count, width), bf16)])
    )


floor_value = -1e30


def initial_positions(block_map, first_row, row_count, block_rows):
    row_ids = first_row + jnp.arange(row_count, dtype=jnp.int32)
    block_ids = row_ids // block_rows
    table_ids = jnp.arange(block_map.shape[0], dtype=jnp.int32)
    mapped = jnp.sum(
        jnp.where(block_ids[:, None] == table_ids[None, :], block_map[None, :], 0), axis=1
    )
    return mapped * block_rows + row_ids % block_rows


def request_index(positions, request_ends):
    return jnp.sum((positions[:, None] >= request_ends[None, :]).astype(jnp.int32), axis=1)


def round_weights(weights):
    rounded = weights.astype(jnp.bfloat16)
    rounded = lax.optimization_barrier(rounded)
    return rounded.astype(jnp.float32)


def softmax_parts(
    dec_heads, projected_key_rows, projected_value_rows, owned, kv_heads, head_dim, score_scale
):
    row_count = projected_key_rows.shape[0]
    scores = (
        jnp.einsum(
            "rgjd,tgd->rgjt",
            dec_heads,
            projected_key_rows.reshape(row_count, kv_heads, head_dim),
            preferred_element_type=jnp.float32,
        )
        * score_scale
    )
    scores = jnp.where(owned, scores, floor_value)
    part_peak = jnp.max(scores, axis=3)
    weights = jnp.where(owned, jnp.exp(scores - part_peak[..., None]), 0.0)
    part_total = jnp.sum(weights, axis=3)
    part_mixed = jnp.einsum(
        "rgjt,tgd->rgjd",
        weights.astype(jnp.bfloat16),
        projected_value_rows.reshape(row_count, kv_heads, head_dim),
        preferred_element_type=jnp.float32,
    )
    return (part_peak, part_total, part_mixed)


def on_device_large(
    tokens, new_token_states, w_query, key_matrix, value_matrix, w_out, lengths, block_map
):
    local_rows = tokens.shape[0]
    block_rows = local_rows // 2
    request_count = new_token_states.shape[0]
    head_dim = HEAD_SIZE
    query_width = w_query.shape[1]
    kv_width = key_matrix.shape[1]
    kv_heads = kv_width // head_dim
    query_group_count = query_width // kv_width
    score_scale = 1.0 / math.sqrt(head_dim)
    device = lax.axis_index("ctx")
    request_ends = jnp.cumsum(lengths)
    inputs = jnp.concatenate([tokens, new_token_states], axis=0)
    shard_pieces = (
        lax.all_gather(w_query, "ctx", axis=0, tiled=True),
        lax.all_gather(key_matrix, "ctx", axis=0, tiled=True),
        lax.all_gather(value_matrix, "ctx", axis=0, tiled=True),
    )
    query_all, key_all, value_all = tuple(
        (jnp.dot(inputs, weight, preferred_element_type=jnp.float32) for weight in shard_pieces)
    )
    query_all = query_all.astype(jnp.bfloat16)
    key_all = key_all.astype(jnp.bfloat16)
    value_all = value_all.astype(jnp.bfloat16)
    local_query = query_all[:local_rows]
    local_keys = key_all[:local_rows]
    local_values = value_all[:local_rows]
    dec_query = query_all[local_rows:]
    decode_key_rows = key_all[local_rows:]
    decode_value_rows = value_all[local_rows:]
    token_pos = initial_positions(block_map, device * local_rows, local_rows, block_rows)
    token_request = request_index(token_pos, request_ends)
    query_heads = local_query.reshape(local_rows, kv_heads, query_group_count, head_dim)

    def attend(running, shard_pieces, first_row):
        peak_run, total_run, mixed_run = running
        key_piece, value_piece = shard_pieces
        row_count = key_piece.shape[0]
        key_pos = initial_positions(block_map, first_row, row_count, block_rows)
        key_request = request_index(key_pos, request_ends)
        allowed = (key_request[None, :] == token_request[:, None]) & (
            key_pos[None, :] <= token_pos[:, None]
        )
        scores = (
            jnp.einsum(
                "tgjd,kgd->gjtk",
                query_heads,
                key_piece.reshape(row_count, kv_heads, head_dim),
                preferred_element_type=jnp.float32,
            )
            * score_scale
        )
        scores = jnp.where(allowed, scores, floor_value)
        peak_new = jnp.maximum(peak_run, jnp.max(scores, axis=3))
        weights = jnp.where(allowed, jnp.exp(scores - peak_new[..., None]), 0.0)
        rescale = jnp.exp(peak_run - peak_new)
        total_new = total_run * rescale + jnp.sum(weights, axis=3)
        mixed_new = mixed_run * rescale[..., None] + jnp.einsum(
            "gjtk,kgd->gjtd",
            weights.astype(jnp.bfloat16),
            value_piece.reshape(row_count, kv_heads, head_dim),
            preferred_element_type=jnp.float32,
        )
        return (peak_new, total_new, mixed_new)

    start_state = (
        jnp.full((kv_heads, query_group_count, local_rows), floor_value, jnp.float32),
        jnp.zeros((kv_heads, query_group_count, local_rows), jnp.float32),
        jnp.zeros((kv_heads, query_group_count, local_rows, head_dim), jnp.float32),
    )
    dec_heads = dec_query.reshape(request_count, kv_heads, query_group_count, head_dim)
    request_ids = jnp.arange(request_count, dtype=jnp.int32)
    cache_keys, cache_values = (
        lax.all_gather(local_keys, "ctx", axis=0, tiled=True),
        lax.all_gather(local_values, "ctx", axis=0, tiled=True),
    )
    total_rows = cache_keys.shape[0]
    shard_count = total_rows // local_rows
    limit = max(1, 1024 // local_rows)
    step_rows = local_rows * math.gcd(shard_count, 1 << limit.bit_length() - 1)

    def key_step(running, step_index):
        first_row = step_index * step_rows
        pieces = (
            lax.dynamic_slice_in_dim(cache_keys, first_row, step_rows, 0),
            lax.dynamic_slice_in_dim(cache_values, first_row, step_rows, 0),
        )
        return (attend(running, pieces, first_row), None)

    final_state, unused = lax.scan(
        key_step, start_state, jnp.arange(total_rows // step_rows, dtype=jnp.int32)
    )
    peak_run, total_run, mixed_run = final_state
    cache_pos = (
        block_map[:, None] * block_rows + jnp.arange(block_rows, dtype=jnp.int32)[None, :]
    ).reshape(total_rows)
    cache_request = request_index(cache_pos, request_ends)
    owned = (cache_request[None, :] == request_ids[:, None])[:, None, None, :]
    cache_peak, cache_total, cache_mixed = softmax_parts(
        dec_heads, cache_keys, cache_values, owned, kv_heads, head_dim, score_scale
    )
    attended = (
        (mixed_run / total_run[..., None]).transpose(2, 0, 1, 3).reshape(local_rows, query_width)
    )
    attended = attended.astype(jnp.bfloat16)
    own_keys = decode_key_rows.reshape(request_count, kv_heads, 1, head_dim).astype(jnp.float32)
    own_values = decode_value_rows.reshape(request_count, kv_heads, 1, head_dim).astype(jnp.float32)
    self_scores = jnp.sum(dec_heads.astype(jnp.float32) * own_keys, axis=3) * score_scale
    peak_all = jnp.maximum(cache_peak, self_scores)
    rescale = jnp.exp(cache_peak - peak_all)
    self_weights = jnp.exp(self_scores - peak_all)
    dec_total = cache_total * rescale + self_weights
    dec_mixed = (
        cache_mixed * rescale[..., None] + round_weights(self_weights)[..., None] * own_values
    )
    dec_attn = (
        (dec_mixed / dec_total[..., None]).reshape(request_count, query_width).astype(jnp.bfloat16)
    )
    attended_all = jnp.concatenate([attended, dec_attn], axis=0)
    head_block = lax.all_gather(w_out, "ctx", axis=1, tiled=True)
    column_block = lax.all_to_all(head_block, "tp", split_axis=1, concat_axis=0, tiled=True)
    summed_rows = jnp.dot(
        lax.all_gather(attended_all, "tp", axis=1, tiled=True),
        column_block,
        preferred_element_type=jnp.float32,
    )
    summed_rows = summed_rows.astype(jnp.bfloat16)
    return (summed_rows[:local_rows], summed_rows[local_rows:])

def solution(mesh):
    steps, tp = mesh.shape["ctx"], mesh.shape["tp"]

    def on_device(tokens, *rest):
        one_head = rest[2].shape[1] == HEAD_SIZE
        two_blocks = rest[-1].shape[0] == 2 * steps
        few = tokens.shape[0] * steps <= 1024
        small = steps == 4 and tp == 8 and one_head and two_blocks and few
        if small:
            return on_device_small(steps, tp, tokens, *rest)
        return on_device_large(tokens, *rest)

    return jax.shard_map(
        on_device,
        mesh=mesh,
        in_specs=(
            P("ctx", None),
            P(),
            P("ctx", "tp"),
            P("ctx", "tp"),
            P("ctx", "tp"),
            P("tp", "ctx"),
            P(),
            P(),
        ),
        out_specs=(P("ctx", "tp"), P(None, "tp")),
        check_vma=False,
    )
```

```python
import functools
import math

import jax
import jax.numpy as jnp
from jax import lax
from jax.experimental import pallas as pl
from jax.experimental.pallas import tpu as pltpu
from jax.sharding import PartitionSpec as P

HEAD_SIZE = 128
FLOOR = -1e30
LAST = 1 << 30
ROW_TILE = 8
VMEM_BYTES = 48 * 1024 * 1024
KEYS, OUTPUTS, HEADS = (2, 1, 0), (2, 0, 1), (2, 1, 0)


def vmem():
    return pl.BlockSpec(memory_space=pltpu.VMEM)


def smem():
    return pl.BlockSpec(memory_space=pltpu.SMEM)


def in_order(order, values):
    return [values[i] for i in order]


def put_back(order, values):
    return [values[order.index(i)] for i in range(len(order))]


def place():
    t = lax.axis_index("tp")
    return lax.axis_index("ctx"), t // 2, t % 2


def fill_rows(inputs, number, mine, theirs):
    _, _, k = place()
    rows = mine.shape[0]
    for core, block in ((k, mine), (1 - k, theirs)):
        first = 2 * rows * number + core * rows
        inputs[pl.ds(pl.multiple_of(first, rows), rows), :] = block[...]


def fill_new(inputs, new):
    count = new.shape[0]
    tail = inputs.shape[0] - 2 * ROW_TILE
    inputs[tail:, :] = jnp.zeros_like(inputs[tail:, :])
    inputs[tail : tail + count, :] = new[...]


def project_both_kernel(mine, theirs, new, wq, wk, wv, out, inputs):
    fill_rows(inputs, 0, mine, theirs)
    fill_new(inputs, new)
    x = inputs[...]
    column = 0
    for weight in (wq[...], jnp.concatenate([wk[...], wv[...]], axis=1)):
        part = jnp.dot(x, weight, preferred_element_type=jnp.float32)
        out[:, column : column + weight.shape[1]] = part[: out.shape[0]].astype(out.dtype)
        column += weight.shape[1]


def project_kernel(own, mine1, mine2, theirs1, theirs2, new, wq, wk, wv, *refs):
    held, first, second, inputs = refs
    rows = own.shape[0]
    tail = 3 * rows
    pad = held.shape[0] - rows
    inputs[:rows, :] = own[...]
    fill_rows(inputs, 1, mine1, theirs1)
    fill_rows(inputs, 2, mine2, theirs2)
    fill_new(inputs, new)
    x = inputs[...]
    column = 0
    for weight in (wq[...], jnp.concatenate([wk[...], wv[...]], axis=1)):
        part = jnp.dot(x, weight, preferred_element_type=jnp.float32)
        to = slice(column, column + weight.shape[1])
        for step, out in enumerate((held, first, second)):
            out[:rows, to] = part[step * rows : (step + 1) * rows].astype(out.dtype)
            out[rows:, to] = part[tail : tail + pad].astype(out.dtype)
        column += weight.shape[1]


def add_kernel(held, part, out):
    out[...] = held[...] + part[...].astype(jnp.float32)


def add_last_kernel(total, first, second, held, new):
    rows = held.shape[0]
    added = first[...].astype(jnp.float32) + second[...].astype(jnp.float32)
    added = (total[...] + added).astype(held.dtype)
    held[...] = added[:rows]
    new[...] = added[rows:]


def request_of(position, ends):
    found = jnp.zeros_like(position)
    for end in ends:
        found = found + jnp.where(position >= end, 1, 0)
    return found


def mask_kernel(block_rows, block_map, lengths, rows_mask, new_mask):
    ends, total = [], 0
    for request in range(lengths.shape[0]):
        total = total + lengths[request]
        ends.append(total)
    c, _, _ = place()
    count = block_map.shape[0]
    per_device = 2
    devices = [per_device * (c ^ mask) for mask in range(count // per_device)]

    def labels(shape, axis, held):
        index = lax.broadcasted_iota(jnp.int32, shape, axis)
        position = jnp.zeros(shape, jnp.int32)
        for number, block in enumerate(held):
            start = number * block_rows
            inside = (index >= start) & (index < start + block_rows)
            position = jnp.where(inside, block_map[block] * block_rows + index - start, position)
        return position, request_of(position, ends)

    keys = new_mask.shape[1]
    halves = [first + number for number in range(per_device) for first in devices]
    q_position, q_request = labels((keys, 1), 0, halves)
    held = [first + number for first in devices for number in range(per_device)]
    k_position, k_request = labels((1, keys), 1, held)
    allowed = (q_request == k_request) & (k_position <= q_position)
    rows_mask[...] = jnp.where(allowed, 0.0, FLOOR)
    request = lax.broadcasted_iota(jnp.int32, (new_mask.shape[0], 1), 0)
    new_mask[...] = jnp.where(request == k_request, 0.0, FLOOR)


def attend_kernel(sent, block_rows, scale, *refs):
    blocks, (new, rows_mask, new_mask), refs = [refs[0], *put_back(KEYS, refs[1:4])], refs[4:7], refs[7:]
    attended = refs[-1]
    features = blocks[0].shape[1]
    head = HEAD_SIZE
    q_width = features - 2 * head
    pad = new.shape[0]
    tail = len(blocks) * block_rows
    _, z, _ = place()
    half = 1 - z % 2 if sent else z % 2
    mask = rows_mask[pl.ds(pl.multiple_of(half * tail, tail), tail), :]
    if sent:
        new_rows = new_mask.shape[0]
        mask = jnp.concatenate([mask, new_mask[...]], axis=0)
        zeros = jnp.zeros((new_rows - pad, features), new.dtype)
        news = jnp.concatenate([new[...], zeros], axis=0)

    def columns(number):
        return slice(number * head, (number + 1) * head)

    def whole(number):
        return jnp.concatenate([block[:, columns(number)] for block in blocks], axis=0)

    def queries(number):
        taken = pl.ds(pl.multiple_of(half * block_rows, block_rows), block_rows)
        parts = [block[taken, columns(number)] for block in blocks]
        return jnp.concatenate(parts + ([news[:, columns(number)]] if sent else []), axis=0)

    key_at, value_at = q_width // head, q_width // head + 1
    keys, values = whole(key_at), whole(value_at)
    for number in range(q_width // head):
        at = columns(number)
        scores = lax.dot_general(
            queries(number), keys, (((1,), (1,)), ((), ())), preferred_element_type=jnp.float32
        )
        scores = scores * scale + mask
        peak = jnp.max(scores, axis=1, keepdims=True)
        if sent:
            own = news[:, at].astype(jnp.float32) * news[:, columns(key_at)].astype(jnp.float32)
            own = jnp.sum(own, axis=1, keepdims=True) * scale
            new_peak = jnp.maximum(peak[tail:], own)
            peak = jnp.concatenate([peak[:tail], new_peak], axis=0)
        weights = jnp.exp(scores - peak)
        denom = jnp.sum(weights, axis=1, keepdims=True)
        mixed = jnp.dot(weights.astype(jnp.bfloat16), values, preferred_element_type=jnp.float32)
        attended[:tail, at] = (mixed[:tail] / denom[:tail]).astype(jnp.bfloat16)
        if sent:
            weight = jnp.exp(own - new_peak)
            rounded = weight.astype(jnp.bfloat16).astype(jnp.float32)
            new_mixed = mixed[tail:] + rounded * news[:, columns(value_at)].astype(jnp.float32)
            new_mixed = new_mixed / (denom[tail:] + weight)
            attended[tail:, at] = new_mixed[:pad].astype(jnp.bfloat16)
    if not sent:
        attended[tail:, :] = refs[0][tail:, :]


def output_kernel(*refs):
    heads, (w_own, *weights), total = refs[:3], refs[3:6], refs[6]
    _, _, k = place()
    width = total.shape[1]
    w_mine = w_own[:, pl.ds(pl.multiple_of(k * width, width), width)]
    added = jnp.dot(heads[0][...], w_mine, preferred_element_type=jnp.float32)
    for ref, weight in zip(heads[1:], weights):
        added += jnp.dot(ref[...], weight[...], preferred_element_type=jnp.float32)
    total[...] = added


def output_last_kernel(rows, total, heads, weight, *outs):
    added = total[...] + jnp.dot(heads[...], weight[...], preferred_element_type=jnp.float32)
    added = added.astype(outs[0].dtype)
    for number, out in enumerate(outs):
        out[:rows, :] = added[number * rows : (number + 1) * rows]
        out[rows:, :] = added[len(outs) * rows :]


def relay_kernel(*refs):
    blocks, outs = [refs[0], *put_back(OUTPUTS, refs[1:4])], refs[4:]
    c, z, _ = place()
    for slot, out in enumerate(outs):
        for mask, block in enumerate(blocks):

            @pl.when((c ^ z ^ slot) == mask)
            def _(out=out, block=block):
                out[...] = block[: out.shape[0], :]


def finish_kernel(*refs):
    parts, (prefill, decode) = [refs[0], *put_back(HEADS, refs[1:4])], refs[4:]
    _, z, _ = place()
    rows = prefill.shape[0] // 2
    for odd in range(2):
        total = parts[odd][...].astype(jnp.float32) + parts[odd + 2][...].astype(jnp.float32)
        total = total.astype(prefill.dtype)
        half = z % 2 if odd == 0 else 1 - z % 2
        prefill[pl.ds(pl.multiple_of(half * rows, rows), rows), :] = total[:rows]
        if odd == 0:
            decode[...] = total[rows : rows + decode.shape[0]]


def on_device_small(
    steps, tp, tokens, new_token_states, w_query, key_matrix, value_matrix, w_out, lengths, block_map
):
    bf16, f32 = jnp.bfloat16, jnp.float32
    rows = tokens.shape[0]
    half = rows // 2
    depth = w_query.shape[0]
    count = new_token_states.shape[0]
    pad = -(-count // ROW_TILE) * ROW_TILE
    q_width = w_query.shape[1]
    features = q_width + 2 * key_matrix.shape[1]
    width = w_out.shape[1] // 2
    all_rows = steps * rows + pad

    def to_core(value):
        return lax.ppermute(value, "tp", [(i, i ^ 1) for i in range(tp)])

    def to_chip(value, step):
        return lax.ppermute(value, "tp", [(i, i ^ (2 * step)) for i in range(tp)])

    def to_partners(values):
        return [
            lax.ppermute(value, "ctx", [(i, i ^ mask) for i in range(steps)])
            for mask, value in enumerate(values, 1)
        ]

    def call(kernel, name, inputs, shapes, scratch=(), spaces=None):
        return pl.pallas_call(
            kernel,
            out_shape=[jax.ShapeDtypeStruct(shape, kind) for shape, kind in shapes],
            in_specs=spaces or [vmem()] * len(inputs),
            out_specs=[vmem()] * len(shapes),
            scratch_shapes=list(scratch),
            compiler_params=pltpu.CompilerParams(vmem_limit_bytes=VMEM_BYTES),
            name=name,
        )(*inputs)

    c, _, k = place()
    sent = [
        lax.dynamic_slice(tokens, (k * half, (c ^ mask) * depth), (half, depth))
        for mask in range(1, steps)
    ]
    own = lax.dynamic_slice_in_dim(tokens, c * depth, depth, 1)
    new_columns = lax.dynamic_slice_in_dim(new_token_states, c * depth, depth, 1)
    mine = to_partners(sent)
    mine[2], own = lax.optimization_barrier((mine[2], own))
    theirs = [to_core(value) for value in mine]

    w_mine = lax.dynamic_slice_in_dim(w_out, k * width, width, 1)
    w_theirs = lax.dynamic_slice_in_dim(w_out, (1 - k) * width, width, 1)
    w_next = to_chip(w_mine, 1)

    part = (rows + pad, features)
    weights = (w_query, key_matrix, value_matrix)
    (both,) = call(
        project_both_kernel,
        "project_both",
        (mine[2], theirs[2], new_columns, *weights),
        [(part, bf16)],
        [pltpu.VMEM((rows + 2 * ROW_TILE, depth), bf16)],
    )
    new_columns, w_next = lax.optimization_barrier((new_columns, w_next))
    own_part, first, second = call(
        project_kernel,
        "project",
        (own, *mine[:2], *theirs[:2], new_columns, *weights),
        [(part, f32)] + [(part, bf16)] * 2,
        [pltpu.VMEM((3 * rows + 2 * ROW_TILE, depth), bf16)],
    )

    w_later, _ = lax.optimization_barrier((w_theirs, both))
    w_next_other = lax.ppermute(w_later, "tp", [(i, i ^ 3) for i in range(tp)])

    first, second, both = to_partners([first, second, both])
    (total,) = call(add_kernel, "add_both", (own_part, both), [(part, f32)])
    held, new = call(
        add_last_kernel,
        "add_last",
        (total, first, second),
        [((rows, features), bf16), ((pad, features), bf16)],
    )

    gathered = [held, *in_order(KEYS, to_partners([held] * (steps - 1)))]
    new, w_next_other = lax.optimization_barrier((new, w_next_other))
    block_rows = steps * rows // block_map.shape[0]

    keys = steps * rows
    masks = call(
        functools.partial(mask_kernel, block_rows),
        "mask",
        (block_map, lengths),
        [((keys, keys), f32), ((2 * ROW_TILE, keys), f32)],
        spaces=[smem()] * 2,
    )

    def attend(sent, *extra):
        (attended,) = call(
            functools.partial(attend_kernel, sent, block_rows, 1.0 / math.sqrt(HEAD_SIZE)),
            "attend_sent" if sent else "attend_kept",
            (*gathered, new, *masks, *extra),
            [((keys // 2 + pad, q_width), bf16)],
        )
        return attended

    sent = attend(True)
    got = to_chip(sent, 1)
    kept = attend(False, sent)
    w_last, _ = lax.optimization_barrier((w_theirs, held))
    w_other = to_core(w_last)

    block = (block_rows + pad, width)
    (total,) = call(
        output_kernel,
        "project_out",
        (kept, to_core(kept), got, w_out, w_other, w_next),
        [((kept.shape[0], width), f32)],
    )
    outs = call(
        functools.partial(output_last_kernel, block_rows),
        "project_last",
        (total, to_core(got), w_next_other),
        [(block, bf16)] * steps,
    )

    slots = call(
        relay_kernel,
        "relay",
        [outs[0], *in_order(OUTPUTS, to_partners(outs[1:]))],
        [(block if i % 2 == 0 else (block_rows, width), bf16) for i in range(steps)],
    )
    arrived = [to_chip(slot, step) for step, slot in enumerate(slots[1:], 1)]
    slots = [slots[0], *in_order(HEADS, arrived)]
    return tuple(
        call(finish_kernel, "finish", slots, [((rows, width), bf16), ((count, width), bf16)])
    )


floor_value = -1e30


def initial_positions(block_map, first_row, row_count, block_rows):
    row_ids = first_row + jnp.arange(row_count, dtype=jnp.int32)
    block_ids = row_ids // block_rows
    table_ids = jnp.arange(block_map.shape[0], dtype=jnp.int32)
    mapped = jnp.sum(
        jnp.where(block_ids[:, None] == table_ids[None, :], block_map[None, :], 0), axis=1
    )
    return mapped * block_rows + row_ids % block_rows


def request_index(positions, request_ends):
    return jnp.sum((positions[:, None] >= request_ends[None, :]).astype(jnp.int32), axis=1)


def round_weights(weights):
    rounded = weights.astype(jnp.bfloat16)
    rounded = lax.optimization_barrier(rounded)
    return rounded.astype(jnp.float32)


def softmax_parts(
    dec_heads, projected_key_rows, projected_value_rows, owned, kv_heads, head_dim, score_scale
):
    row_count = projected_key_rows.shape[0]
    scores = (
        jnp.einsum(
            "rgjd,tgd->rgjt",
            dec_heads,
            projected_key_rows.reshape(row_count, kv_heads, head_dim),
            preferred_element_type=jnp.float32,
        )
        * score_scale
    )
    scores = jnp.where(owned, scores, floor_value)
    part_peak = jnp.max(scores, axis=3)
    weights = jnp.where(owned, jnp.exp(scores - part_peak[..., None]), 0.0)
    part_total = jnp.sum(weights, axis=3)
    part_mixed = jnp.einsum(
        "rgjt,tgd->rgjd",
        weights.astype(jnp.bfloat16),
        projected_value_rows.reshape(row_count, kv_heads, head_dim),
        preferred_element_type=jnp.float32,
    )
    return (part_peak, part_total, part_mixed)


def on_device_large(
    tokens, new_token_states, w_query, key_matrix, value_matrix, w_out, lengths, block_map
):
    local_rows = tokens.shape[0]
    block_rows = local_rows // 2
    request_count = new_token_states.shape[0]
    head_dim = HEAD_SIZE
    query_width = w_query.shape[1]
    kv_width = key_matrix.shape[1]
    kv_heads = kv_width // head_dim
    query_group_count = query_width // kv_width
    score_scale = 1.0 / math.sqrt(head_dim)
    device = lax.axis_index("ctx")
    request_ends = jnp.cumsum(lengths)
    inputs = jnp.concatenate([tokens, new_token_states], axis=0)
    shard_pieces = (
        lax.all_gather(w_query, "ctx", axis=0, tiled=True),
        lax.all_gather(key_matrix, "ctx", axis=0, tiled=True),
        lax.all_gather(value_matrix, "ctx", axis=0, tiled=True),
    )
    query_all, key_all, value_all = tuple(
        (jnp.dot(inputs, weight, preferred_element_type=jnp.float32) for weight in shard_pieces)
    )
    query_all = query_all.astype(jnp.bfloat16)
    key_all = key_all.astype(jnp.bfloat16)
    value_all = value_all.astype(jnp.bfloat16)
    local_query = query_all[:local_rows]
    local_keys = key_all[:local_rows]
    local_values = value_all[:local_rows]
    dec_query = query_all[local_rows:]
    decode_key_rows = key_all[local_rows:]
    decode_value_rows = value_all[local_rows:]
    token_pos = initial_positions(block_map, device * local_rows, local_rows, block_rows)
    token_request = request_index(token_pos, request_ends)
    query_heads = local_query.reshape(local_rows, kv_heads, query_group_count, head_dim)

    def attend(running, shard_pieces, first_row):
        peak_run, total_run, mixed_run = running
        key_piece, value_piece = shard_pieces
        row_count = key_piece.shape[0]
        key_pos = initial_positions(block_map, first_row, row_count, block_rows)
        key_request = request_index(key_pos, request_ends)
        allowed = (key_request[None, :] == token_request[:, None]) & (
            key_pos[None, :] <= token_pos[:, None]
        )
        scores = (
            jnp.einsum(
                "tgjd,kgd->gjtk",
                query_heads,
                key_piece.reshape(row_count, kv_heads, head_dim),
                preferred_element_type=jnp.float32,
            )
            * score_scale
        )
        scores = jnp.where(allowed, scores, floor_value)
        peak_new = jnp.maximum(peak_run, jnp.max(scores, axis=3))
        weights = jnp.where(allowed, jnp.exp(scores - peak_new[..., None]), 0.0)
        rescale = jnp.exp(peak_run - peak_new)
        total_new = total_run * rescale + jnp.sum(weights, axis=3)
        mixed_new = mixed_run * rescale[..., None] + jnp.einsum(
            "gjtk,kgd->gjtd",
            weights.astype(jnp.bfloat16),
            value_piece.reshape(row_count, kv_heads, head_dim),
            preferred_element_type=jnp.float32,
        )
        return (peak_new, total_new, mixed_new)

    start_state = (
        jnp.full((kv_heads, query_group_count, local_rows), floor_value, jnp.float32),
        jnp.zeros((kv_heads, query_group_count, local_rows), jnp.float32),
        jnp.zeros((kv_heads, query_group_count, local_rows, head_dim), jnp.float32),
    )
    dec_heads = dec_query.reshape(request_count, kv_heads, query_group_count, head_dim)
    request_ids = jnp.arange(request_count, dtype=jnp.int32)
    cache_keys, cache_values = (
        lax.all_gather(local_keys, "ctx", axis=0, tiled=True),
        lax.all_gather(local_values, "ctx", axis=0, tiled=True),
    )
    total_rows = cache_keys.shape[0]
    shard_count = total_rows // local_rows
    limit = max(1, 1024 // local_rows)
    step_rows = local_rows * math.gcd(shard_count, 1 << limit.bit_length() - 1)

    def key_step(running, step_index):
        first_row = step_index * step_rows
        pieces = (
            lax.dynamic_slice_in_dim(cache_keys, first_row, step_rows, 0),
            lax.dynamic_slice_in_dim(cache_values, first_row, step_rows, 0),
        )
        return (attend(running, pieces, first_row), None)

    final_state, unused = lax.scan(
        key_step, start_state, jnp.arange(total_rows // step_rows, dtype=jnp.int32)
    )
    peak_run, total_run, mixed_run = final_state
    cache_pos = (
        block_map[:, None] * block_rows + jnp.arange(block_rows, dtype=jnp.int32)[None, :]
    ).reshape(total_rows)
    cache_request = request_index(cache_pos, request_ends)
    owned = (cache_request[None, :] == request_ids[:, None])[:, None, None, :]
    cache_peak, cache_total, cache_mixed = softmax_parts(
        dec_heads, cache_keys, cache_values, owned, kv_heads, head_dim, score_scale
    )
    attended = (
        (mixed_run / total_run[..., None]).transpose(2, 0, 1, 3).reshape(local_rows, query_width)
    )
    attended = attended.astype(jnp.bfloat16)
    own_keys = decode_key_rows.reshape(request_count, kv_heads, 1, head_dim).astype(jnp.float32)
    own_values = decode_value_rows.reshape(request_count, kv_heads, 1, head_dim).astype(jnp.float32)
    self_scores = jnp.sum(dec_heads.astype(jnp.float32) * own_keys, axis=3) * score_scale
    peak_all = jnp.maximum(cache_peak, self_scores)
    rescale = jnp.exp(cache_peak - peak_all)
    self_weights = jnp.exp(self_scores - peak_all)
    dec_total = cache_total * rescale + self_weights
    dec_mixed = (
        cache_mixed * rescale[..., None] + round_weights(self_weights)[..., None] * own_values
    )
    dec_attn = (
        (dec_mixed / dec_total[..., None]).reshape(request_count, query_width).astype(jnp.bfloat16)
    )
    attended_all = jnp.concatenate([attended, dec_attn], axis=0)
    head_block = lax.all_gather(w_out, "ctx", axis=1, tiled=True)
    column_block = lax.all_to_all(head_block, "tp", split_axis=1, concat_axis=0, tiled=True)
    summed_rows = jnp.dot(
        lax.all_gather(attended_all, "tp", axis=1, tiled=True),
        column_block,
        preferred_element_type=jnp.float32,
    )
    summed_rows = summed_rows.astype(jnp.bfloat16)
    return (summed_rows[:local_rows], summed_rows[local_rows:])

def solution(mesh):
    steps, tp = mesh.shape["ctx"], mesh.shape["tp"]

    def on_device(tokens, *rest):
        one_head = rest[2].shape[1] == HEAD_SIZE
        two_blocks = rest[-1].shape[0] == 2 * steps
        few = tokens.shape[0] * steps <= 1024
        small = steps == 4 and tp == 8 and one_head and two_blocks and few
        if small:
            return on_device_small(steps, tp, tokens, *rest)
        return on_device_large(tokens, *rest)

    return jax.shard_map(
        on_device,
        mesh=mesh,
        in_specs=(
            P("ctx", None),
            P(),
            P("ctx", "tp"),
            P("ctx", "tp"),
            P("ctx", "tp"),
            P("tp", "ctx"),
            P(),
            P(),
        ),
        out_specs=(P("ctx", "tp"), P(None, "tp")),
        check_vma=False,
    )
```

```python
import functools
import math

import jax
import jax.numpy as jnp
from jax import lax
from jax.experimental import pallas as pl
from jax.experimental.pallas import tpu as pltpu
from jax.sharding import PartitionSpec as P

HEAD_SIZE = 128
FLOOR = -1e30
LAST = 1 << 30
ROW_TILE = 8
VMEM_BYTES = 24 * 1024 * 1024
KEYS, OUTPUTS, HEADS = (2, 1, 0), (2, 0, 1), (2, 1, 0)


def vmem():
    return pl.BlockSpec(memory_space=pltpu.VMEM)


def smem():
    return pl.BlockSpec(memory_space=pltpu.SMEM)


def in_order(order, values):
    return [values[i] for i in order]


def put_back(order, values):
    return [values[order.index(i)] for i in range(len(order))]


def place():
    t = lax.axis_index("tp")
    return lax.axis_index("ctx"), t // 2, t % 2


def fill_rows(inputs, number, mine, theirs):
    _, _, k = place()
    rows = mine.shape[0]
    for core, block in ((k, mine), (1 - k, theirs)):
        first = 2 * rows * number + core * rows
        inputs[pl.ds(pl.multiple_of(first, rows), rows), :] = block[...]


def fill_new(inputs, new):
    count = new.shape[0]
    tail = inputs.shape[0] - 2 * ROW_TILE
    inputs[tail:, :] = jnp.zeros_like(inputs[tail:, :])
    inputs[tail : tail + count, :] = new[...]


def project_both_kernel(mine, theirs, new, wq, wk, wv, out, inputs):
    fill_rows(inputs, 0, mine, theirs)
    fill_new(inputs, new)
    x = inputs[...]
    column = 0
    for weight in (wq[...], jnp.concatenate([wk[...], wv[...]], axis=1)):
        part = jnp.dot(x, weight, preferred_element_type=jnp.float32)
        out[:, column : column + weight.shape[1]] = part[: out.shape[0]].astype(out.dtype)
        column += weight.shape[1]


def project_kernel(own, mine1, mine2, theirs1, theirs2, new, wq, wk, wv, *refs):
    held, first, second, inputs = refs
    rows = own.shape[0]
    tail = 3 * rows
    pad = held.shape[0] - rows
    inputs[:rows, :] = own[...]
    fill_rows(inputs, 1, mine1, theirs1)
    fill_rows(inputs, 2, mine2, theirs2)
    fill_new(inputs, new)
    x = inputs[...]
    column = 0
    for weight in (wq[...], jnp.concatenate([wk[...], wv[...]], axis=1)):
        part = jnp.dot(x, weight, preferred_element_type=jnp.float32)
        to = slice(column, column + weight.shape[1])
        for step, out in enumerate((held, first, second)):
            out[:rows, to] = part[step * rows : (step + 1) * rows].astype(out.dtype)
            out[rows:, to] = part[tail : tail + pad].astype(out.dtype)
        column += weight.shape[1]


def add_kernel(held, part, out):
    out[...] = held[...] + part[...].astype(jnp.float32)


def add_last_kernel(total, first, second, held, new):
    rows = held.shape[0]
    added = first[...].astype(jnp.float32) + second[...].astype(jnp.float32)
    added = (total[...] + added).astype(held.dtype)
    held[...] = added[:rows]
    new[...] = added[rows:]


def request_of(position, ends):
    found = jnp.zeros_like(position)
    for end in ends:
        found = found + jnp.where(position >= end, 1, 0)
    return found


def mask_kernel(block_rows, block_map, lengths, rows_mask, new_mask):
    ends, total = [], 0
    for request in range(lengths.shape[0]):
        total = total + lengths[request]
        ends.append(total)
    c, _, _ = place()
    count = block_map.shape[0]
    per_device = 2
    devices = [per_device * (c ^ mask) for mask in range(count // per_device)]

    def labels(shape, axis, held):
        index = lax.broadcasted_iota(jnp.int32, shape, axis)
        position = jnp.zeros(shape, jnp.int32)
        for number, block in enumerate(held):
            start = number * block_rows
            inside = (index >= start) & (index < start + block_rows)
            position = jnp.where(inside, block_map[block] * block_rows + index - start, position)
        return position, request_of(position, ends)

    keys = new_mask.shape[1]
    halves = [first + number for number in range(per_device) for first in devices]
    q_position, q_request = labels((keys, 1), 0, halves)
    held = [first + number for first in devices for number in range(per_device)]
    k_position, k_request = labels((1, keys), 1, held)
    allowed = (q_request == k_request) & (k_position <= q_position)
    rows_mask[...] = jnp.where(allowed, 0.0, FLOOR)
    request = lax.broadcasted_iota(jnp.int32, (new_mask.shape[0], 1), 0)
    new_mask[...] = jnp.where(request == k_request, 0.0, FLOOR)


def attend_kernel(sent, block_rows, scale, *refs):
    blocks, (new, rows_mask, new_mask), refs = [refs[0], *put_back(KEYS, refs[1:4])], refs[4:7], refs[7:]
    attended = refs[-1]
    features = blocks[0].shape[1]
    head = HEAD_SIZE
    q_width = features - 2 * head
    pad = new.shape[0]
    tail = len(blocks) * block_rows
    _, z, _ = place()
    half = 1 - z % 2 if sent else z % 2
    mask = rows_mask[pl.ds(pl.multiple_of(half * tail, tail), tail), :]
    if sent:
        new_rows = new_mask.shape[0]
        mask = jnp.concatenate([mask, new_mask[...]], axis=0)
        zeros = jnp.zeros((new_rows - pad, features), new.dtype)
        news = jnp.concatenate([new[...], zeros], axis=0)

    def columns(number):
        return slice(number * head, (number + 1) * head)

    def whole(number):
        return jnp.concatenate([block[:, columns(number)] for block in blocks], axis=0)

    def queries(number):
        taken = pl.ds(pl.multiple_of(half * block_rows, block_rows), block_rows)
        parts = [block[taken, columns(number)] for block in blocks]
        return jnp.concatenate(parts + ([news[:, columns(number)]] if sent else []), axis=0)

    key_at, value_at = q_width // head, q_width // head + 1
    keys, values = whole(key_at), whole(value_at)
    for number in range(q_width // head):
        at = columns(number)
        scores = lax.dot_general(
            queries(number), keys, (((1,), (1,)), ((), ())), preferred_element_type=jnp.float32
        )
        scores = scores * scale + mask
        peak = jnp.max(scores, axis=1, keepdims=True)
        if sent:
            own = news[:, at].astype(jnp.float32) * news[:, columns(key_at)].astype(jnp.float32)
            own = jnp.sum(own, axis=1, keepdims=True) * scale
            new_peak = jnp.maximum(peak[tail:], own)
            peak = jnp.concatenate([peak[:tail], new_peak], axis=0)
        weights = jnp.exp(scores - peak)
        denom = jnp.sum(weights, axis=1, keepdims=True)
        mixed = jnp.dot(weights.astype(jnp.bfloat16), values, preferred_element_type=jnp.float32)
        attended[:tail, at] = (mixed[:tail] / denom[:tail]).astype(jnp.bfloat16)
        if sent:
            weight = jnp.exp(own - new_peak)
            rounded = weight.astype(jnp.bfloat16).astype(jnp.float32)
            new_mixed = mixed[tail:] + rounded * news[:, columns(value_at)].astype(jnp.float32)
            new_mixed = new_mixed / (denom[tail:] + weight)
            attended[tail:, at] = new_mixed[:pad].astype(jnp.bfloat16)
    if not sent:
        attended[tail:, :] = refs[0][tail:, :]


def output_kernel(*refs):
    heads, (w_own, *weights), total = refs[:3], refs[3:6], refs[6]
    _, _, k = place()
    width = total.shape[1]
    w_mine = w_own[:, pl.ds(pl.multiple_of(k * width, width), width)]
    added = jnp.dot(heads[0][...], w_mine, preferred_element_type=jnp.float32)
    for ref, weight in zip(heads[1:], weights):
        added += jnp.dot(ref[...], weight[...], preferred_element_type=jnp.float32)
    total[...] = added


def output_last_kernel(rows, total, heads, weight, *outs):
    added = total[...] + jnp.dot(heads[...], weight[...], preferred_element_type=jnp.float32)
    added = added.astype(outs[0].dtype)
    for number, out in enumerate(outs):
        out[:rows, :] = added[number * rows : (number + 1) * rows]
        out[rows:, :] = added[len(outs) * rows :]


def relay_kernel(*refs):
    blocks, outs = [refs[0], *put_back(OUTPUTS, refs[1:4])], refs[4:]
    c, z, _ = place()
    for slot, out in enumerate(outs):
        for mask, block in enumerate(blocks):

            @pl.when((c ^ z ^ slot) == mask)
            def _(out=out, block=block):
                out[...] = block[: out.shape[0], :]


def finish_kernel(*refs):
    parts, (prefill, decode) = [refs[0], *put_back(HEADS, refs[1:4])], refs[4:]
    _, z, _ = place()
    rows = prefill.shape[0] // 2
    for odd in range(2):
        total = parts[odd][...].astype(jnp.float32) + parts[odd + 2][...].astype(jnp.float32)
        total = total.astype(prefill.dtype)
        half = z % 2 if odd == 0 else 1 - z % 2
        prefill[pl.ds(pl.multiple_of(half * rows, rows), rows), :] = total[:rows]
        if odd == 0:
            decode[...] = total[rows : rows + decode.shape[0]]


def on_device_small(
    steps, tp, tokens, new_token_states, w_query, key_matrix, value_matrix, w_out, lengths, block_map
):
    bf16, f32 = jnp.bfloat16, jnp.float32
    rows = tokens.shape[0]
    half = rows // 2
    depth = w_query.shape[0]
    count = new_token_states.shape[0]
    pad = -(-count // ROW_TILE) * ROW_TILE
    q_width = w_query.shape[1]
    features = q_width + 2 * key_matrix.shape[1]
    width = w_out.shape[1] // 2
    all_rows = steps * rows + pad

    def to_core(value):
        return lax.ppermute(value, "tp", [(i, i ^ 1) for i in range(tp)])

    def to_chip(value, step):
        return lax.ppermute(value, "tp", [(i, i ^ (2 * step)) for i in range(tp)])

    def to_partners(values):
        return [
            lax.ppermute(value, "ctx", [(i, i ^ mask) for i in range(steps)])
            for mask, value in enumerate(values, 1)
        ]

    def call(kernel, name, inputs, shapes, scratch=(), spaces=None):
        return pl.pallas_call(
            kernel,
            out_shape=[jax.ShapeDtypeStruct(shape, kind) for shape, kind in shapes],
            in_specs=spaces or [vmem()] * len(inputs),
            out_specs=[vmem()] * len(shapes),
            scratch_shapes=list(scratch),
            compiler_params=pltpu.CompilerParams(vmem_limit_bytes=VMEM_BYTES),
            name=name,
        )(*inputs)

    c, _, k = place()
    sent = [
        lax.dynamic_slice(tokens, (k * half, (c ^ mask) * depth), (half, depth))
        for mask in range(1, steps)
    ]
    own = lax.dynamic_slice_in_dim(tokens, c * depth, depth, 1)
    new_columns = lax.dynamic_slice_in_dim(new_token_states, c * depth, depth, 1)
    mine = to_partners(sent)
    mine[2], own = lax.optimization_barrier((mine[2], own))
    theirs = [to_core(value) for value in mine]

    w_mine = lax.dynamic_slice_in_dim(w_out, k * width, width, 1)
    w_theirs = lax.dynamic_slice_in_dim(w_out, (1 - k) * width, width, 1)
    w_next = to_chip(w_mine, 1)

    part = (rows + pad, features)
    weights = (w_query, key_matrix, value_matrix)
    (both,) = call(
        project_both_kernel,
        "project_both",
        (mine[2], theirs[2], new_columns, *weights),
        [(part, bf16)],
        [pltpu.VMEM((rows + 2 * ROW_TILE, depth), bf16)],
    )
    new_columns, w_next = lax.optimization_barrier((new_columns, w_next))
    own_part, first, second = call(
        project_kernel,
        "project",
        (own, *mine[:2], *theirs[:2], new_columns, *weights),
        [(part, f32)] + [(part, bf16)] * 2,
        [pltpu.VMEM((3 * rows + 2 * ROW_TILE, depth), bf16)],
    )

    w_later, _ = lax.optimization_barrier((w_theirs, both))
    w_next_other = lax.ppermute(w_later, "tp", [(i, i ^ 3) for i in range(tp)])

    first, second, both = to_partners([first, second, both])
    (total,) = call(add_kernel, "add_both", (own_part, both), [(part, f32)])
    held, new = call(
        add_last_kernel,
        "add_last",
        (total, first, second),
        [((rows, features), bf16), ((pad, features), bf16)],
    )

    gathered = [held, *in_order(KEYS, to_partners([held] * (steps - 1)))]
    new, w_next_other = lax.optimization_barrier((new, w_next_other))
    block_rows = steps * rows // block_map.shape[0]

    keys = steps * rows
    masks = call(
        functools.partial(mask_kernel, block_rows),
        "mask",
        (block_map, lengths),
        [((keys, keys), f32), ((2 * ROW_TILE, keys), f32)],
        spaces=[smem()] * 2,
    )

    def attend(sent, *extra):
        (attended,) = call(
            functools.partial(attend_kernel, sent, block_rows, 1.0 / math.sqrt(HEAD_SIZE)),
            "attend_sent" if sent else "attend_kept",
            (*gathered, new, *masks, *extra),
            [((keys // 2 + pad, q_width), bf16)],
        )
        return attended

    sent = attend(True)
    got = to_chip(sent, 1)
    kept = attend(False, sent)
    w_last, _ = lax.optimization_barrier((w_theirs, held))
    w_other = to_core(w_last)

    block = (block_rows + pad, width)
    (total,) = call(
        output_kernel,
        "project_out",
        (kept, to_core(kept), got, w_out, w_other, w_next),
        [((kept.shape[0], width), f32)],
    )
    outs = call(
        functools.partial(output_last_kernel, block_rows),
        "project_last",
        (total, to_core(got), w_next_other),
        [(block, bf16)] * steps,
    )

    slots = call(
        relay_kernel,
        "relay",
        [outs[0], *in_order(OUTPUTS, to_partners(outs[1:]))],
        [(block if i % 2 == 0 else (block_rows, width), bf16) for i in range(steps)],
    )
    arrived = [to_chip(slot, step) for step, slot in enumerate(slots[1:], 1)]
    slots = [slots[0], *in_order(HEADS, arrived)]
    return tuple(
        call(finish_kernel, "finish", slots, [((rows, width), bf16), ((count, width), bf16)])
    )


floor_value = -1e30


def initial_positions(block_map, first_row, row_count, block_rows):
    row_ids = first_row + jnp.arange(row_count, dtype=jnp.int32)
    block_ids = row_ids // block_rows
    table_ids = jnp.arange(block_map.shape[0], dtype=jnp.int32)
    mapped = jnp.sum(
        jnp.where(block_ids[:, None] == table_ids[None, :], block_map[None, :], 0), axis=1
    )
    return mapped * block_rows + row_ids % block_rows


def request_index(positions, request_ends):
    return jnp.sum((positions[:, None] >= request_ends[None, :]).astype(jnp.int32), axis=1)


def round_weights(weights):
    rounded = weights.astype(jnp.bfloat16)
    rounded = lax.optimization_barrier(rounded)
    return rounded.astype(jnp.float32)


def softmax_parts(
    dec_heads, projected_key_rows, projected_value_rows, owned, kv_heads, head_dim, score_scale
):
    row_count = projected_key_rows.shape[0]
    scores = (
        jnp.einsum(
            "rgjd,tgd->rgjt",
            dec_heads,
            projected_key_rows.reshape(row_count, kv_heads, head_dim),
            preferred_element_type=jnp.float32,
        )
        * score_scale
    )
    scores = jnp.where(owned, scores, floor_value)
    part_peak = jnp.max(scores, axis=3)
    weights = jnp.where(owned, jnp.exp(scores - part_peak[..., None]), 0.0)
    part_total = jnp.sum(weights, axis=3)
    part_mixed = jnp.einsum(
        "rgjt,tgd->rgjd",
        weights.astype(jnp.bfloat16),
        projected_value_rows.reshape(row_count, kv_heads, head_dim),
        preferred_element_type=jnp.float32,
    )
    return (part_peak, part_total, part_mixed)


def on_device_large(
    tokens, new_token_states, w_query, key_matrix, value_matrix, w_out, lengths, block_map
):
    local_rows = tokens.shape[0]
    block_rows = local_rows // 2
    request_count = new_token_states.shape[0]
    head_dim = HEAD_SIZE
    query_width = w_query.shape[1]
    kv_width = key_matrix.shape[1]
    kv_heads = kv_width // head_dim
    query_group_count = query_width // kv_width
    score_scale = 1.0 / math.sqrt(head_dim)
    device = lax.axis_index("ctx")
    request_ends = jnp.cumsum(lengths)
    inputs = jnp.concatenate([tokens, new_token_states], axis=0)
    shard_pieces = (
        lax.all_gather(w_query, "ctx", axis=0, tiled=True),
        lax.all_gather(key_matrix, "ctx", axis=0, tiled=True),
        lax.all_gather(value_matrix, "ctx", axis=0, tiled=True),
    )
    query_all, key_all, value_all = tuple(
        (jnp.dot(inputs, weight, preferred_element_type=jnp.float32) for weight in shard_pieces)
    )
    query_all = query_all.astype(jnp.bfloat16)
    key_all = key_all.astype(jnp.bfloat16)
    value_all = value_all.astype(jnp.bfloat16)
    local_query = query_all[:local_rows]
    local_keys = key_all[:local_rows]
    local_values = value_all[:local_rows]
    dec_query = query_all[local_rows:]
    decode_key_rows = key_all[local_rows:]
    decode_value_rows = value_all[local_rows:]
    token_pos = initial_positions(block_map, device * local_rows, local_rows, block_rows)
    token_request = request_index(token_pos, request_ends)
    query_heads = local_query.reshape(local_rows, kv_heads, query_group_count, head_dim)

    def attend(running, shard_pieces, first_row):
        peak_run, total_run, mixed_run = running
        key_piece, value_piece = shard_pieces
        row_count = key_piece.shape[0]
        key_pos = initial_positions(block_map, first_row, row_count, block_rows)
        key_request = request_index(key_pos, request_ends)
        allowed = (key_request[None, :] == token_request[:, None]) & (
            key_pos[None, :] <= token_pos[:, None]
        )
        scores = (
            jnp.einsum(
                "tgjd,kgd->gjtk",
                query_heads,
                key_piece.reshape(row_count, kv_heads, head_dim),
                preferred_element_type=jnp.float32,
            )
            * score_scale
        )
        scores = jnp.where(allowed, scores, floor_value)
        peak_new = jnp.maximum(peak_run, jnp.max(scores, axis=3))
        weights = jnp.where(allowed, jnp.exp(scores - peak_new[..., None]), 0.0)
        rescale = jnp.exp(peak_run - peak_new)
        total_new = total_run * rescale + jnp.sum(weights, axis=3)
        mixed_new = mixed_run * rescale[..., None] + jnp.einsum(
            "gjtk,kgd->gjtd",
            weights.astype(jnp.bfloat16),
            value_piece.reshape(row_count, kv_heads, head_dim),
            preferred_element_type=jnp.float32,
        )
        return (peak_new, total_new, mixed_new)

    start_state = (
        jnp.full((kv_heads, query_group_count, local_rows), floor_value, jnp.float32),
        jnp.zeros((kv_heads, query_group_count, local_rows), jnp.float32),
        jnp.zeros((kv_heads, query_group_count, local_rows, head_dim), jnp.float32),
    )
    dec_heads = dec_query.reshape(request_count, kv_heads, query_group_count, head_dim)
    request_ids = jnp.arange(request_count, dtype=jnp.int32)
    cache_keys, cache_values = (
        lax.all_gather(local_keys, "ctx", axis=0, tiled=True),
        lax.all_gather(local_values, "ctx", axis=0, tiled=True),
    )
    total_rows = cache_keys.shape[0]
    shard_count = total_rows // local_rows
    limit = max(1, 1024 // local_rows)
    step_rows = local_rows * math.gcd(shard_count, 1 << limit.bit_length() - 1)

    def key_step(running, step_index):
        first_row = step_index * step_rows
        pieces = (
            lax.dynamic_slice_in_dim(cache_keys, first_row, step_rows, 0),
            lax.dynamic_slice_in_dim(cache_values, first_row, step_rows, 0),
        )
        return (attend(running, pieces, first_row), None)

    final_state, unused = lax.scan(
        key_step, start_state, jnp.arange(total_rows // step_rows, dtype=jnp.int32)
    )
    peak_run, total_run, mixed_run = final_state
    cache_pos = (
        block_map[:, None] * block_rows + jnp.arange(block_rows, dtype=jnp.int32)[None, :]
    ).reshape(total_rows)
    cache_request = request_index(cache_pos, request_ends)
    owned = (cache_request[None, :] == request_ids[:, None])[:, None, None, :]
    cache_peak, cache_total, cache_mixed = softmax_parts(
        dec_heads, cache_keys, cache_values, owned, kv_heads, head_dim, score_scale
    )
    attended = (
        (mixed_run / total_run[..., None]).transpose(2, 0, 1, 3).reshape(local_rows, query_width)
    )
    attended = attended.astype(jnp.bfloat16)
    own_keys = decode_key_rows.reshape(request_count, kv_heads, 1, head_dim).astype(jnp.float32)
    own_values = decode_value_rows.reshape(request_count, kv_heads, 1, head_dim).astype(jnp.float32)
    self_scores = jnp.sum(dec_heads.astype(jnp.float32) * own_keys, axis=3) * score_scale
    peak_all = jnp.maximum(cache_peak, self_scores)
    rescale = jnp.exp(cache_peak - peak_all)
    self_weights = jnp.exp(self_scores - peak_all)
    dec_total = cache_total * rescale + self_weights
    dec_mixed = (
        cache_mixed * rescale[..., None] + round_weights(self_weights)[..., None] * own_values
    )
    dec_attn = (
        (dec_mixed / dec_total[..., None]).reshape(request_count, query_width).astype(jnp.bfloat16)
    )
    attended_all = jnp.concatenate([attended, dec_attn], axis=0)
    head_block = lax.all_gather(w_out, "ctx", axis=1, tiled=True)
    column_block = lax.all_to_all(head_block, "tp", split_axis=1, concat_axis=0, tiled=True)
    summed_rows = jnp.dot(
        lax.all_gather(attended_all, "tp", axis=1, tiled=True),
        column_block,
        preferred_element_type=jnp.float32,
    )
    summed_rows = summed_rows.astype(jnp.bfloat16)
    return (summed_rows[:local_rows], summed_rows[local_rows:])

def solution(mesh):
    steps, tp = mesh.shape["ctx"], mesh.shape["tp"]

    def on_device(tokens, *rest):
        one_head = rest[2].shape[1] == HEAD_SIZE
        two_blocks = rest[-1].shape[0] == 2 * steps
        few = tokens.shape[0] * steps <= 1024
        small = steps == 4 and tp == 8 and one_head and two_blocks and few
        if small:
            return on_device_small(steps, tp, tokens, *rest)
        return on_device_large(tokens, *rest)

    return jax.shard_map(
        on_device,
        mesh=mesh,
        in_specs=(
            P("ctx", None),
            P(),
            P("ctx", "tp"),
            P("ctx", "tp"),
            P("ctx", "tp"),
            P("tp", "ctx"),
            P(),
            P(),
        ),
        out_specs=(P("ctx", "tp"), P(None, "tp")),
        check_vma=False,
    )
```

```python
import functools
import math

import jax
import jax.numpy as jnp
from jax import lax
from jax.experimental import pallas as pl
from jax.experimental.pallas import tpu as pltpu
from jax.sharding import PartitionSpec as P

HEAD_SIZE = 128
FLOOR = -1e30
LAST = 1 << 30
ROW_TILE = 8
VMEM_BYTES = 24 * 1024 * 1024
KEYS, OUTPUTS, HEADS = (2, 1, 0), (2, 0, 1), (2, 1, 0)


def vmem():
    return pl.BlockSpec(memory_space=pltpu.VMEM)


def smem():
    return pl.BlockSpec(memory_space=pltpu.SMEM)


def in_order(order, values):
    return [values[i] for i in order]


def put_back(order, values):
    return [values[order.index(i)] for i in range(len(order))]


def place():
    t = lax.axis_index("tp")
    return lax.axis_index("ctx"), t // 2, t % 2


def fill_rows(inputs, number, mine, theirs):
    _, _, k = place()
    rows = mine.shape[0]
    for core, block in ((k, mine), (1 - k, theirs)):
        first = 2 * rows * number + core * rows
        inputs[pl.ds(pl.multiple_of(first, rows), rows), :] = block[...]


def fill_new(inputs, new):
    count = new.shape[0]
    tail = inputs.shape[0] - 2 * ROW_TILE
    inputs[tail:, :] = jnp.zeros_like(inputs[tail:, :])
    inputs[tail : tail + count, :] = new[...]


def project_both_kernel(mine, theirs, new, wq, wk, wv, out, inputs):
    fill_rows(inputs, 0, mine, theirs)
    fill_new(inputs, new)
    x = inputs[...]
    column = 0
    for weight in (wq[...], jnp.concatenate([wk[...], wv[...]], axis=1)):
        part = jnp.dot(x, weight, preferred_element_type=jnp.float32)
        out[:, column : column + weight.shape[1]] = part[: out.shape[0]].astype(out.dtype)
        column += weight.shape[1]


def project_kernel(own, mine1, mine2, theirs1, theirs2, new, wq, wk, wv, *refs):
    held, first, second, inputs = refs
    rows = own.shape[0]
    tail = 3 * rows
    pad = held.shape[0] - rows
    inputs[:rows, :] = own[...]
    fill_rows(inputs, 1, mine1, theirs1)
    fill_rows(inputs, 2, mine2, theirs2)
    fill_new(inputs, new)
    x = inputs[...]
    column = 0
    for weight in (wq[...], jnp.concatenate([wk[...], wv[...]], axis=1)):
        part = jnp.dot(x, weight, preferred_element_type=jnp.float32)
        to = slice(column, column + weight.shape[1])
        for step, out in enumerate((held, first, second)):
            out[:rows, to] = part[step * rows : (step + 1) * rows].astype(out.dtype)
            out[rows:, to] = part[tail : tail + pad].astype(out.dtype)
        column += weight.shape[1]


def add_kernel(held, part, out):
    out[...] = held[...] + part[...].astype(jnp.float32)


def add_last_kernel(total, first, second, held, new):
    rows = held.shape[0]
    added = first[...].astype(jnp.float32) + second[...].astype(jnp.float32)
    added = (total[...] + added).astype(held.dtype)
    held[...] = added[:rows]
    new[...] = added[rows:]


def request_of(position, ends):
    found = jnp.zeros_like(position)
    for end in ends:
        found = found + jnp.where(position >= end, 1, 0)
    return found


def mask_kernel(block_rows, block_map, lengths, rows_mask, new_mask):
    ends, total = [], 0
    for request in range(lengths.shape[0]):
        total = total + lengths[request]
        ends.append(total)
    c, _, _ = place()
    count = block_map.shape[0]
    per_device = 2
    devices = [per_device * (c ^ mask) for mask in range(count // per_device)]

    def labels(shape, axis, held):
        index = lax.broadcasted_iota(jnp.int32, shape, axis)
        position = jnp.zeros(shape, jnp.int32)
        for number, block in enumerate(held):
            start = number * block_rows
            inside = (index >= start) & (index < start + block_rows)
            position = jnp.where(inside, block_map[block] * block_rows + index - start, position)
        return position, request_of(position, ends)

    keys = new_mask.shape[1]
    halves = [first + number for number in range(per_device) for first in devices]
    q_position, q_request = labels((keys, 1), 0, halves)
    held = [first + number for first in devices for number in range(per_device)]
    k_position, k_request = labels((1, keys), 1, held)
    allowed = (q_request == k_request) & (k_position <= q_position)
    rows_mask[...] = jnp.where(allowed, 0.0, FLOOR)
    request = lax.broadcasted_iota(jnp.int32, (new_mask.shape[0], 1), 0)
    new_mask[...] = jnp.where(request == k_request, 0.0, FLOOR)


def attend_kernel(sent, block_rows, scale, *refs):
    blocks, (new, rows_mask, new_mask), refs = [refs[0], *put_back(KEYS, refs[1:4])], refs[4:7], refs[7:]
    attended = refs[-1]
    features = blocks[0].shape[1]
    head = HEAD_SIZE
    q_width = features - 2 * head
    pad = new.shape[0]
    tail = len(blocks) * block_rows
    _, z, _ = place()
    half = 1 - z % 2 if sent else z % 2
    mask = rows_mask[pl.ds(pl.multiple_of(half * tail, tail), tail), :]
    if sent:
        new_rows = new_mask.shape[0]
        mask = jnp.concatenate([mask, new_mask[...]], axis=0)
        zeros = jnp.zeros((new_rows - pad, features), new.dtype)
        news = jnp.concatenate([new[...], zeros], axis=0)

    def columns(number):
        return slice(number * head, (number + 1) * head)

    def whole(number):
        return jnp.concatenate([block[:, columns(number)] for block in blocks], axis=0)

    def queries(number):
        taken = pl.ds(pl.multiple_of(half * block_rows, block_rows), block_rows)
        parts = [block[taken, columns(number)] for block in blocks]
        return jnp.concatenate(parts + ([news[:, columns(number)]] if sent else []), axis=0)

    key_at, value_at = q_width // head, q_width // head + 1
    keys, values = whole(key_at), whole(value_at)
    for number in range(q_width // head):
        at = columns(number)
        scores = lax.dot_general(
            queries(number), keys, (((1,), (1,)), ((), ())), preferred_element_type=jnp.float32
        )
        scores = scores * scale + mask
        peak = jnp.max(scores, axis=1, keepdims=True)
        if sent:
            own = news[:, at].astype(jnp.float32) * news[:, columns(key_at)].astype(jnp.float32)
            own = jnp.sum(own, axis=1, keepdims=True) * scale
            new_peak = jnp.maximum(peak[tail:], own)
            peak = jnp.concatenate([peak[:tail], new_peak], axis=0)
        weights = jnp.exp(scores - peak)
        denom = jnp.sum(weights, axis=1, keepdims=True)
        mixed = jnp.dot(weights.astype(jnp.bfloat16), values, preferred_element_type=jnp.float32)
        attended[:tail, at] = (mixed[:tail] / denom[:tail]).astype(jnp.bfloat16)
        if sent:
            weight = jnp.exp(own - new_peak)
            rounded = weight.astype(jnp.bfloat16).astype(jnp.float32)
            new_mixed = mixed[tail:] + rounded * news[:, columns(value_at)].astype(jnp.float32)
            new_mixed = new_mixed / (denom[tail:] + weight)
            attended[tail:, at] = new_mixed[:pad].astype(jnp.bfloat16)
    if not sent:
        attended[tail:, :] = refs[0][tail:, :]


def output_kernel(*refs):
    heads, (w_own, *weights), total = refs[:3], refs[3:6], refs[6]
    _, _, k = place()
    width = total.shape[1]
    w_mine = w_own[:, pl.ds(pl.multiple_of(k * width, width), width)]
    added = jnp.dot(heads[0][...], w_mine, preferred_element_type=jnp.float32)
    for ref, weight in zip(heads[1:], weights):
        added += jnp.dot(ref[...], weight[...], preferred_element_type=jnp.float32)
    total[...] = added


def output_last_kernel(rows, total, heads, weight, *outs):
    added = total[...] + jnp.dot(heads[...], weight[...], preferred_element_type=jnp.float32)
    added = added.astype(outs[0].dtype)
    for number, out in enumerate(outs):
        out[:rows, :] = added[number * rows : (number + 1) * rows]
        out[rows:, :] = added[len(outs) * rows :]


def relay_kernel(*refs):
    blocks, outs = [refs[0], *put_back(OUTPUTS, refs[1:4])], refs[4:]
    c, z, _ = place()
    for slot, out in enumerate(outs):
        for mask, block in enumerate(blocks):

            @pl.when((c ^ z ^ slot) == mask)
            def _(out=out, block=block):
                out[...] = block[: out.shape[0], :]


def finish_kernel(*refs):
    parts, (prefill, decode) = [refs[0], *put_back(HEADS, refs[1:4])], refs[4:]
    _, z, _ = place()
    rows = prefill.shape[0] // 2
    for odd in range(2):
        total = parts[odd][...].astype(jnp.float32) + parts[odd + 2][...].astype(jnp.float32)
        total = total.astype(prefill.dtype)
        half = z % 2 if odd == 0 else 1 - z % 2
        prefill[pl.ds(pl.multiple_of(half * rows, rows), rows), :] = total[:rows]
        if odd == 0:
            decode[...] = total[rows : rows + decode.shape[0]]


def on_device_small(
    steps, tp, tokens, new_token_states, w_query, key_matrix, value_matrix, w_out, lengths, block_map
):
    bf16, f32 = jnp.bfloat16, jnp.float32
    rows = tokens.shape[0]
    half = rows // 2
    depth = w_query.shape[0]
    count = new_token_states.shape[0]
    pad = -(-count // ROW_TILE) * ROW_TILE
    q_width = w_query.shape[1]
    features = q_width + 2 * key_matrix.shape[1]
    width = w_out.shape[1] // 2
    all_rows = steps * rows + pad

    def to_core(value):
        return lax.ppermute(value, "tp", [(i, i ^ 1) for i in range(tp)])

    def to_chip(value, step):
        return lax.ppermute(value, "tp", [(i, i ^ (2 * step)) for i in range(tp)])

    def to_partners(values):
        return [
            lax.ppermute(value, "ctx", [(i, i ^ mask) for i in range(steps)])
            for mask, value in enumerate(values, 1)
        ]

    def call(kernel, name, inputs, shapes, scratch=(), spaces=None):
        return pl.pallas_call(
            kernel,
            out_shape=[jax.ShapeDtypeStruct(shape, kind) for shape, kind in shapes],
            in_specs=spaces or [vmem()] * len(inputs),
            out_specs=[vmem()] * len(shapes),
            scratch_shapes=list(scratch),
            compiler_params=pltpu.CompilerParams(vmem_limit_bytes=VMEM_BYTES),
            name=name,
        )(*inputs)

    c, _, k = place()
    sent = [
        lax.dynamic_slice(tokens, (k * half, (c ^ mask) * depth), (half, depth))
        for mask in range(1, steps)
    ]
    own = lax.dynamic_slice_in_dim(tokens, c * depth, depth, 1)
    new_columns = lax.dynamic_slice_in_dim(new_token_states, c * depth, depth, 1)
    mine = to_partners(sent)
    mine[2], own = lax.optimization_barrier((mine[2], own))
    theirs = [to_core(value) for value in mine]

    w_mine = lax.dynamic_slice_in_dim(w_out, k * width, width, 1)
    w_theirs = lax.dynamic_slice_in_dim(w_out, (1 - k) * width, width, 1)
    w_next = to_chip(w_mine, 1)

    part = (rows + pad, features)
    weights = (w_query, key_matrix, value_matrix)
    (both,) = call(
        project_both_kernel,
        "project_both",
        (mine[2], theirs[2], new_columns, *weights),
        [(part, bf16)],
        [pltpu.VMEM((rows + 2 * ROW_TILE, depth), bf16)],
    )
    new_columns, w_next = lax.optimization_barrier((new_columns, w_next))
    own_part, first, second = call(
        project_kernel,
        "project",
        (own, *mine[:2], *theirs[:2], new_columns, *weights),
        [(part, f32)] + [(part, bf16)] * 2,
        [pltpu.VMEM((3 * rows + 2 * ROW_TILE, depth), bf16)],
    )

    w_later, _ = lax.optimization_barrier((w_theirs, both))
    w_next_other = lax.ppermute(w_later, "tp", [(i, i ^ 3) for i in range(tp)])

    first, second, both = to_partners([first, second, both])
    (total,) = call(add_kernel, "add_both", (own_part, both), [(part, f32)])
    held, new = call(
        add_last_kernel,
        "add_last",
        (total, first, second),
        [((rows, features), bf16), ((pad, features), bf16)],
    )

    gathered = [held, *in_order(KEYS, to_partners([held] * (steps - 1)))]
    new, w_next_other = lax.optimization_barrier((new, w_next_other))
    block_rows = steps * rows // block_map.shape[0]

    keys = steps * rows
    masks = call(
        functools.partial(mask_kernel, block_rows),
        "mask",
        (block_map, lengths),
        [((keys, keys), f32), ((2 * ROW_TILE, keys), f32)],
        spaces=[smem()] * 2,
    )

    def attend(sent, *extra):
        (attended,) = call(
            functools.partial(attend_kernel, sent, block_rows, 1.0 / math.sqrt(HEAD_SIZE)),
            "attend_sent" if sent else "attend_kept",
            (*gathered, new, *masks, *extra),
            [((keys // 2 + pad, q_width), bf16)],
        )
        return attended

    sent = attend(True)
    got = to_chip(sent, 1)
    kept = attend(False, sent)
    w_last, _ = lax.optimization_barrier((w_theirs, kept))
    w_other = to_core(w_last)

    block = (block_rows + pad, width)
    (total,) = call(
        output_kernel,
        "project_out",
        (kept, to_core(kept), got, w_out, w_other, w_next),
        [((kept.shape[0], width), f32)],
    )
    outs = call(
        functools.partial(output_last_kernel, block_rows),
        "project_last",
        (total, to_core(got), w_next_other),
        [(block, bf16)] * steps,
    )

    slots = call(
        relay_kernel,
        "relay",
        [outs[0], *in_order(OUTPUTS, to_partners(outs[1:]))],
        [(block if i % 2 == 0 else (block_rows, width), bf16) for i in range(steps)],
    )
    arrived = [to_chip(slot, step) for step, slot in enumerate(slots[1:], 1)]
    slots = [slots[0], *in_order(HEADS, arrived)]
    return tuple(
        call(finish_kernel, "finish", slots, [((rows, width), bf16), ((count, width), bf16)])
    )


floor_value = -1e30


def initial_positions(block_map, first_row, row_count, block_rows):
    row_ids = first_row + jnp.arange(row_count, dtype=jnp.int32)
    block_ids = row_ids // block_rows
    table_ids = jnp.arange(block_map.shape[0], dtype=jnp.int32)
    mapped = jnp.sum(
        jnp.where(block_ids[:, None] == table_ids[None, :], block_map[None, :], 0), axis=1
    )
    return mapped * block_rows + row_ids % block_rows


def request_index(positions, request_ends):
    return jnp.sum((positions[:, None] >= request_ends[None, :]).astype(jnp.int32), axis=1)


def round_weights(weights):
    rounded = weights.astype(jnp.bfloat16)
    rounded = lax.optimization_barrier(rounded)
    return rounded.astype(jnp.float32)


def softmax_parts(
    dec_heads, projected_key_rows, projected_value_rows, owned, kv_heads, head_dim, score_scale
):
    row_count = projected_key_rows.shape[0]
    scores = (
        jnp.einsum(
            "rgjd,tgd->rgjt",
            dec_heads,
            projected_key_rows.reshape(row_count, kv_heads, head_dim),
            preferred_element_type=jnp.float32,
        )
        * score_scale
    )
    scores = jnp.where(owned, scores, floor_value)
    part_peak = jnp.max(scores, axis=3)
    weights = jnp.where(owned, jnp.exp(scores - part_peak[..., None]), 0.0)
    part_total = jnp.sum(weights, axis=3)
    part_mixed = jnp.einsum(
        "rgjt,tgd->rgjd",
        weights.astype(jnp.bfloat16),
        projected_value_rows.reshape(row_count, kv_heads, head_dim),
        preferred_element_type=jnp.float32,
    )
    return (part_peak, part_total, part_mixed)


def on_device_large(
    tokens, new_token_states, w_query, key_matrix, value_matrix, w_out, lengths, block_map
):
    local_rows = tokens.shape[0]
    block_rows = local_rows // 2
    request_count = new_token_states.shape[0]
    head_dim = HEAD_SIZE
    query_width = w_query.shape[1]
    kv_width = key_matrix.shape[1]
    kv_heads = kv_width // head_dim
    query_group_count = query_width // kv_width
    score_scale = 1.0 / math.sqrt(head_dim)
    device = lax.axis_index("ctx")
    request_ends = jnp.cumsum(lengths)
    inputs = jnp.concatenate([tokens, new_token_states], axis=0)
    shard_pieces = (
        lax.all_gather(w_query, "ctx", axis=0, tiled=True),
        lax.all_gather(key_matrix, "ctx", axis=0, tiled=True),
        lax.all_gather(value_matrix, "ctx", axis=0, tiled=True),
    )
    query_all, key_all, value_all = tuple(
        (jnp.dot(inputs, weight, preferred_element_type=jnp.float32) for weight in shard_pieces)
    )
    query_all = query_all.astype(jnp.bfloat16)
    key_all = key_all.astype(jnp.bfloat16)
    value_all = value_all.astype(jnp.bfloat16)
    local_query = query_all[:local_rows]
    local_keys = key_all[:local_rows]
    local_values = value_all[:local_rows]
    dec_query = query_all[local_rows:]
    decode_key_rows = key_all[local_rows:]
    decode_value_rows = value_all[local_rows:]
    token_pos = initial_positions(block_map, device * local_rows, local_rows, block_rows)
    token_request = request_index(token_pos, request_ends)
    query_heads = local_query.reshape(local_rows, kv_heads, query_group_count, head_dim)

    def attend(running, shard_pieces, first_row):
        peak_run, total_run, mixed_run = running
        key_piece, value_piece = shard_pieces
        row_count = key_piece.shape[0]
        key_pos = initial_positions(block_map, first_row, row_count, block_rows)
        key_request = request_index(key_pos, request_ends)
        allowed = (key_request[None, :] == token_request[:, None]) & (
            key_pos[None, :] <= token_pos[:, None]
        )
        scores = (
            jnp.einsum(
                "tgjd,kgd->gjtk",
                query_heads,
                key_piece.reshape(row_count, kv_heads, head_dim),
                preferred_element_type=jnp.float32,
            )
            * score_scale
        )
        scores = jnp.where(allowed, scores, floor_value)
        peak_new = jnp.maximum(peak_run, jnp.max(scores, axis=3))
        weights = jnp.where(allowed, jnp.exp(scores - peak_new[..., None]), 0.0)
        rescale = jnp.exp(peak_run - peak_new)
        total_new = total_run * rescale + jnp.sum(weights, axis=3)
        mixed_new = mixed_run * rescale[..., None] + jnp.einsum(
            "gjtk,kgd->gjtd",
            weights.astype(jnp.bfloat16),
            value_piece.reshape(row_count, kv_heads, head_dim),
            preferred_element_type=jnp.float32,
        )
        return (peak_new, total_new, mixed_new)

    start_state = (
        jnp.full((kv_heads, query_group_count, local_rows), floor_value, jnp.float32),
        jnp.zeros((kv_heads, query_group_count, local_rows), jnp.float32),
        jnp.zeros((kv_heads, query_group_count, local_rows, head_dim), jnp.float32),
    )
    dec_heads = dec_query.reshape(request_count, kv_heads, query_group_count, head_dim)
    request_ids = jnp.arange(request_count, dtype=jnp.int32)
    cache_keys, cache_values = (
        lax.all_gather(local_keys, "ctx", axis=0, tiled=True),
        lax.all_gather(local_values, "ctx", axis=0, tiled=True),
    )
    total_rows = cache_keys.shape[0]
    shard_count = total_rows // local_rows
    limit = max(1, 1024 // local_rows)
    step_rows = local_rows * math.gcd(shard_count, 1 << limit.bit_length() - 1)

    def key_step(running, step_index):
        first_row = step_index * step_rows
        pieces = (
            lax.dynamic_slice_in_dim(cache_keys, first_row, step_rows, 0),
            lax.dynamic_slice_in_dim(cache_values, first_row, step_rows, 0),
        )
        return (attend(running, pieces, first_row), None)

    final_state, unused = lax.scan(
        key_step, start_state, jnp.arange(total_rows // step_rows, dtype=jnp.int32)
    )
    peak_run, total_run, mixed_run = final_state
    cache_pos = (
        block_map[:, None] * block_rows + jnp.arange(block_rows, dtype=jnp.int32)[None, :]
    ).reshape(total_rows)
    cache_request = request_index(cache_pos, request_ends)
    owned = (cache_request[None, :] == request_ids[:, None])[:, None, None, :]
    cache_peak, cache_total, cache_mixed = softmax_parts(
        dec_heads, cache_keys, cache_values, owned, kv_heads, head_dim, score_scale
    )
    attended = (
        (mixed_run / total_run[..., None]).transpose(2, 0, 1, 3).reshape(local_rows, query_width)
    )
    attended = attended.astype(jnp.bfloat16)
    own_keys = decode_key_rows.reshape(request_count, kv_heads, 1, head_dim).astype(jnp.float32)
    own_values = decode_value_rows.reshape(request_count, kv_heads, 1, head_dim).astype(jnp.float32)
    self_scores = jnp.sum(dec_heads.astype(jnp.float32) * own_keys, axis=3) * score_scale
    peak_all = jnp.maximum(cache_peak, self_scores)
    rescale = jnp.exp(cache_peak - peak_all)
    self_weights = jnp.exp(self_scores - peak_all)
    dec_total = cache_total * rescale + self_weights
    dec_mixed = (
        cache_mixed * rescale[..., None] + round_weights(self_weights)[..., None] * own_values
    )
    dec_attn = (
        (dec_mixed / dec_total[..., None]).reshape(request_count, query_width).astype(jnp.bfloat16)
    )
    attended_all = jnp.concatenate([attended, dec_attn], axis=0)
    head_block = lax.all_gather(w_out, "ctx", axis=1, tiled=True)
    column_block = lax.all_to_all(head_block, "tp", split_axis=1, concat_axis=0, tiled=True)
    summed_rows = jnp.dot(
        lax.all_gather(attended_all, "tp", axis=1, tiled=True),
        column_block,
        preferred_element_type=jnp.float32,
    )
    summed_rows = summed_rows.astype(jnp.bfloat16)
    return (summed_rows[:local_rows], summed_rows[local_rows:])

def solution(mesh):
    steps, tp = mesh.shape["ctx"], mesh.shape["tp"]

    def on_device(tokens, *rest):
        one_head = rest[2].shape[1] == HEAD_SIZE
        two_blocks = rest[-1].shape[0] == 2 * steps
        few = tokens.shape[0] * steps <= 1024
        small = steps == 4 and tp == 8 and one_head and two_blocks and few
        if small:
            return on_device_small(steps, tp, tokens, *rest)
        return on_device_large(tokens, *rest)

    return jax.shard_map(
        on_device,
        mesh=mesh,
        in_specs=(
            P("ctx", None),
            P(),
            P("ctx", "tp"),
            P("ctx", "tp"),
            P("ctx", "tp"),
            P("tp", "ctx"),
            P(),
            P(),
        ),
        out_specs=(P("ctx", "tp"), P(None, "tp")),
        check_vma=False,
    )
```

```python
import functools
import math

import jax
import jax.numpy as jnp
from jax import lax
from jax.experimental import pallas as pl
from jax.experimental.pallas import tpu as pltpu
from jax.sharding import PartitionSpec as P

HEAD_SIZE = 128
FLOOR = -1e30
LAST = 1 << 30
ROW_TILE = 8
VMEM_BYTES = 24 * 1024 * 1024
KEYS, OUTPUTS, HEADS = (2, 1, 0), (2, 0, 1), (1, 2, 0)


def vmem():
    return pl.BlockSpec(memory_space=pltpu.VMEM)


def smem():
    return pl.BlockSpec(memory_space=pltpu.SMEM)


def in_order(order, values):
    return [values[i] for i in order]


def put_back(order, values):
    return [values[order.index(i)] for i in range(len(order))]


def place():
    t = lax.axis_index("tp")
    return lax.axis_index("ctx"), t // 2, t % 2


def fill_rows(inputs, number, mine, theirs):
    _, _, k = place()
    rows = mine.shape[0]
    for core, block in ((k, mine), (1 - k, theirs)):
        first = 2 * rows * number + core * rows
        inputs[pl.ds(pl.multiple_of(first, rows), rows), :] = block[...]


def fill_new(inputs, new):
    count = new.shape[0]
    tail = inputs.shape[0] - 2 * ROW_TILE
    inputs[tail:, :] = jnp.zeros_like(inputs[tail:, :])
    inputs[tail : tail + count, :] = new[...]


def project_both_kernel(mine, theirs, new, wq, wk, wv, out, inputs):
    fill_rows(inputs, 0, mine, theirs)
    fill_new(inputs, new)
    x = inputs[...]
    column = 0
    for weight in (wq[...], jnp.concatenate([wk[...], wv[...]], axis=1)):
        part = jnp.dot(x, weight, preferred_element_type=jnp.float32)
        out[:, column : column + weight.shape[1]] = part[: out.shape[0]].astype(out.dtype)
        column += weight.shape[1]


def project_kernel(own, mine1, mine2, theirs1, theirs2, new, wq, wk, wv, *refs):
    held, first, second, inputs = refs
    rows = own.shape[0]
    tail = 3 * rows
    pad = held.shape[0] - rows
    inputs[:rows, :] = own[...]
    fill_rows(inputs, 1, mine1, theirs1)
    fill_rows(inputs, 2, mine2, theirs2)
    fill_new(inputs, new)
    x = inputs[...]
    column = 0
    for weight in (wq[...], jnp.concatenate([wk[...], wv[...]], axis=1)):
        part = jnp.dot(x, weight, preferred_element_type=jnp.float32)
        to = slice(column, column + weight.shape[1])
        for step, out in enumerate((held, first, second)):
            out[:rows, to] = part[step * rows : (step + 1) * rows].astype(out.dtype)
            out[rows:, to] = part[tail : tail + pad].astype(out.dtype)
        column += weight.shape[1]


def add_kernel(held, part, out):
    out[...] = held[...] + part[...].astype(jnp.float32)


def add_last_kernel(total, first, second, held, new):
    rows = held.shape[0]
    added = first[...].astype(jnp.float32) + second[...].astype(jnp.float32)
    added = (total[...] + added).astype(held.dtype)
    held[...] = added[:rows]
    new[...] = added[rows:]


def request_of(position, ends):
    found = jnp.zeros_like(position)
    for end in ends:
        found = found + jnp.where(position >= end, 1, 0)
    return found


def mask_kernel(block_rows, block_map, lengths, rows_mask, new_mask):
    ends, total = [], 0
    for request in range(lengths.shape[0]):
        total = total + lengths[request]
        ends.append(total)
    c, _, _ = place()
    count = block_map.shape[0]
    per_device = 2
    devices = [per_device * (c ^ mask) for mask in range(count // per_device)]

    def labels(shape, axis, held):
        index = lax.broadcasted_iota(jnp.int32, shape, axis)
        position = jnp.zeros(shape, jnp.int32)
        for number, block in enumerate(held):
            start = number * block_rows
            inside = (index >= start) & (index < start + block_rows)
            position = jnp.where(inside, block_map[block] * block_rows + index - start, position)
        return position, request_of(position, ends)

    keys = new_mask.shape[1]
    halves = [first + number for number in range(per_device) for first in devices]
    q_position, q_request = labels((keys, 1), 0, halves)
    held = [first + number for first in devices for number in range(per_device)]
    k_position, k_request = labels((1, keys), 1, held)
    allowed = (q_request == k_request) & (k_position <= q_position)
    rows_mask[...] = jnp.where(allowed, 0.0, FLOOR)
    request = lax.broadcasted_iota(jnp.int32, (new_mask.shape[0], 1), 0)
    new_mask[...] = jnp.where(request == k_request, 0.0, FLOOR)


def attend_kernel(sent, block_rows, scale, *refs):
    blocks, (new, rows_mask, new_mask), refs = [refs[0], *put_back(KEYS, refs[1:4])], refs[4:7], refs[7:]
    attended = refs[-1]
    features = blocks[0].shape[1]
    head = HEAD_SIZE
    q_width = features - 2 * head
    pad = new.shape[0]
    tail = len(blocks) * block_rows
    _, z, _ = place()
    half = 1 - z % 2 if sent else z % 2
    mask = rows_mask[pl.ds(pl.multiple_of(half * tail, tail), tail), :]
    if sent:
        new_rows = new_mask.shape[0]
        mask = jnp.concatenate([mask, new_mask[...]], axis=0)
        zeros = jnp.zeros((new_rows - pad, features), new.dtype)
        news = jnp.concatenate([new[...], zeros], axis=0)

    def columns(number):
        return slice(number * head, (number + 1) * head)

    def whole(number):
        return jnp.concatenate([block[:, columns(number)] for block in blocks], axis=0)

    def queries(number):
        taken = pl.ds(pl.multiple_of(half * block_rows, block_rows), block_rows)
        parts = [block[taken, columns(number)] for block in blocks]
        return jnp.concatenate(parts + ([news[:, columns(number)]] if sent else []), axis=0)

    key_at, value_at = q_width // head, q_width // head + 1
    keys, values = whole(key_at), whole(value_at)
    for number in range(q_width // head):
        at = columns(number)
        scores = lax.dot_general(
            queries(number), keys, (((1,), (1,)), ((), ())), preferred_element_type=jnp.float32
        )
        scores = scores * scale + mask
        peak = jnp.max(scores, axis=1, keepdims=True)
        if sent:
            own = news[:, at].astype(jnp.float32) * news[:, columns(key_at)].astype(jnp.float32)
            own = jnp.sum(own, axis=1, keepdims=True) * scale
            new_peak = jnp.maximum(peak[tail:], own)
            peak = jnp.concatenate([peak[:tail], new_peak], axis=0)
        weights = jnp.exp(scores - peak)
        denom = jnp.sum(weights, axis=1, keepdims=True)
        mixed = jnp.dot(weights.astype(jnp.bfloat16), values, preferred_element_type=jnp.float32)
        attended[:tail, at] = (mixed[:tail] / denom[:tail]).astype(jnp.bfloat16)
        if sent:
            weight = jnp.exp(own - new_peak)
            rounded = weight.astype(jnp.bfloat16).astype(jnp.float32)
            new_mixed = mixed[tail:] + rounded * news[:, columns(value_at)].astype(jnp.float32)
            new_mixed = new_mixed / (denom[tail:] + weight)
            attended[tail:, at] = new_mixed[:pad].astype(jnp.bfloat16)
    if not sent:
        attended[tail:, :] = refs[0][tail:, :]


def output_kernel(*refs):
    heads, (w_own, *weights), total = refs[:3], refs[3:6], refs[6]
    _, _, k = place()
    width = total.shape[1]
    w_mine = w_own[:, pl.ds(pl.multiple_of(k * width, width), width)]
    added = jnp.dot(heads[0][...], w_mine, preferred_element_type=jnp.float32)
    for ref, weight in zip(heads[1:], weights):
        added += jnp.dot(ref[...], weight[...], preferred_element_type=jnp.float32)
    total[...] = added


def output_last_kernel(rows, total, heads, weight, *outs):
    added = total[...] + jnp.dot(heads[...], weight[...], preferred_element_type=jnp.float32)
    added = added.astype(outs[0].dtype)
    for number, out in enumerate(outs):
        out[:rows, :] = added[number * rows : (number + 1) * rows]
        out[rows:, :] = added[len(outs) * rows :]


def relay_kernel(*refs):
    blocks, outs = [refs[0], *put_back(OUTPUTS, refs[1:4])], refs[4:]
    c, z, _ = place()
    for slot, out in enumerate(outs):
        for mask, block in enumerate(blocks):

            @pl.when((c ^ z ^ slot) == mask)
            def _(out=out, block=block):
                out[...] = block[: out.shape[0], :]


def finish_kernel(*refs):
    parts, (prefill, decode) = [refs[0], *put_back(HEADS, refs[1:4])], refs[4:]
    _, z, _ = place()
    rows = prefill.shape[0] // 2
    for odd in range(2):
        total = parts[odd][...].astype(jnp.float32) + parts[odd + 2][...].astype(jnp.float32)
        total = total.astype(prefill.dtype)
        half = z % 2 if odd == 0 else 1 - z % 2
        prefill[pl.ds(pl.multiple_of(half * rows, rows), rows), :] = total[:rows]
        if odd == 0:
            decode[...] = total[rows : rows + decode.shape[0]]


def on_device_small(
    steps, tp, tokens, new_token_states, w_query, key_matrix, value_matrix, w_out, lengths, block_map
):
    bf16, f32 = jnp.bfloat16, jnp.float32
    rows = tokens.shape[0]
    half = rows // 2
    depth = w_query.shape[0]
    count = new_token_states.shape[0]
    pad = -(-count // ROW_TILE) * ROW_TILE
    q_width = w_query.shape[1]
    features = q_width + 2 * key_matrix.shape[1]
    width = w_out.shape[1] // 2
    all_rows = steps * rows + pad

    def to_core(value):
        return lax.ppermute(value, "tp", [(i, i ^ 1) for i in range(tp)])

    def to_chip(value, step):
        return lax.ppermute(value, "tp", [(i, i ^ (2 * step)) for i in range(tp)])

    def to_partners(values):
        return [
            lax.ppermute(value, "ctx", [(i, i ^ mask) for i in range(steps)])
            for mask, value in enumerate(values, 1)
        ]

    def call(kernel, name, inputs, shapes, scratch=(), spaces=None):
        return pl.pallas_call(
            kernel,
            out_shape=[jax.ShapeDtypeStruct(shape, kind) for shape, kind in shapes],
            in_specs=spaces or [vmem()] * len(inputs),
            out_specs=[vmem()] * len(shapes),
            scratch_shapes=list(scratch),
            compiler_params=pltpu.CompilerParams(vmem_limit_bytes=VMEM_BYTES),
            name=name,
        )(*inputs)

    c, _, k = place()
    sent = [
        lax.dynamic_slice(tokens, (k * half, (c ^ mask) * depth), (half, depth))
        for mask in range(1, steps)
    ]
    own = lax.dynamic_slice_in_dim(tokens, c * depth, depth, 1)
    new_columns = lax.dynamic_slice_in_dim(new_token_states, c * depth, depth, 1)
    mine = to_partners(sent)
    mine[2], own = lax.optimization_barrier((mine[2], own))
    theirs = [to_core(value) for value in mine]

    w_mine = lax.dynamic_slice_in_dim(w_out, k * width, width, 1)
    w_theirs = lax.dynamic_slice_in_dim(w_out, (1 - k) * width, width, 1)
    w_next = to_chip(w_mine, 1)

    part = (rows + pad, features)
    weights = (w_query, key_matrix, value_matrix)
    (both,) = call(
        project_both_kernel,
        "project_both",
        (mine[2], theirs[2], new_columns, *weights),
        [(part, bf16)],
        [pltpu.VMEM((rows + 2 * ROW_TILE, depth), bf16)],
    )
    new_columns, w_next = lax.optimization_barrier((new_columns, w_next))
    own_part, first, second = call(
        project_kernel,
        "project",
        (own, *mine[:2], *theirs[:2], new_columns, *weights),
        [(part, f32)] + [(part, bf16)] * 2,
        [pltpu.VMEM((3 * rows + 2 * ROW_TILE, depth), bf16)],
    )

    w_later, _ = lax.optimization_barrier((w_theirs, both))
    w_next_other = lax.ppermute(w_later, "tp", [(i, i ^ 3) for i in range(tp)])

    first, second, both = to_partners([first, second, both])
    (total,) = call(add_kernel, "add_both", (own_part, both), [(part, f32)])
    held, new = call(
        add_last_kernel,
        "add_last",
        (total, first, second),
        [((rows, features), bf16), ((pad, features), bf16)],
    )

    gathered = [held, *in_order(KEYS, to_partners([held] * (steps - 1)))]
    new, w_next_other = lax.optimization_barrier((new, w_next_other))
    block_rows = steps * rows // block_map.shape[0]

    keys = steps * rows
    masks = call(
        functools.partial(mask_kernel, block_rows),
        "mask",
        (block_map, lengths),
        [((keys, keys), f32), ((2 * ROW_TILE, keys), f32)],
        spaces=[smem()] * 2,
    )

    def attend(sent, *extra):
        (attended,) = call(
            functools.partial(attend_kernel, sent, block_rows, 1.0 / math.sqrt(HEAD_SIZE)),
            "attend_sent" if sent else "attend_kept",
            (*gathered, new, *masks, *extra),
            [((keys // 2 + pad, q_width), bf16)],
        )
        return attended

    sent = attend(True)
    got = to_chip(sent, 1)
    kept = attend(False, sent)
    w_last, _ = lax.optimization_barrier((w_theirs, kept))
    w_other = to_core(w_last)

    block = (block_rows + pad, width)
    (total,) = call(
        output_kernel,
        "project_out",
        (kept, to_core(kept), got, w_out, w_other, w_next),
        [((kept.shape[0], width), f32)],
    )
    outs = call(
        functools.partial(output_last_kernel, block_rows),
        "project_last",
        (total, to_core(got), w_next_other),
        [(block, bf16)] * steps,
    )

    slots = call(
        relay_kernel,
        "relay",
        [outs[0], *in_order(OUTPUTS, to_partners(outs[1:]))],
        [(block if i % 2 == 0 else (block_rows, width), bf16) for i in range(steps)],
    )
    arrived = [to_chip(slot, step) for step, slot in enumerate(slots[1:], 1)]
    slots = [slots[0], *in_order(HEADS, arrived)]
    return tuple(
        call(finish_kernel, "finish", slots, [((rows, width), bf16), ((count, width), bf16)])
    )


floor_value = -1e30


def initial_positions(block_map, first_row, row_count, block_rows):
    row_ids = first_row + jnp.arange(row_count, dtype=jnp.int32)
    block_ids = row_ids // block_rows
    table_ids = jnp.arange(block_map.shape[0], dtype=jnp.int32)
    mapped = jnp.sum(
        jnp.where(block_ids[:, None] == table_ids[None, :], block_map[None, :], 0), axis=1
    )
    return mapped * block_rows + row_ids % block_rows


def request_index(positions, request_ends):
    return jnp.sum((positions[:, None] >= request_ends[None, :]).astype(jnp.int32), axis=1)


def round_weights(weights):
    rounded = weights.astype(jnp.bfloat16)
    rounded = lax.optimization_barrier(rounded)
    return rounded.astype(jnp.float32)


def softmax_parts(
    dec_heads, projected_key_rows, projected_value_rows, owned, kv_heads, head_dim, score_scale
):
    row_count = projected_key_rows.shape[0]
    scores = (
        jnp.einsum(
            "rgjd,tgd->rgjt",
            dec_heads,
            projected_key_rows.reshape(row_count, kv_heads, head_dim),
            preferred_element_type=jnp.float32,
        )
        * score_scale
    )
    scores = jnp.where(owned, scores, floor_value)
    part_peak = jnp.max(scores, axis=3)
    weights = jnp.where(owned, jnp.exp(scores - part_peak[..., None]), 0.0)
    part_total = jnp.sum(weights, axis=3)
    part_mixed = jnp.einsum(
        "rgjt,tgd->rgjd",
        weights.astype(jnp.bfloat16),
        projected_value_rows.reshape(row_count, kv_heads, head_dim),
        preferred_element_type=jnp.float32,
    )
    return (part_peak, part_total, part_mixed)


def on_device_large(
    tokens, new_token_states, w_query, key_matrix, value_matrix, w_out, lengths, block_map
):
    local_rows = tokens.shape[0]
    block_rows = local_rows // 2
    request_count = new_token_states.shape[0]
    head_dim = HEAD_SIZE
    query_width = w_query.shape[1]
    kv_width = key_matrix.shape[1]
    kv_heads = kv_width // head_dim
    query_group_count = query_width // kv_width
    score_scale = 1.0 / math.sqrt(head_dim)
    device = lax.axis_index("ctx")
    request_ends = jnp.cumsum(lengths)
    inputs = jnp.concatenate([tokens, new_token_states], axis=0)
    shard_pieces = (
        lax.all_gather(w_query, "ctx", axis=0, tiled=True),
        lax.all_gather(key_matrix, "ctx", axis=0, tiled=True),
        lax.all_gather(value_matrix, "ctx", axis=0, tiled=True),
    )
    query_all, key_all, value_all = tuple(
        (jnp.dot(inputs, weight, preferred_element_type=jnp.float32) for weight in shard_pieces)
    )
    query_all = query_all.astype(jnp.bfloat16)
    key_all = key_all.astype(jnp.bfloat16)
    value_all = value_all.astype(jnp.bfloat16)
    local_query = query_all[:local_rows]
    local_keys = key_all[:local_rows]
    local_values = value_all[:local_rows]
    dec_query = query_all[local_rows:]
    decode_key_rows = key_all[local_rows:]
    decode_value_rows = value_all[local_rows:]
    token_pos = initial_positions(block_map, device * local_rows, local_rows, block_rows)
    token_request = request_index(token_pos, request_ends)
    query_heads = local_query.reshape(local_rows, kv_heads, query_group_count, head_dim)

    def attend(running, shard_pieces, first_row):
        peak_run, total_run, mixed_run = running
        key_piece, value_piece = shard_pieces
        row_count = key_piece.shape[0]
        key_pos = initial_positions(block_map, first_row, row_count, block_rows)
        key_request = request_index(key_pos, request_ends)
        allowed = (key_request[None, :] == token_request[:, None]) & (
            key_pos[None, :] <= token_pos[:, None]
        )
        scores = (
            jnp.einsum(
                "tgjd,kgd->gjtk",
                query_heads,
                key_piece.reshape(row_count, kv_heads, head_dim),
                preferred_element_type=jnp.float32,
            )
            * score_scale
        )
        scores = jnp.where(allowed, scores, floor_value)
        peak_new = jnp.maximum(peak_run, jnp.max(scores, axis=3))
        weights = jnp.where(allowed, jnp.exp(scores - peak_new[..., None]), 0.0)
        rescale = jnp.exp(peak_run - peak_new)
        total_new = total_run * rescale + jnp.sum(weights, axis=3)
        mixed_new = mixed_run * rescale[..., None] + jnp.einsum(
            "gjtk,kgd->gjtd",
            weights.astype(jnp.bfloat16),
            value_piece.reshape(row_count, kv_heads, head_dim),
            preferred_element_type=jnp.float32,
        )
        return (peak_new, total_new, mixed_new)

    start_state = (
        jnp.full((kv_heads, query_group_count, local_rows), floor_value, jnp.float32),
        jnp.zeros((kv_heads, query_group_count, local_rows), jnp.float32),
        jnp.zeros((kv_heads, query_group_count, local_rows, head_dim), jnp.float32),
    )
    dec_heads = dec_query.reshape(request_count, kv_heads, query_group_count, head_dim)
    request_ids = jnp.arange(request_count, dtype=jnp.int32)
    cache_keys, cache_values = (
        lax.all_gather(local_keys, "ctx", axis=0, tiled=True),
        lax.all_gather(local_values, "ctx", axis=0, tiled=True),
    )
    total_rows = cache_keys.shape[0]
    shard_count = total_rows // local_rows
    limit = max(1, 1024 // local_rows)
    step_rows = local_rows * math.gcd(shard_count, 1 << limit.bit_length() - 1)

    def key_step(running, step_index):
        first_row = step_index * step_rows
        pieces = (
            lax.dynamic_slice_in_dim(cache_keys, first_row, step_rows, 0),
            lax.dynamic_slice_in_dim(cache_values, first_row, step_rows, 0),
        )
        return (attend(running, pieces, first_row), None)

    final_state, unused = lax.scan(
        key_step, start_state, jnp.arange(total_rows // step_rows, dtype=jnp.int32)
    )
    peak_run, total_run, mixed_run = final_state
    cache_pos = (
        block_map[:, None] * block_rows + jnp.arange(block_rows, dtype=jnp.int32)[None, :]
    ).reshape(total_rows)
    cache_request = request_index(cache_pos, request_ends)
    owned = (cache_request[None, :] == request_ids[:, None])[:, None, None, :]
    cache_peak, cache_total, cache_mixed = softmax_parts(
        dec_heads, cache_keys, cache_values, owned, kv_heads, head_dim, score_scale
    )
    attended = (
        (mixed_run / total_run[..., None]).transpose(2, 0, 1, 3).reshape(local_rows, query_width)
    )
    attended = attended.astype(jnp.bfloat16)
    own_keys = decode_key_rows.reshape(request_count, kv_heads, 1, head_dim).astype(jnp.float32)
    own_values = decode_value_rows.reshape(request_count, kv_heads, 1, head_dim).astype(jnp.float32)
    self_scores = jnp.sum(dec_heads.astype(jnp.float32) * own_keys, axis=3) * score_scale
    peak_all = jnp.maximum(cache_peak, self_scores)
    rescale = jnp.exp(cache_peak - peak_all)
    self_weights = jnp.exp(self_scores - peak_all)
    dec_total = cache_total * rescale + self_weights
    dec_mixed = (
        cache_mixed * rescale[..., None] + round_weights(self_weights)[..., None] * own_values
    )
    dec_attn = (
        (dec_mixed / dec_total[..., None]).reshape(request_count, query_width).astype(jnp.bfloat16)
    )
    attended_all = jnp.concatenate([attended, dec_attn], axis=0)
    head_block = lax.all_gather(w_out, "ctx", axis=1, tiled=True)
    column_block = lax.all_to_all(head_block, "tp", split_axis=1, concat_axis=0, tiled=True)
    summed_rows = jnp.dot(
        lax.all_gather(attended_all, "tp", axis=1, tiled=True),
        column_block,
        preferred_element_type=jnp.float32,
    )
    summed_rows = summed_rows.astype(jnp.bfloat16)
    return (summed_rows[:local_rows], summed_rows[local_rows:])

def solution(mesh):
    steps, tp = mesh.shape["ctx"], mesh.shape["tp"]

    def on_device(tokens, *rest):
        one_head = rest[2].shape[1] == HEAD_SIZE
        two_blocks = rest[-1].shape[0] == 2 * steps
        few = tokens.shape[0] * steps <= 1024
        small = steps == 4 and tp == 8 and one_head and two_blocks and few
        if small:
            return on_device_small(steps, tp, tokens, *rest)
        return on_device_large(tokens, *rest)

    return jax.shard_map(
        on_device,
        mesh=mesh,
        in_specs=(
            P("ctx", None),
            P(),
            P("ctx", "tp"),
            P("ctx", "tp"),
            P("ctx", "tp"),
            P("tp", "ctx"),
            P(),
            P(),
        ),
        out_specs=(P("ctx", "tp"), P(None, "tp")),
        check_vma=False,
    )
```
